32 devices in a mesh: dp: 4 (over x, core), seq: 8 (over z, y).
Axes of the slice: x: 2, y: 2, z: 4, core: 2. Of those that a mesh axis runs over, the one named last changes fastest.
Arguments:
- tokens: bfloat16 [6144, 2048], P(('dp', 'seq')), may hold values from -6 to 6
- lengths: int32 [4, 8], P('dp'), may hold values from 0 to 1536, as said below
- cotangent: bfloat16 [6144, 2048], P(('dp', 'seq')), may hold values from -6 to 6
- norm_one: bfloat16 [2048], P(('dp', 'seq')), may hold values from 0.5 to 1.5
- query_down: bfloat16 [2048, 1024], P(('dp', 'seq')), may hold values from -0.125 to 0.125
- query_gain: bfloat16 [1024], P(('dp', 'seq')), may hold values from 0.5 to 1.5
- query_up: bfloat16 [1024, 4096], P(('dp', 'seq')), may hold values from -0.1875 to 0.1875
- key_proj: bfloat16 [2048, 256], P(('dp', 'seq')), may hold values from -0.125 to 0.125
- value_proj: bfloat16 [2048, 256], P(('dp', 'seq')), may hold values from -0.125 to 0.125
- out_proj: bfloat16 [4096, 2048], P(('dp', 'seq')), may hold values from -0.75 to 0.75
- norm_two: bfloat16 [2048], P(('dp', 'seq')), may hold values from 0.5 to 1.5
- gate_proj: bfloat16 [2048, 5632], P(('dp', 'seq')), may hold values from -0.125 to 0.125
- up_proj: bfloat16 [2048, 5632], P(('dp', 'seq')), may hold values from -0.125 to 0.125
- down_proj: bfloat16 [5632, 2048], P(('dp', 'seq')), may hold values from -0.078125 to 0.078125
Outputs:
- output: bfloat16 [6144, 2048], P(('dp', 'seq'))
- grad_tokens: float32 [6144, 2048], P(('dp', 'seq'))
- grad_norm_one: float32 [2048], P(('dp', 'seq'))
- grad_query_down: float32 [2048, 1024], P(('dp', 'seq'))
- grad_query_gain: float32 [1024], P(('dp', 'seq'))
- grad_query_up: float32 [1024, 4096], P(('dp', 'seq'))
- grad_key_proj: float32 [2048, 256], P(('dp', 'seq'))
- grad_value_proj: float32 [2048, 256], P(('dp', 'seq'))
- grad_out_proj: float32 [4096, 2048], P(('dp', 'seq'))
- grad_norm_two: float32 [2048], P(('dp', 'seq'))
- grad_gate_proj: float32 [2048, 5632], P(('dp', 'seq'))
- grad_up_proj: float32 [2048, 5632], P(('dp', 'seq'))
- grad_down_proj: float32 [5632, 2048], P(('dp', 'seq'))
The draws below stay inside these ranges and needn't reach their ends.
Inputs may be any that keep to these rules, and one draw needn't show every extreme that they name: In one row, drawn from the seed, a single document fills all 1536 slots and the other entries are 0; every other row is filled to between 7/10 and 9/10 of its slots, the rest being padding, with documents of uneven lengths.
All inputs are finite; a program needn't handle non-finite values.
Results may differ from the reference program's by a relative error of at most 0.017.
Values may be sent and summed in bfloat16 or wider, within the bound.
A program may use at most 512 MiB of HBM per device.

```python
import math
import jax
import jax.numpy as jnp
from jax import lax

D = 2048
QL = 1024
H = 16
HD = 256
FF = 5632
SEGS = 8
ROW = 1536
ROWS = 4
TOKENS = 6144


def draw_lengths(key, part):
    key = jax.random.fold_in(key, 11)
    subkeys = jax.random.split(key, 3)
    whole_row = jax.random.randint(subkeys[0], (), 0, ROWS)
    row_ids = jnp.arange(ROWS, dtype=jnp.int32)
    divisors = jax.random.randint(subkeys[1], (ROWS, SEGS), 1, 25)
    raw_docs = jnp.maximum(ROW // divisors, 1).astype(jnp.int32)
    target = (ROW * 7 // 10 + jax.random.randint(subkeys[2], (ROWS, 1), 0, ROW // 5 + 1)).astype(jnp.int32)
    doc_ends = jnp.cumsum(raw_docs, axis=1).astype(jnp.int32)
    doc_begins = doc_ends - raw_docs
    kept_docs = jnp.where(doc_begins < target, jnp.minimum(raw_docs, target - doc_begins), 0).astype(jnp.int32)
    shortfall = target[:, 0] - jnp.sum(kept_docs, axis=1).astype(jnp.int32)
    kept_docs = kept_docs.at[:, SEGS - 1].add(shortfall)
    whole_docs = jnp.zeros((ROWS, SEGS), jnp.int32).at[:, 0].set(ROW)
    return jnp.where(row_ids[:, None] == whole_row, whole_docs, kept_docs).astype(jnp.int32)


def shard_levels(rng, dims, cuts, least, high):
    level, own = 1.0, jax.random.fold_in(rng, 6)
    for position, parts in cuts:
        draws = jnp.exp(jax.random.uniform(jax.random.fold_in(own, position), (parts,), jnp.float32, least / len(cuts), high / len(cuts)))
        level = level * jnp.repeat(draws, dims[position] // parts).reshape([-1 if axis == position else 1 for axis in range(len(dims))])
    return level


def noise(own_key, shape, scale, reach, pieces=(), kind=jnp.bfloat16):
    loudness = shard_levels(own_key, shape, pieces, -0.22, 0.18) if pieces else 1.0
    array = jax.random.normal(own_key, shape, jnp.float32) * scale * loudness
    return jnp.minimum(jnp.maximum(array, -reach), reach).astype(kind)


def setup_inputs(seed: int = 0) -> dict:
    streams_of = jax.random.split(jax.random.key(seed), 15)
    tokens = noise(streams_of[0], (TOKENS, D), 1.0, 6.0, ((0, 32),))
    lengths = draw_lengths(jax.random.fold_in(streams_of[14], 71), 0)
    cotangent = noise(streams_of[2], (TOKENS, D), 1.0, 6.0, ((0, 32),))
    norm_one = jnp.clip(1.0 + 0.1 * jax.random.normal(streams_of[3], (D,), jnp.float32), 0.5, 1.5).astype(jnp.bfloat16)
    query_down = noise(streams_of[4], (D, QL), D ** -0.5, 0.125, ((0, 32),))
    query_gain = jnp.clip(1.0 + 0.1 * jax.random.normal(streams_of[5], (QL,), jnp.float32), 0.5, 1.5).astype(jnp.bfloat16)
    query_up = noise(streams_of[6], (QL, H * HD), QL ** -0.5, 0.1875, ((0, 32),))
    key_proj = noise(streams_of[7], (D, HD), D ** -0.5, 0.125, ((0, 32),))
    value_proj = noise(streams_of[8], (D, HD), D ** -0.5, 0.125, ((0, 32),))
    out_proj = noise(streams_of[9], (H * HD, D), (H * HD // 64) ** -0.5, 0.75, ((0, 32),))
    norm_two = jnp.clip(1.0 + 0.1 * jax.random.normal(streams_of[10], (D,), jnp.float32), 0.5, 1.5).astype(jnp.bfloat16)
    gate_proj = noise(streams_of[11], (D, FF), D ** -0.5, 0.125, ((0, 32),))
    up_proj = noise(streams_of[12], (D, FF), D ** -0.5, 0.125, ((0, 32),))
    down_proj = noise(streams_of[13], (FF, D), FF ** -0.5, 0.078125, ((0, 32),))
    return {"tokens": tokens, "lengths": lengths, "cotangent": cotangent, "norm_one": norm_one, "query_down": query_down, "query_gain": query_gain, "query_up": query_up, "key_proj": key_proj, "value_proj": value_proj, "out_proj": out_proj, "norm_two": norm_two, "gate_proj": gate_proj, "up_proj": up_proj, "down_proj": down_proj}


norm_eps = 1e-05
masked_value = -1e+30

@jax.custom_vjp
def low(v):
    return lax.optimization_barrier(v.astype(jnp.bfloat16)).astype(jnp.float32)

@jax.custom_vjp
def low_back(v):
    return v

def low_keep(v):
    return (low(v), None)

def low_pass(kept, grad):
    return (grad,)

def back_keep(v):
    return (v, None)

def back_low(kept, grad):
    return (low(grad),)
low.defvjp(low_keep, low_pass)
low_back.defvjp(back_keep, back_low)

def highest(left, right):
    return jnp.dot(left, right, precision=lax.Precision.HIGHEST)

def rms_scale(values):
    return lax.rsqrt(lax.optimization_barrier(jnp.mean(values * values, axis=-1, keepdims=True)) + norm_eps)

def rotate(values, cosine, sine):
    half_width = values.shape[-1] // 2
    lower = values[..., :half_width]
    upper = values[..., half_width:]
    return jnp.concatenate([lower * cosine - upper * sine, upper * cosine + lower * sine], axis=-1)

def rope_tables(positions, width):
    half_width = width // 2
    freq_rates = jnp.exp(jnp.arange(half_width, dtype=jnp.float32) * (-math.log(10000.0) / half_width))
    phases = positions.astype(jnp.float32)[..., None] * freq_rates
    return (jnp.cos(phases), jnp.sin(phases))

def doc_layout(row_lengths, row_len):
    places = jnp.arange(row_len, dtype=jnp.int32)
    doc_ends = jnp.cumsum(row_lengths, dtype=jnp.int32)
    doc_starts = doc_ends - row_lengths
    seg_ids = lax.optimization_barrier(jnp.sum((places[:, None] >= doc_ends[None, :]).astype(jnp.int32), axis=1)).astype(jnp.int32)
    filled = doc_ends[-1]
    begins = jnp.concatenate([doc_starts, filled[None]]).astype(jnp.int32)
    chosen = seg_ids[:, None] == jnp.arange(begins.shape[0], dtype=jnp.int32)[None, :]
    offsets = lax.optimization_barrier(jnp.sum(jnp.where(chosen, begins[None, :], 0), axis=1)).astype(jnp.int32)
    return (seg_ids, places - offsets, places < filled)

def head_attend(query_head, keys, values, allowed):
    scores = low_back(highest(query_head, keys.T) * HD ** (-0.5))
    masked = jnp.where(allowed, scores, masked_value)
    row_top = lax.optimization_barrier(jnp.max(masked, axis=-1, keepdims=True))
    weights = jnp.where(allowed, jnp.exp(masked - row_top), 0.0)
    softmax_weights = low(weights / lax.optimization_barrier(jnp.sum(weights, axis=-1, keepdims=True)))
    return highest(softmax_weights, values)

def layer_row(params, carried):
    norm_one, query_down, query_gain, query_up, key_proj, value_proj, out_proj, norm_two, gate_proj, up_proj, down_proj = params
    row_in, seg_ids, is_valid, cosine, sine = carried
    hidden = low(row_in * rms_scale(row_in) * norm_one)
    latent = low_back(highest(hidden, query_down))
    latent_low = low(latent * rms_scale(latent) * query_gain)
    query_raw = low_back(highest(latent_low, query_up)).reshape(ROW, H, HD)
    query = low(rotate(query_raw, cosine[:, None, :], sine[:, None, :]))
    keys = low(rotate(low_back(highest(hidden, key_proj)), cosine, sine))
    values = low(low_back(highest(hidden, value_proj)))
    places = jnp.arange(ROW, dtype=jnp.int32)
    allowed = (seg_ids[:, None] == seg_ids[None, :]) & (places[None, :] <= places[:, None]) & (is_valid[None, :] | (places[None, :] == places[:, None]))
    head_fn = jax.checkpoint(lambda query_head: head_attend(query_head, keys, values, allowed))
    attended = lax.map(head_fn, jnp.transpose(query, (1, 0, 2)))
    mixed = low(low_back(jnp.transpose(attended, (1, 0, 2)).reshape(ROW, H * HD)))
    resid = row_in + low_back(highest(mixed, out_proj))
    hidden_two = low(resid * rms_scale(resid) * norm_two)
    gate = low_back(highest(hidden_two, gate_proj))
    upward = low_back(highest(hidden_two, up_proj))
    inner = low(jax.nn.silu(gate) * upward)
    return resid + low_back(highest(inner, down_proj))

def reference(tokens, lengths, cotangent, norm_one, query_down, query_gain, query_up, key_proj, value_proj, out_proj, norm_two, gate_proj, up_proj, down_proj):
    seg_ids, positions, is_valid = jax.vmap(lambda row_lengths: doc_layout(row_lengths, ROW))(lengths)
    cosines, sines = rope_tables(positions, HD)
    params = tuple((weight.astype(jnp.float32) for weight in (norm_one, query_down, query_gain, query_up, key_proj, value_proj, out_proj, norm_two, gate_proj, up_proj, down_proj)))
    inputs = tokens.astype(jnp.float32)

    def forward(layer_in, layer_params):
        rows_in = layer_in.reshape(ROWS, ROW, D)
        row_fn = jax.checkpoint(lambda carried: layer_row(layer_params, carried))
        results = lax.map(row_fn, (rows_in, seg_ids, is_valid, cosines, sines))
        return results.reshape(TOKENS, D)
    result, pullback = jax.vjp(forward, inputs, params)
    grad_in, grad_params = pullback(cotangent.astype(jnp.float32))
    return (result.astype(jnp.bfloat16), grad_in, grad_params[0], grad_params[1], grad_params[2], grad_params[3], grad_params[4], grad_params[5], grad_params[6], grad_params[7], grad_params[8], grad_params[9], grad_params[10])
```

```python
import functools
import math

import jax
import jax.numpy as jnp
from jax import lax
from jax.experimental import pallas as pl
from jax.experimental.pallas import tpu as pltpu
from jax.sharding import Mesh, PartitionSpec as P

norm_eps = 1e-05
masked_value = -1e30
every = ("x", "c", "h", "l", "y")
group = ("c", "l", "y")
low = jnp.bfloat16
wide = jnp.float32


def rms_scale(values):
    return lax.rsqrt(jnp.mean(values * values, axis=-1, keepdims=True) + norm_eps)


def rotate(values, cosine, sine):
    half = values.shape[-1] // 2
    a, b = values[..., :half], values[..., half:]
    return jnp.concatenate([a * cosine - b * sine, b * cosine + a * sine], axis=-1)


def rotate_back(values, cosine, sine):
    half = values.shape[-1] // 2
    a, b = values[..., :half], values[..., half:]
    return jnp.concatenate([a * cosine + b * sine, b * cosine - a * sine], axis=-1)


def norm_back(incoming, source, scale, gain):
    weighted = incoming * gain
    source_grad = scale * weighted - source * (scale * scale * scale) * jnp.mean(
        weighted * source, axis=-1, keepdims=True
    )
    return source_grad, jnp.sum(incoming * source * scale, axis=0)


def dot(left, right, out=wide):
    return jnp.dot(left, right, preferred_element_type=wide).astype(out)


def outer_sum(left, right, out=wide):
    return lax.dot_general(
        left, right, (((0,), (0,)), ((), ())), preferred_element_type=wide
    ).astype(out)


def times_transposed(left, right, out=wide):
    return lax.dot_general(
        left, right, (((1,), (1,)), ((), ())), preferred_element_type=wide
    ).astype(out)


def pick(array, index, axis=0):
    return lax.dynamic_index_in_dim(array, index, axis, keepdims=False)


def half_of(array, index):
    size = array.shape[0] // 2
    return lax.dynamic_slice_in_dim(array, index * size, size)


def place_kernel(starts, table_ref, *refs):
    out_ref = refs[-1]
    step = pl.program_id(0)
    for ref, (begin, end) in zip(refs[:-1], starts):

        @pl.when((step >= begin) & (step < end))
        def _():
            out_ref[...] = ref[...]


def place(pieces, table):
    rows, columns = pieces[0].shape[1:]
    starts, total = [], 0
    for piece in pieces:
        starts.append((total, total + piece.shape[0]))
        total += piece.shape[0]

    def source(begin, end):
        return pl.BlockSpec(
            (1, rows, columns), lambda g, t: (jnp.clip(g - begin, 0, end - begin - 1), 0, 0)
        )

    size = total * rows * columns * pieces[0].dtype.itemsize
    return pl.pallas_call(
        functools.partial(place_kernel, starts),
        grid_spec=pltpu.PrefetchScalarGridSpec(
            num_scalar_prefetch=1,
            grid=(total,),
            in_specs=[source(*pair) for pair in starts],
            out_specs=pl.BlockSpec((1, rows, columns), lambda g, t: (t[g], 0, 0)),
        ),
        out_shape=jax.ShapeDtypeStruct((total, rows, columns), pieces[0].dtype),
        compiler_params=pltpu.CompilerParams(vmem_limit_bytes=48 * 1024 * 1024),
        cost_estimate=pl.CostEstimate(flops=0, bytes_accessed=2 * size, transcendentals=0),
        name="place",
    )(jnp.stack(table).astype(jnp.int32), *pieces)


def flip(value, axis):
    return lax.ppermute(value, axis, [(0, 1), (1, 0)])


def send(value, offsets):
    return lax.ppermute(value, group, [(i, i ^ offsets[i // 4]) for i in range(8)])


def swap_home(value):
    moved = lax.ppermute(value, ("c", "h"), [(1, 2), (2, 1)])
    return jnp.where(lax.axis_index("c") == lax.axis_index("h"), value, moved)


def group_place():
    return (
        lax.axis_index("c") * lax.axis_size("l") + lax.axis_index("l")
    ) * 2 + lax.axis_index("y")


def gather_row(value):
    if lax.axis_size("l") != 2:
        return lax.all_gather(value, group, axis=0, tiled=True)
    value = value[None]
    me = group_place()
    core = lax.axis_index("c")
    first, second = 1 + core, 2 - core
    near = send(value, (1, 2))
    side = send(value, (2, 1))
    far = send(near, (2, 1))
    pieces = [value, near, side, far]
    pieces += [send(piece, (4, 4)) for piece in pieces]
    table = [me, me ^ first, me ^ second, me ^ 3]
    table += [me ^ 4, me ^ 4 ^ second, me ^ 4 ^ first, me ^ 7]
    return place(pieces, table).reshape(-1, value.shape[-1])


def scatter_row(make):
    core = lax.axis_index("c")
    if lax.axis_size("l") != 2:
        terms = jnp.concatenate([make(0), make(1)], axis=0)
        return lax.psum_scatter(terms.astype(wide), group, scatter_dimension=0, tiled=True)
    theirs = make(1 - core)
    moved = flip(theirs, "c")
    own = make(core)
    width = own.shape[-1]
    own = own.reshape(4, -1, width)
    moved = moved.reshape(own.shape)
    me = lax.axis_index("l") * 2 + lax.axis_index("y")
    first, second = 1 + core, 2 - core

    def block(index):
        return pick(own, index).astype(wide) + pick(moved, index).astype(wide)

    far = send(block(me ^ 3).astype(low), (2, 1))
    side = send(block(me ^ second).astype(low), (2, 1))
    near = send((block(me ^ first) + far.astype(wide)).astype(low), (1, 2))
    return block(me) + side.astype(wide) + near.astype(wide)


def all_to_all_row(blocks):
    if lax.axis_size("l") != 2:
        return lax.all_to_all(blocks, group, 0, 0, tiled=True)
    me = group_place()
    pieces, table = [], []
    for k in range(8):
        piece = lax.dynamic_slice_in_dim(blocks, me ^ k, 1)
        pieces.append(piece if k == 0 else send(piece, (k, k)))
        table.append(me ^ k)
    return place(pieces, table)


def gather_columns(value):
    if lax.axis_size("x") != 2:
        return lax.all_gather(lax.all_gather(value, "h", axis=0), "x", axis=0)
    x, h = lax.axis_index("x"), lax.axis_index("h")
    other = flip(value, "h")
    across, corner = flip(value, "x"), flip(other, "x")
    count = value.shape[0]
    table = []
    for place_x, place_h in ((x, h), (x, 1 - h), (1 - x, h), (1 - x, 1 - h)):
        table += [(place_x * 2 + place_h) * count + i for i in range(count)]
    return place([value, other, across, corner], table).reshape((2, 2) + value.shape)


def sum_axis(terms, axis, dim):
    if lax.axis_size(axis) != 2:
        moved = jnp.moveaxis(terms, dim, 0).astype(wide)
        return lax.psum_scatter(moved, axis, scatter_dimension=0, tiled=False).astype(low)
    me = lax.axis_index(axis)
    came = flip(pick(terms, 1 - me, dim), axis)
    return (pick(terms, me, dim).astype(wide) + came.astype(wide)).astype(low)


def first_allowed(ends_ref, count, places):
    start = jnp.zeros_like(places)
    for j in range(count):
        end = ends_ref[j]
        start = jnp.where(places >= end, end, start)
    return jnp.where(places >= ends_ref[count - 1], places, start)


def tile_mask(lows, row_start, column_start, tile):
    rows = row_start + lax.broadcasted_iota(jnp.int32, (tile, tile), 0)
    columns = column_start + lax.broadcasted_iota(jnp.int32, (tile, tile), 1)
    return (columns >= lows) & (columns <= rows)


def contract(left, right, dims):
    return lax.dot_general(left, right, (dims, ((), ())), preferred_element_type=wide)


def attend_kernel(heads, tile, ends_ref, q_ref, k_ref, v_ref, o_ref, log_ref):
    step = pl.program_id(0)
    width = k_ref.shape[1]
    count = ends_ref.shape[0]
    row_start = step * tile
    lows = first_allowed(ends_ref, count, row_start + lax.broadcasted_iota(jnp.int32, (tile, 1), 0))
    begin = first_allowed(ends_ref, count, row_start) // tile
    queries = [q_ref[:, j * width : (j + 1) * width] for j in range(heads)]

    def body(index, carry):
        at = pl.multiple_of(index * tile, tile)
        keys, values = k_ref[pl.ds(at, tile), :], v_ref[pl.ds(at, tile), :]
        mask = tile_mask(lows, row_start, at, tile)
        out = []
        for j in range(heads):
            top, total, acc = carry[j]
            scores = jnp.where(mask, contract(queries[j], keys, ((1,), (1,))), masked_value)
            new_top = jnp.maximum(top, jnp.max(scores, axis=1, keepdims=True))
            weights = jnp.where(mask, jnp.exp(scores - new_top), 0.0)
            shrink = jnp.exp(top - new_top)
            total = total * shrink + jnp.sum(weights, axis=1, keepdims=True)
            acc = acc * shrink + contract(weights.astype(low), values, ((1,), (0,)))
            out.append((new_top, total, acc))
        return tuple(out)

    start = tuple(
        (
            jnp.full((tile, 1), masked_value, wide),
            jnp.zeros((tile, 1), wide),
            jnp.zeros((tile, width), wide),
        )
        for _ in range(heads)
    )
    for j, (top, total, acc) in enumerate(lax.fori_loop(begin, step + 1, body, start)):
        o_ref[:, j * width : (j + 1) * width] = (acc / total).astype(low)
        log_ref[j] = jnp.broadcast_to(top + jnp.log(total), (tile, 128))


def attend_back_kernel(
    heads, tile, scale, ends_ref, q_ref, g_ref, o_ref, k_ref, v_ref, log_ref, cos_ref, sin_ref,
    dq_ref, dkv_ref,
):
    step = pl.program_id(0)
    width = k_ref.shape[1]
    count = ends_ref.shape[0]
    row_start = step * tile
    lows = first_allowed(ends_ref, count, row_start + lax.broadcasted_iota(jnp.int32, (tile, 1), 0))
    begin = first_allowed(ends_ref, count, row_start) // tile

    @pl.when(step == 0)
    def _():
        dkv_ref[...] = jnp.zeros_like(dkv_ref)

    parts = [slice(j * width, (j + 1) * width) for j in range(heads)]
    queries = [q_ref[:, part] for part in parts]
    grads = [g_ref[:, part] for part in parts]
    deltas = [
        jnp.sum(g.astype(wide) * o_ref[:, part].astype(wide), axis=1, keepdims=True)
        for g, part in zip(grads, parts)
    ]
    logs = [log_ref[j][:, :1] for j in range(heads)]

    def body(index, carry):
        at = pl.multiple_of(index * tile, tile)
        keys, values = k_ref[pl.ds(at, tile), :], v_ref[pl.ds(at, tile), :]
        mask = tile_mask(lows, row_start, at, tile)
        out = []
        dkeys, dvalues = 0.0, 0.0
        for j in range(heads):
            scores = contract(queries[j], keys, ((1,), (1,)))
            weights = jnp.where(mask, jnp.exp(scores - logs[j]), 0.0)
            dprob = contract(grads[j], values, ((1,), (1,)))
            dscore = (weights * (dprob - deltas[j])).astype(low)
            dvalues = dvalues + contract(weights.astype(low), grads[j], ((0,), (0,)))
            dkeys = dkeys + contract(dscore, queries[j], ((0,), (0,)))
            out.append(carry[j] + contract(dscore, keys, ((1,), (0,))))
        dkv_ref[pl.ds(at, tile), :width] += dkeys
        dkv_ref[pl.ds(at, tile), width:] += dvalues
        return tuple(out)

    start = tuple(jnp.zeros((tile, width), wide) for _ in range(heads))
    half = width // 2
    cosine, sine = cos_ref[...], sin_ref[...]
    for part, acc in zip(parts, lax.fori_loop(begin, step + 1, body, start)):
        acc = acc * scale
        a, b = acc[:, :half], acc[:, half:]
        dq_ref[:, part.start : part.start + half] = (a * cosine + b * sine).astype(low)
        dq_ref[:, part.start + half : part.stop] = (b * cosine - a * sine).astype(low)


def tile_of(length):
    return next(t for t in (256, 128, 64, 32, 16, 8) if length % t == 0)


def attend(ends, query, packed, heads):
    length, width = query.shape[0], query.shape[1] // heads
    tile = tile_of(length)
    first = packed.shape[1] // width - 2
    return pl.pallas_call(
        functools.partial(attend_kernel, heads, tile),
        grid=(length // tile,),
        in_specs=[
            pl.BlockSpec(memory_space=pltpu.SMEM),
            pl.BlockSpec((tile, heads * width), lambda i: (i, 0)),
            pl.BlockSpec((length, width), lambda i: (0, first)),
            pl.BlockSpec((length, width), lambda i: (0, first + 1)),
        ],
        out_specs=[
            pl.BlockSpec((tile, heads * width), lambda i: (i, 0)),
            pl.BlockSpec((heads, tile, 128), lambda i: (0, i, 0)),
        ],
        out_shape=[
            jax.ShapeDtypeStruct((length, heads * width), low),
            jax.ShapeDtypeStruct((heads, length, 128), wide),
        ],
        compiler_params=pltpu.CompilerParams(vmem_limit_bytes=48 * 1024 * 1024),
        cost_estimate=pl.CostEstimate(
            flops=2 * length * length * width * heads,
            bytes_accessed=8 * length * width * heads,
            transcendentals=length * length * heads // 2,
        ),
        name="attend",
    )(ends, query, packed, packed)


def attend_back(ends, query, grad, mixed, packed, logs, cosine, sine, heads, scale):
    length, width = query.shape[0], query.shape[1] // heads
    tile = tile_of(length)
    first = packed.shape[1] // width - 2
    rows = pl.BlockSpec((tile, heads * width), lambda i: (i, 0))
    angle = pl.BlockSpec((tile, width // 2), lambda i: (i, 0))
    return pl.pallas_call(
        functools.partial(attend_back_kernel, heads, tile, scale),
        grid=(length // tile,),
        in_specs=[
            pl.BlockSpec(memory_space=pltpu.SMEM),
            rows,
            rows,
            rows,
            pl.BlockSpec((length, width), lambda i: (0, first)),
            pl.BlockSpec((length, width), lambda i: (0, first + 1)),
            pl.BlockSpec((heads, tile, 128), lambda i: (0, i, 0)),
            angle,
            angle,
        ],
        out_specs=[rows, pl.BlockSpec((length, 2 * width), lambda i: (0, 0))],
        out_shape=[
            jax.ShapeDtypeStruct((length, heads * width), low),
            jax.ShapeDtypeStruct((length, 2 * width), wide),
        ],
        compiler_params=pltpu.CompilerParams(vmem_limit_bytes=48 * 1024 * 1024),
        cost_estimate=pl.CostEstimate(
            flops=5 * length * length * width * heads,
            bytes_accessed=16 * length * width * heads,
            transcendentals=length * length * heads // 2,
        ),
        name="attend_back",
    )(ends, query, grad, mixed, packed, packed, logs, cosine, sine)


def on_device(
    tokens,
    lengths,
    cotangent,
    norm_one,
    query_down,
    query_gain,
    query_up,
    key_proj,
    value_proj,
    out_proj,
    norm_two,
    gate_proj,
    up_proj,
    down_proj,
):
    n_x, n_l = lax.axis_size("x"), lax.axis_size("l")
    x, c, h, l, y = [lax.axis_index(a) for a in every]
    n_dev = n_x * 8 * n_l
    n_group = 4 * n_l
    me = group_place()
    count, width = tokens.shape
    row_len = count * n_group
    latent_width = query_down.shape[1]
    head_dim = key_proj.shape[1]
    shard = query_down.shape[0]
    heads = query_up.shape[1] // head_dim // n_group
    ff_part = down_proj.shape[0]
    ff_own = ff_part * n_x * 2
    ff_pad = -(-ff_own // 128) * 128
    natural = n_x == 2 and n_l == 2
    scale = 1.0 / math.sqrt(head_dim)

    inputs = swap_home(tokens).astype(wide)
    row_lengths = swap_home(lengths)[0]
    ends = jnp.cumsum(row_lengths, dtype=jnp.int32)
    places = jnp.arange(row_len, dtype=jnp.int32)
    begins = jnp.max(jnp.where(places[:, None] >= ends[None, :], ends[None, :], 0), axis=1)
    rates = jnp.exp(
        jnp.arange(head_dim // 2, dtype=wide) * (-math.log(10000.0) / (head_dim // 2))
    )
    phases = (places - begins).astype(wide)[:, None] * rates
    cosine, sine = jnp.cos(phases), jnp.sin(phases)
    own_cos = lax.dynamic_slice_in_dim(cosine, me * count, count)
    own_sin = lax.dynamic_slice_in_dim(sine, me * count, count)

    gains = jnp.zeros((16, latent_width + 2 * head_dim), low)
    gains = gains.at[0, :shard].set(norm_one).at[1, :shard].set(norm_two)
    gains = gains.at[2, : query_gain.shape[0]].set(query_gain)
    small = jnp.concatenate(
        [jnp.concatenate([query_down, key_proj, value_proj], axis=1), gains], axis=0
    )
    small = lax.all_gather(small, every, axis=0)
    in_full = small[:, :shard].reshape(width, -1)
    gain_one = small[:, shard, :shard].reshape(width).astype(wide)
    gain_two = small[:, shard + 1, :shard].reshape(width).astype(wide)
    gain_latent = small[:, shard + 2, : query_gain.shape[0]].reshape(latent_width).astype(wide)

    def by_place(weight, part):
        rows = weight.shape[0]
        split = weight.reshape(rows, n_x, 2, 2, n_l, 2, part)
        return split.transpose(2, 4, 5, 0, 1, 3, 6).reshape(n_group, rows, -1)

    def pad_columns(value):
        return jnp.pad(value, ((0, 0), (0, 0), (0, ff_pad - ff_own)))

    rows_up = query_up.shape[0]
    if natural:
        head_cols = query_up.reshape(rows_up, 2, 2, 2, 2, head_dim)
        head_cols = head_cols.transpose(2, 4, 3, 0, 1, 5)
    else:
        head_cols = query_up.reshape(rows_up, n_group, -1).transpose(1, 0, 2)
    head_cols = head_cols.reshape(n_group, rows_up, heads * head_dim)
    ffn_cols = jnp.concatenate(
        [pad_columns(by_place(gate_proj, ff_part)), pad_columns(by_place(up_proj, ff_part))], axis=2
    )

    def whole_columns(cols):
        came = all_to_all_row(cols)
        rows, wide_cols = came.shape[1:]
        came = came.reshape(2, 2 * n_l * rows, wide_cols)
        every_part = gather_columns(came)
        return every_part.transpose(0, 2, 1, 3, 4).reshape(-1, wide_cols)

    up_query = whole_columns(head_cols)
    if natural:
        other = flip(out_proj, "h")
        zero_h = jnp.where(h == 0, out_proj, other)
        one_h = jnp.where(h == 0, other, out_proj)
        kept = jnp.where(y == 0, zero_h, one_h)
        came = flip(jnp.where(y == 0, one_h, zero_h), "y")
        head_rows = jnp.concatenate(
            [jnp.where(y == 0, kept, came), jnp.where(y == 0, came, kept)], axis=0
        )
        across = flip(head_rows, "x")
        out_own = jnp.concatenate(
            [jnp.where(x == 0, head_rows, across), jnp.where(x == 0, across, head_rows)], axis=0
        )
    else:
        out_full = lax.all_gather(out_proj, every, axis=0, tiled=True)
        out_own = lax.dynamic_slice_in_dim(out_full, me * heads * head_dim, heads * head_dim)
    ffn_own = whole_columns(ffn_cols)
    down_own = gather_columns(down_proj[None]).reshape(ff_own, width)
    down_own = jnp.pad(down_own, ((0, ff_pad - ff_own), (0, 0)))

    scale_one = rms_scale(inputs)
    hidden = (inputs * scale_one * gain_one).astype(low)
    mapped = dot(hidden, in_full)
    latent = mapped[:, :latent_width]
    scale_latent = rms_scale(latent)
    latent_low = (latent * scale_latent * gain_latent).astype(low)
    keys = rotate(mapped[:, latent_width : latent_width + head_dim], own_cos, own_sin).astype(low)
    values = mapped[:, latent_width + head_dim :].astype(low)
    packed = gather_row(jnp.concatenate([latent_low, keys, values], axis=1))
    all_latent = packed[:, :latent_width]
    query_raw = dot(all_latent, up_query)
    query = jnp.concatenate(
        [
            rotate(query_raw[:, j * head_dim : (j + 1) * head_dim], cosine, sine)
            for j in range(heads)
        ],
        axis=1,
    ).astype(low) * jnp.asarray(scale, low)
    mixed, logs = attend(ends, query, packed, heads)

    def rows_of(value, core):
        return half_of(value, core)

    attended = scatter_row(lambda core: dot(rows_of(mixed, core), out_own, low))
    resid = inputs + attended
    scale_two = rms_scale(resid)
    all_two = gather_row((resid * scale_two * gain_two).astype(low))
    gate_up = dot(all_two, ffn_own)
    gate, upward = gate_up[:, :ff_pad], gate_up[:, ff_pad:]
    sigma = jax.nn.sigmoid(gate)
    inner = (gate * sigma * upward).astype(low)

    grad_home = swap_home(cotangent)
    grad_all = gather_row(grad_home)
    dinner = times_transposed(grad_all, down_own)
    dgate = (dinner * upward * sigma * (1.0 + gate * (1.0 - sigma))).astype(low)
    dupward = (dinner * gate * sigma).astype(low)
    dboth = jnp.concatenate([dgate, dupward], axis=1)
    dhidden_two = scatter_row(lambda core: times_transposed(rows_of(dboth, core), ffn_own, low))
    final = resid + scatter_row(lambda core: dot(rows_of(inner, core), down_own, low))
    output = swap_home(final.astype(low))

    def sum_columns(terms, rows):
        columns = terms.shape[-1]
        terms = terms.reshape(n_x, 2, 2, 2 * n_l * rows, columns)
        terms = sum_axis(sum_axis(terms, "x", 0), "h", 1)
        return all_to_all_row(terms.reshape(n_group, rows, columns))

    grad_down = outer_sum(inner, grad_all, low)[:ff_own].reshape(n_x, 2, ff_part, width)
    grad_down = sum_axis(sum_axis(grad_down, "x", 0), "h", 0).astype(wide)
    ffn_terms = sum_columns(outer_sum(all_two, dboth, low), shard)

    def from_place(blocks, part):
        rows = blocks.shape[1]
        split = blocks.reshape(2, n_l, 2, rows, n_x, 2, part)
        return split.transpose(3, 4, 0, 5, 1, 2, 6).reshape(rows, -1).astype(wide)

    grad_gate = from_place(ffn_terms[:, :, :ff_own], ff_part)
    grad_upward = from_place(ffn_terms[:, :, ff_pad : ff_pad + ff_own], ff_part)

    dresid_part, dgain_two = norm_back(dhidden_two, resid, scale_two, gain_two)
    dresid = grad_home.astype(wide) + dresid_part
    branch_all = gather_row(dresid.astype(low))
    dmixed = times_transposed(branch_all, out_own, low)
    dquery, dkv = attend_back(
        ends, query, dmixed, mixed, packed, logs, cosine, sine, heads, scale
    )
    dlow_dkv = scatter_row(
        lambda core: jnp.concatenate(
            [
                times_transposed(rows_of(dquery, core), up_query, low),
                rows_of(dkv, core).astype(low),
            ],
            axis=1,
        )
    )
    grad_out = outer_sum(mixed, branch_all, low)
    if natural:
        grad_out = sum_axis(grad_out.reshape(2, 2, head_dim // 2, width), "x", 0)
        kept = pick(grad_out, y)
        came = flip(pick(grad_out, 1 - y), "y")
        by_h = jnp.stack([jnp.where(y == 0, kept, came), jnp.where(y == 0, came, kept)])
        grad_out = sum_axis(by_h, "h", 0).astype(wide)
    else:
        whole = jnp.zeros((n_group * heads * head_dim, width), wide)
        whole = lax.dynamic_update_slice_in_dim(
            whole, grad_out.astype(wide), me * heads * head_dim, 0
        )
        grad_out = lax.psum_scatter(whole, every, scatter_dimension=0, tiled=True)
    head_terms = sum_columns(outer_sum(all_latent, dquery, low), rows_up)
    if natural:
        grad_uquery = head_terms.reshape(2, 2, 2, rows_up, 2, head_dim)
        grad_uquery = grad_uquery.transpose(3, 4, 0, 2, 1, 5)
    else:
        grad_uquery = head_terms.transpose(1, 0, 2)
    grad_uquery = grad_uquery.reshape(rows_up, -1).astype(wide)

    dkeys = rotate_back(
        dlow_dkv[:, latent_width : latent_width + head_dim], own_cos, own_sin
    ).astype(low)
    dvalues = dlow_dkv[:, latent_width + head_dim :].astype(low)
    dlatent, dgain_latent = norm_back(dlow_dkv[:, :latent_width], latent, scale_latent, gain_latent)
    dmapped = jnp.concatenate([dlatent.astype(low), dkeys, dvalues], axis=1)
    dhidden = times_transposed(dmapped, in_full)
    dinput_part, dgain_one = norm_back(dhidden, inputs, scale_one, gain_one)
    grad_tokens = swap_home((dresid + dinput_part).astype(low)).astype(wide)
    grad_in = outer_sum(hidden, dmapped, low).reshape(n_dev, shard, -1)
    gain_terms = jnp.zeros((n_dev, 16, grad_in.shape[-1]), low)
    gain_terms = gain_terms.at[:, 0, :shard].set(dgain_one.reshape(n_dev, -1).astype(low))
    gain_terms = gain_terms.at[:, 1, :shard].set(dgain_two.reshape(n_dev, -1).astype(low))
    gain_terms = gain_terms.at[:, 2, : query_gain.shape[0]].set(
        dgain_latent.reshape(n_dev, -1).astype(low)
    )
    terms = jnp.concatenate([grad_in, gain_terms], axis=1)
    terms = terms.reshape((n_x, 2, 2, n_l, 2) + terms.shape[1:])
    third = terms.shape[-1] // 3
    order = ["x", "l", "y"]
    dims = {"x": 0, "c": 1, "h": 2, "l": 3, "y": 4}
    sums = []
    for i in range(3):
        part = terms[..., i * third : (i + 1) * third]
        left = ["x", "c", "h", "l", "y"]
        for axis in ["c"] + order[i:] + order[:i] + ["h"]:
            part = sum_axis(part, axis, left.index(axis))
            left.remove(axis)
        sums.append(part)
    summed = jnp.concatenate(sums, axis=-1).astype(wide)
    grad_dquery = summed[:shard, :latent_width]
    grad_key = summed[:shard, latent_width : latent_width + head_dim]
    grad_value = summed[:shard, latent_width + head_dim :]
    return (
        output,
        grad_tokens,
        summed[shard, :shard],
        grad_dquery,
        summed[shard + 2, : query_gain.shape[0]],
        grad_uquery,
        grad_key,
        grad_value,
        grad_out,
        summed[shard + 1, :shard],
        grad_gate,
        grad_upward,
        grad_down,
    )


def solution(mesh):
    n_dp, n_seq = mesh.shape["dp"], mesh.shape["seq"]
    fine = Mesh(mesh.devices.reshape(n_dp // 2, 2, 2, n_seq // 4, 2), every)
    rows, flat = P(every, None), P(every)
    placed = (rows, P(("x", "c"), None), rows, flat, rows, flat) + (rows,) * 4 + (flat,) + (rows,) * 3
    return jax.shard_map(
        on_device,
        mesh=fine,
        in_specs=placed,
        out_specs=(rows, rows, flat, rows, flat) + (rows,) * 4 + (flat,) + (rows,) * 3,
        check_vma=False,
    )
```

```python
import functools
import math

import jax
import jax.numpy as jnp
from jax import lax
from jax.experimental import pallas as pl
from jax.experimental.pallas import tpu as pltpu
from jax.sharding import Mesh, PartitionSpec as P

norm_eps = 1e-05
masked_value = -1e30
every = ("x", "c", "h", "l", "y")
group = ("c", "l", "y")
low = jnp.bfloat16
wide = jnp.float32


def rms_scale(values):
    return lax.rsqrt(jnp.mean(values * values, axis=-1, keepdims=True) + norm_eps)


def rotate(values, cosine, sine):
    half = values.shape[-1] // 2
    a, b = values[..., :half], values[..., half:]
    return jnp.concatenate([a * cosine - b * sine, b * cosine + a * sine], axis=-1)


def rotate_back(values, cosine, sine):
    half = values.shape[-1] // 2
    a, b = values[..., :half], values[..., half:]
    return jnp.concatenate([a * cosine + b * sine, b * cosine - a * sine], axis=-1)


def norm_back(incoming, source, scale, gain):
    weighted = incoming * gain
    source_grad = scale * weighted - source * (scale * scale * scale) * jnp.mean(
        weighted * source, axis=-1, keepdims=True
    )
    return source_grad, jnp.sum(incoming * source * scale, axis=0)


def dot(left, right, out=wide):
    return jnp.dot(left, right, preferred_element_type=wide).astype(out)


def outer_sum(left, right, out=wide):
    return lax.dot_general(
        left, right, (((0,), (0,)), ((), ())), preferred_element_type=wide
    ).astype(out)


def times_transposed(left, right, out=wide):
    return lax.dot_general(
        left, right, (((1,), (1,)), ((), ())), preferred_element_type=wide
    ).astype(out)


def pick(array, index, axis=0):
    return lax.dynamic_index_in_dim(array, index, axis, keepdims=False)


def together(*values):
    return lax.optimization_barrier(values)


def half_of(array, index):
    size = array.shape[0] // 2
    return lax.dynamic_slice_in_dim(array, index * size, size)


def place_kernel(starts, table_ref, *refs):
    out_ref = refs[-1]
    step = pl.program_id(0)
    for ref, (begin, end) in zip(refs[:-1], starts):

        @pl.when((step >= begin) & (step < end))
        def _():
            out_ref[...] = ref[...]


def place(pieces, table):
    rows, columns = pieces[0].shape[1:]
    starts, total = [], 0
    for piece in pieces:
        starts.append((total, total + piece.shape[0]))
        total += piece.shape[0]

    def source(begin, end):
        return pl.BlockSpec(
            (1, rows, columns), lambda g, t: (jnp.clip(g - begin, 0, end - begin - 1), 0, 0)
        )

    size = total * rows * columns * pieces[0].dtype.itemsize
    return pl.pallas_call(
        functools.partial(place_kernel, starts),
        grid_spec=pltpu.PrefetchScalarGridSpec(
            num_scalar_prefetch=1,
            grid=(total,),
            in_specs=[source(*pair) for pair in starts],
            out_specs=pl.BlockSpec((1, rows, columns), lambda g, t: (t[g], 0, 0)),
        ),
        out_shape=jax.ShapeDtypeStruct((total, rows, columns), pieces[0].dtype),
        compiler_params=pltpu.CompilerParams(vmem_limit_bytes=48 * 1024 * 1024),
        cost_estimate=pl.CostEstimate(flops=0, bytes_accessed=2 * size, transcendentals=0),
        name="place",
    )(jnp.stack(table).astype(jnp.int32), *pieces)


def flip(value, axis):
    return lax.ppermute(value, axis, [(0, 1), (1, 0)])


def flip_cross(value):
    return lax.ppermute(value, ("c", "h"), [(1, 2), (2, 1)])


def choose_home(value, moved):
    return jnp.where(lax.axis_index("c") == lax.axis_index("h"), value, moved)


def swap_home(value):
    return choose_home(value, flip_cross(value))


def group_place():
    return (
        lax.axis_index("c") * lax.axis_size("l") + lax.axis_index("l")
    ) * 2 + lax.axis_index("y")


def all_to_all_row(blocks):
    return lax.all_to_all(blocks, group, 0, 0, tiled=True)


def gather_columns(own, beside, across, corner):
    x, h = lax.axis_index("x"), lax.axis_index("h")
    count = own.shape[0]
    table = []
    for place_x, place_h in ((x, h), (x, 1 - h), (1 - x, h), (1 - x, 1 - h)):
        table += [(place_x * count + i) * 2 + place_h for i in range(count)]
    pieces = place([own, beside, across, corner], table)
    return pieces.reshape((2, count, 2) + own.shape[1:])


def stack_kernel(table_ref, *refs):
    out_ref, parts = refs[-1], refs[:-1]
    halves = len(parts) // 4
    rows, width = parts[0].shape
    for j, ref in enumerate(parts):
        at = pl.multiple_of(table_ref[j % 4] * rows, 16)
        out_ref[pl.ds(at, rows), j // 4 * width : (j // 4 + 1) * width] = ref[...]
    out_ref[4 * rows :, :] = jnp.zeros(
        (out_ref.shape[0] - 4 * rows, halves * width), out_ref.dtype
    )


def gather_rows(parts, total):
    x, h = lax.axis_index("x"), lax.axis_index("h")
    flat = [piece for part in parts for piece in part]
    width = flat[0].shape[1] * len(parts)
    table = [x * 2 + h, x * 2 + 1 - h, (1 - x) * 2 + h, (1 - x) * 2 + 1 - h]
    return pl.pallas_call(
        stack_kernel,
        in_specs=[pl.BlockSpec(memory_space=pltpu.SMEM)]
        + [pl.BlockSpec(memory_space=pltpu.VMEM)] * len(flat),
        out_specs=pl.BlockSpec(memory_space=pltpu.VMEM),
        out_shape=jax.ShapeDtypeStruct((total, width), low),
        compiler_params=pltpu.CompilerParams(vmem_limit_bytes=24 * 1024 * 1024),
        cost_estimate=pl.CostEstimate(
            flops=0, bytes_accessed=4 * total * width, transcendentals=0
        ),
        name="gather_rows",
    )(jnp.stack(table).astype(jnp.int32), *flat)


def send(value, offsets):
    return lax.ppermute(value, group, [(i, i ^ offsets[i // 4]) for i in range(8)])


def scatter_row_async(terms):
    if lax.axis_size("l") != 2:
        return lax.psum_scatter(terms.astype(wide), group, scatter_dimension=0, tiled=True)
    core = lax.axis_index("c")
    width = terms.shape[-1]
    terms = terms.reshape(8, -1, width)
    moved = flip(half_of(terms, 1 - core), "c")
    own = half_of(terms, core)
    me = lax.axis_index("l") * 2 + lax.axis_index("y")
    first, second = 1 + core, 2 - core

    def block(index):
        return pick(own, index).astype(wide) + pick(moved, index).astype(wide)

    far = send(block(me ^ 3).astype(low), (2, 1))
    side = send(block(me ^ second).astype(low), (2, 1))
    near = send((block(me ^ first) + far.astype(wide)).astype(low), (1, 2))
    return block(me) + side.astype(wide) + near.astype(wide)


def halves(terms, axis, dim):
    me = lax.axis_index(axis)
    if lax.axis_size(axis) != 2:
        moved = jnp.moveaxis(terms, dim, 0).astype(wide)
        total = lax.psum_scatter(moved, axis, scatter_dimension=0, tiled=False).astype(low)
        return total, jnp.zeros_like(total)
    return pick(terms, me, dim), flip(pick(terms, 1 - me, dim), axis)


def add(own, came):
    return (own.astype(wide) + came.astype(wide)).astype(low)


def other(value, flag=1):
    return value + flag * (1 - 2 * value)


def greet(peers):
    barrier = pltpu.get_barrier_semaphore()
    for peer in peers:
        pl.semaphore_signal(barrier, inc=1, device_id=peer, device_id_type=pl.DeviceIdType.MESH)
    pl.semaphore_wait(barrier, len(peers))


def remote(source, target, send_sem, recv_sem, peer):
    return pltpu.make_async_remote_copy(
        src_ref=source,
        dst_ref=target,
        send_sem=send_sem,
        recv_sem=recv_sem,
        device_id=peer,
        device_id_type=pl.DeviceIdType.MESH,
    )


def in_hbm():
    return pl.BlockSpec(memory_space=pl.ANY)


def open_kernel(n_sets, n_swaps, small_ref, out_ref, *refs):
    sets, refs = refs[:n_sets], refs[n_sets:]
    swaps, refs = refs[:n_swaps], refs[n_swaps:]
    (full_ref, heads_ref), refs = refs[:2], refs[2:]
    set_outs, refs = refs[:n_sets], refs[n_sets:]
    swap_outs, refs = refs[:n_swaps], refs[n_swaps:]
    (small_buf, out_buf), refs = refs[:2], refs[2:]
    set_bufs, refs = refs[:n_sets], refs[n_sets:]
    swap_bufs, refs = refs[:n_swaps], refs[n_swaps:]
    sends, recvs, swap_sends, swap_recvs, set_sends, set_recvs, out_sems, loads_sem, stores_sem = refs
    x, c, h, l, y = [lax.axis_index(a) for a in every]
    hops = {
        1: {"h": other(h)},
        2: {"l": other(l)},
        4: {"y": other(y)},
        8: {"x": other(x)},
        16: {"c": other(c)},
    }
    cross = {"c": other(c), "h": other(h)}
    me = (c * 2 + l) * 2 + y

    def group_peer(k):
        return {"c": other(c, k // 4), "l": other(l, k // 2 % 2), "y": other(y, k % 2)}

    def group_index(k):
        peer = group_peer(k)
        return (peer["c"] * 2 + peer["l"]) * 2 + peer["y"]

    def index(code):
        at_x, at_l = other(x, code // 8 % 2), other(l, code // 2 % 2)
        return (((at_x * 2 + c) * 2 + other(h, code % 2)) * 2 + at_l) * 2 + other(y, code // 4 % 2)

    beside, corner = {"y": other(y)}, {"h": other(h), "y": h}
    greet(
        [hops[1], hops[8], cross, {"h": other(h), "y": other(y)}]
        + [group_peer(k) for k in range(1, 8)]
    )
    copies = []
    half = heads_ref.at[y]
    to_beside = remote(out_ref, half, out_sems.at[0], out_sems.at[1], beside)
    differ = y + h - 2 * y * h
    to_corner = remote(out_ref, half, out_sems.at[2], out_sems.at[3 + differ], corner)

    def push(code):
        block = full_ref.at[index(code)]
        source = small_ref if code == 0 else block
        for hop in (1, 2, 4, 8, 16):
            if code < hop:
                name = code + hop
                copy = remote(source, block, sends.at[name], recvs.at[name], hops[hop])
                copy.start()
                copies.append(copy)

    push(0)
    moving = [
        remote(source, target, swap_sends.at[i], swap_recvs.at[i], cross)
        for i, (source, target) in enumerate(zip(swaps, swap_outs))
    ]

    @pl.when(c != h)
    def _():
        for copy in moving:
            copy.start()

    @pl.when(y != h)
    def _():
        to_beside.start()

    to_corner.start()
    loads, stores = [], []
    locals_in = [small_ref, out_ref] + [ref.at[me] for ref in sets] + list(swaps)
    locals_buf = [small_buf, out_buf] + list(set_bufs) + list(swap_bufs)
    locals_out = [full_ref.at[index(0)], half] + [ref.at[me] for ref in set_outs]
    for i, (source, buf) in enumerate(zip(locals_in, locals_buf)):
        loads.append(pltpu.make_async_copy(source, buf, loads_sem.at[i]))
        loads[-1].start()
    for load in loads:
        load.wait()
    for i, (buf, target) in enumerate(zip(locals_buf, locals_out)):
        stores.append(pltpu.make_async_copy(buf, target, stores_sem.at[i]))
    keep_out = stores.pop(1)
    for store in stores:
        store.start()

    @pl.when(y == h)
    def _():
        keep_out.start()

    keeps = [
        pltpu.make_async_copy(buf, target, stores_sem.at[2 + n_sets + i])
        for i, (buf, target) in enumerate(zip(swap_bufs, swap_outs))
    ]

    @pl.when(c == h)
    def _():
        for keep in keeps:
            keep.start()

    def arrived(name):
        remote(small_ref, small_ref, sends.at[name], recvs.at[name], hops[16]).wait_recv()

    def set_push(i):
        for k in range(1, 8):
            copy = remote(
                sets[i].at[group_index(k)], set_outs[i].at[me], set_sends.at[i, k],
                set_recvs.at[i, k], group_peer(k),
            )
            copy.start()
            set_copies.append(copy)

    set_copies = []
    for n, code in enumerate((2, 4, 1, 6, 3, 5, 7, 8, 9, 10, 11, 12, 13, 14, 15)):
        arrived(code)
        push(code)
        if n == 6:
            for i in range(n_sets):
                set_push(i)
    for code in range(16):
        arrived(16 + code)
    for copy in copies:
        copy.wait_send()
    for copy in set_copies:
        copy.wait()
    for store in stores:
        store.wait()
    to_corner.wait_send()

    @pl.when(y != h)
    def _():
        to_beside.wait_send()
        remote(out_ref, half, out_sems.at[2], out_sems.at[3], corner).wait_recv()
        remote(out_ref, half, out_sems.at[2], out_sems.at[4], corner).wait_recv()

    @pl.when(y == h)
    def _():
        keep_out.wait()
        to_beside.wait_recv()

    @pl.when(c != h)
    def _():
        for copy in moving:
            copy.wait()

    @pl.when(c == h)
    def _():
        for keep in keeps:
            keep.wait()


def open_exchange(small, out_rows, sets, swaps):
    n_sets, n_swaps = len(sets), len(swaps)
    args = [small, out_rows] + sets + swaps
    out_shape = [
        jax.ShapeDtypeStruct((32,) + small.shape, low),
        jax.ShapeDtypeStruct((2,) + out_rows.shape, low),
    ]
    out_shape += [jax.ShapeDtypeStruct(a.shape, a.dtype) for a in sets + swaps]
    sem = pltpu.SemaphoreType.DMA
    out = pl.pallas_call(
        functools.partial(open_kernel, n_sets, n_swaps),
        in_specs=[in_hbm()] * len(args),
        out_specs=[in_hbm()] * len(args),
        out_shape=out_shape,
        scratch_shapes=[pltpu.VMEM(small.shape, low), pltpu.VMEM(out_rows.shape, low)]
        + [pltpu.VMEM(a.shape[1:], a.dtype) for a in sets]
        + [pltpu.VMEM(a.shape, a.dtype) for a in swaps]
        + [sem((32,)), sem((32,)), sem((n_swaps,)), sem((n_swaps,))]
        + [sem((n_sets, 8)), sem((n_sets, 8)), sem((5,)), sem((len(args),)), sem((len(args),))],
        compiler_params=pltpu.CompilerParams(
            collective_id=1, has_side_effects=True, vmem_limit_bytes=16 * 1024 * 1024
        ),
        cost_estimate=pl.CostEstimate(flops=0, bytes_accessed=150 * 1024 * 1024, transcendentals=0),
        name="open_exchange",
    )(*args)
    return out[0], out[1], out[2 : 2 + n_sets], out[2 + n_sets :]


def row_peers():
    c, l, y = [lax.axis_index(a) for a in group]
    near = {"l": other(l, c), "y": other(y, 1 - c)}
    side = {"l": other(l, 1 - c), "y": other(y, c)}
    return c, l, y, near, side, {"c": other(c)}


def gather_kernel(chunks, extra, own_ref, *refs):
    if extra:
        more_ref, out_ref, more_out, buf, more_buf, sends, recvs, local_sems, more_sends, more_recvs = refs
    else:
        out_ref, buf, sends, recvs, local_sems = refs
    c, l, y, near, side, twin = row_peers()
    rows = own_ref.shape[0] // chunks
    me = (c * 2 + l) * 2 + y
    places = {
        "own": me,
        "near": (c * 2 + near["l"]) * 2 + near["y"],
        "side": (c * 2 + side["l"]) * 2 + side["y"],
        "far": (c * 2 + other(l)) * 2 + other(y),
    }
    peers = [near, side, twin]
    if extra:
        x, h = lax.axis_index("x"), lax.axis_index("h")
        up, over = {"h": other(h)}, {"x": other(x)}
        peers += [up, over]
    greet(peers)
    copies = []

    def start(name, k, slot, peer):
        span = pl.ds(k * rows, rows)
        target = out_ref.at[places[name], span]
        source = own_ref.at[span] if name == "own" else target
        copy = remote(source, target, sends.at[slot, k], recvs.at[slot, k], peer)
        copy.start()
        copies.append(copy)

    def arrived(slot, k):
        span = own_ref.at[pl.ds(k * rows, rows)]
        remote(span, span, sends.at[slot, k], recvs.at[slot, k], twin).wait_recv()

    def start_more(source, target, slot, peer):
        copy = remote(source, target, more_sends.at[slot], more_recvs.at[slot], peer)
        copy.start()
        copies.append(copy)

    for k in range(chunks):
        start("own", k, 0, near)
        start("own", k, 1, side)
        start("own", k, 3, twin)
    if extra:
        mine = more_out.at[x, :, h]
        start_more(more_ref, mine, 0, up)
        start_more(more_ref, mine, 1, over)
        more_load = pltpu.make_async_copy(more_ref, more_buf, local_sems.at[2])
        more_load.start()
    load = pltpu.make_async_copy(own_ref, buf, local_sems.at[0])
    load.start()
    load.wait()
    store = pltpu.make_async_copy(buf, out_ref.at[me], local_sems.at[1])
    store.start()
    if extra:
        more_load.wait()
        more_store = pltpu.make_async_copy(more_buf, mine, local_sems.at[3])
        more_store.start()
    for k in range(chunks):
        arrived(0, k)
        start("near", k, 2, side)
        start("near", k, 4, twin)
        arrived(1, k)
        start("side", k, 5, twin)
    if extra:
        theirs = more_out.at[x, :, other(h)]
        remote(more_ref, more_ref, more_sends.at[0], more_recvs.at[0], twin).wait_recv()
        start_more(theirs, theirs, 2, over)
    for k in range(chunks):
        arrived(2, k)
        start("far", k, 6, twin)
    for slot in (3, 4, 5, 6):
        for k in range(chunks):
            arrived(slot, k)
    if extra:
        for slot in (1, 2):
            remote(more_ref, more_ref, more_sends.at[slot], more_recvs.at[slot], twin).wait_recv()
        more_store.wait()
    for copy in copies:
        copy.wait_send()
    store.wait()


def gather_row(value, number, more=None):
    if lax.axis_size("l") != 2:
        out = lax.all_gather(value, group, axis=0, tiled=True)
        if more is None:
            return out
        more = lax.all_gather(lax.all_gather(more, "h", axis=1), "x", axis=0)
        return out, more
    chunks = 4 if value.shape[0] % 64 == 0 else 1
    out_shape = [jax.ShapeDtypeStruct((8,) + value.shape, low)]
    scratch = [pltpu.VMEM(value.shape, low)]
    sems = [
        pltpu.SemaphoreType.DMA((7, chunks)),
        pltpu.SemaphoreType.DMA((7, chunks)),
        pltpu.SemaphoreType.DMA((4,)),
    ]
    args = [value]
    if more is not None:
        args.append(more)
        out_shape.append(jax.ShapeDtypeStruct((2, more.shape[0], 2) + more.shape[1:], low))
        scratch.append(pltpu.VMEM(more.shape, low))
        sems += [pltpu.SemaphoreType.DMA((3,))] * 2
    out = pl.pallas_call(
        functools.partial(gather_kernel, chunks, more is not None),
        in_specs=[in_hbm()] * len(args),
        out_specs=[in_hbm()] * len(args),
        out_shape=out_shape,
        scratch_shapes=scratch + sems,
        compiler_params=pltpu.CompilerParams(
            collective_id=number, has_side_effects=True, vmem_limit_bytes=16 * 1024 * 1024
        ),
        cost_estimate=pl.CostEstimate(flops=0, bytes_accessed=80 * 1024 * 1024, transcendentals=0),
        name="gather_row",
    )(*args)
    rows = out[0].reshape(-1, value.shape[1])
    return rows if more is None else (rows, out[1])


def scatter_kernel(chunks, n, *refs):
    terms, refs = refs[:n], refs[n:]
    outs, refs = refs[:n], refs[n:]
    bufs, (sends, recvs, local_sems) = refs[: 8 * n], refs[8 * n :]
    bufs = [bufs[8 * a : 8 * a + 8] for a in range(n)]
    c, l, y, near, side, twin = row_peers()
    rows = outs[0].shape[0] // chunks
    me = l * 2 + y
    near_at, side_at = near["l"] * 2 + near["y"], side["l"] * 2 + side["y"]
    far_at = other(l) * 2 + other(y)
    greet([near, side, twin])
    copies = []

    def start(source, target, a, slot, k, peer):
        copy = remote(source, target, sends.at[a, slot, k], recvs.at[a, slot, k], peer)
        copy.start()
        copies.append(copy)

    parts = [(a, k, pl.ds(k * rows, rows)) for k in range(chunks) for a in range(n)]
    for slot, place in ((3, far_at), (4, near_at), (5, side_at), (6, me)):
        for a, k, span in parts:
            start(
                terms[a].at[other(c) * 4 + place, span], bufs[a][1].at[place, span], a, slot, k, twin
            )
    loads = []
    for slot, place in ((0, far_at), (1, side_at), (2, near_at), (3, me)):
        for a in range(n):
            load = pltpu.make_async_copy(
                terms[a].at[c * 4 + place], bufs[a][0].at[place], local_sems.at[a, slot]
            )
            load.start()
            loads.append(load)

    def arrived(a, slot, k):
        span = bufs[a][5].at[pl.ds(k * rows, rows)]
        remote(span, span, sends.at[a, slot, k], recvs.at[a, slot, k], twin).wait_recv()

    def both(a, place, span):
        own, came = bufs[a][0], bufs[a][1]
        return own[place, span, :].astype(wide) + came[place, span, :].astype(wide)

    for load in loads[: 2 * n]:
        load.wait()
    for a, k, span in parts:
        far_out, far_in = bufs[a][2], bufs[a][5]
        arrived(a, 3, k)
        far_out[span, :] = both(a, far_at, span).astype(low)
        start(far_out.at[span], far_in.at[span], a, 0, k, side)
    for a, k, span in parts:
        side_out, side_in = bufs[a][3], bufs[a][6]
        arrived(a, 4, k)
        side_out[span, :] = both(a, side_at, span).astype(low)
        start(side_out.at[span], side_in.at[span], a, 1, k, side)
    for load in loads[2 * n :]:
        load.wait()
    for a, k, span in parts:
        near_out, far_in, near_in = bufs[a][4], bufs[a][5], bufs[a][7]
        arrived(a, 5, k)
        arrived(a, 0, k)
        near_out[span, :] = (both(a, near_at, span) + far_in[span, :].astype(wide)).astype(low)
        start(near_out.at[span], near_in.at[span], a, 2, k, near)
    for a, k, span in parts:
        arrived(a, 6, k)
        arrived(a, 1, k)
        outs[a][span, :] = both(a, me, span) + bufs[a][6][span, :].astype(wide)
    for a, k, span in parts:
        arrived(a, 2, k)
        outs[a][span, :] += bufs[a][7][span, :].astype(wide)
    for copy in copies:
        copy.wait_send()


def scatter_row(number, *terms):
    if lax.axis_size("l") != 2:
        return [
            lax.psum_scatter(t.astype(wide), group, scatter_dimension=0, tiled=True) for t in terms
        ]
    terms = [t.reshape(8, -1, t.shape[1]) for t in terms]
    n, count = len(terms), terms[0].shape[1]
    chunks = 4 if count % 64 == 0 else 1
    scratch = []
    for t in terms:
        scratch += [pltpu.VMEM((4, count, t.shape[2]), low)] * 2
        scratch += [pltpu.VMEM((count, t.shape[2]), low)] * 6
    return pl.pallas_call(
        functools.partial(scatter_kernel, chunks, n),
        in_specs=[in_hbm()] * n,
        out_specs=[pl.BlockSpec(memory_space=pltpu.VMEM)] * n,
        out_shape=[jax.ShapeDtypeStruct((count, t.shape[2]), wide) for t in terms],
        scratch_shapes=scratch
        + [
            pltpu.SemaphoreType.DMA((n, 7, chunks)),
            pltpu.SemaphoreType.DMA((n, 7, chunks)),
            pltpu.SemaphoreType.DMA((n, 4)),
        ],
        compiler_params=pltpu.CompilerParams(
            collective_id=number, has_side_effects=True, vmem_limit_bytes=24 * 1024 * 1024
        ),
        cost_estimate=pl.CostEstimate(flops=0, bytes_accessed=80 * 1024 * 1024, transcendentals=0),
        name="scatter_row",
    )(*terms)


def shut_kernel(
    terms_ref, swap_ref, out_ref, swap_out, own_buf, twin_buf, held, came, swap_buf, sends, recvs,
    local_sems, swap_sems,
):
    x, c, h, l, y = [lax.axis_index(a) for a in every]
    hops = {
        1: {"h": other(h)},
        2: {"x": other(x, c), "l": other(l, 1 - c)},
        4: {"y": other(y)},
        8: {"x": other(x, 1 - c), "l": other(l, c)},
    }
    twin = {"c": other(c)}
    cross = {"c": other(c), "h": other(h)}

    def index(code, core):
        near, far = code // 2 % 2, code // 8 % 2
        at_x = other(x, core * near + (1 - core) * far)
        at_l = other(l, (1 - core) * near + core * far)
        return (((at_x * 2 + core) * 2 + other(h, code % 2)) * 2 + at_l) * 2 + other(y, code // 4 % 2)

    greet(list(hops.values()) + [twin, cross])
    copies = []

    def start(source, target, slot, peer):
        copy = remote(source, target, sends.at[slot], recvs.at[slot], peer)
        copy.start()
        copies.append(copy)

    def arrived(slot):
        remote(came.at[0], came.at[0], sends.at[slot], recvs.at[slot], twin).wait_recv()

    loads = {}
    for code in range(15, -1, -1):
        start(terms_ref.at[index(code, 1 - c)], twin_buf.at[code], 16 + code, twin)
        load = pltpu.make_async_copy(
            terms_ref.at[index(code, c)], own_buf.at[code], local_sems.at[code]
        )
        load.start()
        loads[code] = load
    moving = remote(swap_ref, swap_out, swap_sems.at[0], swap_sems.at[1], cross)

    @pl.when(c != h)
    def _():
        moving.start()

    @pl.when(c == h)
    def _():
        load = pltpu.make_async_copy(swap_ref, swap_buf, swap_sems.at[2])
        load.start()
        load.wait()
        store = pltpu.make_async_copy(swap_buf, swap_out, swap_sems.at[3])
        store.start()
        store.wait()

    for code in range(15, -1, -1):
        arrived(16 + code)
        loads[code].wait()
        total = own_buf[code].astype(wide) + twin_buf[code].astype(wide)
        for hop in (8, 4, 2, 1):
            if code < hop:
                arrived(code + hop)
                total = total + came[code + hop].astype(wide)
        if code == 0:
            out_ref[...] = total
        else:
            held[code] = total.astype(low)
            hop = 1 << (code.bit_length() - 1)
            start(held.at[code], came.at[code], code, hops[hop])
    for copy in copies:
        copy.wait_send()

    @pl.when(c != h)
    def _():
        moving.wait()


def shut_sum(terms, swap, number):
    rows, width = terms.shape[1:]
    blocks = pltpu.VMEM((16, rows, width), low)
    return pl.pallas_call(
        shut_kernel,
        in_specs=[in_hbm()] * 2,
        out_specs=[pl.BlockSpec(memory_space=pltpu.VMEM), in_hbm()],
        out_shape=[
            jax.ShapeDtypeStruct((rows, width), wide),
            jax.ShapeDtypeStruct(swap.shape, low),
        ],
        scratch_shapes=[blocks] * 4
        + [pltpu.VMEM(swap.shape, low)]
        + [
            pltpu.SemaphoreType.DMA((32,)),
            pltpu.SemaphoreType.DMA((32,)),
            pltpu.SemaphoreType.DMA((16,)),
            pltpu.SemaphoreType.DMA((4,)),
        ],
        compiler_params=pltpu.CompilerParams(
            collective_id=number, has_side_effects=True, vmem_limit_bytes=32 * 1024 * 1024
        ),
        cost_estimate=pl.CostEstimate(flops=0, bytes_accessed=100 * 1024 * 1024, transcendentals=0),
        name="shut_sum",
    )(terms, swap)


def split_kernel(part, order, a_ref, b_ref, a_out, b_out):
    for source, target in ((a_ref, a_out), (b_ref, b_out)):
        used, total = len(order[0]) * part, target.shape[2]
        for place, blocks in enumerate(order):
            for j, block in enumerate(blocks):
                target[place, :, j * part : (j + 1) * part] = source[
                    :, block * part : (block + 1) * part
                ]
            if used < total:
                target[place, :, used:] = jnp.zeros((target.shape[1], total - used), target.dtype)


def join_kernel(part, order, a_ref, b_ref, a_out, b_out):
    for source, target in ((a_ref, a_out), (b_ref, b_out)):
        for place, blocks in enumerate(order):
            for j, block in enumerate(blocks):
                target[:, block * part : (block + 1) * part] = source[
                    place, :, j * part : (j + 1) * part
                ].astype(wide)


def column_order(n_x, n_l):
    return [
        [
            (((x * 2 + c) * 2 + h) * n_l + l) * 2 + y
            for x in range(n_x)
            for h in range(2)
        ]
        for c in range(2)
        for l in range(n_l)
        for y in range(2)
    ]


def split_columns(a, b, part, order, total):
    shape = jax.ShapeDtypeStruct((len(order), a.shape[0], total), a.dtype)
    return pl.pallas_call(
        functools.partial(split_kernel, part, order), out_shape=[shape] * 2, name="split_columns"
    )(a, b)


def join_columns(a, b, part, order):
    shape = jax.ShapeDtypeStruct((a.shape[1], len(order) * len(order[0]) * part), wide)
    return pl.pallas_call(
        functools.partial(join_kernel, part, order), out_shape=[shape] * 2, name="join_columns"
    )(a, b)


def first_allowed(ends_ref, count, places):
    start = jnp.zeros_like(places)
    for j in range(count):
        end = ends_ref[j]
        start = jnp.where(places >= end, end, start)
    return jnp.where(places >= ends_ref[count - 1], places, start)


def contract(left, right, dims):
    return lax.dot_general(left, right, (dims, ((), ())), preferred_element_type=wide)


def stacked(ref, span, heads, width):
    return jnp.concatenate(
        [ref[span, j * width : (j + 1) * width] for j in range(heads)], axis=0
    )


def tile_mask(ends_ref, begin, tile, length, heads):
    rows = begin + lax.broadcasted_iota(jnp.int32, (tile, 1), 0)
    lows = first_allowed(ends_ref, ends_ref.shape[0], rows)
    rows = jnp.concatenate([rows] * heads, axis=0)
    lows = jnp.concatenate([lows] * heads, axis=0)
    columns = lax.broadcasted_iota(jnp.int32, (heads * tile, length), 1)
    return (columns >= lows) & (columns <= rows)


def attend_kernel(heads, tile, ends_ref, q_ref, k_ref, v_ref, o_ref, log_ref):
    width = k_ref.shape[1]
    for i in range(q_ref.shape[0] // tile):
        span, length = slice(i * tile, (i + 1) * tile), (i + 1) * tile
        mask = tile_mask(ends_ref, i * tile, tile, length, heads)
        scores = contract(stacked(q_ref, span, heads, width), k_ref[:length, :], ((1,), (1,)))
        scores = jnp.where(mask, scores, masked_value)
        top = jnp.max(scores, axis=1, keepdims=True)
        weights = jnp.exp(scores - top)
        total = jnp.sum(weights, axis=1, keepdims=True)
        mixed = contract(weights.astype(low), v_ref[:length, :], ((1,), (0,))) / total
        log = jnp.broadcast_to(top + jnp.log(total), (heads * tile, 128))
        for j in range(heads):
            part = slice(j * tile, (j + 1) * tile)
            o_ref[span, j * width : (j + 1) * width] = mixed[part].astype(low)
            log_ref[j, span, :] = log[part]


def attend_back_kernel(
    heads, tile, scale, ends_ref, q_ref, g_ref, o_ref, k_ref, v_ref, log_ref, cos_ref, sin_ref,
    dq_ref, dkv_ref, sum_ref,
):
    width = k_ref.shape[1]
    half = width // 2
    sum_ref[...] = jnp.zeros_like(sum_ref)
    for i in range(q_ref.shape[0] // tile):
        span, length = slice(i * tile, (i + 1) * tile), (i + 1) * tile
        mask = tile_mask(ends_ref, i * tile, tile, length, heads)
        queries = stacked(q_ref, span, heads, width)
        grads = stacked(g_ref, span, heads, width)
        outs = stacked(o_ref, span, heads, width)
        delta = jnp.sum(grads.astype(wide) * outs.astype(wide), axis=1, keepdims=True)
        log = jnp.concatenate([log_ref[j, span, :1] for j in range(heads)], axis=0)
        keys, values = k_ref[:length, :], v_ref[:length, :]
        scores = contract(queries, keys, ((1,), (1,)))
        weights = jnp.where(mask, jnp.exp(scores - log), 0.0)
        dprob = contract(grads, values, ((1,), (1,)))
        dscore = (weights * (dprob - delta)).astype(low)
        sum_ref[:length, width:] += contract(weights.astype(low), grads, ((0,), (0,)))
        sum_ref[:length, :width] += contract(dscore, queries, ((0,), (0,)))
        dquery = contract(dscore, keys, ((1,), (0,))) * scale
        cosine, sine = cos_ref[span, :], sin_ref[span, :]
        for j in range(heads):
            a = dquery[j * tile : (j + 1) * tile, :half]
            b = dquery[j * tile : (j + 1) * tile, half:]
            at = j * width
            dq_ref[span, at : at + half] = (a * cosine + b * sine).astype(low)
            dq_ref[span, at + half : at + width] = (b * cosine - a * sine).astype(low)
    dkv_ref[...] = sum_ref[...].astype(low)


def tile_of(length):
    return next(t for t in (256, 128, 64, 32, 16, 8) if length % t == 0)


def attend(ends, query, packed, heads):
    length, width = query.shape[0], query.shape[1] // heads
    tile = tile_of(length)
    first = packed.shape[1] // width - 2
    return pl.pallas_call(
        functools.partial(attend_kernel, heads, tile),
        grid=(1,),
        in_specs=[
            pl.BlockSpec(memory_space=pltpu.SMEM),
            pl.BlockSpec((length, heads * width), lambda i: (0, 0)),
            pl.BlockSpec((length, width), lambda i: (0, first)),
            pl.BlockSpec((length, width), lambda i: (0, first + 1)),
        ],
        out_specs=[
            pl.BlockSpec((length, heads * width), lambda i: (0, 0)),
            pl.BlockSpec((heads, length, 128), lambda i: (0, 0, 0)),
        ],
        out_shape=[
            jax.ShapeDtypeStruct((length, heads * width), low),
            jax.ShapeDtypeStruct((heads, length, 128), wide),
        ],
        compiler_params=pltpu.CompilerParams(vmem_limit_bytes=56 * 1024 * 1024),
        cost_estimate=pl.CostEstimate(
            flops=6 * length * length * width * heads,
            bytes_accessed=8 * length * width * heads,
            transcendentals=length * length * heads // 2,
        ),
        name="attend",
    )(ends, query, packed, packed)


def attend_back(ends, query, grad, mixed, packed, logs, cosine, sine, heads, scale):
    length, width = query.shape[0], query.shape[1] // heads
    tile = tile_of(length)
    first = packed.shape[1] // width - 2
    rows = pl.BlockSpec((length, heads * width), lambda i: (0, 0))
    angle = pl.BlockSpec((length, width // 2), lambda i: (0, 0))
    return pl.pallas_call(
        functools.partial(attend_back_kernel, heads, tile, scale),
        grid=(1,),
        in_specs=[
            pl.BlockSpec(memory_space=pltpu.SMEM),
            rows,
            rows,
            rows,
            pl.BlockSpec((length, width), lambda i: (0, first)),
            pl.BlockSpec((length, width), lambda i: (0, first + 1)),
            pl.BlockSpec((heads, length, 128), lambda i: (0, 0, 0)),
            angle,
            angle,
        ],
        out_specs=[rows, pl.BlockSpec((length, 2 * width), lambda i: (0, 0))],
        out_shape=[
            jax.ShapeDtypeStruct((length, heads * width), low),
            jax.ShapeDtypeStruct((length, 2 * width), low),
        ],
        scratch_shapes=[pltpu.VMEM((length, 2 * width), wide)],
        compiler_params=pltpu.CompilerParams(vmem_limit_bytes=56 * 1024 * 1024),
        cost_estimate=pl.CostEstimate(
            flops=10 * length * length * width * heads,
            bytes_accessed=16 * length * width * heads,
            transcendentals=length * length * heads // 2,
        ),
        name="attend_back",
    )(ends, query, grad, mixed, packed, packed, logs, cosine, sine)


def on_device(
    tokens,
    lengths,
    cotangent,
    norm_one,
    query_down,
    query_gain,
    query_up,
    key_proj,
    value_proj,
    out_proj,
    norm_two,
    gate_proj,
    up_proj,
    down_proj,
):
    n_x, n_l = lax.axis_size("x"), lax.axis_size("l")
    x, c, h, l, y = [lax.axis_index(a) for a in every]
    n_dev = n_x * 8 * n_l
    n_group = 4 * n_l
    me = group_place()
    count, width = tokens.shape
    row_len = count * n_group
    latent_width = query_down.shape[1]
    head_dim = key_proj.shape[1]
    shard = query_down.shape[0]
    heads = query_up.shape[1] // head_dim // n_group
    ff_part = down_proj.shape[0]
    ff_own = ff_part * n_x * 2
    ff_pad = -(-ff_own // 128) * 128
    natural = n_x == 2 and n_l == 2
    scale = 1.0 / math.sqrt(head_dim)
    order = column_order(n_x, n_l)
    mapped_width = latent_width + 2 * head_dim

    gains = jnp.zeros((shard, 128), low)
    gains = gains.at[0, :shard].set(norm_one).at[1, :shard].set(norm_two)
    gains = gains.at[2, : query_gain.shape[0]].set(query_gain)
    small = jnp.concatenate([query_down, key_proj, value_proj, gains], axis=1)
    rows_up = query_up.shape[0]
    if natural:
        head_cols = query_up.reshape(rows_up, 2, 2, 2, 2, head_dim)
        head_cols = head_cols.transpose(2, 4, 3, 0, 1, 5)
    else:
        head_cols = query_up.reshape(rows_up, n_group, -1).transpose(1, 0, 2)
    head_cols = head_cols.reshape(n_group, rows_up, heads * head_dim)
    gate_cols, up_cols = split_columns(gate_proj, up_proj, ff_part, order, ff_pad)
    if natural:
        lens = jnp.pad(lengths, ((0, 7), (0, 128 - lengths.shape[1])))
        in_full, own_heads, (head_rows, gate_rows, up_rows), (home, lens) = open_exchange(
            small, out_proj, [head_cols, gate_cols, up_cols], [tokens, lens]
        )
        row_lengths = lens[0, : lengths.shape[1]]
    else:
        in_full = lax.all_gather(small, every, axis=0)
        home, row_lengths = [swap_home(a) for a in (tokens, lengths)]
        row_lengths = row_lengths[0]
        head_rows, gate_rows, up_rows = [
            all_to_all_row(a) for a in (head_cols, gate_cols, up_cols)
        ]
    gate_rows = gate_rows.reshape(2, -1, ff_pad)
    up_rows = up_rows.reshape(2, -1, ff_pad)
    gain_one = in_full[:, 0, mapped_width : mapped_width + shard].reshape(width).astype(wide)
    gain_two = in_full[:, 1, mapped_width : mapped_width + shard].reshape(width).astype(wide)
    gain_latent = in_full[:, 2, mapped_width : mapped_width + query_gain.shape[0]]
    gain_latent = gain_latent.reshape(latent_width).astype(wide)
    in_full = in_full.reshape(width, -1)

    inputs = home.astype(wide)
    ends = jnp.cumsum(row_lengths, dtype=jnp.int32)
    places = jnp.arange(row_len, dtype=jnp.int32)
    begins = jnp.max(jnp.where(places[:, None] >= ends[None, :], ends[None, :], 0), axis=1)
    rates = jnp.exp(
        jnp.arange(head_dim // 2, dtype=wide) * (-math.log(10000.0) / (head_dim // 2))
    )
    phases = (places - begins).astype(wide)[:, None] * rates
    cosine, sine = jnp.cos(phases), jnp.sin(phases)
    own_cos = lax.dynamic_slice_in_dim(cosine, me * count, count)
    own_sin = lax.dynamic_slice_in_dim(sine, me * count, count)

    if natural:
        own_heads = own_heads.reshape(-1, width)
        gate_h, heads_x = flip(gate_rows, "h"), flip(own_heads, "x")
        grad_moved = flip_cross(cotangent)
    else:
        out_full = lax.all_gather(out_proj, every, axis=0, tiled=True)
        out_own = lax.dynamic_slice_in_dim(out_full, me * heads * head_dim, heads * head_dim)
        gate_own, up_own = [
            lax.all_gather(lax.all_gather(a, "h", axis=1), "x", axis=0).reshape(width, -1)
            for a in (gate_rows, up_rows)
        ]
        down_own = lax.all_gather(lax.all_gather(down_proj, "h", axis=0), "x", axis=0)
        down_own = jnp.pad(down_own.reshape(-1, width), ((0, ff_pad - ff_own), (0, 0)))
        grad_home = swap_home(cotangent)

    scale_one = rms_scale(inputs)
    hidden = (inputs * scale_one * gain_one).astype(low)
    mapped = dot(hidden, in_full)
    latent = mapped[:, :latent_width]
    scale_latent = rms_scale(latent)
    latent_low = (latent * scale_latent * gain_latent).astype(low)
    keys = rotate(mapped[:, latent_width : latent_width + head_dim], own_cos, own_sin).astype(low)
    values = mapped[:, latent_width + head_dim : mapped_width].astype(low)
    packed, up_query = gather_row(
        jnp.concatenate([latent_low, keys, values], axis=1),
        2,
        head_rows.reshape(2, -1, heads * head_dim),
    )
    up_query = up_query.reshape(latent_width, -1)
    if natural:
        packed, up_query, gate_h, heads_x, grad_moved = together(
            packed, up_query, gate_h, heads_x, grad_moved
        )
        out_own = jnp.concatenate(
            [jnp.where(x == 0, own_heads, heads_x), jnp.where(x == 0, heads_x, own_heads)], axis=0
        )
        grad_home = choose_home(cotangent, grad_moved)
        gate_x, gate_xh, up_h = flip(gate_rows, "x"), flip(gate_h, "x"), flip(up_rows, "h")
        down_a, down_b = down_proj[:, : width // 2], down_proj[:, width // 2 :]
        down_a_h = flip(down_a, "h")
    grad_all = lax.all_gather(grad_home, group, axis=0, tiled=True)
    all_latent = packed[:, :latent_width]
    query_raw = dot(all_latent, up_query)
    query = jnp.concatenate(
        [
            rotate(query_raw[:, j * head_dim : (j + 1) * head_dim], cosine, sine)
            for j in range(heads)
        ],
        axis=1,
    ).astype(low) * jnp.asarray(scale, low)
    mixed, logs = attend(ends, query, packed, heads)
    attended = scatter_row(3, dot(mixed, out_own, low))[0]
    if natural:
        attended, gate_x, gate_xh, up_h, down_a_h = together(
            attended, gate_x, gate_xh, up_h, down_a_h
        )
        gate_own = gather_columns(gate_rows, gate_h, gate_x, gate_xh).reshape(width, -1)
        up_x, up_xh = flip(up_rows, "x"), flip(up_h, "x")
        down_b_h = flip(down_b, "h")
        down_a_x, down_a_xh = flip(down_a, "x"), flip(down_a_h, "x")
    resid = inputs + attended
    scale_two = rms_scale(resid)
    all_two = gather_row((resid * scale_two * gain_two).astype(low), 4)
    if natural:
        all_two, up_x, up_xh, down_b_h, down_a_x, down_a_xh = together(
            all_two, up_x, up_xh, down_b_h, down_a_x, down_a_xh
        )
        up_own = gather_columns(up_rows, up_h, up_x, up_xh).reshape(width, -1)
        down_b_x, down_b_xh = flip(down_b, "x"), flip(down_b_h, "x")
    gate = dot(all_two, gate_own)
    upward = dot(all_two, up_own)
    if natural:
        gate, upward, down_b_x, down_b_xh = together(gate, upward, down_b_x, down_b_xh)
        down_own = gather_rows(
            [[down_a, down_a_h, down_a_x, down_a_xh], [down_b, down_b_h, down_b_x, down_b_xh]], ff_pad
        )
    sigma = jax.nn.sigmoid(gate)
    inner = (gate * sigma * upward).astype(low)

    spread = scatter_row_async(dot(inner, down_own, low))
    grad_down = outer_sum(inner, grad_all, low)[:ff_own].reshape(n_x, 2, ff_part, width)
    grad_down, down_x = halves(grad_down, "x", 0)
    dinner = times_transposed(grad_all, down_own)
    dgate = (dinner * upward * sigma * (1.0 + gate * (1.0 - sigma))).astype(low)
    dupward = (dinner * gate * sigma).astype(low)
    by_rows = (n_x, 2, 2, -1, ff_pad)
    gate_terms, gate_x = halves(outer_sum(all_two, dgate, low).reshape(by_rows), "x", 0)
    up_terms = outer_sum(all_two, dupward, low).reshape(by_rows)
    dhidden_two = (times_transposed(dgate, gate_own) + times_transposed(dupward, up_own)).astype(low)
    dhidden_two, spread, down_x = together(dhidden_two, spread, down_x)
    final = (resid + spread).astype(low)
    grad_down, down_h = halves(add(grad_down, down_x), "h", 0)
    up_terms, up_x = halves(up_terms, "x", 0)
    dhidden_two = scatter_row(5, dhidden_two)[0]
    dhidden_two, gate_x, down_h = together(dhidden_two, gate_x, down_h)
    gate_terms, gate_h = halves(add(gate_terms, gate_x), "h", 1)
    grad_down = grad_down.astype(wide) + down_h.astype(wide)

    dresid_part, dgain_two = norm_back(dhidden_two, resid, scale_two, gain_two)
    dresid = grad_home.astype(wide) + dresid_part
    branch_all = gather_row(dresid.astype(low), 7)
    branch_all, up_x, gate_h = together(branch_all, up_x, gate_h)
    up_terms, up_h = halves(add(up_terms, up_x), "h", 1)
    gate_terms = add(gate_terms, gate_h).reshape(n_group, shard, ff_pad)
    gate_terms = all_to_all_row(gate_terms)
    dmixed = times_transposed(branch_all, out_own, low)
    grad_out = outer_sum(mixed, branch_all, low)
    if natural:
        grad_out, out_x = halves(grad_out.reshape(2, 2, head_dim // 2, width), "x", 0)
    else:
        whole = jnp.zeros((n_group * heads * head_dim, width), wide)
        whole = lax.dynamic_update_slice_in_dim(
            whole, grad_out.astype(wide), me * heads * head_dim, 0
        )
        grad_out = lax.psum_scatter(whole, every, scatter_dimension=0, tiled=True)
        out_x = jnp.zeros((8, 128), low)
    dquery, dkv = attend_back(
        ends, query, dmixed, mixed, packed, logs, cosine, sine, heads, scale
    )
    head_terms = outer_sum(all_latent, dquery, low).reshape(n_x, 2, 2, -1, heads * head_dim)
    head_terms, head_x = halves(head_terms, "x", 0)
    dlow = times_transposed(dquery, up_query, low)
    dlow, gate_terms = together(dlow, gate_terms)
    dlow, dkv = scatter_row(8, dlow, dkv)
    dlow, up_h, out_x, head_x = together(dlow, up_h, out_x, head_x)
    up_terms = add(up_terms, up_h).reshape(n_group, shard, ff_pad)
    up_terms = all_to_all_row(up_terms)
    head_terms, head_h = halves(add(head_terms, head_x), "h", 1)
    if natural:
        grad_out = add(grad_out, out_x)
        kept, out_y = pick(grad_out, y), flip(pick(grad_out, 1 - y), "y")

    dkeys = rotate_back(dkv[:, :head_dim], own_cos, own_sin).astype(low)
    dvalues = dkv[:, head_dim:].astype(low)
    dlatent, dgain_latent = norm_back(dlow, latent, scale_latent, gain_latent)
    nothing = jnp.zeros((count, 128), low)
    dmapped = jnp.concatenate([dlatent.astype(low), dkeys, dvalues, nothing], axis=1)
    dhidden = times_transposed(dmapped, in_full)
    dinput_part, dgain_one = norm_back(dhidden, inputs, scale_one, gain_one)
    grad_tokens = (dresid + dinput_part).astype(low)
    grad_in = outer_sum(hidden, dmapped[:, :mapped_width], low).reshape(n_dev, shard, -1)
    gain_terms = jnp.zeros((n_dev, shard, 128), low)
    gain_terms = gain_terms.at[:, 0, :shard].set(dgain_one.reshape(n_dev, -1).astype(low))
    gain_terms = gain_terms.at[:, 1, :shard].set(dgain_two.reshape(n_dev, -1).astype(low))
    gain_terms = gain_terms.at[:, 2, : query_gain.shape[0]].set(
        dgain_latent.reshape(n_dev, -1).astype(low)
    )
    terms = jnp.concatenate([grad_in, gain_terms], axis=2)
    terms, up_terms = together(terms, up_terms)
    if natural:
        terms, out_y, head_h = together(terms, out_y, head_h)
        by_h = jnp.stack([jnp.where(y == 0, kept, out_y), jnp.where(y == 0, out_y, kept)])
        kept, out_h = halves(by_h, "h", 0)
        output = flip_cross(final)
        head_terms = add(head_terms, head_h).reshape(n_group, rows_up, heads * head_dim)
        head_terms = all_to_all_row(head_terms)
        summed, grad_tokens = shut_sum(terms, grad_tokens, 9)
        summed, out_h, output, head_terms = together(summed, out_h, output, head_terms)
        output = choose_home(final, output)
        grad_out = kept.astype(wide) + out_h.astype(wide)
    else:
        summed = lax.psum_scatter(terms.astype(wide), every, scatter_dimension=0, tiled=False)
        grad_tokens = swap_home(grad_tokens)
        output = swap_home(final)
        head_terms = add(head_terms, head_h).reshape(n_group, rows_up, heads * head_dim)
        head_terms = all_to_all_row(head_terms)
    grad_gate, grad_upward = join_columns(gate_terms, up_terms, ff_part, order)
    if natural:
        grad_uquery = head_terms.reshape(2, 2, 2, rows_up, 2, head_dim)
        grad_uquery = grad_uquery.transpose(3, 4, 0, 2, 1, 5)
    else:
        grad_uquery = head_terms.transpose(1, 0, 2)
    grad_uquery = grad_uquery.reshape(rows_up, -1).astype(wide)
    return (
        output,
        grad_tokens.astype(wide),
        summed[0, mapped_width : mapped_width + shard],
        summed[:, :latent_width],
        summed[2, mapped_width : mapped_width + query_gain.shape[0]],
        grad_uquery,
        summed[:, latent_width : latent_width + head_dim],
        summed[:, latent_width + head_dim : mapped_width],
        grad_out,
        summed[1, mapped_width : mapped_width + shard],
        grad_gate,
        grad_upward,
        grad_down,
    )


def solution(mesh):
    n_dp, n_seq = mesh.shape["dp"], mesh.shape["seq"]
    fine = Mesh(mesh.devices.reshape(n_dp // 2, 2, 2, n_seq // 4, 2), every)
    rows, flat = P(every, None), P(every)
    placed = (rows, P(("x", "c"), None), rows, flat, rows, flat) + (rows,) * 4 + (flat,) + (rows,) * 3
    return jax.shard_map(
        on_device,
        mesh=fine,
        in_specs=placed,
        out_specs=(rows, rows, flat, rows, flat) + (rows,) * 4 + (flat,) + (rows,) * 3,
        check_vma=False,
    )
```

```python
import functools
import math

import jax
import jax.numpy as jnp
from jax import lax
from jax.experimental import pallas as pl
from jax.experimental.pallas import tpu as pltpu
from jax.sharding import Mesh, PartitionSpec as P

norm_eps = 1e-05
masked_value = -1e30
every = ("x", "c", "h", "l", "y")
group = ("c", "l", "y")
low = jnp.bfloat16
wide = jnp.float32


def rms_scale(values):
    return lax.rsqrt(jnp.mean(values * values, axis=-1, keepdims=True) + norm_eps)


def rotate(values, cosine, sine):
    half = values.shape[-1] // 2
    a, b = values[..., :half], values[..., half:]
    return jnp.concatenate([a * cosine - b * sine, b * cosine + a * sine], axis=-1)


def rotate_back(values, cosine, sine):
    half = values.shape[-1] // 2
    a, b = values[..., :half], values[..., half:]
    return jnp.concatenate([a * cosine + b * sine, b * cosine - a * sine], axis=-1)


def norm_back(incoming, source, scale, gain):
    weighted = incoming * gain
    source_grad = scale * weighted - source * (scale * scale * scale) * jnp.mean(
        weighted * source, axis=-1, keepdims=True
    )
    return source_grad, jnp.sum(incoming * source * scale, axis=0)


def dot(left, right, out=wide):
    return jnp.dot(left, right, preferred_element_type=wide).astype(out)


def outer_sum(left, right, out=wide):
    return lax.dot_general(
        left, right, (((0,), (0,)), ((), ())), preferred_element_type=wide
    ).astype(out)


def times_transposed(left, right, out=wide):
    return lax.dot_general(
        left, right, (((1,), (1,)), ((), ())), preferred_element_type=wide
    ).astype(out)


def pick(array, index, axis=0):
    return lax.dynamic_index_in_dim(array, index, axis, keepdims=False)


def after(value, *done):
    return lax.optimization_barrier((value,) + done)[0]


def together(*values):
    return lax.optimization_barrier(values)


def flip(value, axis):
    return lax.ppermute(value, axis, [(0, 1), (1, 0)])


def flip_cross(value):
    return lax.ppermute(value, ("c", "h"), [(1, 2), (2, 1)])


def choose_home(value, moved):
    return jnp.where(lax.axis_index("c") == lax.axis_index("h"), value, moved)


def swap_home(value):
    return choose_home(value, flip_cross(value))


def group_place():
    return (
        lax.axis_index("c") * lax.axis_size("l") + lax.axis_index("l")
    ) * 2 + lax.axis_index("y")


def all_to_all_row(blocks):
    return lax.all_to_all(blocks, group, 0, 0, tiled=True)


def send(value, offsets):
    return lax.ppermute(value, group, [(i, i ^ offsets[i // 4]) for i in range(8)])


def scatter_row_async(state, stage):
    core = lax.axis_index("c")
    me = lax.axis_index("l") * 2 + lax.axis_index("y")
    first, second = 1 + core, 2 - core
    if stage == 0:
        return state[0], flip(state[1], "c")
    own, moved = state[:2]

    def block(index):
        return pick(own, index).astype(wide) + pick(moved, index).astype(wide)

    if stage == 1:
        far = send(block(me ^ 3).astype(low), (2, 1))
        return own, moved, far, send(block(me ^ second).astype(low), (2, 1))
    far, side = state[2:4]
    if stage == 2:
        return state + (send((block(me ^ first) + far.astype(wide)).astype(low), (1, 2)),)
    return block(me) + side.astype(wide) + state[4].astype(wide)


def sum_columns(terms, h_dim):
    for axis, dim in (("x", 0), ("h", h_dim)):
        terms = jnp.moveaxis(terms, dim, 0).astype(wide)
        terms = lax.psum_scatter(terms, axis, scatter_dimension=0, tiled=False).astype(low)
    return terms


def halves(terms, axis, dim):
    me = lax.axis_index(axis)
    return pick(terms, me, dim), flip(pick(terms, 1 - me, dim), axis)


def add(own, came):
    return (own.astype(wide) + came.astype(wide)).astype(low)


def other(value, flag=1):
    return value + flag * (1 - 2 * value)


def greet(peers):
    barrier = pltpu.get_barrier_semaphore()
    for peer in peers:
        pl.semaphore_signal(barrier, inc=1, device_id=peer, device_id_type=pl.DeviceIdType.MESH)
    pl.semaphore_wait(barrier, len(peers))


def remote(source, target, send_sem, recv_sem, peer):
    return pltpu.make_async_remote_copy(
        src_ref=source,
        dst_ref=target,
        send_sem=send_sem,
        recv_sem=recv_sem,
        device_id=peer,
        device_id_type=pl.DeviceIdType.MESH,
    )


def in_hbm():
    return pl.BlockSpec(memory_space=pl.ANY)


def open_kernel(n_sets, n_swaps, small_ref, out_ref, *refs):
    sets, refs = refs[:n_sets], refs[n_sets:]
    swaps, refs = refs[:n_swaps], refs[n_swaps:]
    (full_ref, heads_ref), refs = refs[:2], refs[2:]
    set_outs, refs = refs[:n_sets], refs[n_sets:]
    swap_outs, refs = refs[:n_swaps], refs[n_swaps:]
    (small_buf, out_buf), refs = refs[:2], refs[2:]
    set_bufs, refs = refs[:n_sets], refs[n_sets:]
    swap_bufs, refs = refs[:n_swaps], refs[n_swaps:]
    sends, recvs, swap_sends, swap_recvs, set_sends, set_recvs, out_sems, head_sems, loads_sem, stores_sem = refs
    x, c, h, l, y = [lax.axis_index(a) for a in every]
    hops = {
        1: {"h": other(h)},
        2: {"l": other(l)},
        4: {"y": other(y)},
        8: {"x": other(x)},
        16: {"c": other(c)},
    }
    cross = {"c": other(c), "h": other(h)}
    me = (c * 2 + l) * 2 + y

    def group_peer(k):
        return {"c": other(c, k // 4), "l": other(l, k // 2 % 2), "y": other(y, k % 2)}

    def group_index(k):
        peer = group_peer(k)
        return (peer["c"] * 2 + peer["l"]) * 2 + peer["y"]

    def index(code):
        at_x, at_l = other(x, code // 8 % 2), other(l, code // 2 % 2)
        return (((at_x * 2 + c) * 2 + other(h, code % 2)) * 2 + at_l) * 2 + other(y, code // 4 % 2)

    beside, corner = {"y": other(y)}, {"h": other(h), "y": h}
    greet(
        [hops[1], hops[8], cross, {"h": other(h), "y": other(y)}]
        + [group_peer(k) for k in range(1, 8)]
    )
    copies = []
    half = heads_ref.at[y]
    to_beside = remote(out_ref, half, out_sems.at[0], out_sems.at[1], beside)
    differ = y + h - 2 * y * h
    to_corner = remote(out_ref, half, out_sems.at[2], out_sems.at[3 + differ], corner)

    def push(code):
        block = full_ref.at[index(code)]
        source = small_ref if code == 0 else block
        for hop in (1, 2, 4, 8, 16):
            if code < hop:
                name = code + hop
                copy = remote(source, block, sends.at[name], recvs.at[name], hops[hop])
                copy.start()
                copies.append(copy)

    def set_slot(i):
        return set_outs[0].at[x, c, h, l * 2 + y] if i == 0 else set_outs[i].at[me]

    set_copies = []

    def set_push(i):
        for k in range(1, 8):
            copy = remote(
                sets[i].at[group_index(k)], set_slot(i), set_sends.at[i, k], set_recvs.at[i, k],
                group_peer(k),
            )
            copy.start()
            set_copies.append(copy)

    push(0)
    set_push(0)
    moving = [
        remote(source, target, swap_sends.at[i], swap_recvs.at[i], cross)
        for i, (source, target) in enumerate(zip(swaps, swap_outs))
    ]

    def push_moves():
        @pl.when(c != h)
        def _():
            for copy in moving:
                copy.start()

        @pl.when(y != h)
        def _():
            to_beside.start()

        to_corner.start()

    loads, stores = [], []
    locals_in = [small_ref, out_ref] + [ref.at[me] for ref in sets] + list(swaps)
    locals_buf = [small_buf, out_buf] + list(set_bufs) + list(swap_bufs)
    locals_out = [full_ref.at[index(0)], half] + [set_slot(i) for i in range(n_sets)]
    for i, (source, buf) in enumerate(zip(locals_in, locals_buf)):
        loads.append(pltpu.make_async_copy(source, buf, loads_sem.at[i]))
        loads[-1].start()
    for load in loads:
        load.wait()
    for i, (buf, target) in enumerate(zip(locals_buf, locals_out)):
        stores.append(pltpu.make_async_copy(buf, target, stores_sem.at[i]))
    keep_out = stores.pop(1)
    for store in stores:
        store.start()

    @pl.when(y == h)
    def _():
        keep_out.start()

    keeps = [
        pltpu.make_async_copy(buf, target, stores_sem.at[2 + n_sets + i])
        for i, (buf, target) in enumerate(zip(swap_bufs, swap_outs))
    ]

    @pl.when(c == h)
    def _():
        for keep in keeps:
            keep.start()

    def arrived(name):
        remote(small_ref, small_ref, sends.at[name], recvs.at[name], hops[16]).wait_recv()

    def head_copy(at_h, slot, peer):
        part = set_outs[0].at[x, :, at_h]
        copy = remote(part, part, head_sems.at[slot], head_sems.at[3 + slot], peer)
        copy.start()
        return copy

    head_copies = []
    for n, code in enumerate((2, 4, 1, 6, 3, 5, 7, 8, 9, 10, 11, 12, 13, 14, 15)):
        arrived(code)
        push(code)
        if n == 2:
            for copy in set_copies:
                copy.wait()
            for store in stores:
                store.wait()
            done = len(set_copies)
            for i in range(1, n_sets):
                set_push(i)
            head_copies.append(head_copy(h, 0, hops[1]))
            head_copies.append(head_copy(h, 1, hops[8]))
            push_moves()
        if n == 9:
            head_copies[0].wait_recv()
            head_copies.append(head_copy(other(h), 2, hops[8]))
    for code in range(16):
        arrived(16 + code)
    for copy in copies:
        copy.wait_send()
    for copy in set_copies[done:]:
        copy.wait()
    head_copies[0].wait_send()
    for copy in head_copies[1:]:
        copy.wait()
    to_corner.wait_send()

    @pl.when(y != h)
    def _():
        to_beside.wait_send()
        remote(out_ref, half, out_sems.at[2], out_sems.at[3], corner).wait_recv()
        remote(out_ref, half, out_sems.at[2], out_sems.at[4], corner).wait_recv()

    @pl.when(y == h)
    def _():
        keep_out.wait()
        to_beside.wait_recv()

    @pl.when(c != h)
    def _():
        for copy in moving:
            copy.wait()

    @pl.when(c == h)
    def _():
        for keep in keeps:
            keep.wait()


def open_exchange(small, out_rows, sets, swaps):
    n_sets, n_swaps = len(sets), len(swaps)
    args = [small, out_rows] + sets + swaps
    out_shape = [
        jax.ShapeDtypeStruct((32,) + small.shape, low),
        jax.ShapeDtypeStruct((2,) + out_rows.shape, low),
    ]
    out_shape += [jax.ShapeDtypeStruct((2, 2, 2, 4) + sets[0].shape[1:], low)]
    out_shape += [jax.ShapeDtypeStruct(a.shape, a.dtype) for a in sets[1:] + swaps]
    sem = pltpu.SemaphoreType.DMA
    out = pl.pallas_call(
        functools.partial(open_kernel, n_sets, n_swaps),
        in_specs=[in_hbm()] * len(args),
        out_specs=[in_hbm()] * len(args),
        out_shape=out_shape,
        scratch_shapes=[pltpu.VMEM(small.shape, low), pltpu.VMEM(out_rows.shape, low)]
        + [pltpu.VMEM(a.shape[1:], a.dtype) for a in sets]
        + [pltpu.VMEM(a.shape, a.dtype) for a in swaps]
        + [sem((32,)), sem((32,)), sem((n_swaps,)), sem((n_swaps,))]
        + [sem((n_sets, 8)), sem((n_sets, 8)), sem((5,)), sem((6,))]
        + [sem((len(args),)), sem((len(args),))],
        compiler_params=pltpu.CompilerParams(
            collective_id=1, has_side_effects=True, vmem_limit_bytes=16 * 1024 * 1024
        ),
        cost_estimate=pl.CostEstimate(flops=0, bytes_accessed=150 * 1024 * 1024, transcendentals=0),
        name="open_exchange",
    )(*args)
    return out[0], out[1], out[2 : 2 + n_sets], out[2 + n_sets :]


def row_peers(even):
    c, l, y = [lax.axis_index(a) for a in group]
    if even:
        near = {"l": other(l, c), "y": other(y, 1 - c)}
        side = {"l": other(l, 1 - c), "y": other(y, c)}
    else:
        near = {"l": other(l), "y": y}
        side = {"l": l, "y": other(y)}
    return c, l, y, near, side, {"c": other(c)}


def gather_kernel(even, chunks, kinds, own_ref, *refs):
    n = len(kinds)
    more, out_ref, more_out = refs[:n], refs[n], refs[n + 1 : 2 * n + 1]
    buf, sends, recvs, local_sems = refs[2 * n + 1 : 2 * n + 5]
    beside = Beside(kinds, more, more_out, refs[-1])
    flow = RowGather(even, chunks, own_ref, out_ref, sends, recvs)
    flow.begin(beside.peers)
    beside.start()
    load = pltpu.make_async_copy(own_ref, buf, local_sems.at[0])
    load.start()
    load.wait()
    store = pltpu.make_async_copy(buf, out_ref.at[flow.me], local_sems.at[1])
    store.start()
    flow.take_near()
    flow.take_side()
    flow.take_far()
    for slot in (3, 4, 5, 6):
        flow.take(slot)
    flow.end()
    store.wait()
    beside.wait()


class Beside:
    def __init__(self, kinds, sources, targets, sems):
        x, c, h = [lax.axis_index(a) for a in ("x", "c", "h")]
        ways = {"x": {"x": other(x)}, "h": {"h": other(h)}, "cross": {"c": other(c), "h": other(h)}}
        self.peers = [ways[k] for k in sorted(set(kinds))]
        self.moves = c != h
        self.copies = [
            (kind, remote(source, target, sems.at[0, i], sems.at[1, i], ways[kind]))
            for i, (kind, source, target) in enumerate(zip(kinds, sources, targets))
        ]

    def start(self, span=slice(None)):
        for kind, copy in self.copies[span]:
            if kind == "cross":
                pl.when(self.moves)(copy.start)
            else:
                copy.start()

    def wait(self, span=slice(None)):
        for kind, copy in self.copies[span]:
            if kind == "cross":
                pl.when(self.moves)(copy.wait)
            else:
                copy.wait()


class RowGather:
    def __init__(self, even, chunks, own_ref, out_ref, sends, recvs, in_slots=False):
        c, l, y, near, side, twin = row_peers(even)
        self.peers = near, side, twin
        self.chunks, self.rows = chunks, own_ref.shape[0] // chunks
        self.own_ref, self.out_ref, self.sends, self.recvs = own_ref, out_ref, sends, recvs
        at = l * 2 + y
        near_at, side_at = near["l"] * 2 + near["y"], side["l"] * 2 + side["y"]
        far_at = other(l) * 2 + other(y)
        self.me = c * 4 + at
        self.places = [c * 4 + p for p in (near_at, side_at, far_at)]
        twins = (at, side_at, near_at, far_at) if even else (at, near_at, side_at, far_at)
        self.places += [other(c) * 4 + p for p in twins]
        self.copies = []
        self.lands = (2, 3, 6, 1, 4, 5, 7) if in_slots else None

    def land(self, slot):
        return self.lands[slot] if self.lands else self.places[slot]

    def start(self, held, k, slot, peer):
        span = pl.ds(k * self.rows, self.rows)
        source = self.own_ref.at[span] if held is None else self.out_ref.at[self.land(held), span]
        if self.lands:
            target = self.out_ref.at[self.lands[slot], span]
        else:
            target = self.out_ref.at[self.me if held is None else self.places[held], span]
        copy = remote(source, target, self.sends.at[slot, k], self.recvs.at[slot, k], peer)
        copy.start()
        self.copies.append(copy)

    def begin(self, more_peers=()):
        near, side, twin = self.peers
        greet([near, side, twin, *more_peers])
        for k in range(self.chunks):
            self.start(None, k, 0, near)
            self.start(None, k, 1, side)
            self.start(None, k, 3, twin)

    def arrived(self, slot, k):
        span = self.own_ref.at[pl.ds(k * self.rows, self.rows)]
        target = self.out_ref.at[self.land(slot), pl.ds(k * self.rows, self.rows)]
        remote(
            span, target, self.sends.at[slot, k], self.recvs.at[slot, k], self.peers[2]
        ).wait_recv()

    def take(self, slot):
        for k in range(self.chunks):
            self.arrived(slot, k)

    def take_near(self):
        near, side, twin = self.peers
        for k in range(self.chunks):
            self.arrived(0, k)
            self.start(0, k, 2, side)
            self.start(0, k, 4, twin)

    def take_side(self):
        for k in range(self.chunks):
            self.arrived(1, k)
            self.start(1, k, 5, self.peers[2])

    def take_far(self):
        for k in range(self.chunks):
            self.arrived(2, k)
            self.start(2, k, 6, self.peers[2])

    def end(self):
        for copy in self.copies:
            copy.wait_send()


def gather_row(value, number, even=False, kinds=(), more=()):
    if lax.axis_size("l") != 2:
        return lax.all_gather(value, group, axis=0, tiled=True)
    chunks = 4 if value.shape[0] % 64 == 0 else 1
    args = [value, *more]
    out_shape = [jax.ShapeDtypeStruct((8,) + value.shape, low)]
    out_shape += [jax.ShapeDtypeStruct(a.shape, low) for a in more]
    out = pl.pallas_call(
        functools.partial(gather_kernel, even, chunks, kinds),
        in_specs=[in_hbm()] * len(args),
        out_specs=[in_hbm()] * len(args),
        out_shape=out_shape,
        scratch_shapes=[
            pltpu.VMEM(value.shape, low),
            pltpu.SemaphoreType.DMA((7, chunks)),
            pltpu.SemaphoreType.DMA((7, chunks)),
            pltpu.SemaphoreType.DMA((2,)),
            pltpu.SemaphoreType.DMA((2, max(1, len(more)))),
        ],
        compiler_params=pltpu.CompilerParams(
            collective_id=number, has_side_effects=True, vmem_limit_bytes=16 * 1024 * 1024
        ),
        cost_estimate=pl.CostEstimate(flops=0, bytes_accessed=80 * 1024 * 1024, transcendentals=0),
        name="gather_row",
    )(*args)
    rows = out[0].reshape(-1, value.shape[1])
    return (rows, *out[1:]) if kinds else rows


def load_columns(pieces, target, sem, first):
    x, h = lax.axis_index("x"), lax.axis_index("h")
    rows = pieces[0].shape[0]
    loads = []
    for i, piece in enumerate(pieces):
        at_x = x if i < 4 else other(x)
        at_h = h if i // 2 % 2 == 0 else other(h)
        at = pl.multiple_of(((at_x * 2 + i % 2) * 2 + at_h) * rows, rows)
        loads.append(
            pltpu.make_async_copy(piece, target.at[pl.ds(at, rows)], sem.at[first + i])
        )
    return loads


def load_rows(parts, target, sem):
    x, h = lax.axis_index("x"), lax.axis_index("h")
    rows, width = parts[0][0].shape
    loads = []
    for s, part in enumerate(parts):
        for i, (at_x, at_h) in enumerate(
            ((x, h), (x, other(h)), (other(x), h), (other(x), other(h)))
        ):
            at = pl.multiple_of((at_x * 2 + at_h) * rows, 16)
            loads.append(
                pltpu.make_async_copy(
                    part[i],
                    target.at[pl.ds(at, rows), pl.ds(s * width, width)],
                    sem.at[len(loads)],
                )
            )
            loads[-1].start()
    return loads


def wait_all(copies):
    for copy in copies:
        copy.wait()


def for_tiles(total, tile, body):
    def step(j, carry):
        body(pl.ds(pl.multiple_of(j * tile, tile), tile))
        return carry

    lax.fori_loop(0, total // tile, step, 0)


def feed_kernel(even, chunks, *refs):
    own_ref, gates, ups, grad_ref = refs[0], refs[1:9], refs[9:13], refs[13]
    up_b, up_b_h, down_a, down_a_h, down_b, refs = *refs[14:19], refs[19:]
    all_ref, inner_ref, a_ref, b_ref, down_ref, across_ref = refs[:6]
    up_b_x, up_b_xh, down_a_x, down_a_xh, down_b_x, down_b_h, down_b_xh = refs[6:13]
    xs, wg, wu, gs, total, inner_s, a_s, b_s, sends, recvs = refs[13:23]
    weight_sems, grad_sems, store_sems, own_sem, more_sems = refs[23:]
    flow = RowGather(even, chunks, own_ref, xs, sends, recvs, in_slots=True)
    beside = Beside(
        ("x", "x", "x", "x", "x", "h", "x"),
        (up_b, up_b_h, down_a, down_a_h, down_b, down_b, down_b_h),
        (up_b_x, up_b_xh, down_a_x, down_a_xh, down_b_x, down_b_h, down_b_xh),
        more_sems,
    )
    flow.begin(beside.peers)
    beside.start(slice(0, 6))
    own_load = pltpu.make_async_copy(own_ref, xs.at[0], own_sem)
    own_load.start()
    weights = load_columns(gates, wg, weight_sems, 0)
    u0, u0_h, u0_x, u0_xh = ups
    all_ups = load_columns(
        (u0, up_b, u0_h, up_b_h, u0_x, up_b_x, u0_xh, up_b_xh), wu, weight_sems, 8
    )
    late, weights = [all_ups[5], all_ups[7]], weights + all_ups[:5] + [all_ups[6]]
    for load in weights:
        load.start()
    order = [flow.me] + [flow.places[s] for s in (3, 0, 1, 4, 5, 2, 6)]
    grads = [
        pltpu.make_async_copy(grad_ref.at[place], gs.at[i], grad_sems.at[i])
        for i, place in enumerate(order)
    ]
    for load in grads:
        load.start()
    stores = []
    columns, width = wg.shape[1], wg.shape[0]

    def work(pair):
        both = pl.ds(2 * pair, 2)
        x = xs[both].reshape(-1, width)

        def tile(cols):
            gate = jnp.dot(x, wg[:, cols], preferred_element_type=wide)
            upward = jnp.dot(x, wu[:, cols], preferred_element_type=wide)
            sigma = jax.nn.sigmoid(gate)
            swish = gate * sigma
            shape = (2, -1, upward.shape[1])
            inner_s[both, :, cols] = (swish * upward).astype(low).reshape(shape)
            b_s[both, :, cols] = swish.astype(low).reshape(shape)
            factor = upward * sigma * (1.0 + gate * (1.0 - sigma))
            a_s[both, :, cols] = factor.astype(low).reshape(shape)

        tile(slice(None))
        for i in (2 * pair, 2 * pair + 1):
            place = order[i]
            for j, (buf, target) in enumerate(
                ((xs, all_ref), (inner_s, inner_ref), (a_s, a_ref), (b_s, b_ref))
            ):
                store = pltpu.make_async_copy(buf.at[i], target.at[place], store_sems.at[i, j])
                store.start()
                stores.append(store)
            grads[i].wait()
        inner = inner_s[both].reshape(-1, columns)

        def down_tile(cols):
            part = contract(inner, gs[both, :, cols].reshape(inner.shape[0], -1), ((0,), (0,)))
            if pair == 0:
                total[:, cols] = part
            else:
                total[:, cols] += part

        for_tiles(width, width // 2, down_tile)

    own_load.wait()
    flow.take(3)
    flow.take_near()
    flow.take_side()
    beside.wait(slice(0, 2))
    for load in late:
        load.start()
    wait_all(weights + late)
    work(0)
    work(1)
    flow.take(4)
    flow.take(5)
    beside.wait(slice(5, 6))
    beside.start(slice(6, 7))
    work(2)
    flow.take_far()
    flow.take(6)
    work(3)
    rows = down_ref.shape[0]
    x = lax.axis_index("x")
    down_ref[...] = total[pl.ds(pl.multiple_of(x * rows, 16), rows), :].astype(low)
    across_ref[...] = total[pl.ds(pl.multiple_of(other(x) * rows, 16), rows), :].astype(low)
    flow.end()
    wait_all(stores)
    beside.wait(slice(2, 5))
    beside.wait(slice(6, 7))


def feed_forward(own, gates, ups, grad_all, up_b, downs, used, number):
    count, width = own.shape
    columns = gates[0].shape[1]
    chunks = 4 if count % 64 == 0 else 1
    row, part = (8, count, width), (8, count, columns)
    sem = pltpu.SemaphoreType.DMA
    flops = 2 * 8 * count * width * columns * 3
    args = [own, *gates, *ups, grad_all.reshape(row), *up_b, *downs]
    down_shape = downs[0].shape
    moved = [up_b[0].shape] * 2 + [down_shape] * 5
    shapes = [row, part, part, part, (used // 2, width), (used // 2, width)] + moved
    vmem = pl.BlockSpec(memory_space=pltpu.VMEM)
    return pl.pallas_call(
        functools.partial(feed_kernel, False, chunks),
        in_specs=[in_hbm()] * len(args),
        out_specs=[in_hbm()] * 4 + [vmem] * 2 + [in_hbm()] * 7,
        out_shape=[jax.ShapeDtypeStruct(s, low) for s in shapes],
        scratch_shapes=[
            pltpu.VMEM(row, low),
            pltpu.VMEM((width, columns), low),
            pltpu.VMEM((width, columns), low),
            pltpu.VMEM(row, low),
            pltpu.VMEM((columns, width), wide),
            pltpu.VMEM(part, low),
            pltpu.VMEM(part, low),
            pltpu.VMEM(part, low),
            sem((7, chunks)),
            sem((7, chunks)),
            sem((16,)),
            sem((8,)),
            sem((8, 4)),
            sem,
            sem((2, 7)),
        ],
        compiler_params=pltpu.CompilerParams(
            collective_id=number, has_side_effects=True, vmem_limit_bytes=56 * 1024 * 1024
        ),
        cost_estimate=pl.CostEstimate(
            flops=flops, bytes_accessed=100 * 1024 * 1024, transcendentals=0
        ),
        name="feed_forward",
    )(*args)


def feed_back_kernel(
    even, chunks, *refs,
):
    grad_ref, a_ref, b_ref, inner_ref, all_ref = refs[:5]
    gates, ups, downs, refs = refs[5:13], refs[13:21], refs[21:29], refs[29:]
    out_ref, terms_own, terms_twin, gate_own, gate_across, up_own, up_across = refs[:7]
    refs = refs[7:]
    gx, wg, wu, wd, a_s, b_s, inner_s, terms_s, own_buf, twin_buf, twin_out = refs[:11]
    far_out, side_out, near_out, far_in, side_in, near_in = refs[11:17]
    sends, recvs, weight_sems, down_sems, block_sems, all_sems, terms_sems = refs[17:]
    c, l, y, near, side, twin = row_peers(even)
    rows = out_ref.shape[0] // chunks
    columns, width = wd.shape
    used = 4 * downs[0].shape[0]
    me = l * 2 + y
    near_at, side_at = near["l"] * 2 + near["y"], side["l"] * 2 + side["y"]
    far_at = other(l) * 2 + other(y)
    own_order = (far_at, side_at, near_at, me)
    twin_order = (far_at, near_at, side_at, me) if even else own_order
    pairs = []
    for p, q in zip(twin_order, own_order):
        pairs += [(other(c) * 4 + p, p, True), (c * 4 + q, q, False)]
    downs = load_rows((downs[:4], downs[4:]), wd, down_sems)
    blocks = []
    for i, (place, _, _) in enumerate(pairs):
        loads = [
            pltpu.make_async_copy(source.at[place], buf.at[i], block_sems.at[i, j])
            for j, (source, buf) in enumerate(
                ((grad_ref, gx), (a_ref, a_s), (b_ref, b_s), (inner_ref, inner_s))
            )
        ]
        for load in loads:
            load.start()
        blocks.append(loads)
    weights = load_columns(gates, wg, weight_sems, 0) + load_columns(ups, wu, weight_sems, 8)
    for load in weights:
        load.start()
    wd[used:, :] = jnp.zeros((columns - used, width), low)
    greet([near, side, twin])
    copies = []

    def start(source, target, slot, k, peer):
        copy = remote(source, target, sends.at[slot, k], recvs.at[slot, k], peer)
        copy.start()
        copies.append(copy)

    def arrived(slot, k):
        span = far_in.at[pl.ds(k * rows, rows)]
        remote(span, span, sends.at[slot, k], recvs.at[slot, k], twin).wait_recv()

    def block_arrived(slot):
        remote(
            own_buf.at[0], twin_buf.at[0], sends.at[slot, 0], recvs.at[slot, 0], twin
        ).wait_recv()

    def term(pair, twin_target, own_target):
        span = pl.ds(2 * pair, 2)
        wait_all(blocks[2 * pair] + blocks[2 * pair + 1])
        grads = gx[span].reshape(-1, width)

        dinner = contract(grads, wd[...], ((1,), (1,))).reshape(2, -1, columns)
        a_s[span] = (dinner * a_s[span].astype(wide)).astype(low)
        b_s[span] = (dinner * b_s[span].astype(wide)).astype(low)
        if pair == 0:
            wait_all(weights)
        dgate = a_s[span].reshape(-1, columns)
        dup = b_s[span].reshape(-1, columns)

        def second(cols):
            part = contract(dgate, wg[cols, :], ((1,), (1,)))
            part = (part + contract(dup, wu[cols, :], ((1,), (1,)))).astype(low)
            half = part.shape[0] // 2
            twin_target[:, cols] = part[:half]
            own_target[:, cols] = part[half:]

        for_tiles(width, width // 2, second)

    def both(place, span):
        return own_buf[place, span, :].astype(wide) + twin_buf[place, span, :].astype(wide)

    spans = [(k, pl.ds(k * rows, rows)) for k in range(chunks)]
    wait_all(downs)
    for i in range(4):
        twin_place, own_place = pairs[2 * i][1], pairs[2 * i + 1][1]
        term(i, twin_out.at[i], own_buf.at[own_place])
        start(twin_out.at[i], twin_buf.at[twin_place], 3 + i, 0, twin)
        if i >= 1:
            block_arrived(2 + i)
        if i == 1:
            for k, span in spans:
                far_out[span, :] = both(far_at, span).astype(low)
                start(far_out.at[span], far_in.at[span], 0, k, side)
        if i == 2:
            for k, span in spans:
                side_out[span, :] = both(side_at, span).astype(low)
                start(side_out.at[span], side_in.at[span], 1, k, side)
    block_arrived(6)
    all_loads = [
        pltpu.make_async_copy(all_ref.at[pairs[i][0]], gx.at[i], all_sems.at[i]) for i in range(8)
    ]
    for load in all_loads:
        load.start()
    stores = []

    def output_term(pair):
        span = pl.ds(2 * pair, 2)
        if pair:
            wait_all(stores[2 * pair - 2 :])
        inner = inner_s[span].reshape(-1, columns)

        def tile(cols):
            part = jnp.dot(inner, wd[:, cols], preferred_element_type=wide)
            terms_s[:, :, cols] = part.astype(low).reshape(2, -1, width // 2)

        for_tiles(width, width // 2, tile)
        for i in range(2):
            _, place, is_twin = pairs[2 * pair + i]
            store = pltpu.make_async_copy(
                terms_s.at[i],
                (terms_twin if is_twin else terms_own).at[place],
                terms_sems.at[2 * pair + i],
            )
            store.start()
            stores.append(store)

    for i in range(2):
        output_term(i)
    for k, span in spans:
        arrived(0, k)
        near_out[span, :] = (both(near_at, span) + far_in[span, :].astype(wide)).astype(low)
        start(near_out.at[span], near_in.at[span], 2, k, near)
    for i in range(2, 4):
        output_term(i)
    wait_all(all_loads)
    dgates = a_s[...].reshape(-1, columns)
    dups = b_s[...].reshape(-1, columns)

    x_at = lax.axis_index("x")
    half = width // 2
    for gate_ref, up_ref, at in ((gate_across, up_across, other(x_at)), (gate_own, up_own, x_at)):
        for j in range(2):
            cols = pl.ds(pl.multiple_of(at * half + j * (half // 2), 128), half // 2)
            rows_out = slice(j * (half // 2), (j + 1) * (half // 2))
            x = gx[:, :, cols].reshape(-1, half // 2)
            gate_ref[rows_out, :] = contract(x, dgates, ((0,), (0,))).astype(low)
            up_ref[rows_out, :] = contract(x, dups, ((0,), (0,))).astype(low)
    for k, span in spans:
        arrived(1, k)
        arrived(2, k)
        out_ref[span, :] = (
            both(me, span) + side_in[span, :].astype(wide) + near_in[span, :].astype(wide)
        )
    wait_all(stores[6:])
    for copy in copies:
        copy.wait_send()


def feed_back(grad_all, a, b, inner, all_two, gate_pieces, up_pieces, down_parts, number):
    count, width = a.shape[1], all_two.shape[2]
    columns = a.shape[2]
    chunks = 4 if count % 64 == 0 else 1
    row, part = (8, count, width), (8, count, columns)
    sem = pltpu.SemaphoreType.DMA
    block = pltpu.VMEM((count, width), low)
    vmem = pl.BlockSpec(memory_space=pltpu.VMEM)
    flops = 2 * 8 * count * width * columns * 6
    args = [grad_all.reshape(row), a, b, inner, all_two, *gate_pieces, *up_pieces]
    args += [piece for parts in down_parts for piece in parts]
    return pl.pallas_call(
        functools.partial(feed_back_kernel, True, chunks),
        in_specs=[in_hbm()] * len(args),
        out_specs=[vmem, in_hbm(), in_hbm(), vmem, vmem, vmem, vmem],
        out_shape=[jax.ShapeDtypeStruct((count, width), wide)]
        + [jax.ShapeDtypeStruct((4, count, width), low)] * 2
        + [jax.ShapeDtypeStruct((width // 2, columns), low)] * 4,
        scratch_shapes=[
            pltpu.VMEM(row, low),
            pltpu.VMEM((width, columns), low),
            pltpu.VMEM((width, columns), low),
            pltpu.VMEM((columns, width), low),
            pltpu.VMEM(part, low),
            pltpu.VMEM(part, low),
            pltpu.VMEM(part, low),
            pltpu.VMEM((2, count, width), low),
            pltpu.VMEM((4, count, width), low),
            pltpu.VMEM((4, count, width), low),
            pltpu.VMEM((4, count, width), low),
        ]
        + [block] * 6
        + [
            sem((7, chunks)),
            sem((7, chunks)),
            sem((16,)),
            sem((8,)),
            sem((8, 4)),
            sem((8,)),
            sem((8,)),
        ],
        compiler_params=pltpu.CompilerParams(
            collective_id=number, has_side_effects=True, vmem_limit_bytes=60 * 1024 * 1024
        ),
        cost_estimate=pl.CostEstimate(
            flops=flops, bytes_accessed=100 * 1024 * 1024, transcendentals=0
        ),
        name="feed_back",
    )(*args)


def scatter_kernel(even, chunks, n, kinds, *refs):
    m = len(kinds)
    terms, more, refs = refs[:n], refs[n : n + m], refs[n + m :]
    outs, more_out, refs = refs[:n], refs[n : n + m], refs[n + m :]
    bufs, (sends, recvs, local_sems, more_sems) = refs[: 8 * n], refs[8 * n :]
    beside = Beside(kinds, more, more_out, more_sems)
    bufs = [bufs[8 * a : 8 * a + 8] for a in range(n)]
    c, l, y, near, side, twin = row_peers(even)
    rows = outs[0].shape[0] // chunks
    me = l * 2 + y
    near_at, side_at = near["l"] * 2 + near["y"], side["l"] * 2 + side["y"]
    far_at = other(l) * 2 + other(y)
    greet([near, side, twin] + beside.peers)
    beside.start()
    copies = []

    def start(source, target, a, slot, k, peer):
        copy = remote(source, target, sends.at[a, slot, k], recvs.at[a, slot, k], peer)
        copy.start()
        copies.append(copy)

    parts = [(a, k, pl.ds(k * rows, rows)) for k in range(chunks) for a in range(n)]
    twin_side, twin_near = (near_at, side_at) if even else (side_at, near_at)
    for slot, place in ((3, far_at), (4, twin_side), (5, twin_near), (6, me)):
        for a, k, span in parts:
            start(
                terms[a].at[other(c) * 4 + place, span], bufs[a][1].at[place, span], a, slot, k, twin
            )
    loads = []
    for slot, place in ((0, far_at), (1, side_at), (2, near_at), (3, me)):
        for a in range(n):
            load = pltpu.make_async_copy(
                terms[a].at[c * 4 + place], bufs[a][0].at[place], local_sems.at[a, slot]
            )
            load.start()
            loads.append(load)

    def arrived(a, slot, k):
        span = bufs[a][5].at[pl.ds(k * rows, rows)]
        remote(span, span, sends.at[a, slot, k], recvs.at[a, slot, k], twin).wait_recv()

    def both(a, place, span):
        own, came = bufs[a][0], bufs[a][1]
        return own[place, span, :].astype(wide) + came[place, span, :].astype(wide)

    for load in loads[: 2 * n]:
        load.wait()
    for a, k, span in parts:
        far_out, far_in = bufs[a][2], bufs[a][5]
        arrived(a, 3, k)
        far_out[span, :] = both(a, far_at, span).astype(low)
        start(far_out.at[span], far_in.at[span], a, 0, k, side)
    for a, k, span in parts:
        side_out, side_in = bufs[a][3], bufs[a][6]
        arrived(a, 4, k)
        side_out[span, :] = both(a, side_at, span).astype(low)
        start(side_out.at[span], side_in.at[span], a, 1, k, side)
    for load in loads[2 * n :]:
        load.wait()
    for a, k, span in parts:
        near_out, far_in, near_in = bufs[a][4], bufs[a][5], bufs[a][7]
        arrived(a, 5, k)
        arrived(a, 0, k)
        near_out[span, :] = (both(a, near_at, span) + far_in[span, :].astype(wide)).astype(low)
        start(near_out.at[span], near_in.at[span], a, 2, k, near)
    for a, k, span in parts:
        arrived(a, 6, k)
        arrived(a, 1, k)
        outs[a][span, :] = both(a, me, span) + bufs[a][6][span, :].astype(wide)
    for a, k, span in parts:
        arrived(a, 2, k)
        outs[a][span, :] += bufs[a][7][span, :].astype(wide)
    for copy in copies:
        copy.wait_send()
    beside.wait()


def scatter_row(number, *terms, even=False, kinds=(), more=()):
    if lax.axis_size("l") != 2:
        return [
            lax.psum_scatter(t.astype(wide), group, scatter_dimension=0, tiled=True) for t in terms
        ]
    terms = [t.reshape(8, -1, t.shape[1]) for t in terms]
    n, count = len(terms), terms[0].shape[1]
    chunks = 4 if count % 64 == 0 else 1
    scratch = []
    for t in terms:
        scratch += [pltpu.VMEM((4, count, t.shape[2]), low)] * 2
        scratch += [pltpu.VMEM((count, t.shape[2]), low)] * 6
    return pl.pallas_call(
        functools.partial(scatter_kernel, even, chunks, n, kinds),
        in_specs=[in_hbm()] * (n + len(more)),
        out_specs=[pl.BlockSpec(memory_space=pltpu.VMEM)] * n + [in_hbm()] * len(more),
        out_shape=[jax.ShapeDtypeStruct((count, t.shape[2]), wide) for t in terms]
        + [jax.ShapeDtypeStruct(a.shape, low) for a in more],
        scratch_shapes=scratch
        + [
            pltpu.SemaphoreType.DMA((n, 7, chunks)),
            pltpu.SemaphoreType.DMA((n, 7, chunks)),
            pltpu.SemaphoreType.DMA((n, 4)),
            pltpu.SemaphoreType.DMA((2, max(1, len(more)))),
        ],
        compiler_params=pltpu.CompilerParams(
            collective_id=number, has_side_effects=True, vmem_limit_bytes=24 * 1024 * 1024
        ),
        cost_estimate=pl.CostEstimate(flops=0, bytes_accessed=80 * 1024 * 1024, transcendentals=0),
        name="scatter_row",
    )(*terms, *more)


def norm_back_rows(incoming, source, gain):
    scale = rms_scale(source)
    weighted = incoming * gain
    mean = jnp.mean(weighted * source, axis=-1, keepdims=True)
    grad = scale * weighted - source * (scale * scale * scale) * mean
    return grad, jnp.sum(incoming * source * scale, axis=0, keepdims=True)


def shut_kernel(part, head_dim, order, n_in, n_out, *refs):
    ins, outs, refs = refs[:n_in], refs[n_in : n_in + n_out], refs[n_in + n_out :]
    (
        dlow_ref, dkv_ref, latent_ref, gain_latent_ref, cos_ref, sin_ref, hidden_ref, in_full_ref,
        home_ref, gain_one_ref, dresid_ref, gain_two_ref, gate_ref, up_ref, heads_ref, final_ref,
        kept_ref, across_ref,
    ) = ins
    sum_ref, tokens_ref, output_ref, gate_out, up_out, heads_out, out_ref = outs
    full, mapped, terms, gains, twin_buf, held, came, moved, swap_buf = refs[:9]
    gate_in, up_in, heads_in, final_buf, across_in = refs[9:14]
    sends, recvs, set_sends, set_recvs, swap_sems, local_sems = refs[14:]
    x, c, h, l, y = [lax.axis_index(a) for a in every]
    hops = {
        1: {"h": other(h)},
        2: {"l": other(l)},
        4: {"y": other(y)},
        8: {"x": other(x)},
    }
    twin = {"c": other(c)}
    cross = {"c": other(c), "h": other(h)}
    me = (c * 2 + l) * 2 + y

    def group_peer(k):
        return {"c": other(c, k // 4), "l": other(l, k // 2 % 2), "y": other(y, k % 2)}

    def group_index(k):
        peer = group_peer(k)
        return (peer["c"] * 2 + peer["l"]) * 2 + peer["y"]

    def index(code, core):
        at_x, at_l = other(x, code // 8 % 2), other(l, code // 2 % 2)
        return (((at_x * 2 + core) * 2 + other(h, code % 2)) * 2 + at_l) * 2 + other(y, code // 4 % 2)

    load = pltpu.make_async_copy(in_full_ref, full, local_sems.at[0])
    load.start()
    greet([hops[1], hops[8], cross] + [group_peer(k) for k in range(1, 8)])
    set_copies = []
    for i, (source, target) in enumerate(
        ((heads_ref, heads_in), (gate_ref, gate_in), (up_ref, up_in))
    ):
        for k in range(1, 8):
            copy = remote(
                source.at[group_index(k)], target.at[me], set_sends.at[i, k], set_recvs.at[i, k],
                group_peer(k),
            )
            copy.start()
            set_copies.append(copy)
    set_loads = [
        pltpu.make_async_copy(source.at[me], target.at[me], local_sems.at[1 + i])
        for i, (source, target) in enumerate(
            ((heads_ref, heads_in), (gate_ref, gate_in), (up_ref, up_in))
        )
    ]
    for copy in set_loads:
        copy.start()
    exchange = remote(across_ref, across_in, swap_sems.at[0], swap_sems.at[1], hops[1])
    output_move = remote(final_ref, output_ref, swap_sems.at[2], swap_sems.at[3], cross)
    tokens_move = remote(swap_buf, moved, swap_sems.at[4], swap_sems.at[5], cross)
    final_load = pltpu.make_async_copy(final_ref, final_buf, local_sems.at[4])
    final_store = pltpu.make_async_copy(final_buf, output_ref, local_sems.at[5])

    @pl.when(c != h)
    def _():
        output_move.start()

    @pl.when(c == h)
    def _():
        final_load.start()

    width, low_width = hidden_ref.shape[1], latent_ref.shape[1]
    half = head_dim // 2
    dlatent, dgain_latent = norm_back_rows(dlow_ref[...], latent_ref[...], gain_latent_ref[...])
    mapped[:, :low_width] = dlatent.astype(low)
    a, b = dkv_ref[:, :half], dkv_ref[:, half:head_dim]
    cosine, sine = cos_ref[...], sin_ref[...]
    mapped[:, low_width : low_width + half] = (a * cosine + b * sine).astype(low)
    mapped[:, low_width + half : low_width + head_dim] = (b * cosine - a * sine).astype(low)
    mapped[:, low_width + head_dim : low_width + 2 * head_dim] = dkv_ref[:, head_dim:].astype(low)
    mapped[:, low_width + 2 * head_dim :] = jnp.zeros((mapped.shape[0], 128), low)
    load.wait()
    dmapped = mapped[...]
    weights = full[...].reshape(width, -1)
    dhidden = contract(dmapped, weights, ((1,), (1,)))
    dinput, dgain_one = norm_back_rows(dhidden, home_ref[...].astype(wide), gain_one_ref[...])
    dtokens = dresid_ref[...] + dinput
    tokens_ref[...] = dtokens
    swap_buf[...] = dtokens.astype(low)

    gains[...] = jnp.zeros_like(gains)
    gains[0:1, :width] = dgain_one
    gains[1:2, :width] = gain_two_ref[...]
    gains[2:3, :low_width] = dgain_latent
    rows = terms.shape[1]
    low_part = low_width // 32
    used = low_width + 2 * head_dim
    for at in range(0, 32, 4):
        left = hidden_ref[:, at * rows : (at + 4) * rows]
        block = contract(left, dmapped[:, :used], ((0,), (0,))).astype(low)
        terms[at : at + 4, :, :used] = block.reshape(4, rows, used)
        for i in range(at, at + 4):
            tile = jnp.concatenate(
                [
                    gains[0:2, i * rows : i * rows + 128],
                    gains[2:3, i * low_part : i * low_part + 128],
                    jnp.zeros((rows - 3, 128), wide),
                ],
                axis=0,
            )
            terms[i, :, used:] = tile.astype(low)
    copies = []

    def start(source, target, slot, peer):
        copy = remote(source, target, sends.at[slot], recvs.at[slot], peer)
        copy.start()
        copies.append(copy)

    def arrived(slot):
        remote(came.at[0], came.at[0], sends.at[slot], recvs.at[slot], twin).wait_recv()

    for code in range(15, -1, -1):
        start(terms.at[index(code, 1 - c)], twin_buf.at[code], 16 + code, twin)
    for code in range(15, -1, -1):
        arrived(16 + code)
        total = terms[index(code, c)].astype(wide) + twin_buf[code].astype(wide)
        for hop in (8, 4, 2, 1):
            if code < hop:
                arrived(code + hop)
                total = total + came[code + hop].astype(wide)
        if code == 0:
            sum_ref[...] = total
        else:
            held[code] = total.astype(low)
            hop = 1 << (code.bit_length() - 1)
            start(held.at[code], came.at[code], code, hops[hop])
        if code == 8:

            @pl.when(c != h)
            def _():
                tokens_move.start()

            exchange.start()

        if code == 4:
            for copy in set_loads:
                copy.wait()
            for copy in set_copies:
                copy.wait()
            for source, target in ((gate_in, gate_out), (up_in, up_out)):
                for place, blocks in enumerate(order):
                    for j, block in enumerate(blocks):
                        target[:, block * part : (block + 1) * part] = source[
                            place, :, j * part : (j + 1) * part
                        ].astype(wide)
            for place in range(8):
                core, at_l, at_y = place // 4, place // 2 % 2, place % 2
                for j in range(2):
                    head = ((j * 2 + core) * 2 + at_y) * 2 + at_l
                    heads_out[:, head * head_dim : (head + 1) * head_dim] = heads_in[
                        place, :, j * head_dim : (j + 1) * head_dim
                    ].astype(wide)
    exchange.wait()
    out_ref[...] = kept_ref[...].astype(wide) + across_in[...].astype(wide)
    for copy in copies:
        copy.wait_send()

    @pl.when(c != h)
    def _():
        output_move.wait()
        tokens_move.wait()
        tokens_ref[...] = moved[...].astype(wide)

    @pl.when(c == h)
    def _():
        final_load.wait()
        final_store.start()
        final_store.wait()


def shut(
    dlow, dkv, latent, gain_latent, cosine, sine, hidden, in_full, home, gain_one, dresid, dgain_two,
    gate_terms, up_terms, head_terms, final, kept, across, part, order, number,
):
    count, width = hidden.shape
    head_dim = dkv.shape[1] // 2
    rows, columns = in_full.shape[1:]
    vmem, sem = pl.BlockSpec(memory_space=pltpu.VMEM), pltpu.SemaphoreType.DMA
    args = [
        dlow, dkv, latent, gain_latent, cosine, sine, hidden, in_full, home, gain_one, dresid,
        dgain_two, gate_terms, up_terms, head_terms, final, kept, across,
    ]
    hbm = {7, 12, 13, 14, 15, 17}
    ff = len(order) * len(order[0]) * part
    shapes = [
        ((rows, columns), wide),
        ((count, width), wide),
        ((count, width), low),
        ((gate_terms.shape[1], ff), wide),
        ((up_terms.shape[1], ff), wide),
        ((head_terms.shape[1], 8 * head_terms.shape[2]), wide),
        (kept.shape, wide),
    ]
    blocks = pltpu.VMEM((16, rows, columns), low)
    return pl.pallas_call(
        functools.partial(shut_kernel, part, head_dim, order, len(args), len(shapes)),
        in_specs=[in_hbm() if i in hbm else vmem for i in range(len(args))],
        out_specs=[in_hbm() if i == 2 else vmem for i in range(len(shapes))],
        out_shape=[jax.ShapeDtypeStruct(*s) for s in shapes],
        scratch_shapes=[
            pltpu.VMEM(in_full.shape, low),
            pltpu.VMEM((count, columns), low),
            pltpu.VMEM(in_full.shape, low),
            pltpu.VMEM((16, width + 128), wide),
            blocks,
            blocks,
            blocks,
            pltpu.VMEM((count, width), low),
            pltpu.VMEM((count, width), low),
            pltpu.VMEM(gate_terms.shape, low),
            pltpu.VMEM(up_terms.shape, low),
            pltpu.VMEM(head_terms.shape, low),
            pltpu.VMEM((count, width), low),
            pltpu.VMEM(across.shape, low),
            sem((32,)),
            sem((32,)),
            sem((3, 8)),
            sem((3, 8)),
            sem((6,)),
            sem((6,)),
        ],
        compiler_params=pltpu.CompilerParams(
            collective_id=number, has_side_effects=True, vmem_limit_bytes=60 * 1024 * 1024
        ),
        cost_estimate=pl.CostEstimate(flops=0, bytes_accessed=150 * 1024 * 1024, transcendentals=0),
        name="shut",
    )(*args)


def split_kernel(part, order, a_ref, b_ref, a_out, b_out):
    for source, target in ((a_ref, a_out), (b_ref, b_out)):
        used, total = len(order[0]) * part, target.shape[2]
        for place, blocks in enumerate(order):
            for j, block in enumerate(blocks):
                target[place, :, j * part : (j + 1) * part] = source[
                    :, block * part : (block + 1) * part
                ]
            if used < total:
                target[place, :, used:] = jnp.zeros((target.shape[1], total - used), target.dtype)


def join_kernel(part, order, a_ref, b_ref, a_out, b_out):
    for source, target in ((a_ref, a_out), (b_ref, b_out)):
        for place, blocks in enumerate(order):
            for j, block in enumerate(blocks):
                target[:, block * part : (block + 1) * part] = source[
                    place, :, j * part : (j + 1) * part
                ].astype(wide)


def column_order(n_x, n_l):
    return [
        [
            (((x * 2 + c) * 2 + h) * n_l + l) * 2 + y
            for x in range(n_x)
            for h in range(2)
        ]
        for c in range(2)
        for l in range(n_l)
        for y in range(2)
    ]


def split_columns(a, b, part, order, total):
    shape = jax.ShapeDtypeStruct((len(order), a.shape[0], total), a.dtype)
    return pl.pallas_call(
        functools.partial(split_kernel, part, order), out_shape=[shape] * 2, name="split_columns"
    )(a, b)


def join_columns(a, b, part, order):
    shape = jax.ShapeDtypeStruct((a.shape[1], len(order) * len(order[0]) * part), wide)
    return pl.pallas_call(
        functools.partial(join_kernel, part, order), out_shape=[shape] * 2, name="join_columns"
    )(a, b)


def first_allowed(ends_ref, count, places):
    start = jnp.zeros_like(places)
    for j in range(count):
        end = ends_ref[j]
        start = jnp.where(places >= end, end, start)
    return jnp.where(places >= ends_ref[count - 1], places, start)


def contract(left, right, dims):
    return lax.dot_general(left, right, (dims, ((), ())), preferred_element_type=wide)


def stacked(ref, span, heads, width):
    return jnp.concatenate(
        [ref[span, j * width : (j + 1) * width] for j in range(heads)], axis=0
    )


def tile_mask(ends_ref, begin, tile, length, heads):
    rows = begin + lax.broadcasted_iota(jnp.int32, (tile, 1), 0)
    lows = first_allowed(ends_ref, ends_ref.shape[0], rows)
    rows = jnp.concatenate([rows] * heads, axis=0)
    lows = jnp.concatenate([lows] * heads, axis=0)
    columns = lax.broadcasted_iota(jnp.int32, (heads * tile, length), 1)
    return (columns >= lows) & (columns <= rows)


def attend_kernel(heads, tile, ends_ref, q_ref, k_ref, v_ref, o_ref, log_ref):
    width = k_ref.shape[1]
    for i in range(q_ref.shape[0] // tile):
        span, length = slice(i * tile, (i + 1) * tile), (i + 1) * tile
        mask = tile_mask(ends_ref, i * tile, tile, length, heads)
        scores = contract(stacked(q_ref, span, heads, width), k_ref[:length, :], ((1,), (1,)))
        scores = jnp.where(mask, scores, masked_value)
        top = jnp.max(scores, axis=1, keepdims=True)
        weights = jnp.exp(scores - top)
        total = jnp.sum(weights, axis=1, keepdims=True)
        mixed = contract(weights.astype(low), v_ref[:length, :], ((1,), (0,))) / total
        log = jnp.broadcast_to(top + jnp.log(total), (heads * tile, 128))
        for j in range(heads):
            part = slice(j * tile, (j + 1) * tile)
            o_ref[span, j * width : (j + 1) * width] = mixed[part].astype(low)
            log_ref[j, span, :] = log[part]


def attend_back_kernel(
    heads, tile, scale, ends_ref, q_ref, g_ref, o_ref, k_ref, v_ref, log_ref, cos_ref, sin_ref,
    dq_ref, dkv_ref, sum_ref,
):
    width = k_ref.shape[1]
    half = width // 2
    sum_ref[...] = jnp.zeros_like(sum_ref)
    for i in range(q_ref.shape[0] // tile):
        span, length = slice(i * tile, (i + 1) * tile), (i + 1) * tile
        mask = tile_mask(ends_ref, i * tile, tile, length, heads)
        queries = stacked(q_ref, span, heads, width)
        grads = stacked(g_ref, span, heads, width)
        outs = stacked(o_ref, span, heads, width)
        delta = jnp.sum(grads.astype(wide) * outs.astype(wide), axis=1, keepdims=True)
        log = jnp.concatenate([log_ref[j, span, :1] for j in range(heads)], axis=0)
        keys, values = k_ref[:length, :], v_ref[:length, :]
        scores = contract(queries, keys, ((1,), (1,)))
        weights = jnp.where(mask, jnp.exp(scores - log), 0.0)
        dprob = contract(grads, values, ((1,), (1,)))
        dscore = (weights * (dprob - delta)).astype(low)
        sum_ref[:length, width:] += contract(weights.astype(low), grads, ((0,), (0,)))
        sum_ref[:length, :width] += contract(dscore, queries, ((0,), (0,)))
        dquery = contract(dscore, keys, ((1,), (0,))) * scale
        cosine, sine = cos_ref[span, :], sin_ref[span, :]
        for j in range(heads):
            a = dquery[j * tile : (j + 1) * tile, :half]
            b = dquery[j * tile : (j + 1) * tile, half:]
            at = j * width
            dq_ref[span, at : at + half] = (a * cosine + b * sine).astype(low)
            dq_ref[span, at + half : at + width] = (b * cosine - a * sine).astype(low)
    dkv_ref[...] = sum_ref[...].astype(low)


def tile_of(length):
    return next(t for t in (256, 128, 64, 32, 16, 8) if length % t == 0)


def attend(ends, query, packed, heads):
    length, width = query.shape[0], query.shape[1] // heads
    tile = tile_of(length)
    first = packed.shape[1] // width - 2
    return pl.pallas_call(
        functools.partial(attend_kernel, heads, tile),
        grid=(1,),
        in_specs=[
            pl.BlockSpec(memory_space=pltpu.SMEM),
            pl.BlockSpec((length, heads * width), lambda i: (0, 0)),
            pl.BlockSpec((length, width), lambda i: (0, first)),
            pl.BlockSpec((length, width), lambda i: (0, first + 1)),
        ],
        out_specs=[
            pl.BlockSpec((length, heads * width), lambda i: (0, 0)),
            pl.BlockSpec((heads, length, 128), lambda i: (0, 0, 0)),
        ],
        out_shape=[
            jax.ShapeDtypeStruct((length, heads * width), low),
            jax.ShapeDtypeStruct((heads, length, 128), wide),
        ],
        compiler_params=pltpu.CompilerParams(vmem_limit_bytes=56 * 1024 * 1024),
        cost_estimate=pl.CostEstimate(
            flops=6 * length * length * width * heads,
            bytes_accessed=8 * length * width * heads,
            transcendentals=length * length * heads // 2,
        ),
        name="attend",
    )(ends, query, packed, packed)


def attend_back(ends, query, grad, mixed, packed, logs, cosine, sine, heads, scale):
    length, width = query.shape[0], query.shape[1] // heads
    tile = tile_of(length)
    first = packed.shape[1] // width - 2
    rows = pl.BlockSpec((length, heads * width), lambda i: (0, 0))
    angle = pl.BlockSpec((length, width // 2), lambda i: (0, 0))
    return pl.pallas_call(
        functools.partial(attend_back_kernel, heads, tile, scale),
        grid=(1,),
        in_specs=[
            pl.BlockSpec(memory_space=pltpu.SMEM),
            rows,
            rows,
            rows,
            pl.BlockSpec((length, width), lambda i: (0, first)),
            pl.BlockSpec((length, width), lambda i: (0, first + 1)),
            pl.BlockSpec((heads, length, 128), lambda i: (0, 0, 0)),
            angle,
            angle,
        ],
        out_specs=[rows, pl.BlockSpec((length, 2 * width), lambda i: (0, 0))],
        out_shape=[
            jax.ShapeDtypeStruct((length, heads * width), low),
            jax.ShapeDtypeStruct((length, 2 * width), low),
        ],
        scratch_shapes=[pltpu.VMEM((length, 2 * width), wide)],
        compiler_params=pltpu.CompilerParams(vmem_limit_bytes=56 * 1024 * 1024),
        cost_estimate=pl.CostEstimate(
            flops=10 * length * length * width * heads,
            bytes_accessed=16 * length * width * heads,
            transcendentals=length * length * heads // 2,
        ),
        name="attend_back",
    )(ends, query, grad, mixed, packed, packed, logs, cosine, sine)


def on_device(
    tokens,
    lengths,
    cotangent,
    norm_one,
    query_down,
    query_gain,
    query_up,
    key_proj,
    value_proj,
    out_proj,
    norm_two,
    gate_proj,
    up_proj,
    down_proj,
):
    n_x, n_l = lax.axis_size("x"), lax.axis_size("l")
    x, c, h, l, y = [lax.axis_index(a) for a in every]
    n_dev = n_x * 8 * n_l
    n_group = 4 * n_l
    me = group_place()
    count, width = tokens.shape
    row_len = count * n_group
    latent_width = query_down.shape[1]
    head_dim = key_proj.shape[1]
    shard = query_down.shape[0]
    heads = query_up.shape[1] // head_dim // n_group
    ff_part = down_proj.shape[0]
    ff_own = ff_part * n_x * 2
    ff_pad = -(-ff_own // 128) * 128
    natural = n_x == 2 and n_l == 2
    scale = 1.0 / math.sqrt(head_dim)
    order = column_order(n_x, n_l)
    mapped_width = latent_width + 2 * head_dim

    gains = jnp.zeros((shard, 128), low)
    gains = gains.at[0, :shard].set(norm_one).at[1, :shard].set(norm_two)
    gains = gains.at[2, : query_gain.shape[0]].set(query_gain)
    small = jnp.concatenate([query_down, key_proj, value_proj, gains], axis=1)
    rows_up = query_up.shape[0]
    if natural:
        head_cols = query_up.reshape(rows_up, 2, 2, 2, 2, head_dim)
        head_cols = head_cols.transpose(2, 4, 3, 0, 1, 5)
    else:
        head_cols = query_up.reshape(rows_up, n_group, -1).transpose(1, 0, 2)
    head_cols = head_cols.reshape(n_group, rows_up, heads * head_dim)
    gate_cols, up_cols = split_columns(gate_proj, up_proj, ff_part, order, ff_pad)
    if natural:
        lens = jnp.pad(lengths, ((0, 7), (0, 128 - lengths.shape[1])))
        in_full, own_heads, (up_query, gate_rows, up_rows), (home, lens, grad_home) = open_exchange(
            small, out_proj, [head_cols, gate_cols, up_cols], [tokens, lens, cotangent]
        )
        row_lengths = lens[0, : lengths.shape[1]]
    else:
        in_full = lax.all_gather(small, every, axis=0)
        home, grad_home, row_lengths = [swap_home(a) for a in (tokens, cotangent, lengths)]
        row_lengths = row_lengths[0]
        up_query, gate_rows, up_rows = [
            all_to_all_row(a) for a in (head_cols, gate_cols, up_cols)
        ]
        up_query = up_query.reshape((2, -1) + up_query.shape[1:])
        up_query = lax.all_gather(lax.all_gather(up_query, "h", axis=1), "x", axis=0)
    up_query = up_query.reshape(latent_width, -1)
    gate_rows = gate_rows.reshape(2, -1, ff_pad)
    up_rows = up_rows.reshape(2, -1, ff_pad)
    gain_one = in_full[:, 0, mapped_width : mapped_width + shard].reshape(width).astype(wide)
    gain_two = in_full[:, 1, mapped_width : mapped_width + shard].reshape(width).astype(wide)
    gain_latent = in_full[:, 2, mapped_width : mapped_width + query_gain.shape[0]]
    gain_latent = gain_latent.reshape(latent_width).astype(wide)
    in_full = in_full.reshape(width, -1)

    inputs = home.astype(wide)
    ends = jnp.cumsum(row_lengths, dtype=jnp.int32)
    places = jnp.arange(row_len, dtype=jnp.int32)
    begins = jnp.max(jnp.where(places[:, None] >= ends[None, :], ends[None, :], 0), axis=1)
    rates = jnp.exp(
        jnp.arange(head_dim // 2, dtype=wide) * (-math.log(10000.0) / (head_dim // 2))
    )
    phases = (places - begins).astype(wide)[:, None] * rates
    cosine, sine = jnp.cos(phases), jnp.sin(phases)
    own_cos = lax.dynamic_slice_in_dim(cosine, me * count, count)
    own_sin = lax.dynamic_slice_in_dim(sine, me * count, count)

    if natural:
        own_heads = own_heads.reshape(-1, width)
        gate_a, gate_b, up_a, up_b = gate_rows[0], gate_rows[1], up_rows[0], up_rows[1]
        down_a, down_b = down_proj[:, : width // 2], down_proj[:, width // 2 :]
        gate_a_h, heads_x = flip(gate_a, "h"), flip(own_heads, "x")
    else:
        out_full = lax.all_gather(out_proj, every, axis=0, tiled=True)
        out_own = lax.dynamic_slice_in_dim(out_full, me * heads * head_dim, heads * head_dim)
        gate_own, up_own = [
            lax.all_gather(lax.all_gather(a, "h", axis=1), "x", axis=0).reshape(width, -1)
            for a in (gate_rows, up_rows)
        ]
        down_own = lax.all_gather(lax.all_gather(down_proj, "h", axis=0), "x", axis=0)
        down_own = jnp.pad(down_own.reshape(-1, width), ((0, ff_pad - ff_own), (0, 0)))

    scale_one = rms_scale(inputs)
    hidden = (inputs * scale_one * gain_one).astype(low)
    mapped = dot(hidden, in_full)
    latent = mapped[:, :latent_width]
    scale_latent = rms_scale(latent)
    latent_low = (latent * scale_latent * gain_latent).astype(low)
    keys = rotate(mapped[:, latent_width : latent_width + head_dim], own_cos, own_sin).astype(low)
    values = mapped[:, latent_width + head_dim : mapped_width].astype(low)
    packed = jnp.concatenate([latent_low, keys, values], axis=1)
    if natural:
        packed, gate_a_h, heads_x = together(packed, gate_a_h, heads_x)
        packed, gate_b_h = gather_row(packed, 2, kinds=("h",), more=(gate_b,))
        packed, gate_b_h, up_a = together(packed, gate_b_h, up_a)
        up_a_h = flip(up_a, "h")
        out_own = jnp.concatenate(
            [jnp.where(x == 0, own_heads, heads_x), jnp.where(x == 0, heads_x, own_heads)], axis=0
        )
        gate_x = [flip(a, "x") for a in (gate_a, gate_b, gate_a_h, gate_b_h)]
    else:
        packed = gather_row(packed, 2)
    grad_all = lax.all_gather(grad_home, group, axis=0, tiled=True)
    all_latent = packed[:, :latent_width]
    query_raw = dot(all_latent, up_query)
    query = jnp.concatenate(
        [
            rotate(query_raw[:, j * head_dim : (j + 1) * head_dim], cosine, sine)
            for j in range(heads)
        ],
        axis=1,
    ).astype(low) * jnp.asarray(scale, low)
    mixed, logs = attend(ends, query, packed, heads)
    terms = dot(mixed, out_own, low)
    if natural:
        terms, up_a_h = together(terms, up_a_h)
        up_a_x, up_a_xh = flip(up_a, "x"), flip(up_a_h, "x")
        attended, up_b_h, down_a_h = scatter_row(3, terms, kinds=("h", "h"), more=(up_b, down_a))
        attended, gate_x, up_a_x, up_a_xh = together(attended, gate_x, up_a_x, up_a_xh)
    else:
        attended = scatter_row(3, terms)[0]
    resid = inputs + attended
    scale_two = rms_scale(resid)
    hidden_two = (resid * scale_two * gain_two).astype(low)
    if natural:
        gate_parts = [gate_a, gate_b, gate_a_h, gate_b_h] + list(gate_x)
        (
            all_two, inner, gate_factor, up_factor, grad_down, down_x,
            up_b_x, up_b_xh, down_a_x, down_a_xh, down_b_x, down_b_h, down_b_xh,
        ) = feed_forward(
            hidden_two,
            gate_parts,
            (up_a, up_a_h, up_a_x, up_a_xh),
            grad_all,
            (up_b, up_b_h),
            (down_a, down_a_h, down_b),
            ff_own,
            4,
        )
        up_parts = [up_a, up_b, up_a_h, up_b_h, up_a_x, up_b_x, up_a_xh, up_b_xh]
    else:
        all_two = gather_row(hidden_two, 4)
        gate = dot(all_two, gate_own)
        upward = dot(all_two, up_own)
        sigma = jax.nn.sigmoid(gate)
        inner = (gate * sigma * upward).astype(low)
        grad_down = outer_sum(inner, grad_all, low)

    if natural:
        down_x = flip(down_x, "x")
        dhidden_two, *spread, gate_terms, gate_x, up_terms, up_x = feed_back(
            grad_all,
            gate_factor,
            up_factor,
            inner,
            all_two,
            gate_parts,
            up_parts,
            [
                (down_a, down_a_h, down_a_x, down_a_xh),
                (down_b, down_b_h, down_b_x, down_b_xh),
            ],
            5,
        )
        down_terms = grad_down.reshape(2, ff_part, width)
        spread = scatter_row_async(spread, 0)
        gate_x, up_x = flip(gate_x, "x"), flip(up_x, "x")
        dhidden_two, down_x = together(dhidden_two, down_x)
        down_terms = add(down_terms, down_x.reshape(down_terms.shape))
        down_terms, down_h = pick(down_terms, h), pick(down_terms, 1 - h)
    else:
        dinner = times_transposed(grad_all, down_own)
        dgate = (dinner * upward * sigma * (1.0 + gate * (1.0 - sigma))).astype(low)
        dupward = (dinner * gate * sigma).astype(low)
        grad_gate, grad_upward = outer_sum(all_two, dgate, low), outer_sum(all_two, dupward, low)
        dhidden_two = times_transposed(dgate, gate_own) + times_transposed(dupward, up_own)
        dhidden_two = scatter_row(5, dhidden_two.astype(low))[0]
        spread = scatter_row(6, dot(inner, down_own, low))[0]
        grad_down = sum_columns(grad_down[:ff_own].reshape(n_x, 2, ff_part, width), 0).astype(wide)
        gate_terms, up_terms = [
            sum_columns(a.reshape(n_x, 2, 2, -1, ff_pad), 1) for a in (grad_gate, grad_upward)
        ]

    dresid_part, dgain_two = norm_back(dhidden_two, resid, scale_two, gain_two)
    dresid = grad_home.astype(wide) + dresid_part
    branch = dresid.astype(low)
    if natural:
        branch_all, down_h = gather_row(branch, 7, kinds=("h",), more=(down_h,))
        branch_all, gate_x, spread = together(branch_all, gate_x, spread)
        grad_down = down_terms.astype(wide) + down_h.astype(wide)
        gate_terms = add(gate_terms, gate_x).reshape(2, 2, -1, ff_pad)
        gate_terms, gate_h = halves(gate_terms, "h", 1)
        spread = scatter_row_async(spread, 1)
    else:
        branch_all = gather_row(branch, 7)
    dmixed = times_transposed(branch_all, out_own, low)
    grad_out = outer_sum(mixed, branch_all, low)
    if natural:
        out_terms, out_x = halves(grad_out.reshape(2, 2, head_dim // 2, width), "x", 0)
    dquery, dkv = attend_back(
        ends, query, dmixed, mixed, packed, logs, cosine, sine, heads, scale
    )
    head_terms = outer_sum(all_latent, dquery, low).reshape(n_x, 2, 2, -1, heads * head_dim)
    dlow = times_transposed(dquery, up_query, low)
    if natural:
        head_terms, head_x = halves(head_terms, "x", 0)
        spread = scatter_row_async(spread, 2)
        dlow, gate_h, up_x, out_x, spread = together(dlow, gate_h, up_x, out_x, spread)
        out_terms = add(out_terms, out_x)
        kept, out_y = pick(out_terms, y), flip(pick(out_terms, 1 - y), "y")
        final = (resid + scatter_row_async(spread, 3)).astype(low)
        up_terms = add(up_terms, up_x).reshape(2, 2, -1, ff_pad)
        up_terms, up_h = pick(up_terms, h, 1), pick(up_terms, 1 - h, 1)
        dlow, dkv, up_h = scatter_row(8, dlow, dkv, kinds=("h",), more=(up_h,))
        dlow, out_y, head_x = together(dlow, out_y, head_x)
        by_h = jnp.stack([jnp.where(y == 0, kept, out_y), jnp.where(y == 0, out_y, kept)])
        gate_terms = add(gate_terms, gate_h).reshape(n_group, shard, ff_pad)
        up_terms = add(up_terms, up_h).reshape(n_group, shard, ff_pad)
        head_terms, head_h = halves(add(head_terms, head_x), "h", 1)
        dlow, head_h = together(dlow, head_h)
        head_terms = add(head_terms, head_h).reshape(n_group, rows_up, heads * head_dim)
        summed, grad_tokens, output, grad_gate, grad_upward, grad_uquery, grad_out = shut(
            dlow, dkv, latent, gain_latent[None], own_cos, own_sin, hidden,
            in_full.reshape(n_dev, shard, -1), home, gain_one[None], dresid, dgain_two[None],
            gate_terms, up_terms, head_terms, final, pick(by_h, h), pick(by_h, 1 - h), ff_part,
            order, 9,
        )
    else:
        dlow, dkv = scatter_row(8, dlow, dkv)
        whole = jnp.zeros((n_group * heads * head_dim, width), wide)
        whole = lax.dynamic_update_slice_in_dim(
            whole, grad_out.astype(wide), me * heads * head_dim, 0
        )
        grad_out = lax.psum_scatter(whole, every, scatter_dimension=0, tiled=True)
        final = (resid + spread).astype(low)
        dkeys = rotate_back(dkv[:, :head_dim], own_cos, own_sin).astype(low)
        dvalues = dkv[:, head_dim:].astype(low)
        dlatent, dgain_latent = norm_back(dlow, latent, scale_latent, gain_latent)
        nothing = jnp.zeros((count, 128), low)
        dmapped = jnp.concatenate([dlatent.astype(low), dkeys, dvalues, nothing], axis=1)
        dhidden = times_transposed(dmapped, in_full)
        dinput_part, dgain_one = norm_back(dhidden, inputs, scale_one, gain_one)
        grad_tokens = (dresid + dinput_part).astype(low)
        grad_in = outer_sum(hidden, dmapped[:, :mapped_width], low).reshape(n_dev, shard, -1)
        gain_terms = jnp.zeros((n_dev, shard, 128), low)
        gain_terms = gain_terms.at[:, 0, :shard].set(dgain_one.reshape(n_dev, -1).astype(low))
        gain_terms = gain_terms.at[:, 1, :shard].set(dgain_two.reshape(n_dev, -1).astype(low))
        gain_terms = gain_terms.at[:, 2, : query_gain.shape[0]].set(
            dgain_latent.reshape(n_dev, -1).astype(low)
        )
        terms = jnp.concatenate([grad_in, gain_terms], axis=2)
        summed = lax.psum_scatter(terms.astype(wide), every, scatter_dimension=0, tiled=False)
        grad_tokens, output = swap_home(grad_tokens), swap_home(final)
        head_terms = all_to_all_row(
            sum_columns(head_terms, 1).reshape(n_group, rows_up, heads * head_dim)
        )
        gate_terms, up_terms = [
            all_to_all_row(a.reshape(n_group, shard, ff_pad)) for a in (gate_terms, up_terms)
        ]
        grad_gate, grad_upward = join_columns(gate_terms, up_terms, ff_part, order)
        grad_uquery = head_terms.transpose(1, 0, 2).reshape(rows_up, -1).astype(wide)
    return (
        output,
        grad_tokens.astype(wide),
        summed[0, mapped_width : mapped_width + shard],
        summed[:, :latent_width],
        summed[2, mapped_width : mapped_width + query_gain.shape[0]],
        grad_uquery,
        summed[:, latent_width : latent_width + head_dim],
        summed[:, latent_width + head_dim : mapped_width],
        grad_out,
        summed[1, mapped_width : mapped_width + shard],
        grad_gate,
        grad_upward,
        grad_down,
    )


def solution(mesh):
    n_dp, n_seq = mesh.shape["dp"], mesh.shape["seq"]
    fine = Mesh(mesh.devices.reshape(n_dp // 2, 2, 2, n_seq // 4, 2), every)
    rows, flat = P(every, None), P(every)
    placed = (rows, P(("x", "c"), None), rows, flat, rows, flat) + (rows,) * 4 + (flat,) + (rows,) * 3
    return jax.shard_map(
        on_device,
        mesh=fine,
        in_specs=placed,
        out_specs=(rows, rows, flat, rows, flat) + (rows,) * 4 + (flat,) + (rows,) * 3,
        check_vma=False,
    )
```

```python
import functools
import math

import jax
import jax.numpy as jnp
from jax import lax
from jax.experimental import pallas as pl
from jax.experimental.pallas import tpu as pltpu
from jax.sharding import Mesh, PartitionSpec as P

norm_eps = 1e-05
masked_value = -1e30
every = ("x", "c", "h", "l", "y")
group = ("c", "l", "y")
low = jnp.bfloat16
wide = jnp.float32


def rms_scale(values):
    return lax.rsqrt(jnp.mean(values * values, axis=-1, keepdims=True) + norm_eps)


def rotate(values, cosine, sine):
    half = values.shape[-1] // 2
    a, b = values[..., :half], values[..., half:]
    return jnp.concatenate([a * cosine - b * sine, b * cosine + a * sine], axis=-1)


def rotate_back(values, cosine, sine):
    half = values.shape[-1] // 2
    a, b = values[..., :half], values[..., half:]
    return jnp.concatenate([a * cosine + b * sine, b * cosine - a * sine], axis=-1)


def norm_back(incoming, source, scale, gain):
    weighted = incoming * gain
    source_grad = scale * weighted - source * (scale * scale * scale) * jnp.mean(
        weighted * source, axis=-1, keepdims=True
    )
    return source_grad, jnp.sum(incoming * source * scale, axis=0)


def dot(left, right, out=wide):
    return jnp.dot(left, right, preferred_element_type=wide).astype(out)


def outer_sum(left, right, out=wide):
    return lax.dot_general(
        left, right, (((0,), (0,)), ((), ())), preferred_element_type=wide
    ).astype(out)


def times_transposed(left, right, out=wide):
    return lax.dot_general(
        left, right, (((1,), (1,)), ((), ())), preferred_element_type=wide
    ).astype(out)


def pick(array, index, axis=0):
    return lax.dynamic_index_in_dim(array, index, axis, keepdims=False)


def after(value, *done):
    return lax.optimization_barrier((value,) + done)[0]


def together(*values):
    return lax.optimization_barrier(values)


def flip(value, axis):
    return lax.ppermute(value, axis, [(0, 1), (1, 0)])


def flip_cross(value):
    return lax.ppermute(value, ("c", "h"), [(1, 2), (2, 1)])


def choose_home(value, moved):
    return jnp.where(lax.axis_index("c") == lax.axis_index("h"), value, moved)


def swap_home(value):
    return choose_home(value, flip_cross(value))


def group_place():
    return (
        lax.axis_index("c") * lax.axis_size("l") + lax.axis_index("l")
    ) * 2 + lax.axis_index("y")


def all_to_all_row(blocks):
    return lax.all_to_all(blocks, group, 0, 0, tiled=True)


def send(value, offsets):
    return lax.ppermute(value, group, [(i, i ^ offsets[i // 4]) for i in range(8)])


def scatter_row_async(state, stage):
    core = lax.axis_index("c")
    me = lax.axis_index("l") * 2 + lax.axis_index("y")
    first, second = 1 + core, 2 - core
    if stage == 0:
        return state[0], flip(state[1], "c")
    own, moved = state[:2]

    def block(index):
        return pick(own, index).astype(wide) + pick(moved, index).astype(wide)

    if stage == 1:
        far = send(block(me ^ 3).astype(low), (2, 1))
        return own, moved, far, send(block(me ^ second).astype(low), (2, 1))
    far, side = state[2:4]
    if stage == 2:
        return state + (send((block(me ^ first) + far.astype(wide)).astype(low), (1, 2)),)
    return block(me) + side.astype(wide) + state[4].astype(wide)


def sum_columns(terms, h_dim):
    for axis, dim in (("x", 0), ("h", h_dim)):
        terms = jnp.moveaxis(terms, dim, 0).astype(wide)
        terms = lax.psum_scatter(terms, axis, scatter_dimension=0, tiled=False).astype(low)
    return terms


def halves(terms, axis, dim):
    me = lax.axis_index(axis)
    return pick(terms, me, dim), flip(pick(terms, 1 - me, dim), axis)


def add(own, came):
    return (own.astype(wide) + came.astype(wide)).astype(low)


def other(value, flag=1):
    return value + flag * (1 - 2 * value)


def greet(peers):
    barrier = pltpu.get_barrier_semaphore()
    for peer in peers:
        pl.semaphore_signal(barrier, inc=1, device_id=peer, device_id_type=pl.DeviceIdType.MESH)
    pl.semaphore_wait(barrier, len(peers))


def remote(source, target, send_sem, recv_sem, peer):
    return pltpu.make_async_remote_copy(
        src_ref=source,
        dst_ref=target,
        send_sem=send_sem,
        recv_sem=recv_sem,
        device_id=peer,
        device_id_type=pl.DeviceIdType.MESH,
    )


def in_hbm():
    return pl.BlockSpec(memory_space=pl.ANY)


def open_kernel(n_sets, n_swaps, small_ref, out_ref, *refs):
    sets, refs = refs[:n_sets], refs[n_sets:]
    swaps, refs = refs[:n_swaps], refs[n_swaps:]
    (full_ref, heads_ref), refs = refs[:2], refs[2:]
    set_outs, refs = refs[:n_sets], refs[n_sets:]
    swap_outs, refs = refs[:n_swaps], refs[n_swaps:]
    (small_buf, out_buf), refs = refs[:2], refs[2:]
    set_bufs, refs = refs[:n_sets], refs[n_sets:]
    swap_bufs, refs = refs[:n_swaps], refs[n_swaps:]
    sends, recvs, swap_sends, swap_recvs, set_sends, set_recvs, out_sems, head_sems, loads_sem, stores_sem = refs
    x, c, h, l, y = [lax.axis_index(a) for a in every]
    hops = {
        1: {"h": other(h)},
        2: {"l": other(l)},
        4: {"y": other(y)},
        8: {"x": other(x)},
        16: {"c": other(c)},
    }
    cross = {"c": other(c), "h": other(h)}
    me = (c * 2 + l) * 2 + y

    def group_peer(k):
        return {"c": other(c, k // 4), "l": other(l, k // 2 % 2), "y": other(y, k % 2)}

    def group_index(k):
        peer = group_peer(k)
        return (peer["c"] * 2 + peer["l"]) * 2 + peer["y"]

    def index(code):
        at_x, at_l = other(x, code // 8 % 2), other(l, code // 2 % 2)
        return (((at_x * 2 + c) * 2 + other(h, code % 2)) * 2 + at_l) * 2 + other(y, code // 4 % 2)

    beside, corner = {"y": other(y)}, {"h": other(h), "y": h}
    greet(
        [hops[1], hops[8], cross, {"h": other(h), "y": other(y)}]
        + [group_peer(k) for k in range(1, 8)]
    )
    copies = []
    half = heads_ref.at[y]
    to_beside = remote(out_ref, half, out_sems.at[0], out_sems.at[1], beside)
    differ = y + h - 2 * y * h
    to_corner = remote(out_ref, half, out_sems.at[2], out_sems.at[3 + differ], corner)

    def push(code):
        block = full_ref.at[index(code)]
        source = small_ref if code == 0 else block
        for hop in (1, 2, 4, 8, 16):
            if code < hop:
                name = code + hop
                copy = remote(source, block, sends.at[name], recvs.at[name], hops[hop])
                copy.start()
                copies.append(copy)

    def set_slot(i):
        return set_outs[0].at[x, c, h, l * 2 + y] if i == 0 else set_outs[i].at[me]

    set_copies = []

    def set_push(i):
        for k in range(1, 8):
            copy = remote(
                sets[i].at[group_index(k)], set_slot(i), set_sends.at[i, k], set_recvs.at[i, k],
                group_peer(k),
            )
            copy.start()
            set_copies.append(copy)

    push(0)
    set_push(0)
    moving = [
        remote(source, target, swap_sends.at[i], swap_recvs.at[i], cross)
        for i, (source, target) in enumerate(zip(swaps, swap_outs))
    ]

    def push_moves():
        @pl.when(c != h)
        def _():
            for copy in moving:
                copy.start()

        @pl.when(y != h)
        def _():
            to_beside.start()

        to_corner.start()

    loads, stores = [], []
    locals_in = [small_ref, out_ref] + [ref.at[me] for ref in sets] + list(swaps)
    locals_buf = [small_buf, out_buf] + list(set_bufs) + list(swap_bufs)
    locals_out = [full_ref.at[index(0)], half] + [set_slot(i) for i in range(n_sets)]
    for i, (source, buf) in enumerate(zip(locals_in, locals_buf)):
        loads.append(pltpu.make_async_copy(source, buf, loads_sem.at[i]))
        loads[-1].start()
    for load in loads:
        load.wait()
    for i, (buf, target) in enumerate(zip(locals_buf, locals_out)):
        stores.append(pltpu.make_async_copy(buf, target, stores_sem.at[i]))
    keep_out = stores.pop(1)
    for store in stores:
        store.start()

    @pl.when(y == h)
    def _():
        keep_out.start()

    keeps = [
        pltpu.make_async_copy(buf, target, stores_sem.at[2 + n_sets + i])
        for i, (buf, target) in enumerate(zip(swap_bufs, swap_outs))
    ]

    @pl.when(c == h)
    def _():
        for keep in keeps:
            keep.start()

    def arrived(name):
        remote(small_ref, small_ref, sends.at[name], recvs.at[name], hops[16]).wait_recv()

    def head_copy(at_h, slot, peer):
        part = set_outs[0].at[x, :, at_h]
        copy = remote(part, part, head_sems.at[slot], head_sems.at[3 + slot], peer)
        copy.start()
        return copy

    head_copies = []
    for n, code in enumerate((2, 4, 1, 6, 3, 5, 7, 8, 9, 10, 11, 12, 13, 14, 15)):
        arrived(code)
        push(code)
        if n == 2:
            for copy in set_copies:
                copy.wait()
            for store in stores:
                store.wait()
            done = len(set_copies)
            for i in range(1, n_sets):
                set_push(i)
            head_copies.append(head_copy(h, 0, hops[1]))
            head_copies.append(head_copy(h, 1, hops[8]))
            push_moves()
        if n == 9:
            head_copies[0].wait_recv()
            head_copies.append(head_copy(other(h), 2, hops[8]))
    for code in range(16):
        arrived(16 + code)
    for copy in copies:
        copy.wait_send()
    for copy in set_copies[done:]:
        copy.wait()
    head_copies[0].wait_send()
    for copy in head_copies[1:]:
        copy.wait()
    to_corner.wait_send()

    @pl.when(y != h)
    def _():
        to_beside.wait_send()
        remote(out_ref, half, out_sems.at[2], out_sems.at[3], corner).wait_recv()
        remote(out_ref, half, out_sems.at[2], out_sems.at[4], corner).wait_recv()

    @pl.when(y == h)
    def _():
        keep_out.wait()
        to_beside.wait_recv()

    @pl.when(c != h)
    def _():
        for copy in moving:
            copy.wait()

    @pl.when(c == h)
    def _():
        for keep in keeps:
            keep.wait()


def open_exchange(small, out_rows, sets, swaps):
    n_sets, n_swaps = len(sets), len(swaps)
    args = [small, out_rows] + sets + swaps
    out_shape = [
        jax.ShapeDtypeStruct((32,) + small.shape, low),
        jax.ShapeDtypeStruct((2,) + out_rows.shape, low),
    ]
    out_shape += [jax.ShapeDtypeStruct((2, 2, 2, 4) + sets[0].shape[1:], low)]
    out_shape += [jax.ShapeDtypeStruct(a.shape, a.dtype) for a in sets[1:] + swaps]
    sem = pltpu.SemaphoreType.DMA
    out = pl.pallas_call(
        functools.partial(open_kernel, n_sets, n_swaps),
        in_specs=[in_hbm()] * len(args),
        out_specs=[in_hbm()] * len(args),
        out_shape=out_shape,
        scratch_shapes=[pltpu.VMEM(small.shape, low), pltpu.VMEM(out_rows.shape, low)]
        + [pltpu.VMEM(a.shape[1:], a.dtype) for a in sets]
        + [pltpu.VMEM(a.shape, a.dtype) for a in swaps]
        + [sem((32,)), sem((32,)), sem((n_swaps,)), sem((n_swaps,))]
        + [sem((n_sets, 8)), sem((n_sets, 8)), sem((5,)), sem((6,))]
        + [sem((len(args),)), sem((len(args),))],
        compiler_params=pltpu.CompilerParams(
            collective_id=1, has_side_effects=True, vmem_limit_bytes=16 * 1024 * 1024
        ),
        cost_estimate=pl.CostEstimate(flops=0, bytes_accessed=150 * 1024 * 1024, transcendentals=0),
        name="open_exchange",
    )(*args)
    return out[0], out[1], out[2 : 2 + n_sets], out[2 + n_sets :]


def row_peers(even):
    c, l, y = [lax.axis_index(a) for a in group]
    if even == "l":
        near = {"l": l, "y": other(y)}
        side = {"l": other(l), "y": y}
    elif even:
        near = {"l": other(l, c), "y": other(y, 1 - c)}
        side = {"l": other(l, 1 - c), "y": other(y, c)}
    else:
        near = {"l": other(l), "y": y}
        side = {"l": l, "y": other(y)}
    return c, l, y, near, side, {"c": other(c)}


class SumColumns:
    def __init__(self, mine_ref, across_ref, out_ref, mine, came_x, came_h, sems, load_sem):
        self.h = lax.axis_index("h")
        self.over_x, self.over_h = {"x": other(lax.axis_index("x"))}, {"h": other(self.h)}
        self.out_ref, self.mine, self.came_x, self.came_h = out_ref, mine, came_x, came_h
        self.sems = sems
        rows = mine.shape[2] // 2
        self.parts = [(c, pl.ds(i * rows, rows)) for c in range(2) for i in range(2)]
        self.steps_x = [
            remote(
                across_ref.at[c, :, s], came_x.at[c, :, s], sems.at[0, i], sems.at[1, i], self.over_x
            )
            for i, (c, s) in enumerate(self.parts)
        ]
        self.steps_h = []
        self.load = pltpu.make_async_copy(mine_ref, mine, load_sem)

    def start(self):
        for copy in self.steps_x:
            copy.start()
        self.load.start()

    def step(self, i):
        c, s = self.parts[i]
        if i == 0:
            self.load.wait()
        self.steps_x[i].wait_recv()
        total = self.mine[c, :, s].astype(wide) + self.came_x[c, :, s].astype(wide)
        self.mine[c, :, s] = total.astype(low)
        copy = remote(
            self.mine.at[c, other(self.h), s], self.came_h.at[c, s], self.sems.at[0, 4 + i],
            self.sems.at[1, 4 + i], self.over_h,
        )
        copy.start()
        self.steps_h.append(copy)

    def end(self):
        for (c, s), copy in zip(self.parts, self.steps_h):
            copy.wait()
            total = self.mine[c, self.h, s].astype(wide) + self.came_h[c, s].astype(wide)
            self.out_ref[c, s] = total.astype(low)
        for copy in self.steps_x:
            copy.wait_send()


def gather_sum_kernel(even, chunks, own_ref, mine_ref, across_ref, out_ref, sum_ref, *refs):
    buf, sends, recvs, local_sems, mine, came_x, came_h, sum_sems = refs
    sums = SumColumns(
        mine_ref, across_ref, sum_ref, mine, came_x, came_h, sum_sems, local_sems.at[2]
    )
    flow = RowGather(even, chunks, own_ref, out_ref, sends, recvs)
    flow.begin([sums.over_x, sums.over_h])
    sums.start()
    load = pltpu.make_async_copy(own_ref, buf, local_sems.at[0])
    load.start()
    load.wait()
    store = pltpu.make_async_copy(buf, out_ref.at[flow.me], local_sems.at[1])
    store.start()
    sums.step(0)
    flow.take_near()
    sums.step(1)
    flow.take_side()
    sums.step(2)
    flow.take(3)
    flow.take(4)
    flow.take_far()
    sums.step(3)
    flow.take(5)
    flow.take(6)
    flow.end()
    store.wait()
    sums.end()


def gather_sum(value, mine, across, number):
    chunks = 4
    kept = (mine.shape[0],) + mine.shape[2:]
    out = pl.pallas_call(
        functools.partial(gather_sum_kernel, False, chunks),
        in_specs=[in_hbm()] * 3,
        out_specs=[in_hbm(), pl.BlockSpec(memory_space=pltpu.VMEM)],
        out_shape=[
            jax.ShapeDtypeStruct((8,) + value.shape, low),
            jax.ShapeDtypeStruct(kept, low),
        ],
        scratch_shapes=[
            pltpu.VMEM(value.shape, low),
            pltpu.SemaphoreType.DMA((7, chunks)),
            pltpu.SemaphoreType.DMA((7, chunks)),
            pltpu.SemaphoreType.DMA((3,)),
            pltpu.VMEM(mine.shape, low),
            pltpu.VMEM(mine.shape, low),
            pltpu.VMEM(kept, low),
            pltpu.SemaphoreType.DMA((2, 8)),
        ],
        compiler_params=pltpu.CompilerParams(
            collective_id=number, has_side_effects=True, vmem_limit_bytes=24 * 1024 * 1024
        ),
        cost_estimate=pl.CostEstimate(flops=0, bytes_accessed=120 * 1024 * 1024, transcendentals=0),
        name="gather_sum",
    )(value, mine, across)
    return out[0].reshape(-1, value.shape[1]), out[1]


def turn(values, cosine, sine):
    half = values.shape[1] // 2
    a, b = values[:, :half], values[:, half:]
    return a * cosine - b * sine, b * cosine + a * sine


def angles(ends_ref, rates, begin, count):
    places = begin + lax.broadcasted_iota(jnp.int32, (count, 1), 0)
    start = jnp.zeros_like(places)
    for j in range(ends_ref.shape[0]):
        end = ends_ref[j]
        start = jnp.where(places >= end, end, start)
    phases = (places - start).astype(wide) * rates
    return jnp.cos(phases), jnp.sin(phases)


def front_kernel(kinds, ends_ref, home_ref, full_ref, gain_ref, low_gain_ref, rates_ref, *refs):
    n = len(kinds)
    more, refs = refs[:n], refs[n:]
    out_ref, hidden_ref, latent_ref, cos_ref, sin_ref, refs = *refs[:5], refs[5:]
    more_out, refs = refs[:n], refs[n:]
    full, own, sends, recvs, load_sem, store_sem, more_sems = refs
    beside = Beside(kinds, more, more_out, more_sems)
    flow = RowGather(False, sends.shape[1], own, out_ref, sends, recvs)
    load = pltpu.make_async_copy(full_ref, full, load_sem)
    load.start()
    near, side, twin = flow.peers
    greet([near, side, twin, *beside.peers])
    count = home_ref.shape[0]
    low_width, head_dim = latent_ref.shape[1], 2 * cos_ref.shape[1]
    half = head_dim // 2
    values = home_ref[...].astype(wide)
    hidden = (values * rms_scale(values) * gain_ref[...]).astype(low)
    hidden_ref[...] = hidden
    cosine, sine = angles(ends_ref, rates_ref[...], flow.me * count, count)
    load.wait()
    mapped = jnp.dot(hidden, full[...], preferred_element_type=wide)
    latent = mapped[:, :low_width]
    latent_ref[...] = latent
    own[:, :low_width] = (latent * rms_scale(latent) * low_gain_ref[...]).astype(low)
    a, b = turn(mapped[:, low_width : low_width + head_dim], cosine, sine)
    own[:, low_width : low_width + half] = a.astype(low)
    own[:, low_width + half : low_width + head_dim] = b.astype(low)
    end = low_width + 2 * head_dim
    own[:, low_width + head_dim :] = mapped[:, low_width + head_dim : end].astype(low)
    flow.begin(None)
    beside.start()
    store = pltpu.make_async_copy(own, out_ref.at[flow.me], store_sem)
    store.start()

    def tables(begin, rows):
        cos_ref[begin : begin + rows, :], sin_ref[begin : begin + rows, :] = angles(
            ends_ref, rates_ref[...], begin, rows
        )

    quarter = cos_ref.shape[0] // 4
    tables(0, quarter)
    tables(quarter, quarter)
    flow.take_near()
    tables(2 * quarter, quarter)
    flow.take_side()
    tables(3 * quarter, quarter)
    flow.take_far()
    for slot in (3, 4, 5, 6):
        flow.take(slot)
    flow.end()
    store.wait()
    beside.wait()


def front(ends, home, in_full, gain_one, gain_latent, rates, row_len, number, kinds, more):
    count, width = home.shape
    low_width = gain_latent.shape[1]
    half = rates.shape[1]
    packed = (count, low_width + 4 * half)
    vmem, sem = pl.BlockSpec(memory_space=pltpu.VMEM), pltpu.SemaphoreType.DMA
    out = pl.pallas_call(
        functools.partial(front_kernel, kinds),
        in_specs=[pl.BlockSpec(memory_space=pltpu.SMEM), vmem, in_hbm(), vmem, vmem, vmem]
        + [in_hbm()] * len(more),
        out_specs=[in_hbm()] + [vmem] * 4 + [in_hbm()] * len(more),
        out_shape=[
            jax.ShapeDtypeStruct((8,) + packed, low),
            jax.ShapeDtypeStruct((count, width), low),
            jax.ShapeDtypeStruct((count, low_width), wide),
            jax.ShapeDtypeStruct((row_len, half), wide),
            jax.ShapeDtypeStruct((row_len, half), wide),
        ]
        + [jax.ShapeDtypeStruct(a.shape, low) for a in more],
        scratch_shapes=[
            pltpu.VMEM(in_full.shape, low),
            pltpu.VMEM(packed, low),
            sem((7, 4)),
            sem((7, 4)),
            sem,
            sem,
            sem((2, len(more))),
        ],
        compiler_params=pltpu.CompilerParams(
            collective_id=number, has_side_effects=True, vmem_limit_bytes=32 * 1024 * 1024
        ),
        cost_estimate=pl.CostEstimate(flops=0, bytes_accessed=100 * 1024 * 1024, transcendentals=0),
        name="front",
    )(ends, home, in_full, gain_one, gain_latent, rates, *more)
    return (out[0].reshape(-1, packed[1]), *out[1:])


def gather_kernel(even, chunks, kinds, own_ref, *refs):
    n = len(kinds)
    more, out_ref, more_out = refs[:n], refs[n], refs[n + 1 : 2 * n + 1]
    buf, sends, recvs, local_sems = refs[2 * n + 1 : 2 * n + 5]
    beside = Beside(kinds, more, more_out, refs[-1])
    flow = RowGather(even, chunks, own_ref, out_ref, sends, recvs)
    flow.begin(beside.peers)
    beside.start()
    load = pltpu.make_async_copy(own_ref, buf, local_sems.at[0])
    load.start()
    load.wait()
    store = pltpu.make_async_copy(buf, out_ref.at[flow.me], local_sems.at[1])
    store.start()
    flow.take_near()
    flow.take_side()
    flow.take_far()
    for slot in (3, 4, 5, 6):
        flow.take(slot)
    flow.end()
    store.wait()
    beside.wait()


class Beside:
    def __init__(self, kinds, sources, targets, sems):
        x, c, h = [lax.axis_index(a) for a in ("x", "c", "h")]
        ways = {"x": {"x": other(x)}, "h": {"h": other(h)}, "cross": {"c": other(c), "h": other(h)}}
        self.peers = [ways[k] for k in sorted(set(kinds))]
        self.moves = c != h
        self.copies = [
            (kind, remote(source, target, sems.at[0, i], sems.at[1, i], ways[kind]))
            for i, (kind, source, target) in enumerate(zip(kinds, sources, targets))
        ]

    def start(self, span=slice(None)):
        for kind, copy in self.copies[span]:
            if kind == "cross":
                pl.when(self.moves)(copy.start)
            else:
                copy.start()

    def wait(self, span=slice(None)):
        for kind, copy in self.copies[span]:
            if kind == "cross":
                pl.when(self.moves)(copy.wait)
            else:
                copy.wait()


class RowGather:
    def __init__(self, even, chunks, own_ref, out_ref, sends, recvs, in_slots=False):
        c, l, y, near, side, twin = row_peers(even)
        self.peers = near, side, twin
        self.chunks, self.rows = chunks, own_ref.shape[0] // chunks
        self.own_ref, self.out_ref, self.sends, self.recvs = own_ref, out_ref, sends, recvs
        at = l * 2 + y
        near_at, side_at = near["l"] * 2 + near["y"], side["l"] * 2 + side["y"]
        far_at = other(l) * 2 + other(y)
        self.me = c * 4 + at
        self.places = [c * 4 + p for p in (near_at, side_at, far_at)]
        swapped = even is True
        twins = (at, side_at, near_at, far_at) if swapped else (at, near_at, side_at, far_at)
        self.places += [other(c) * 4 + p for p in twins]
        self.copies = []
        self.lands = (2, 3, 6, 1, 4, 5, 7) if in_slots else None

    def land(self, slot):
        return self.lands[slot] if self.lands else self.places[slot]

    def start(self, held, k, slot, peer):
        span = pl.ds(k * self.rows, self.rows)
        source = self.own_ref.at[span] if held is None else self.out_ref.at[self.land(held), span]
        if self.lands:
            target = self.out_ref.at[self.lands[slot], span]
        else:
            target = self.out_ref.at[self.me if held is None else self.places[held], span]
        copy = remote(source, target, self.sends.at[slot, k], self.recvs.at[slot, k], peer)
        copy.start()
        self.copies.append(copy)

    def begin(self, more_peers=()):
        near, side, twin = self.peers
        if more_peers is not None:
            greet([near, side, twin, *more_peers])
        for k in range(self.chunks):
            self.start(None, k, 0, near)
            self.start(None, k, 1, side)
            self.start(None, k, 3, twin)

    def arrived(self, slot, k):
        span = self.own_ref.at[pl.ds(k * self.rows, self.rows)]
        target = self.out_ref.at[self.land(slot), pl.ds(k * self.rows, self.rows)]
        remote(
            span, target, self.sends.at[slot, k], self.recvs.at[slot, k], self.peers[2]
        ).wait_recv()

    def take(self, slot):
        for k in range(self.chunks):
            self.arrived(slot, k)

    def take_near(self):
        near, side, twin = self.peers
        for k in range(self.chunks):
            self.arrived(0, k)
            self.start(0, k, 2, side)
            self.start(0, k, 4, twin)

    def take_side(self):
        for k in range(self.chunks):
            self.arrived(1, k)
            self.start(1, k, 5, self.peers[2])

    def take_far(self):
        for k in range(self.chunks):
            self.arrived(2, k)
            self.start(2, k, 6, self.peers[2])

    def end(self):
        for copy in self.copies:
            copy.wait_send()


def gather_row(value, number, even=False, kinds=(), more=()):
    if lax.axis_size("l") != 2:
        return lax.all_gather(value, group, axis=0, tiled=True)
    chunks = 4 if value.shape[0] % 64 == 0 else 1
    args = [value, *more]
    out_shape = [jax.ShapeDtypeStruct((8,) + value.shape, low)]
    out_shape += [jax.ShapeDtypeStruct(a.shape, low) for a in more]
    out = pl.pallas_call(
        functools.partial(gather_kernel, even, chunks, kinds),
        in_specs=[in_hbm()] * len(args),
        out_specs=[in_hbm()] * len(args),
        out_shape=out_shape,
        scratch_shapes=[
            pltpu.VMEM(value.shape, low),
            pltpu.SemaphoreType.DMA((7, chunks)),
            pltpu.SemaphoreType.DMA((7, chunks)),
            pltpu.SemaphoreType.DMA((2,)),
            pltpu.SemaphoreType.DMA((2, max(1, len(more)))),
        ],
        compiler_params=pltpu.CompilerParams(
            collective_id=number, has_side_effects=True, vmem_limit_bytes=16 * 1024 * 1024
        ),
        cost_estimate=pl.CostEstimate(flops=0, bytes_accessed=80 * 1024 * 1024, transcendentals=0),
        name="gather_row",
    )(*args)
    rows = out[0].reshape(-1, value.shape[1])
    return (rows, *out[1:]) if kinds else rows


def load_columns(pieces, target, sem, first):
    x, h = lax.axis_index("x"), lax.axis_index("h")
    rows = pieces[0].shape[0]
    loads = []
    for i, piece in enumerate(pieces):
        at_x = x if i < 4 else other(x)
        at_h = h if i // 2 % 2 == 0 else other(h)
        at = pl.multiple_of(((at_x * 2 + i % 2) * 2 + at_h) * rows, rows)
        loads.append(
            pltpu.make_async_copy(piece, target.at[pl.ds(at, rows)], sem.at[first + i])
        )
    return loads


def load_rows(parts, target, sem):
    x, h = lax.axis_index("x"), lax.axis_index("h")
    rows, width = parts[0][0].shape
    loads = []
    for s, part in enumerate(parts):
        for i, (at_x, at_h) in enumerate(
            ((x, h), (x, other(h)), (other(x), h), (other(x), other(h)))
        ):
            at = pl.multiple_of((at_x * 2 + at_h) * rows, 16)
            loads.append(
                pltpu.make_async_copy(
                    part[i],
                    target.at[pl.ds(at, rows), pl.ds(s * width, width)],
                    sem.at[len(loads)],
                )
            )
            loads[-1].start()
    return loads


def wait_all(copies):
    for copy in copies:
        copy.wait()


def for_tiles(total, tile, body):
    def step(j, carry):
        body(pl.ds(pl.multiple_of(j * tile, tile), tile))
        return carry

    lax.fori_loop(0, total // tile, step, 0)


def feed_kernel(even, chunks, *refs):
    own_ref, gates, ups = refs[0], refs[1:9], refs[9:17]
    downs, grad_ref, refs = refs[17:21], refs[21], refs[22:]
    all_ref, inner_ref, a_ref, b_ref = refs[:4]
    downs_x, home_ref, grads_ref, refs = refs[4:8], refs[8], refs[9], refs[10:]
    xs, wg, wu, inner_s, a_s, b_s, grad_buf, sends, recvs, grad_sends, grad_recvs = refs[:11]
    weight_sems, store_sems, own_sem, more_sems, grad_sems = refs[11:]
    flow = RowGather(even, chunks, own_ref, xs, sends, recvs, in_slots=True)
    beside = Beside(
        ("cross", "x", "x", "x", "x"),
        (grad_ref, *downs),
        (home_ref, *downs_x),
        more_sems,
    )
    away = lax.axis_index("c") != lax.axis_index("h")
    grad_flow = RowGather("l", chunks, home_ref, grads_ref, grad_sends, grad_recvs)
    flow.begin(beside.peers)
    beside.start()
    grad_load = pltpu.make_async_copy(grad_ref, grad_buf, grad_sems.at[0])
    grad_load.start()
    own_load = pltpu.make_async_copy(own_ref, xs.at[0], own_sem)
    own_load.start()
    weights = load_columns(gates, wg, weight_sems, 0) + load_columns(ups, wu, weight_sems, 8)
    for load in weights:
        load.start()
    grad_load.wait()
    to_home = pltpu.make_async_copy(grad_buf, home_ref, grad_sems.at[1])

    @pl.when(jnp.logical_not(away))
    def _():
        to_home.start()
        to_home.wait()

    order = [flow.me] + [flow.places[s] for s in (3, 0, 1, 4, 5, 2, 6)]
    stores = []
    columns, width = wg.shape[1], wg.shape[0]

    def work(pair):
        both = pl.ds(2 * pair, 2)
        x = xs[both].reshape(-1, width)

        def tile(cols):
            gate = jnp.dot(x, wg[:, cols], preferred_element_type=wide)
            upward = jnp.dot(x, wu[:, cols], preferred_element_type=wide)
            sigma = jax.nn.sigmoid(gate)
            swish = gate * sigma
            shape = (2, -1, upward.shape[1])
            inner_s[both, :, cols] = (swish * upward).astype(low).reshape(shape)
            b_s[both, :, cols] = swish.astype(low).reshape(shape)
            factor = upward * sigma * (1.0 + gate * (1.0 - sigma))
            a_s[both, :, cols] = factor.astype(low).reshape(shape)

        tile(slice(None))
        for i in (2 * pair, 2 * pair + 1):
            place = order[i]
            for j, (buf, target) in enumerate(
                ((xs, all_ref), (inner_s, inner_ref), (a_s, a_ref), (b_s, b_ref))
            ):
                store = pltpu.make_async_copy(buf.at[i], target.at[place], store_sems.at[i, j])
                store.start()
                stores.append(store)

    own_load.wait()
    flow.take(3)
    wait_all(weights)
    work(0)
    flow.take_near()
    flow.take_side()
    beside.wait(slice(0, 1))
    grad_flow.begin(None)
    home_load = pltpu.make_async_copy(home_ref, grad_buf, grad_sems.at[2])
    home_load.start()
    work(1)
    home_load.wait()
    own_store = pltpu.make_async_copy(grad_buf, grads_ref.at[grad_flow.me], grad_sems.at[3])
    own_store.start()
    flow.take(4)
    flow.take(5)
    work(2)
    flow.take_far()
    grad_flow.take_near()
    grad_flow.take_side()
    flow.take(6)
    work(3)
    grad_flow.take_far()
    for slot in (3, 4, 5, 6):
        grad_flow.take(slot)
    flow.end()
    grad_flow.end()
    wait_all(stores + [own_store])
    beside.wait(slice(1, 5))


def feed_forward(own, gates, ups, downs, grad, number):
    count, width = own.shape
    columns = gates[0].shape[1]
    chunks = 4 if count % 64 == 0 else 1
    row, part = (8, count, width), (8, count, columns)
    sem = pltpu.SemaphoreType.DMA
    flops = 2 * 8 * count * width * columns * 2
    args = [own, *gates, *ups, *downs, grad]
    shapes = [row, part, part, part] + [a.shape for a in downs] + [grad.shape, row]
    return pl.pallas_call(
        functools.partial(feed_kernel, False, chunks),
        in_specs=[in_hbm()] * len(args),
        out_specs=[in_hbm()] * len(shapes),
        out_shape=[jax.ShapeDtypeStruct(s, low) for s in shapes],
        scratch_shapes=[
            pltpu.VMEM(row, low),
            pltpu.VMEM((width, columns), low),
            pltpu.VMEM((width, columns), low),
            pltpu.VMEM(part, low),
            pltpu.VMEM(part, low),
            pltpu.VMEM(part, low),
            pltpu.VMEM(grad.shape, low),
            sem((7, chunks)),
            sem((7, chunks)),
            sem((7, chunks)),
            sem((7, chunks)),
            sem((16,)),
            sem((8, 4)),
            sem,
            sem((2, 5)),
            sem((4,)),
        ],
        compiler_params=pltpu.CompilerParams(
            collective_id=number, has_side_effects=True, vmem_limit_bytes=56 * 1024 * 1024
        ),
        cost_estimate=pl.CostEstimate(
            flops=flops, bytes_accessed=100 * 1024 * 1024, transcendentals=0
        ),
        name="feed_forward",
    )(*args)


def feed_back_kernel(
    even, chunks, *refs,
):
    grad_ref, a_ref, b_ref, inner_ref, all_ref = refs[:5]
    gates, ups, downs, refs = refs[5:13], refs[13:21], refs[21:29], refs[29:]
    out_ref, terms_own, terms_twin, gate_own, gate_across, up_own, up_across = refs[:7]
    down_own, down_across, down_came, refs = refs[7], refs[8], refs[9], refs[10:]
    gx, wg, wu, wd, a_s, b_s, inner_s, terms_s, own_buf, twin_buf, twin_out, down_s = refs[:12]
    far_out, side_out, near_out, far_in, side_in, near_in = refs[12:18]
    sends, recvs, weight_sems, down_sems, block_sems, all_sems, terms_sems, more_sems = refs[18:]
    beside = Beside(("x",), (down_across,), (down_came,), more_sems)
    c, l, y, near, side, twin = row_peers(even)
    rows = out_ref.shape[0] // chunks
    columns, width = wd.shape
    used = 4 * downs[0].shape[0]
    me = l * 2 + y
    near_at, side_at = near["l"] * 2 + near["y"], side["l"] * 2 + side["y"]
    far_at = other(l) * 2 + other(y)
    own_order = (far_at, side_at, near_at, me)
    twin_order = (far_at, near_at, side_at, me) if even else own_order
    pairs = []
    for p, q in zip(twin_order, own_order):
        pairs += [(other(c) * 4 + p, p, True), (c * 4 + q, q, False)]
    downs = load_rows((downs[:4], downs[4:]), wd, down_sems)
    blocks = []
    for i, (place, _, _) in enumerate(pairs):
        loads = [
            pltpu.make_async_copy(source.at[place], buf.at[i], block_sems.at[i, j])
            for j, (source, buf) in enumerate(
                ((grad_ref, gx), (a_ref, a_s), (b_ref, b_s), (inner_ref, inner_s))
            )
        ]
        for load in loads:
            load.start()
        blocks.append(loads)
    weights = load_columns(gates, wg, weight_sems, 0) + load_columns(ups, wu, weight_sems, 8)
    for load in weights:
        load.start()
    wd[used:, :] = jnp.zeros((columns - used, width), low)
    greet([near, side, twin, *beside.peers])
    copies = []

    def start(source, target, slot, k, peer):
        copy = remote(source, target, sends.at[slot, k], recvs.at[slot, k], peer)
        copy.start()
        copies.append(copy)

    def arrived(slot, k):
        span = far_in.at[pl.ds(k * rows, rows)]
        remote(span, span, sends.at[slot, k], recvs.at[slot, k], twin).wait_recv()

    def block_arrived(slot):
        remote(
            own_buf.at[0], twin_buf.at[0], sends.at[slot, 0], recvs.at[slot, 0], twin
        ).wait_recv()

    def term(pair, twin_target, own_target):
        span = pl.ds(2 * pair, 2)
        grads = gx[span].reshape(-1, width)

        dinner = contract(grads, wd[...], ((1,), (1,))).reshape(2, -1, columns)
        a_s[span] = (dinner * a_s[span].astype(wide)).astype(low)
        b_s[span] = (dinner * b_s[span].astype(wide)).astype(low)
        if pair == 0:
            wait_all(weights)
        dgate = a_s[span].reshape(-1, columns)
        dup = b_s[span].reshape(-1, columns)

        def second(cols):
            part = contract(dgate, wg[cols, :], ((1,), (1,)))
            part = (part + contract(dup, wu[cols, :], ((1,), (1,)))).astype(low)
            half = part.shape[0] // 2
            twin_target[:, cols] = part[:half]
            own_target[:, cols] = part[half:]

        for_tiles(width, width // 2, second)

    def both(place, span):
        return own_buf[place, span, :].astype(wide) + twin_buf[place, span, :].astype(wide)

    spans = [(k, pl.ds(k * rows, rows)) for k in range(chunks)]
    for loads in blocks:
        wait_all(loads)
    inners = inner_s[...].reshape(-1, columns)
    x_at = lax.axis_index("x")
    down_rows = down_own.shape[0]

    def down_tile(j):
        span = slice(j * (width // 4), (j + 1) * (width // 4))
        part = contract(inners, gx[:, :, span].reshape(-1, width // 4), ((0,), (0,))).astype(low)
        down_s[...] = part
        at = pl.multiple_of(x_at * down_rows, 16)
        down_own[:, span] = down_s[pl.ds(at, down_rows), :]
        at = pl.multiple_of(other(x_at) * down_rows, 16)
        down_across[:, span] = down_s[pl.ds(at, down_rows), :]

    for j in range(4):
        down_tile(j)
    beside.start()
    wait_all(downs)
    for i in range(4):
        twin_place, own_place = pairs[2 * i][1], pairs[2 * i + 1][1]
        term(i, twin_out.at[i], own_buf.at[own_place])
        start(twin_out.at[i], twin_buf.at[twin_place], 3 + i, 0, twin)
        if i >= 1:
            block_arrived(2 + i)
        if i == 1:
            for k, span in spans:
                far_out[span, :] = both(far_at, span).astype(low)
                start(far_out.at[span], far_in.at[span], 0, k, side)
        if i == 2:
            for k, span in spans:
                side_out[span, :] = both(side_at, span).astype(low)
                start(side_out.at[span], side_in.at[span], 1, k, side)
    block_arrived(6)
    all_loads = [
        pltpu.make_async_copy(all_ref.at[pairs[i][0]], gx.at[i], all_sems.at[i]) for i in range(8)
    ]
    for load in all_loads:
        load.start()
    stores = []

    def output_term(pair):
        span = pl.ds(2 * pair, 2)
        if pair:
            wait_all(stores[2 * pair - 2 :])
        inner = inner_s[span].reshape(-1, columns)

        def tile(cols):
            part = jnp.dot(inner, wd[:, cols], preferred_element_type=wide)
            terms_s[:, :, cols] = part.astype(low).reshape(2, -1, width // 2)

        for_tiles(width, width // 2, tile)
        for i in range(2):
            _, place, is_twin = pairs[2 * pair + i]
            store = pltpu.make_async_copy(
                terms_s.at[i],
                (terms_twin if is_twin else terms_own).at[place],
                terms_sems.at[2 * pair + i],
            )
            store.start()
            stores.append(store)

    for i in range(2):
        output_term(i)
    for k, span in spans:
        arrived(0, k)
        near_out[span, :] = (both(near_at, span) + far_in[span, :].astype(wide)).astype(low)
        start(near_out.at[span], near_in.at[span], 2, k, near)
    for i in range(2, 4):
        output_term(i)
    wait_all(all_loads)
    dgates = a_s[...].reshape(-1, columns)
    dups = b_s[...].reshape(-1, columns)

    half = width // 2
    for gate_ref, up_ref, at in ((gate_across, up_across, other(x_at)), (gate_own, up_own, x_at)):
        for j in range(2):
            cols = pl.ds(pl.multiple_of(at * half + j * (half // 2), 128), half // 2)
            rows_out = slice(j * (half // 2), (j + 1) * (half // 2))
            x = gx[:, :, cols].reshape(-1, half // 2)
            gate_ref[rows_out, :] = contract(x, dgates, ((0,), (0,))).astype(low)
            up_ref[rows_out, :] = contract(x, dups, ((0,), (0,))).astype(low)
    for k, span in spans:
        arrived(1, k)
        arrived(2, k)
        out_ref[span, :] = (
            both(me, span) + side_in[span, :].astype(wide) + near_in[span, :].astype(wide)
        )
    wait_all(stores[6:])
    for copy in copies:
        copy.wait_send()
    beside.wait()


def feed_back(grad_all, a, b, inner, all_two, gate_pieces, up_pieces, down_parts, number):
    count, width = a.shape[1], all_two.shape[2]
    columns = a.shape[2]
    chunks = 4 if count % 64 == 0 else 1
    row, part = (8, count, width), (8, count, columns)
    sem = pltpu.SemaphoreType.DMA
    block = pltpu.VMEM((count, width), low)
    vmem = pl.BlockSpec(memory_space=pltpu.VMEM)
    flops = 2 * 8 * count * width * columns * 6
    args = [grad_all.reshape(row), a, b, inner, all_two, *gate_pieces, *up_pieces]
    args += [piece for parts in down_parts for piece in parts]
    return pl.pallas_call(
        functools.partial(feed_back_kernel, True, chunks),
        in_specs=[in_hbm()] * len(args),
        out_specs=[vmem, in_hbm(), in_hbm()] + [vmem] * 6 + [in_hbm()],
        out_shape=[jax.ShapeDtypeStruct((count, width), wide)]
        + [jax.ShapeDtypeStruct((4, count, width), low)] * 2
        + [jax.ShapeDtypeStruct((width // 2, columns), low)] * 4
        + [jax.ShapeDtypeStruct((2 * down_parts[0][0].shape[0], width), low)] * 3,
        scratch_shapes=[
            pltpu.VMEM(row, low),
            pltpu.VMEM((width, columns), low),
            pltpu.VMEM((width, columns), low),
            pltpu.VMEM((columns, width), low),
            pltpu.VMEM(part, low),
            pltpu.VMEM(part, low),
            pltpu.VMEM(part, low),
            pltpu.VMEM((2, count, width), low),
            pltpu.VMEM((4, count, width), low),
            pltpu.VMEM((4, count, width), low),
            pltpu.VMEM((4, count, width), low),
            pltpu.VMEM((columns, width // 4), low),
        ]
        + [block] * 6
        + [
            sem((7, chunks)),
            sem((7, chunks)),
            sem((16,)),
            sem((8,)),
            sem((8, 4)),
            sem((8,)),
            sem((8,)),
            sem((2, 1)),
        ],
        compiler_params=pltpu.CompilerParams(
            collective_id=number, has_side_effects=True, vmem_limit_bytes=60 * 1024 * 1024
        ),
        cost_estimate=pl.CostEstimate(
            flops=flops, bytes_accessed=100 * 1024 * 1024, transcendentals=0
        ),
        name="feed_back",
    )(*args)


def scatter_kernel(even, chunks, n, kinds, *refs):
    m = len(kinds)
    terms, more, refs = refs[:n], refs[n : n + m], refs[n + m :]
    outs, more_out, refs = refs[:n], refs[n : n + m], refs[n + m :]
    bufs, (sends, recvs, local_sems, more_sems) = refs[: 8 * n], refs[8 * n :]
    beside = Beside(kinds, more, more_out, more_sems)
    bufs = [bufs[8 * a : 8 * a + 8] for a in range(n)]
    c, l, y, near, side, twin = row_peers(even)
    rows = outs[0].shape[0] // chunks
    me = l * 2 + y
    near_at, side_at = near["l"] * 2 + near["y"], side["l"] * 2 + side["y"]
    far_at = other(l) * 2 + other(y)
    greet([near, side, twin] + beside.peers)
    beside.start()
    copies = []

    def start(source, target, a, slot, k, peer):
        copy = remote(source, target, sends.at[a, slot, k], recvs.at[a, slot, k], peer)
        copy.start()
        copies.append(copy)

    parts = [(a, k, pl.ds(k * rows, rows)) for k in range(chunks) for a in range(n)]
    twin_side, twin_near = (near_at, side_at) if even else (side_at, near_at)
    for slot, place in ((3, far_at), (4, twin_side), (5, twin_near), (6, me)):
        for a, k, span in parts:
            start(
                terms[a].at[other(c) * 4 + place, span], bufs[a][1].at[place, span], a, slot, k, twin
            )
    loads = []
    for slot, place in ((0, far_at), (1, side_at), (2, near_at), (3, me)):
        for a in range(n):
            load = pltpu.make_async_copy(
                terms[a].at[c * 4 + place], bufs[a][0].at[place], local_sems.at[a, slot]
            )
            load.start()
            loads.append(load)

    def arrived(a, slot, k):
        span = bufs[a][5].at[pl.ds(k * rows, rows)]
        remote(span, span, sends.at[a, slot, k], recvs.at[a, slot, k], twin).wait_recv()

    def both(a, place, span):
        own, came = bufs[a][0], bufs[a][1]
        return own[place, span, :].astype(wide) + came[place, span, :].astype(wide)

    for load in loads[: 2 * n]:
        load.wait()
    for a, k, span in parts:
        far_out, far_in = bufs[a][2], bufs[a][5]
        arrived(a, 3, k)
        far_out[span, :] = both(a, far_at, span).astype(low)
        start(far_out.at[span], far_in.at[span], a, 0, k, side)
    for a, k, span in parts:
        side_out, side_in = bufs[a][3], bufs[a][6]
        arrived(a, 4, k)
        side_out[span, :] = both(a, side_at, span).astype(low)
        start(side_out.at[span], side_in.at[span], a, 1, k, side)
    for load in loads[2 * n :]:
        load.wait()
    for a, k, span in parts:
        near_out, far_in, near_in = bufs[a][4], bufs[a][5], bufs[a][7]
        arrived(a, 5, k)
        arrived(a, 0, k)
        near_out[span, :] = (both(a, near_at, span) + far_in[span, :].astype(wide)).astype(low)
        start(near_out.at[span], near_in.at[span], a, 2, k, near)
    for a, k, span in parts:
        arrived(a, 6, k)
        arrived(a, 1, k)
        outs[a][span, :] = both(a, me, span) + bufs[a][6][span, :].astype(wide)
    for a, k, span in parts:
        arrived(a, 2, k)
        outs[a][span, :] += bufs[a][7][span, :].astype(wide)
    for copy in copies:
        copy.wait_send()
    beside.wait()


def scatter_row(number, *terms, even=False, kinds=(), more=()):
    if lax.axis_size("l") != 2:
        return [
            lax.psum_scatter(t.astype(wide), group, scatter_dimension=0, tiled=True) for t in terms
        ]
    terms = [t.reshape(8, -1, t.shape[1]) for t in terms]
    n, count = len(terms), terms[0].shape[1]
    chunks = 4 if count % 64 == 0 else 1
    scratch = []
    for t in terms:
        scratch += [pltpu.VMEM((4, count, t.shape[2]), low)] * 2
        scratch += [pltpu.VMEM((count, t.shape[2]), low)] * 6
    return pl.pallas_call(
        functools.partial(scatter_kernel, even, chunks, n, kinds),
        in_specs=[in_hbm()] * (n + len(more)),
        out_specs=[pl.BlockSpec(memory_space=pltpu.VMEM)] * n + [in_hbm()] * len(more),
        out_shape=[jax.ShapeDtypeStruct((count, t.shape[2]), wide) for t in terms]
        + [jax.ShapeDtypeStruct(a.shape, low) for a in more],
        scratch_shapes=scratch
        + [
            pltpu.SemaphoreType.DMA((n, 7, chunks)),
            pltpu.SemaphoreType.DMA((n, 7, chunks)),
            pltpu.SemaphoreType.DMA((n, 4)),
            pltpu.SemaphoreType.DMA((2, max(1, len(more)))),
        ],
        compiler_params=pltpu.CompilerParams(
            collective_id=number, has_side_effects=True, vmem_limit_bytes=24 * 1024 * 1024
        ),
        cost_estimate=pl.CostEstimate(flops=0, bytes_accessed=80 * 1024 * 1024, transcendentals=0),
        name="scatter_row",
    )(*terms, *more)


def norm_back_rows(incoming, source, gain):
    scale = rms_scale(source)
    weighted = incoming * gain
    mean = jnp.mean(weighted * source, axis=-1, keepdims=True)
    grad = scale * weighted - source * (scale * scale * scale) * mean
    return grad, jnp.sum(incoming * source * scale, axis=0, keepdims=True)


def shut_kernel(part, head_dim, order, n_in, n_out, *refs):
    ins, outs, refs = refs[:n_in], refs[n_in : n_in + n_out], refs[n_in + n_out :]
    (
        dlow_ref, dkv_ref, latent_ref, gain_latent_ref, cos_ref, sin_ref, hidden_ref, in_full_ref,
        home_ref, gain_one_ref, dresid_ref, gain_two_ref, gate_ref, up_ref, heads_ref, final_ref,
        kept_ref, across_ref,
    ) = ins
    sum_ref, tokens_ref, output_ref, gate_out, up_out, heads_out, out_ref = outs
    full, mapped, terms, gains, twin_buf, held, came, moved, swap_buf = refs[:9]
    gate_in, up_in, heads_in, final_buf, across_in = refs[9:14]
    sends, recvs, set_sends, set_recvs, swap_sems, local_sems = refs[14:]
    x, c, h, l, y = [lax.axis_index(a) for a in every]
    hops = {
        1: {"h": other(h)},
        2: {"l": other(l)},
        4: {"y": other(y)},
        8: {"x": other(x)},
    }
    twin = {"c": other(c)}
    cross = {"c": other(c), "h": other(h)}
    me = (c * 2 + l) * 2 + y

    def group_peer(k):
        return {"c": other(c, k // 4), "l": other(l, k // 2 % 2), "y": other(y, k % 2)}

    def group_index(k):
        peer = group_peer(k)
        return (peer["c"] * 2 + peer["l"]) * 2 + peer["y"]

    def index(code, core):
        at_x, at_l = other(x, code // 8 % 2), other(l, code // 2 % 2)
        return (((at_x * 2 + core) * 2 + other(h, code % 2)) * 2 + at_l) * 2 + other(y, code // 4 % 2)

    load = pltpu.make_async_copy(in_full_ref, full, local_sems.at[0])
    load.start()
    greet([hops[1], hops[8], cross] + [group_peer(k) for k in range(1, 8)])
    set_copies = []
    for i, (source, target) in enumerate(
        ((heads_ref, heads_in), (gate_ref, gate_in), (up_ref, up_in))
    ):
        for k in range(1, 8):
            copy = remote(
                source.at[group_index(k)], target.at[me], set_sends.at[i, k], set_recvs.at[i, k],
                group_peer(k),
            )
            copy.start()
            set_copies.append(copy)
    set_loads = [
        pltpu.make_async_copy(source.at[me], target.at[me], local_sems.at[1 + i])
        for i, (source, target) in enumerate(
            ((heads_ref, heads_in), (gate_ref, gate_in), (up_ref, up_in))
        )
    ]
    for copy in set_loads:
        copy.start()
    exchange = remote(across_ref, across_in, swap_sems.at[0], swap_sems.at[1], hops[1])
    output_move = remote(final_ref, output_ref, swap_sems.at[2], swap_sems.at[3], cross)
    tokens_move = remote(swap_buf, moved, swap_sems.at[4], swap_sems.at[5], cross)
    final_load = pltpu.make_async_copy(final_ref, final_buf, local_sems.at[4])
    final_store = pltpu.make_async_copy(final_buf, output_ref, local_sems.at[5])

    @pl.when(c != h)
    def _():
        output_move.start()

    @pl.when(c == h)
    def _():
        final_load.start()

    width, low_width = hidden_ref.shape[1], latent_ref.shape[1]
    half = head_dim // 2
    dlatent, dgain_latent = norm_back_rows(dlow_ref[...], latent_ref[...], gain_latent_ref[...])
    mapped[:, :low_width] = dlatent.astype(low)
    a, b = dkv_ref[:, :half], dkv_ref[:, half:head_dim]
    cosine, sine = cos_ref[...], sin_ref[...]
    mapped[:, low_width : low_width + half] = (a * cosine + b * sine).astype(low)
    mapped[:, low_width + half : low_width + head_dim] = (b * cosine - a * sine).astype(low)
    mapped[:, low_width + head_dim : low_width + 2 * head_dim] = dkv_ref[:, head_dim:].astype(low)
    mapped[:, low_width + 2 * head_dim :] = jnp.zeros((mapped.shape[0], 128), low)
    load.wait()
    dmapped = mapped[...]
    weights = full[...].reshape(width, -1)
    dhidden = contract(dmapped, weights, ((1,), (1,)))
    dinput, dgain_one = norm_back_rows(dhidden, home_ref[...].astype(wide), gain_one_ref[...])
    dtokens = dresid_ref[...] + dinput
    tokens_ref[...] = dtokens
    swap_buf[...] = dtokens.astype(low)

    gains[...] = jnp.zeros_like(gains)
    gains[0:1, :width] = dgain_one
    gains[1:2, :width] = gain_two_ref[...]
    gains[2:3, :low_width] = dgain_latent
    rows = terms.shape[1]
    low_part = low_width // 32
    used = low_width + 2 * head_dim
    for at in range(0, 32, 4):
        left = hidden_ref[:, at * rows : (at + 4) * rows]
        block = contract(left, dmapped[:, :used], ((0,), (0,))).astype(low)
        terms[at : at + 4, :, :used] = block.reshape(4, rows, used)
        for i in range(at, at + 4):
            tile = jnp.concatenate(
                [
                    gains[0:2, i * rows : i * rows + 128],
                    gains[2:3, i * low_part : i * low_part + 128],
                    jnp.zeros((rows - 3, 128), wide),
                ],
                axis=0,
            )
            terms[i, :, used:] = tile.astype(low)
    copies = []

    def start(source, target, slot, peer):
        copy = remote(source, target, sends.at[slot], recvs.at[slot], peer)
        copy.start()
        copies.append(copy)

    def arrived(slot):
        remote(came.at[0], came.at[0], sends.at[slot], recvs.at[slot], twin).wait_recv()

    for code in range(15, -1, -1):
        start(terms.at[index(code, 1 - c)], twin_buf.at[code], 16 + code, twin)
    for code in range(15, -1, -1):
        arrived(16 + code)
        total = terms[index(code, c)].astype(wide) + twin_buf[code].astype(wide)
        for hop in (8, 4, 2, 1):
            if code < hop:
                arrived(code + hop)
                total = total + came[code + hop].astype(wide)
        if code == 0:
            sum_ref[...] = total
        else:
            held[code] = total.astype(low)
            hop = 1 << (code.bit_length() - 1)
            start(held.at[code], came.at[code], code, hops[hop])
        if code == 8:

            @pl.when(c != h)
            def _():
                tokens_move.start()

            exchange.start()

        if code == 4:
            for copy in set_loads:
                copy.wait()
            for copy in set_copies:
                copy.wait()
            for source, target in ((gate_in, gate_out), (up_in, up_out)):
                for place, blocks in enumerate(order):
                    for j, block in enumerate(blocks):
                        target[:, block * part : (block + 1) * part] = source[
                            place, :, j * part : (j + 1) * part
                        ].astype(wide)
            for place in range(8):
                core, at_l, at_y = place // 4, place // 2 % 2, place % 2
                for j in range(2):
                    head = ((j * 2 + core) * 2 + at_y) * 2 + at_l
                    heads_out[:, head * head_dim : (head + 1) * head_dim] = heads_in[
                        place, :, j * head_dim : (j + 1) * head_dim
                    ].astype(wide)
    exchange.wait()
    out_ref[...] = kept_ref[...].astype(wide) + across_in[...].astype(wide)
    for copy in copies:
        copy.wait_send()

    @pl.when(c != h)
    def _():
        output_move.wait()
        tokens_move.wait()
        tokens_ref[...] = moved[...].astype(wide)

    @pl.when(c == h)
    def _():
        final_load.wait()
        final_store.start()
        final_store.wait()


def shut(
    dlow, dkv, latent, gain_latent, cosine, sine, hidden, in_full, home, gain_one, dresid, dgain_two,
    gate_terms, up_terms, head_terms, final, kept, across, part, order, number,
):
    count, width = hidden.shape
    head_dim = dkv.shape[1] // 2
    rows, columns = in_full.shape[1:]
    vmem, sem = pl.BlockSpec(memory_space=pltpu.VMEM), pltpu.SemaphoreType.DMA
    args = [
        dlow, dkv, latent, gain_latent, cosine, sine, hidden, in_full, home, gain_one, dresid,
        dgain_two, gate_terms, up_terms, head_terms, final, kept, across,
    ]
    hbm = {7, 12, 13, 14, 15, 17}
    ff = len(order) * len(order[0]) * part
    shapes = [
        ((rows, columns), wide),
        ((count, width), wide),
        ((count, width), low),
        ((gate_terms.shape[1], ff), wide),
        ((up_terms.shape[1], ff), wide),
        ((head_terms.shape[1], 8 * head_terms.shape[2]), wide),
        (kept.shape, wide),
    ]
    blocks = pltpu.VMEM((16, rows, columns), low)
    return pl.pallas_call(
        functools.partial(shut_kernel, part, head_dim, order, len(args), len(shapes)),
        in_specs=[in_hbm() if i in hbm else vmem for i in range(len(args))],
        out_specs=[in_hbm() if i == 2 else vmem for i in range(len(shapes))],
        out_shape=[jax.ShapeDtypeStruct(*s) for s in shapes],
        scratch_shapes=[
            pltpu.VMEM(in_full.shape, low),
            pltpu.VMEM((count, columns), low),
            pltpu.VMEM(in_full.shape, low),
            pltpu.VMEM((16, width + 128), wide),
            blocks,
            blocks,
            blocks,
            pltpu.VMEM((count, width), low),
            pltpu.VMEM((count, width), low),
            pltpu.VMEM(gate_terms.shape, low),
            pltpu.VMEM(up_terms.shape, low),
            pltpu.VMEM(head_terms.shape, low),
            pltpu.VMEM((count, width), low),
            pltpu.VMEM(across.shape, low),
            sem((32,)),
            sem((32,)),
            sem((3, 8)),
            sem((3, 8)),
            sem((6,)),
            sem((6,)),
        ],
        compiler_params=pltpu.CompilerParams(
            collective_id=number, has_side_effects=True, vmem_limit_bytes=60 * 1024 * 1024
        ),
        cost_estimate=pl.CostEstimate(flops=0, bytes_accessed=150 * 1024 * 1024, transcendentals=0),
        name="shut",
    )(*args)


def split_kernel(part, order, a_ref, b_ref, a_out, b_out):
    for source, target in ((a_ref, a_out), (b_ref, b_out)):
        used, total = len(order[0]) * part, target.shape[2]
        for place, blocks in enumerate(order):
            for j, block in enumerate(blocks):
                target[place, :, j * part : (j + 1) * part] = source[
                    :, block * part : (block + 1) * part
                ]
            if used < total:
                target[place, :, used:] = jnp.zeros((target.shape[1], total - used), target.dtype)


def join_kernel(part, order, a_ref, b_ref, a_out, b_out):
    for source, target in ((a_ref, a_out), (b_ref, b_out)):
        for place, blocks in enumerate(order):
            for j, block in enumerate(blocks):
                target[:, block * part : (block + 1) * part] = source[
                    place, :, j * part : (j + 1) * part
                ].astype(wide)


def column_order(n_x, n_l):
    return [
        [
            (((x * 2 + c) * 2 + h) * n_l + l) * 2 + y
            for x in range(n_x)
            for h in range(2)
        ]
        for c in range(2)
        for l in range(n_l)
        for y in range(2)
    ]


def split_columns(a, b, part, order, total):
    shape = jax.ShapeDtypeStruct((len(order), a.shape[0], total), a.dtype)
    return pl.pallas_call(
        functools.partial(split_kernel, part, order), out_shape=[shape] * 2, name="split_columns"
    )(a, b)


def join_columns(a, b, part, order):
    shape = jax.ShapeDtypeStruct((a.shape[1], len(order) * len(order[0]) * part), wide)
    return pl.pallas_call(
        functools.partial(join_kernel, part, order), out_shape=[shape] * 2, name="join_columns"
    )(a, b)


def first_allowed(ends_ref, count, places):
    start = jnp.zeros_like(places)
    for j in range(count):
        end = ends_ref[j]
        start = jnp.where(places >= end, end, start)
    return jnp.where(places >= ends_ref[count - 1], places, start)


def contract(left, right, dims):
    return lax.dot_general(left, right, (dims, ((), ())), preferred_element_type=wide)


def stacked(ref, span, heads, width):
    return jnp.concatenate(
        [ref[span, j * width : (j + 1) * width] for j in range(heads)], axis=0
    )


def tile_mask(ends_ref, begin, tile, length, heads):
    rows = begin + lax.broadcasted_iota(jnp.int32, (tile, 1), 0)
    lows = first_allowed(ends_ref, ends_ref.shape[0], rows)
    rows = jnp.concatenate([rows] * heads, axis=0)
    lows = jnp.concatenate([lows] * heads, axis=0)
    columns = lax.broadcasted_iota(jnp.int32, (heads * tile, length), 1)
    return (columns >= lows) & (columns <= rows)


def attend_kernel(heads, tile, ends_ref, q_ref, k_ref, v_ref, o_ref, log_ref):
    width = k_ref.shape[1]
    for i in range(q_ref.shape[0] // tile):
        span, length = slice(i * tile, (i + 1) * tile), (i + 1) * tile
        mask = tile_mask(ends_ref, i * tile, tile, length, heads)
        scores = contract(stacked(q_ref, span, heads, width), k_ref[:length, :], ((1,), (1,)))
        scores = jnp.where(mask, scores, masked_value)
        top = jnp.max(scores, axis=1, keepdims=True)
        weights = jnp.exp(scores - top)
        total = jnp.sum(weights, axis=1, keepdims=True)
        mixed = contract(weights.astype(low), v_ref[:length, :], ((1,), (0,))) / total
        log = jnp.broadcast_to(top + jnp.log(total), (heads * tile, 128))
        for j in range(heads):
            part = slice(j * tile, (j + 1) * tile)
            o_ref[span, j * width : (j + 1) * width] = mixed[part].astype(low)
            log_ref[j, span, :] = log[part]


def attend_back_kernel(
    heads, tile, scale, ends_ref, q_ref, g_ref, o_ref, k_ref, v_ref, log_ref, cos_ref, sin_ref,
    dq_ref, dkv_ref, sum_ref,
):
    width = k_ref.shape[1]
    half = width // 2
    sum_ref[...] = jnp.zeros_like(sum_ref)
    for i in range(q_ref.shape[0] // tile):
        span, length = slice(i * tile, (i + 1) * tile), (i + 1) * tile
        mask = tile_mask(ends_ref, i * tile, tile, length, heads)
        queries = stacked(q_ref, span, heads, width)
        grads = stacked(g_ref, span, heads, width)
        outs = stacked(o_ref, span, heads, width)
        delta = jnp.sum(grads.astype(wide) * outs.astype(wide), axis=1, keepdims=True)
        log = jnp.concatenate([log_ref[j, span, :1] for j in range(heads)], axis=0)
        keys, values = k_ref[:length, :], v_ref[:length, :]
        scores = contract(queries, keys, ((1,), (1,)))
        weights = jnp.where(mask, jnp.exp(scores - log), 0.0)
        dprob = contract(grads, values, ((1,), (1,)))
        dscore = (weights * (dprob - delta)).astype(low)
        sum_ref[:length, width:] += contract(weights.astype(low), grads, ((0,), (0,)))
        sum_ref[:length, :width] += contract(dscore, queries, ((0,), (0,)))
        dquery = contract(dscore, keys, ((1,), (0,))) * scale
        cosine, sine = cos_ref[span, :], sin_ref[span, :]
        for j in range(heads):
            a = dquery[j * tile : (j + 1) * tile, :half]
            b = dquery[j * tile : (j + 1) * tile, half:]
            at = j * width
            dq_ref[span, at : at + half] = (a * cosine + b * sine).astype(low)
            dq_ref[span, at + half : at + width] = (b * cosine - a * sine).astype(low)
    dkv_ref[...] = sum_ref[...].astype(low)


def attend_whole_kernel(
    heads, tile, scale, ends_ref, packed_ref, up_ref, cos_ref, sin_ref, own_ref, other_ref,
    q_ref, o_ref, log_ref, terms_ref, out_ref,
):
    x = lax.axis_index("x")
    width = up_ref.shape[1] // heads
    half, low_width = width // 2, up_ref.shape[0]
    rows = own_ref.shape[0]
    out_ref[pl.ds(pl.multiple_of(x * rows, rows), rows), :] = own_ref[...]
    out_ref[pl.ds(pl.multiple_of(other(x) * rows, rows), rows), :] = other_ref[...]
    for i in range(q_ref.shape[0] // tile):
        span, length = slice(i * tile, (i + 1) * tile), (i + 1) * tile
        raw = jnp.dot(packed_ref[span, :low_width], up_ref[...], preferred_element_type=wide)
        cosine, sine = cos_ref[span, :] * scale, sin_ref[span, :] * scale
        queries = []
        for j in range(heads):
            a, b = turn(raw[:, j * width : (j + 1) * width], cosine, sine)
            q_ref[span, j * width : j * width + half] = a.astype(low)
            q_ref[span, j * width + half : (j + 1) * width] = b.astype(low)
        mask = tile_mask(ends_ref, i * tile, tile, length, heads)
        keys = packed_ref[:length, low_width : low_width + width]
        values = packed_ref[:length, low_width + width :]
        scores = contract(stacked(q_ref, span, heads, width), keys, ((1,), (1,)))
        scores = jnp.where(mask, scores, masked_value)
        top = jnp.max(scores, axis=1, keepdims=True)
        weights = jnp.exp(scores - top)
        total = jnp.sum(weights, axis=1, keepdims=True)
        mixed = contract(weights.astype(low), values, ((1,), (0,))) / total
        log = jnp.broadcast_to(top + jnp.log(total), (heads * tile, 128))
        for j in range(heads):
            part = slice(j * tile, (j + 1) * tile)
            o_ref[span, j * width : (j + 1) * width] = mixed[part].astype(low)
            log_ref[j, span, :] = log[part]
        terms_ref[span, :] = jnp.dot(
            o_ref[span, :], out_ref[...], preferred_element_type=wide
        ).astype(low)


def attend_whole(ends, packed, up_query, cosine, sine, own_heads, other_heads, heads, scale):
    length, width = packed.shape[0], own_heads.shape[1]
    columns = up_query.shape[1]
    vmem = pl.BlockSpec(memory_space=pltpu.VMEM)
    return pl.pallas_call(
        functools.partial(attend_whole_kernel, heads, tile_of(length), scale),
        in_specs=[pl.BlockSpec(memory_space=pltpu.SMEM)] + [vmem] * 6,
        out_specs=[vmem] * 5,
        out_shape=[
            jax.ShapeDtypeStruct((length, columns), low),
            jax.ShapeDtypeStruct((length, columns), low),
            jax.ShapeDtypeStruct((heads, length, 128), wide),
            jax.ShapeDtypeStruct((length, width), low),
            jax.ShapeDtypeStruct((columns, width), low),
        ],
        compiler_params=pltpu.CompilerParams(vmem_limit_bytes=56 * 1024 * 1024),
        cost_estimate=pl.CostEstimate(
            flops=12 * length * length * columns,
            bytes_accessed=16 * length * columns,
            transcendentals=length * length * heads // 2,
        ),
        name="attend",
    )(ends, packed, up_query, cosine, sine, own_heads, other_heads)


def attend_whole_back_kernel(
    heads, tile, scale, ends_ref, q_ref, branch_ref, o_ref, packed_ref, log_ref, cos_ref, sin_ref,
    out_ref, up_ref, dq_ref, dlow_ref, dkv_ref, sum_ref,
):
    width = up_ref.shape[1] // heads
    half, low_width = width // 2, up_ref.shape[0]
    sum_ref[...] = jnp.zeros_like(sum_ref)
    for i in range(q_ref.shape[0] // tile):
        span, length = slice(i * tile, (i + 1) * tile), (i + 1) * tile
        mask = tile_mask(ends_ref, i * tile, tile, length, heads)
        queries = stacked(q_ref, span, heads, width)
        dmixed = contract(branch_ref[span, :], out_ref[...], ((1,), (1,))).astype(low)
        grads = jnp.concatenate(
            [dmixed[:, j * width : (j + 1) * width] for j in range(heads)], axis=0
        )
        outs = stacked(o_ref, span, heads, width)
        delta = jnp.sum(grads.astype(wide) * outs.astype(wide), axis=1, keepdims=True)
        log = jnp.concatenate([log_ref[j, span, :1] for j in range(heads)], axis=0)
        keys = packed_ref[:length, low_width : low_width + width]
        values = packed_ref[:length, low_width + width :]
        scores = contract(queries, keys, ((1,), (1,)))
        weights = jnp.where(mask, jnp.exp(scores - log), 0.0)
        dprob = contract(grads, values, ((1,), (1,)))
        dscore = (weights * (dprob - delta)).astype(low)
        sum_ref[:length, width:] += contract(weights.astype(low), grads, ((0,), (0,)))
        sum_ref[:length, :width] += contract(dscore, queries, ((0,), (0,)))
        dquery = contract(dscore, keys, ((1,), (0,))) * scale
        cosine, sine = cos_ref[span, :], sin_ref[span, :]
        for j in range(heads):
            a = dquery[j * tile : (j + 1) * tile, :half]
            b = dquery[j * tile : (j + 1) * tile, half:]
            at = j * width
            dq_ref[span, at : at + half] = (a * cosine + b * sine).astype(low)
            dq_ref[span, at + half : at + width] = (b * cosine - a * sine).astype(low)
        dlow_ref[span, :] = contract(dq_ref[span, :], up_ref[...], ((1,), (1,))).astype(low)
    dkv_ref[...] = sum_ref[...].astype(low)


def attend_whole_back(
    ends, query, branch, mixed, packed, logs, cosine, sine, out_own, up_query, heads, scale
):
    length, columns = query.shape
    width = columns // heads
    vmem = pl.BlockSpec(memory_space=pltpu.VMEM)
    return pl.pallas_call(
        functools.partial(attend_whole_back_kernel, heads, tile_of(length), scale),
        in_specs=[pl.BlockSpec(memory_space=pltpu.SMEM)] + [vmem] * 9,
        out_specs=[vmem] * 3,
        out_shape=[
            jax.ShapeDtypeStruct((length, columns), low),
            jax.ShapeDtypeStruct((length, up_query.shape[0]), low),
            jax.ShapeDtypeStruct((length, 2 * width), low),
        ],
        scratch_shapes=[pltpu.VMEM((length, 2 * width), wide)],
        compiler_params=pltpu.CompilerParams(vmem_limit_bytes=56 * 1024 * 1024),
        cost_estimate=pl.CostEstimate(
            flops=18 * length * length * columns,
            bytes_accessed=30 * length * columns,
            transcendentals=length * length * heads // 2,
        ),
        name="attend_back",
    )(ends, query, branch, mixed, packed, logs, cosine, sine, out_own, up_query)


def tile_of(length):
    return next(t for t in (256, 128, 64, 32, 16, 8) if length % t == 0)


def attend(ends, query, packed, heads):
    length, width = query.shape[0], query.shape[1] // heads
    tile = tile_of(length)
    first = packed.shape[1] // width - 2
    return pl.pallas_call(
        functools.partial(attend_kernel, heads, tile),
        grid=(1,),
        in_specs=[
            pl.BlockSpec(memory_space=pltpu.SMEM),
            pl.BlockSpec((length, heads * width), lambda i: (0, 0)),
            pl.BlockSpec((length, width), lambda i: (0, first)),
            pl.BlockSpec((length, width), lambda i: (0, first + 1)),
        ],
        out_specs=[
            pl.BlockSpec((length, heads * width), lambda i: (0, 0)),
            pl.BlockSpec((heads, length, 128), lambda i: (0, 0, 0)),
        ],
        out_shape=[
            jax.ShapeDtypeStruct((length, heads * width), low),
            jax.ShapeDtypeStruct((heads, length, 128), wide),
        ],
        compiler_params=pltpu.CompilerParams(vmem_limit_bytes=56 * 1024 * 1024),
        cost_estimate=pl.CostEstimate(
            flops=6 * length * length * width * heads,
            bytes_accessed=8 * length * width * heads,
            transcendentals=length * length * heads // 2,
        ),
        name="attend",
    )(ends, query, packed, packed)


def attend_back(ends, query, grad, mixed, packed, logs, cosine, sine, heads, scale):
    length, width = query.shape[0], query.shape[1] // heads
    tile = tile_of(length)
    first = packed.shape[1] // width - 2
    rows = pl.BlockSpec((length, heads * width), lambda i: (0, 0))
    angle = pl.BlockSpec((length, width // 2), lambda i: (0, 0))
    return pl.pallas_call(
        functools.partial(attend_back_kernel, heads, tile, scale),
        grid=(1,),
        in_specs=[
            pl.BlockSpec(memory_space=pltpu.SMEM),
            rows,
            rows,
            rows,
            pl.BlockSpec((length, width), lambda i: (0, first)),
            pl.BlockSpec((length, width), lambda i: (0, first + 1)),
            pl.BlockSpec((heads, length, 128), lambda i: (0, 0, 0)),
            angle,
            angle,
        ],
        out_specs=[rows, pl.BlockSpec((length, 2 * width), lambda i: (0, 0))],
        out_shape=[
            jax.ShapeDtypeStruct((length, heads * width), low),
            jax.ShapeDtypeStruct((length, 2 * width), low),
        ],
        scratch_shapes=[pltpu.VMEM((length, 2 * width), wide)],
        compiler_params=pltpu.CompilerParams(vmem_limit_bytes=56 * 1024 * 1024),
        cost_estimate=pl.CostEstimate(
            flops=10 * length * length * width * heads,
            bytes_accessed=16 * length * width * heads,
            transcendentals=length * length * heads // 2,
        ),
        name="attend_back",
    )(ends, query, grad, mixed, packed, packed, logs, cosine, sine)


def on_device(
    tokens,
    lengths,
    cotangent,
    norm_one,
    query_down,
    query_gain,
    query_up,
    key_proj,
    value_proj,
    out_proj,
    norm_two,
    gate_proj,
    up_proj,
    down_proj,
):
    n_x, n_l = lax.axis_size("x"), lax.axis_size("l")
    x, c, h, l, y = [lax.axis_index(a) for a in every]
    n_dev = n_x * 8 * n_l
    n_group = 4 * n_l
    me = group_place()
    count, width = tokens.shape
    row_len = count * n_group
    latent_width = query_down.shape[1]
    head_dim = key_proj.shape[1]
    shard = query_down.shape[0]
    heads = query_up.shape[1] // head_dim // n_group
    ff_part = down_proj.shape[0]
    ff_own = ff_part * n_x * 2
    ff_pad = -(-ff_own // 128) * 128
    natural = n_x == 2 and n_l == 2
    scale = 1.0 / math.sqrt(head_dim)
    order = column_order(n_x, n_l)
    mapped_width = latent_width + 2 * head_dim

    gains = jnp.zeros((shard, 128), low)
    gains = gains.at[0, :shard].set(norm_one).at[1, :shard].set(norm_two)
    gains = gains.at[2, : query_gain.shape[0]].set(query_gain)
    small = jnp.concatenate([query_down, key_proj, value_proj, gains], axis=1)
    rows_up = query_up.shape[0]
    if natural:
        head_cols = query_up.reshape(rows_up, 2, 2, 2, 2, head_dim)
        head_cols = head_cols.transpose(2, 4, 3, 0, 1, 5)
    else:
        head_cols = query_up.reshape(rows_up, n_group, -1).transpose(1, 0, 2)
    head_cols = head_cols.reshape(n_group, rows_up, heads * head_dim)
    gate_cols, up_cols = split_columns(gate_proj, up_proj, ff_part, order, ff_pad)
    if natural:
        lens = jnp.pad(lengths, ((0, 7), (0, 128 - lengths.shape[1])))
        in_full, own_heads, (up_query, gate_rows, up_rows), (home, lens) = open_exchange(
            small, out_proj, [head_cols, gate_cols, up_cols], [tokens, lens]
        )
        row_lengths = lens[0, : lengths.shape[1]]
    else:
        in_full = lax.all_gather(small, every, axis=0)
        home, grad_home, row_lengths = [swap_home(a) for a in (tokens, cotangent, lengths)]
        row_lengths = row_lengths[0]
        up_query, gate_rows, up_rows = [
            all_to_all_row(a) for a in (head_cols, gate_cols, up_cols)
        ]
        up_query = up_query.reshape((2, -1) + up_query.shape[1:])
        up_query = lax.all_gather(lax.all_gather(up_query, "h", axis=1), "x", axis=0)
    up_query = up_query.reshape(latent_width, -1)
    gate_rows = gate_rows.reshape(2, -1, ff_pad)
    up_rows = up_rows.reshape(2, -1, ff_pad)
    gain_one = in_full[:, 0, mapped_width : mapped_width + shard].reshape(width).astype(wide)
    gain_two = in_full[:, 1, mapped_width : mapped_width + shard].reshape(width).astype(wide)
    gain_latent = in_full[:, 2, mapped_width : mapped_width + query_gain.shape[0]]
    gain_latent = gain_latent.reshape(latent_width).astype(wide)
    in_full = in_full.reshape(width, -1)

    inputs = home.astype(wide)
    mapped_rates = jnp.exp(
        jnp.arange(head_dim // 2, dtype=wide) * (-math.log(10000.0) / (head_dim // 2))
    )
    ends = jnp.cumsum(row_lengths, dtype=jnp.int32)
    places = jnp.arange(row_len, dtype=jnp.int32)
    begins = jnp.max(jnp.where(places[:, None] >= ends[None, :], ends[None, :], 0), axis=1)
    if not natural:
        phases = (places - begins).astype(wide)[:, None] * mapped_rates
        cosine, sine = jnp.cos(phases), jnp.sin(phases)
        own_cos = lax.dynamic_slice_in_dim(cosine, me * count, count)
        own_sin = lax.dynamic_slice_in_dim(sine, me * count, count)

    if natural:
        own_heads = own_heads.reshape(-1, width)
        gate_a, gate_b, up_a, up_b = gate_rows[0], gate_rows[1], up_rows[0], up_rows[1]
        down_a, down_b = down_proj[:, : width // 2], down_proj[:, width // 2 :]
        heads_x = flip(own_heads, "x")
    else:
        out_full = lax.all_gather(out_proj, every, axis=0, tiled=True)
        out_own = lax.dynamic_slice_in_dim(out_full, me * heads * head_dim, heads * head_dim)
        gate_own, up_own = [
            lax.all_gather(lax.all_gather(a, "h", axis=1), "x", axis=0).reshape(width, -1)
            for a in (gate_rows, up_rows)
        ]
        down_own = lax.all_gather(lax.all_gather(down_proj, "h", axis=0), "x", axis=0)
        down_own = jnp.pad(down_own.reshape(-1, width), ((0, ff_pad - ff_own), (0, 0)))

    scale_one = rms_scale(inputs)
    if natural:
        packed, hidden, latent, cosine, sine, gate_a_h, gate_b_h = front(
            ends, home, in_full, gain_one[None], gain_latent[None], mapped_rates[None], row_len, 2,
            ("h", "h"), (gate_a, gate_b),
        )
        own_cos = lax.dynamic_slice_in_dim(cosine, me * count, count)
        own_sin = lax.dynamic_slice_in_dim(sine, me * count, count)
        packed, heads_x, up_a = together(packed, heads_x, up_a)
        up_a_h, up_b_h = flip(up_a, "h"), flip(after(up_b, packed), "h")
        gate_x = [flip(a, "x") for a in (gate_a, gate_b, gate_a_h, gate_b_h)]
        all_latent = packed[:, :latent_width]
        query, mixed, logs, terms, out_own = attend_whole(
            ends, packed, up_query, cosine, sine, own_heads, heads_x, heads, scale
        )
        terms, up_a_h, up_b_h = together(terms, up_a_h, up_b_h)
        up_x = [flip(a, "x") for a in (up_a, up_b, up_a_h, up_b_h)]
        attended, down_a_h, down_b_h = scatter_row(3, terms, kinds=("h", "h"), more=(down_a, down_b))
        attended, gate_x, up_x = together(attended, gate_x, up_x)
    else:
        hidden = (inputs * scale_one * gain_one).astype(low)
        mapped = dot(hidden, in_full)
        latent = mapped[:, :latent_width]
        scale_latent = rms_scale(latent)
        latent_low = (latent * scale_latent * gain_latent).astype(low)
        keys = mapped[:, latent_width : latent_width + head_dim]
        keys = rotate(keys, own_cos, own_sin).astype(low)
        values = mapped[:, latent_width + head_dim : mapped_width].astype(low)
        packed = gather_row(jnp.concatenate([latent_low, keys, values], axis=1), 2)
        grad_all = lax.all_gather(grad_home, group, axis=0, tiled=True)
        all_latent = packed[:, :latent_width]
        query_raw = dot(all_latent, up_query)
        query = jnp.concatenate(
            [
                rotate(query_raw[:, j * head_dim : (j + 1) * head_dim], cosine, sine)
                for j in range(heads)
            ],
            axis=1,
        ).astype(low) * jnp.asarray(scale, low)
        mixed, logs = attend(ends, query, packed, heads)
        attended = scatter_row(3, dot(mixed, out_own, low))[0]
    resid = inputs + attended
    scale_two = rms_scale(resid)
    hidden_two = (resid * scale_two * gain_two).astype(low)
    if natural:
        gate_parts = [gate_a, gate_b, gate_a_h, gate_b_h] + list(gate_x)
        up_parts = [up_a, up_b, up_a_h, up_b_h] + list(up_x)
        (
            all_two, inner, gate_factor, up_factor, down_a_x, down_a_xh, down_b_x, down_b_xh,
            grad_home, grad_all,
        ) = feed_forward(
            hidden_two, gate_parts, up_parts, (down_a, down_a_h, down_b, down_b_h), cotangent, 4
        )
    else:
        all_two = gather_row(hidden_two, 4)
        gate = dot(all_two, gate_own)
        upward = dot(all_two, up_own)
        sigma = jax.nn.sigmoid(gate)
        inner = (gate * sigma * upward).astype(low)
        grad_down = outer_sum(inner, grad_all, low)

    if natural:
        (
            dhidden_two, *spread, gate_terms, gate_x, up_terms, up_x, grad_down, _, down_x
        ) = feed_back(
            grad_all,
            gate_factor,
            up_factor,
            inner,
            all_two,
            gate_parts,
            up_parts,
            [
                (down_a, down_a_h, down_a_x, down_a_xh),
                (down_b, down_b_h, down_b_x, down_b_xh),
            ],
            5,
        )
        spread = scatter_row_async(spread, 0)
        gate_x, up_x = flip(gate_x, "x"), flip(up_x, "x")
        down_terms = add(grad_down, down_x).reshape(2, ff_part, width)
        down_terms, down_h = pick(down_terms, h), pick(down_terms, 1 - h)
    else:
        dinner = times_transposed(grad_all, down_own)
        dgate = (dinner * upward * sigma * (1.0 + gate * (1.0 - sigma))).astype(low)
        dupward = (dinner * gate * sigma).astype(low)
        grad_gate, grad_upward = outer_sum(all_two, dgate, low), outer_sum(all_two, dupward, low)
        dhidden_two = times_transposed(dgate, gate_own) + times_transposed(dupward, up_own)
        dhidden_two = scatter_row(5, dhidden_two.astype(low))[0]
        spread = scatter_row(6, dot(inner, down_own, low))[0]
        grad_down = sum_columns(grad_down[:ff_own].reshape(n_x, 2, ff_part, width), 0).astype(wide)
        gate_terms, up_terms = [
            sum_columns(a.reshape(n_x, 2, 2, -1, ff_pad), 1) for a in (grad_gate, grad_upward)
        ]

    dresid_part, dgain_two = norm_back(dhidden_two, resid, scale_two, gain_two)
    dresid = grad_home.astype(wide) + dresid_part
    branch = dresid.astype(low)
    if natural:
        by_h = (2, 2, -1, ff_pad)
        branch_all, down_h = gather_row(branch, 7, kinds=("h",), more=(down_h,))
        branch_all, gate_x, spread = together(branch_all, gate_x, spread)
        grad_down = down_terms.astype(wide) + down_h.astype(wide)
        gate_terms, gate_h = halves(add(gate_terms, gate_x).reshape(by_h), "h", 1)
        spread = scatter_row_async(spread, 1)
    else:
        branch_all = gather_row(branch, 7)
    grad_out = outer_sum(mixed, branch_all, low)
    if natural:
        out_terms, out_x = halves(grad_out.reshape(2, 2, head_dim // 2, width), "x", 0)
        dquery, dlow, dkv = attend_whole_back(
            ends, query, branch_all, mixed, packed, logs, cosine, sine, out_own, up_query, heads, scale
        )
    else:
        dmixed = times_transposed(branch_all, out_own, low)
        dquery, dkv = attend_back(
            ends, query, dmixed, mixed, packed, logs, cosine, sine, heads, scale
        )
        dlow = times_transposed(dquery, up_query, low)
    head_terms = outer_sum(all_latent, dquery, low).reshape(n_x, 2, 2, -1, heads * head_dim)
    if natural:
        head_terms, head_x = halves(head_terms, "x", 0)
        spread = scatter_row_async(spread, 2)
        dlow, gate_h, up_x, out_x, spread = together(dlow, gate_h, up_x, out_x, spread)
        out_terms = add(out_terms, out_x)
        kept, out_y = pick(out_terms, y), flip(pick(out_terms, 1 - y), "y")
        final = (resid + scatter_row_async(spread, 3)).astype(low)
        up_terms = add(up_terms, up_x).reshape(2, 2, -1, ff_pad)
        up_terms, up_h = pick(up_terms, h, 1), pick(up_terms, 1 - h, 1)
        dlow, dkv, up_h = scatter_row(8, dlow, dkv, kinds=("h",), more=(up_h,))
        dlow, out_y, head_x = together(dlow, out_y, head_x)
        by_h = jnp.stack([jnp.where(y == 0, kept, out_y), jnp.where(y == 0, out_y, kept)])
        gate_terms = add(gate_terms, gate_h).reshape(n_group, shard, ff_pad)
        up_terms = add(up_terms, up_h).reshape(n_group, shard, ff_pad)
        head_terms, head_h = halves(add(head_terms, head_x), "h", 1)
        dlow, head_h = together(dlow, head_h)
        head_terms = add(head_terms, head_h).reshape(n_group, rows_up, heads * head_dim)
        summed, grad_tokens, output, grad_gate, grad_upward, grad_uquery, grad_out = shut(
            dlow, dkv, latent, gain_latent[None], own_cos, own_sin, hidden,
            in_full.reshape(n_dev, shard, -1), home, gain_one[None], dresid, dgain_two[None],
            gate_terms, up_terms, head_terms, final, pick(by_h, h), pick(by_h, 1 - h), ff_part,
            order, 9,
        )
    else:
        dlow, dkv = scatter_row(8, dlow, dkv)
        whole = jnp.zeros((n_group * heads * head_dim, width), wide)
        whole = lax.dynamic_update_slice_in_dim(
            whole, grad_out.astype(wide), me * heads * head_dim, 0
        )
        grad_out = lax.psum_scatter(whole, every, scatter_dimension=0, tiled=True)
        final = (resid + spread).astype(low)
        dkeys = rotate_back(dkv[:, :head_dim], own_cos, own_sin).astype(low)
        dvalues = dkv[:, head_dim:].astype(low)
        dlatent, dgain_latent = norm_back(dlow, latent, scale_latent, gain_latent)
        nothing = jnp.zeros((count, 128), low)
        dmapped = jnp.concatenate([dlatent.astype(low), dkeys, dvalues, nothing], axis=1)
        dhidden = times_transposed(dmapped, in_full)
        dinput_part, dgain_one = norm_back(dhidden, inputs, scale_one, gain_one)
        grad_tokens = (dresid + dinput_part).astype(low)
        grad_in = outer_sum(hidden, dmapped[:, :mapped_width], low).reshape(n_dev, shard, -1)
        gain_terms = jnp.zeros((n_dev, shard, 128), low)
        gain_terms = gain_terms.at[:, 0, :shard].set(dgain_one.reshape(n_dev, -1).astype(low))
        gain_terms = gain_terms.at[:, 1, :shard].set(dgain_two.reshape(n_dev, -1).astype(low))
        gain_terms = gain_terms.at[:, 2, : query_gain.shape[0]].set(
            dgain_latent.reshape(n_dev, -1).astype(low)
        )
        terms = jnp.concatenate([grad_in, gain_terms], axis=2)
        summed = lax.psum_scatter(terms.astype(wide), every, scatter_dimension=0, tiled=False)
        grad_tokens, output = swap_home(grad_tokens), swap_home(final)
        head_terms = all_to_all_row(
            sum_columns(head_terms, 1).reshape(n_group, rows_up, heads * head_dim)
        )
        gate_terms, up_terms = [
            all_to_all_row(a.reshape(n_group, shard, ff_pad)) for a in (gate_terms, up_terms)
        ]
        grad_gate, grad_upward = join_columns(gate_terms, up_terms, ff_part, order)
        grad_uquery = head_terms.transpose(1, 0, 2).reshape(rows_up, -1).astype(wide)
    return (
        output,
        grad_tokens.astype(wide),
        summed[0, mapped_width : mapped_width + shard],
        summed[:, :latent_width],
        summed[2, mapped_width : mapped_width + query_gain.shape[0]],
        grad_uquery,
        summed[:, latent_width : latent_width + head_dim],
        summed[:, latent_width + head_dim : mapped_width],
        grad_out,
        summed[1, mapped_width : mapped_width + shard],
        grad_gate,
        grad_upward,
        grad_down,
    )


def solution(mesh):
    n_dp, n_seq = mesh.shape["dp"], mesh.shape["seq"]
    fine = Mesh(mesh.devices.reshape(n_dp // 2, 2, 2, n_seq // 4, 2), every)
    rows, flat = P(every, None), P(every)
    placed = (rows, P(("x", "c"), None), rows, flat, rows, flat) + (rows,) * 4 + (flat,) + (rows,) * 3
    return jax.shard_map(
        on_device,
        mesh=fine,
        in_specs=placed,
        out_specs=(rows, rows, flat, rows, flat) + (rows,) * 4 + (flat,) + (rows,) * 3,
        check_vma=False,
    )
```

```python
import functools
import math

import jax
import jax.numpy as jnp
from jax import lax
from jax.experimental import pallas as pl
from jax.experimental.pallas import tpu as pltpu
from jax.sharding import Mesh, PartitionSpec as P

norm_eps = 1e-05
masked_value = -1e30
every = ("x", "c", "h", "l", "y")
group = ("c", "l", "y")
low = jnp.bfloat16
wide = jnp.float32


def rms_scale(values):
    return lax.rsqrt(jnp.mean(values * values, axis=-1, keepdims=True) + norm_eps)


def rotate(values, cosine, sine):
    half = values.shape[-1] // 2
    a, b = values[..., :half], values[..., half:]
    return jnp.concatenate([a * cosine - b * sine, b * cosine + a * sine], axis=-1)


def rotate_back(values, cosine, sine):
    half = values.shape[-1] // 2
    a, b = values[..., :half], values[..., half:]
    return jnp.concatenate([a * cosine + b * sine, b * cosine - a * sine], axis=-1)


def norm_back(incoming, source, scale, gain):
    weighted = incoming * gain
    source_grad = scale * weighted - source * (scale * scale * scale) * jnp.mean(
        weighted * source, axis=-1, keepdims=True
    )
    return source_grad, jnp.sum(incoming * source * scale, axis=0)


def dot(left, right, out=wide):
    return jnp.dot(left, right, preferred_element_type=wide).astype(out)


def outer_sum(left, right, out=wide):
    return lax.dot_general(
        left, right, (((0,), (0,)), ((), ())), preferred_element_type=wide
    ).astype(out)


def times_transposed(left, right, out=wide):
    return lax.dot_general(
        left, right, (((1,), (1,)), ((), ())), preferred_element_type=wide
    ).astype(out)


def pick(array, index, axis=0):
    return lax.dynamic_index_in_dim(array, index, axis, keepdims=False)


def after(value, *done):
    return lax.optimization_barrier((value,) + done)[0]


def together(*values):
    return lax.optimization_barrier(values)


def flip(value, axis):
    return lax.ppermute(value, axis, [(0, 1), (1, 0)])


def flip_cross(value):
    return lax.ppermute(value, ("c", "h"), [(1, 2), (2, 1)])


def choose_home(value, moved):
    return jnp.where(lax.axis_index("c") == lax.axis_index("h"), value, moved)


def swap_home(value):
    return choose_home(value, flip_cross(value))


def group_place():
    return (
        lax.axis_index("c") * lax.axis_size("l") + lax.axis_index("l")
    ) * 2 + lax.axis_index("y")


def all_to_all_row(blocks):
    return lax.all_to_all(blocks, group, 0, 0, tiled=True)


def send(value, offsets):
    return lax.ppermute(value, group, [(i, i ^ offsets[i // 4]) for i in range(8)])


def scatter_row_async(state, stage):
    core = lax.axis_index("c")
    me = lax.axis_index("l") * 2 + lax.axis_index("y")
    first, second = 1 + core, 2 - core
    if stage == 0:
        return state[0], flip(state[1], "c")
    own, moved = state[:2]

    def block(index):
        return pick(own, index).astype(wide) + pick(moved, index).astype(wide)

    if stage == 1:
        far = send(block(me ^ 3).astype(low), (2, 1))
        return own, moved, far, send(block(me ^ second).astype(low), (2, 1))
    far, side = state[2:4]
    if stage == 2:
        return state + (send((block(me ^ first) + far.astype(wide)).astype(low), (1, 2)),)
    return block(me) + side.astype(wide) + state[4].astype(wide)


def sum_columns(terms, h_dim):
    for axis, dim in (("x", 0), ("h", h_dim)):
        terms = jnp.moveaxis(terms, dim, 0).astype(wide)
        terms = lax.psum_scatter(terms, axis, scatter_dimension=0, tiled=False).astype(low)
    return terms


def halves(terms, axis, dim):
    me = lax.axis_index(axis)
    return pick(terms, me, dim), flip(pick(terms, 1 - me, dim), axis)


def add(own, came):
    return (own.astype(wide) + came.astype(wide)).astype(low)


def other(value, flag=1):
    return value + flag * (1 - 2 * value)


def greet(peers):
    barrier = pltpu.get_barrier_semaphore()
    for peer in peers:
        pl.semaphore_signal(barrier, inc=1, device_id=peer, device_id_type=pl.DeviceIdType.MESH)
    pl.semaphore_wait(barrier, len(peers))


def remote(source, target, send_sem, recv_sem, peer):
    return pltpu.make_async_remote_copy(
        src_ref=source,
        dst_ref=target,
        send_sem=send_sem,
        recv_sem=recv_sem,
        device_id=peer,
        device_id_type=pl.DeviceIdType.MESH,
    )


def in_hbm():
    return pl.BlockSpec(memory_space=pl.ANY)


def open_kernel(n_sets, n_swaps, small_ref, out_ref, *refs):
    sets, refs = refs[:n_sets], refs[n_sets:]
    swaps, refs = refs[:n_swaps], refs[n_swaps:]
    (full_ref, heads_ref), refs = refs[:2], refs[2:]
    set_outs, refs = refs[:n_sets], refs[n_sets:]
    swap_outs, refs = refs[:n_swaps], refs[n_swaps:]
    (small_buf, out_buf), refs = refs[:2], refs[2:]
    set_bufs, refs = refs[:n_sets], refs[n_sets:]
    swap_bufs, refs = refs[:n_swaps], refs[n_swaps:]
    sends, recvs, swap_sends, swap_recvs, set_sends, set_recvs, out_sems, head_sems, loads_sem, stores_sem = refs
    x, c, h, l, y = [lax.axis_index(a) for a in every]
    hops = {
        1: {"h": other(h)},
        2: {"l": other(l)},
        4: {"y": other(y)},
        8: {"x": other(x)},
        16: {"c": other(c)},
    }
    cross = {"c": other(c), "h": other(h)}
    me = (c * 2 + l) * 2 + y

    def group_peer(k):
        return {"c": other(c, k // 4), "l": other(l, k // 2 % 2), "y": other(y, k % 2)}

    def group_index(k):
        peer = group_peer(k)
        return (peer["c"] * 2 + peer["l"]) * 2 + peer["y"]

    def index(code):
        at_x, at_l = other(x, code // 8 % 2), other(l, code // 2 % 2)
        return (((at_x * 2 + c) * 2 + other(h, code % 2)) * 2 + at_l) * 2 + other(y, code // 4 % 2)

    beside, corner = {"y": other(y)}, {"h": other(h), "y": h}
    greet(
        [hops[1], hops[8], cross, {"h": other(h), "y": other(y)}]
        + [group_peer(k) for k in range(1, 8)]
    )
    copies = []
    half = heads_ref.at[y]
    to_beside = remote(out_ref, half, out_sems.at[0], out_sems.at[1], beside)
    differ = y + h - 2 * y * h
    to_corner = remote(out_ref, half, out_sems.at[2], out_sems.at[3 + differ], corner)

    def push(code):
        block = full_ref.at[index(code)]
        source = small_ref if code == 0 else block
        for hop in (1, 2, 4, 8, 16):
            if code < hop:
                name = code + hop
                copy = remote(source, block, sends.at[name], recvs.at[name], hops[hop])
                copy.start()
                copies.append(copy)

    def set_slot(i):
        return set_outs[0].at[x, c, h, l * 2 + y] if i == 0 else set_outs[i].at[me]

    set_copies = []

    def set_push(i):
        for k in range(1, 8):
            copy = remote(
                sets[i].at[group_index(k)], set_slot(i), set_sends.at[i, k], set_recvs.at[i, k],
                group_peer(k),
            )
            copy.start()
            set_copies.append(copy)

    push(0)
    set_push(0)
    moving = [
        remote(source, target, swap_sends.at[i], swap_recvs.at[i], cross)
        for i, (source, target) in enumerate(zip(swaps, swap_outs))
    ]

    def push_moves():
        @pl.when(c != h)
        def _():
            for copy in moving:
                copy.start()

        @pl.when(y != h)
        def _():
            to_beside.start()

        to_corner.start()

    loads, stores = [], []
    locals_in = [small_ref, out_ref] + [ref.at[me] for ref in sets] + list(swaps)
    locals_buf = [small_buf, out_buf] + list(set_bufs) + list(swap_bufs)
    locals_out = [full_ref.at[index(0)], half] + [set_slot(i) for i in range(n_sets)]
    for i, (source, buf) in enumerate(zip(locals_in, locals_buf)):
        loads.append(pltpu.make_async_copy(source, buf, loads_sem.at[i]))
        loads[-1].start()
    for load in loads:
        load.wait()
    for i, (buf, target) in enumerate(zip(locals_buf, locals_out)):
        stores.append(pltpu.make_async_copy(buf, target, stores_sem.at[i]))
    keep_out = stores.pop(1)
    for store in stores:
        store.start()

    @pl.when(y == h)
    def _():
        keep_out.start()

    keeps = [
        pltpu.make_async_copy(buf, target, stores_sem.at[2 + n_sets + i])
        for i, (buf, target) in enumerate(zip(swap_bufs, swap_outs))
    ]

    @pl.when(c == h)
    def _():
        for keep in keeps:
            keep.start()

    def arrived(name):
        remote(small_ref, small_ref, sends.at[name], recvs.at[name], hops[16]).wait_recv()

    def head_copy(at_h, slot, peer):
        part = set_outs[0].at[x, :, at_h]
        copy = remote(part, part, head_sems.at[slot], head_sems.at[3 + slot], peer)
        copy.start()
        return copy

    head_copies = []
    for n, code in enumerate((2, 4, 1, 6, 3, 5, 7, 8, 9, 10, 11, 12, 13, 14, 15)):
        arrived(code)
        push(code)
        if n == 2:
            for copy in set_copies:
                copy.wait()
            for store in stores:
                store.wait()
            done = len(set_copies)
            for i in range(1, n_sets):
                set_push(i)
            head_copies.append(head_copy(h, 0, hops[1]))
            head_copies.append(head_copy(h, 1, hops[8]))
            push_moves()
        if n == 9:
            head_copies[0].wait_recv()
            head_copies.append(head_copy(other(h), 2, hops[8]))
    for code in range(16):
        arrived(16 + code)
    for copy in copies:
        copy.wait_send()
    for copy in set_copies[done:]:
        copy.wait()
    head_copies[0].wait_send()
    for copy in head_copies[1:]:
        copy.wait()
    to_corner.wait_send()

    @pl.when(y != h)
    def _():
        to_beside.wait_send()
        remote(out_ref, half, out_sems.at[2], out_sems.at[3], corner).wait_recv()
        remote(out_ref, half, out_sems.at[2], out_sems.at[4], corner).wait_recv()

    @pl.when(y == h)
    def _():
        keep_out.wait()
        to_beside.wait_recv()

    @pl.when(c != h)
    def _():
        for copy in moving:
            copy.wait()

    @pl.when(c == h)
    def _():
        for keep in keeps:
            keep.wait()


def open_exchange(small, out_rows, sets, swaps):
    n_sets, n_swaps = len(sets), len(swaps)
    args = [small, out_rows] + sets + swaps
    out_shape = [
        jax.ShapeDtypeStruct((32,) + small.shape, low),
        jax.ShapeDtypeStruct((2,) + out_rows.shape, low),
    ]
    out_shape += [jax.ShapeDtypeStruct((2, 2, 2, 4) + sets[0].shape[1:], low)]
    out_shape += [jax.ShapeDtypeStruct(a.shape, a.dtype) for a in sets[1:] + swaps]
    sem = pltpu.SemaphoreType.DMA
    out = pl.pallas_call(
        functools.partial(open_kernel, n_sets, n_swaps),
        in_specs=[in_hbm()] * len(args),
        out_specs=[in_hbm()] * len(args),
        out_shape=out_shape,
        scratch_shapes=[pltpu.VMEM(small.shape, low), pltpu.VMEM(out_rows.shape, low)]
        + [pltpu.VMEM(a.shape[1:], a.dtype) for a in sets]
        + [pltpu.VMEM(a.shape, a.dtype) for a in swaps]
        + [sem((32,)), sem((32,)), sem((n_swaps,)), sem((n_swaps,))]
        + [sem((n_sets, 8)), sem((n_sets, 8)), sem((5,)), sem((6,))]
        + [sem((len(args),)), sem((len(args),))],
        compiler_params=pltpu.CompilerParams(
            collective_id=1, has_side_effects=True, vmem_limit_bytes=16 * 1024 * 1024
        ),
        cost_estimate=pl.CostEstimate(flops=0, bytes_accessed=150 * 1024 * 1024, transcendentals=0),
        name="open_exchange",
    )(*args)
    return out[0], out[1], out[2 : 2 + n_sets], out[2 + n_sets :]


def row_peers(even):
    c, l, y = [lax.axis_index(a) for a in group]
    if even == "l":
        near = {"l": l, "y": other(y)}
        side = {"l": other(l), "y": y}
    elif even:
        near = {"l": other(l, c), "y": other(y, 1 - c)}
        side = {"l": other(l, 1 - c), "y": other(y, c)}
    else:
        near = {"l": other(l), "y": y}
        side = {"l": l, "y": other(y)}
    return c, l, y, near, side, {"c": other(c)}


def turn(values, cosine, sine):
    half = values.shape[1] // 2
    a, b = values[:, :half], values[:, half:]
    return a * cosine - b * sine, b * cosine + a * sine


def angles(ends_ref, rates, begin, count):
    places = begin + lax.broadcasted_iota(jnp.int32, (count, 1), 0)
    start = jnp.zeros_like(places)
    for j in range(ends_ref.shape[0]):
        end = ends_ref[j]
        start = jnp.where(places >= end, end, start)
    phases = (places - start).astype(wide) * rates
    return jnp.cos(phases), jnp.sin(phases)


def front_kernel(kinds, ends_ref, home_ref, full_ref, gain_ref, low_gain_ref, rates_ref, *refs):
    n = len(kinds)
    more, refs = refs[:n], refs[n:]
    out_ref, hidden_ref, latent_ref, cos_ref, sin_ref, refs = *refs[:5], refs[5:]
    more_out, refs = refs[:n], refs[n:]
    full, own, sends, recvs, load_sem, store_sem, more_sems = refs
    beside = Beside(kinds, more, more_out, more_sems)
    flow = RowGather(False, sends.shape[1], own, out_ref, sends, recvs)
    load = pltpu.make_async_copy(full_ref, full, load_sem)
    load.start()
    near, side, twin = flow.peers
    greet([near, side, twin, *beside.peers])
    count = home_ref.shape[0]
    low_width, head_dim = latent_ref.shape[1], 2 * cos_ref.shape[1]
    half = head_dim // 2
    values = home_ref[...].astype(wide)
    hidden = (values * rms_scale(values) * gain_ref[...]).astype(low)
    hidden_ref[...] = hidden
    cosine, sine = angles(ends_ref, rates_ref[...], flow.me * count, count)
    load.wait()
    mapped = jnp.dot(hidden, full[...], preferred_element_type=wide)
    latent = mapped[:, :low_width]
    latent_ref[...] = latent
    own[:, :low_width] = (latent * rms_scale(latent) * low_gain_ref[...]).astype(low)
    a, b = turn(mapped[:, low_width : low_width + head_dim], cosine, sine)
    own[:, low_width : low_width + half] = a.astype(low)
    own[:, low_width + half : low_width + head_dim] = b.astype(low)
    end = low_width + 2 * head_dim
    own[:, low_width + head_dim :] = mapped[:, low_width + head_dim : end].astype(low)
    flow.begin(None)
    beside.start()
    store = pltpu.make_async_copy(own, out_ref.at[flow.me], store_sem)
    store.start()

    def tables(begin, rows):
        cos_ref[begin : begin + rows, :], sin_ref[begin : begin + rows, :] = angles(
            ends_ref, rates_ref[...], begin, rows
        )

    quarter = cos_ref.shape[0] // 4
    tables(0, quarter)
    tables(quarter, quarter)
    flow.take_near()
    tables(2 * quarter, quarter)
    flow.take_side()
    tables(3 * quarter, quarter)
    flow.take_far()
    for slot in (3, 4, 5, 6):
        flow.take(slot)
    flow.end()
    store.wait()
    beside.wait()


def front(ends, home, in_full, gain_one, gain_latent, rates, row_len, number, kinds, more):
    count, width = home.shape
    low_width = gain_latent.shape[1]
    half = rates.shape[1]
    packed = (count, low_width + 4 * half)
    vmem, sem = pl.BlockSpec(memory_space=pltpu.VMEM), pltpu.SemaphoreType.DMA
    out = pl.pallas_call(
        functools.partial(front_kernel, kinds),
        in_specs=[pl.BlockSpec(memory_space=pltpu.SMEM), vmem, in_hbm(), vmem, vmem, vmem]
        + [in_hbm()] * len(more),
        out_specs=[in_hbm()] + [vmem] * 4 + [in_hbm()] * len(more),
        out_shape=[
            jax.ShapeDtypeStruct((8,) + packed, low),
            jax.ShapeDtypeStruct((count, width), low),
            jax.ShapeDtypeStruct((count, low_width), wide),
            jax.ShapeDtypeStruct((row_len, half), wide),
            jax.ShapeDtypeStruct((row_len, half), wide),
        ]
        + [jax.ShapeDtypeStruct(a.shape, low) for a in more],
        scratch_shapes=[
            pltpu.VMEM(in_full.shape, low),
            pltpu.VMEM(packed, low),
            sem((7, 4)),
            sem((7, 4)),
            sem,
            sem,
            sem((2, len(more))),
        ],
        compiler_params=pltpu.CompilerParams(
            collective_id=number, has_side_effects=True, vmem_limit_bytes=32 * 1024 * 1024
        ),
        cost_estimate=pl.CostEstimate(flops=0, bytes_accessed=100 * 1024 * 1024, transcendentals=0),
        name="front",
    )(ends, home, in_full, gain_one, gain_latent, rates, *more)
    return (out[0].reshape(-1, packed[1]), *out[1:])


def gather_kernel(even, chunks, kinds, own_ref, *refs):
    n = len(kinds)
    more, out_ref, more_out = refs[:n], refs[n], refs[n + 1 : 2 * n + 1]
    buf, sends, recvs, local_sems = refs[2 * n + 1 : 2 * n + 5]
    beside = Beside(kinds, more, more_out, refs[-1])
    flow = RowGather(even, chunks, own_ref, out_ref, sends, recvs)
    flow.begin(beside.peers)
    beside.start()
    load = pltpu.make_async_copy(own_ref, buf, local_sems.at[0])
    load.start()
    load.wait()
    store = pltpu.make_async_copy(buf, out_ref.at[flow.me], local_sems.at[1])
    store.start()
    flow.take_near()
    flow.take_side()
    flow.take_far()
    for slot in (3, 4, 5, 6):
        flow.take(slot)
    flow.end()
    store.wait()
    beside.wait()


class Beside:
    def __init__(self, kinds, sources, targets, sems):
        x, c, h = [lax.axis_index(a) for a in ("x", "c", "h")]
        ways = {"x": {"x": other(x)}, "h": {"h": other(h)}, "cross": {"c": other(c), "h": other(h)}}
        self.peers = [ways[k] for k in sorted(set(kinds))]
        self.moves = c != h
        self.copies = [
            (kind, remote(source, target, sems.at[0, i], sems.at[1, i], ways[kind]))
            for i, (kind, source, target) in enumerate(zip(kinds, sources, targets))
        ]

    def start(self, span=slice(None)):
        for kind, copy in self.copies[span]:
            if kind == "cross":
                pl.when(self.moves)(copy.start)
            else:
                copy.start()

    def wait(self, span=slice(None)):
        for kind, copy in self.copies[span]:
            if kind == "cross":
                pl.when(self.moves)(copy.wait)
            else:
                copy.wait()


class RowGather:
    def __init__(self, even, chunks, own_ref, out_ref, sends, recvs, in_slots=False):
        c, l, y, near, side, twin = row_peers(even)
        self.peers = near, side, twin
        self.chunks, self.rows = chunks, own_ref.shape[0] // chunks
        self.own_ref, self.out_ref, self.sends, self.recvs = own_ref, out_ref, sends, recvs
        at = l * 2 + y
        near_at, side_at = near["l"] * 2 + near["y"], side["l"] * 2 + side["y"]
        far_at = other(l) * 2 + other(y)
        self.me = c * 4 + at
        self.places = [c * 4 + p for p in (near_at, side_at, far_at)]
        swapped = even is True
        twins = (at, side_at, near_at, far_at) if swapped else (at, near_at, side_at, far_at)
        self.places += [other(c) * 4 + p for p in twins]
        self.copies = []
        self.lands = (2, 3, 6, 1, 4, 5, 7) if in_slots else None

    def land(self, slot):
        return self.lands[slot] if self.lands else self.places[slot]

    def start(self, held, k, slot, peer):
        span = pl.ds(k * self.rows, self.rows)
        source = self.own_ref.at[span] if held is None else self.out_ref.at[self.land(held), span]
        if self.lands:
            target = self.out_ref.at[self.lands[slot], span]
        else:
            target = self.out_ref.at[self.me if held is None else self.places[held], span]
        copy = remote(source, target, self.sends.at[slot, k], self.recvs.at[slot, k], peer)
        copy.start()
        self.copies.append(copy)

    def begin(self, more_peers=()):
        near, side, twin = self.peers
        if more_peers is not None:
            greet([near, side, twin, *more_peers])
        for k in range(self.chunks):
            self.start(None, k, 0, near)
            self.start(None, k, 1, side)
            self.start(None, k, 3, twin)

    def arrived(self, slot, k):
        span = self.own_ref.at[pl.ds(k * self.rows, self.rows)]
        target = self.out_ref.at[self.land(slot), pl.ds(k * self.rows, self.rows)]
        remote(
            span, target, self.sends.at[slot, k], self.recvs.at[slot, k], self.peers[2]
        ).wait_recv()

    def take(self, slot):
        for k in range(self.chunks):
            self.arrived(slot, k)

    def take_near(self):
        near, side, twin = self.peers
        for k in range(self.chunks):
            self.arrived(0, k)
            self.start(0, k, 2, side)
            self.start(0, k, 4, twin)

    def take_side(self):
        for k in range(self.chunks):
            self.arrived(1, k)
            self.start(1, k, 5, self.peers[2])

    def take_far(self):
        for k in range(self.chunks):
            self.arrived(2, k)
            self.start(2, k, 6, self.peers[2])

    def end(self):
        for copy in self.copies:
            copy.wait_send()


def gather_row(value, number, even=False, kinds=(), more=()):
    if lax.axis_size("l") != 2:
        return lax.all_gather(value, group, axis=0, tiled=True)
    chunks = 4 if value.shape[0] % 64 == 0 else 1
    args = [value, *more]
    out_shape = [jax.ShapeDtypeStruct((8,) + value.shape, low)]
    out_shape += [jax.ShapeDtypeStruct(a.shape, low) for a in more]
    out = pl.pallas_call(
        functools.partial(gather_kernel, even, chunks, kinds),
        in_specs=[in_hbm()] * len(args),
        out_specs=[in_hbm()] * len(args),
        out_shape=out_shape,
        scratch_shapes=[
            pltpu.VMEM(value.shape, low),
            pltpu.SemaphoreType.DMA((7, chunks)),
            pltpu.SemaphoreType.DMA((7, chunks)),
            pltpu.SemaphoreType.DMA((2,)),
            pltpu.SemaphoreType.DMA((2, max(1, len(more)))),
        ],
        compiler_params=pltpu.CompilerParams(
            collective_id=number, has_side_effects=True, vmem_limit_bytes=16 * 1024 * 1024
        ),
        cost_estimate=pl.CostEstimate(flops=0, bytes_accessed=80 * 1024 * 1024, transcendentals=0),
        name="gather_row",
    )(*args)
    rows = out[0].reshape(-1, value.shape[1])
    return (rows, *out[1:]) if kinds else rows


def load_columns(pieces, target, sem, first):
    x, h = lax.axis_index("x"), lax.axis_index("h")
    rows = pieces[0].shape[0]
    loads = []
    for i, piece in enumerate(pieces):
        at_x = x if i < 4 else other(x)
        at_h = h if i // 2 % 2 == 0 else other(h)
        at = pl.multiple_of(((at_x * 2 + i % 2) * 2 + at_h) * rows, rows)
        loads.append(
            pltpu.make_async_copy(piece, target.at[pl.ds(at, rows)], sem.at[first + i])
        )
    return loads


def load_rows(parts, target, sem):
    x, h = lax.axis_index("x"), lax.axis_index("h")
    rows, width = parts[0][0].shape
    loads = []
    for s, part in enumerate(parts):
        for i, (at_x, at_h) in enumerate(
            ((x, h), (x, other(h)), (other(x), h), (other(x), other(h)))
        ):
            at = pl.multiple_of((at_x * 2 + at_h) * rows, 16)
            loads.append(
                pltpu.make_async_copy(
                    part[i],
                    target.at[pl.ds(at, rows), pl.ds(s * width, width)],
                    sem.at[len(loads)],
                )
            )
            loads[-1].start()
    return loads


def wait_all(copies):
    for copy in copies:
        copy.wait()


def for_tiles(total, tile, body):
    def step(j, carry):
        body(pl.ds(pl.multiple_of(j * tile, tile), tile))
        return carry

    lax.fori_loop(0, total // tile, step, 0)


def feed_kernel(even, chunks, *refs):
    own_ref, gates, ups = refs[0], refs[1:9], refs[9:17]
    downs, grad_ref, refs = refs[17:21], refs[21], refs[22:]
    all_ref, inner_ref, a_ref, b_ref = refs[:4]
    downs_x, home_ref, grads_ref, refs = refs[4:8], refs[8], refs[9], refs[10:]
    xs, wg, wu, inner_s, a_s, b_s, grad_buf, sends, recvs, grad_sends, grad_recvs = refs[:11]
    weight_sems, store_sems, own_sem, more_sems, grad_sems = refs[11:]
    flow = RowGather(even, chunks, own_ref, xs, sends, recvs, in_slots=True)
    beside = Beside(
        ("cross", "x", "x", "x", "x"),
        (grad_ref, *downs),
        (home_ref, *downs_x),
        more_sems,
    )
    away = lax.axis_index("c") != lax.axis_index("h")
    grad_flow = RowGather("l", chunks, home_ref, grads_ref, grad_sends, grad_recvs)
    flow.begin(beside.peers)
    beside.start()
    grad_load = pltpu.make_async_copy(grad_ref, grad_buf, grad_sems.at[0])
    grad_load.start()
    own_load = pltpu.make_async_copy(own_ref, xs.at[0], own_sem)
    own_load.start()
    weights = load_columns(gates, wg, weight_sems, 0) + load_columns(ups, wu, weight_sems, 8)
    for load in weights:
        load.start()
    grad_load.wait()
    to_home = pltpu.make_async_copy(grad_buf, home_ref, grad_sems.at[1])

    @pl.when(jnp.logical_not(away))
    def _():
        to_home.start()
        to_home.wait()

    order = [flow.me] + [flow.places[s] for s in (3, 0, 1, 4, 5, 2, 6)]
    stores = []
    columns, width = wg.shape[1], wg.shape[0]

    def work(pair):
        both = pl.ds(2 * pair, 2)
        x = xs[both].reshape(-1, width)

        def tile(cols):
            gate = jnp.dot(x, wg[:, cols], preferred_element_type=wide)
            upward = jnp.dot(x, wu[:, cols], preferred_element_type=wide)
            sigma = jax.nn.sigmoid(gate)
            swish = gate * sigma
            shape = (2, -1, upward.shape[1])
            inner_s[both, :, cols] = (swish * upward).astype(low).reshape(shape)
            b_s[both, :, cols] = swish.astype(low).reshape(shape)
            factor = upward * sigma * (1.0 + gate * (1.0 - sigma))
            a_s[both, :, cols] = factor.astype(low).reshape(shape)

        tile(slice(None))
        for i in (2 * pair, 2 * pair + 1):
            place = order[i]
            for j, (buf, target) in enumerate(
                ((xs, all_ref), (inner_s, inner_ref), (a_s, a_ref), (b_s, b_ref))
            ):
                store = pltpu.make_async_copy(buf.at[i], target.at[place], store_sems.at[i, j])
                store.start()
                stores.append(store)

    own_load.wait()
    flow.take(3)
    wait_all(weights)
    work(0)
    flow.take_near()
    flow.take_side()
    beside.wait(slice(0, 1))
    grad_flow.begin(None)
    home_load = pltpu.make_async_copy(home_ref, grad_buf, grad_sems.at[2])
    home_load.start()
    work(1)
    home_load.wait()
    own_store = pltpu.make_async_copy(grad_buf, grads_ref.at[grad_flow.me], grad_sems.at[3])
    own_store.start()
    flow.take(4)
    flow.take(5)
    work(2)
    flow.take_far()
    grad_flow.take_near()
    grad_flow.take_side()
    flow.take(6)
    work(3)
    grad_flow.take_far()
    for slot in (3, 4, 5, 6):
        grad_flow.take(slot)
    flow.end()
    grad_flow.end()
    wait_all(stores + [own_store])
    beside.wait(slice(1, 5))


def feed_forward(own, gates, ups, downs, grad, number):
    count, width = own.shape
    columns = gates[0].shape[1]
    chunks = 4 if count % 64 == 0 else 1
    row, part = (8, count, width), (8, count, columns)
    sem = pltpu.SemaphoreType.DMA
    flops = 2 * 8 * count * width * columns * 2
    args = [own, *gates, *ups, *downs, grad]
    shapes = [row, part, part, part] + [a.shape for a in downs] + [grad.shape, row]
    return pl.pallas_call(
        functools.partial(feed_kernel, False, chunks),
        in_specs=[in_hbm()] * len(args),
        out_specs=[in_hbm()] * len(shapes),
        out_shape=[jax.ShapeDtypeStruct(s, low) for s in shapes],
        scratch_shapes=[
            pltpu.VMEM(row, low),
            pltpu.VMEM((width, columns), low),
            pltpu.VMEM((width, columns), low),
            pltpu.VMEM(part, low),
            pltpu.VMEM(part, low),
            pltpu.VMEM(part, low),
            pltpu.VMEM(grad.shape, low),
            sem((7, chunks)),
            sem((7, chunks)),
            sem((7, chunks)),
            sem((7, chunks)),
            sem((16,)),
            sem((8, 4)),
            sem,
            sem((2, 5)),
            sem((4,)),
        ],
        compiler_params=pltpu.CompilerParams(
            collective_id=number, has_side_effects=True, vmem_limit_bytes=56 * 1024 * 1024
        ),
        cost_estimate=pl.CostEstimate(
            flops=flops, bytes_accessed=100 * 1024 * 1024, transcendentals=0
        ),
        name="feed_forward",
    )(*args)


def feed_back_kernel(
    even, chunks, *refs,
):
    grad_ref, a_ref, b_ref, inner_ref, all_ref = refs[:5]
    gates, ups, downs, refs = refs[5:13], refs[13:21], refs[21:29], refs[29:]
    out_ref, terms_own, terms_twin, gate_own, gate_across, up_own, up_across = refs[:7]
    down_sum, down_across, down_came, refs = refs[7], refs[8], refs[9], refs[10:]
    down_own, down_stage, came_h, refs = refs[0], refs[1], refs[2], refs[3:]
    gx, wg, wu, wd, a_s, b_s, inner_s, terms_s, own_buf, twin_buf, twin_out, down_s = refs[:12]
    far_out, side_out, near_out, far_in, side_in, near_in = refs[12:18]
    sends, recvs, weight_sems, down_sems, block_sems, all_sems, terms_sems, more_sems = refs[18:]
    over_x, over_h = {"x": other(lax.axis_index("x"))}, {"h": other(lax.axis_index("h"))}
    at_h = lax.axis_index("h")
    halves_at = [pl.ds(0, grad_ref.shape[2] // 2), pl.ds(grad_ref.shape[2] // 2, grad_ref.shape[2] // 2)]
    steps_x = [
        remote(down_across.at[:, s], down_came.at[:, s], more_sems.at[0, i], more_sems.at[1, i], over_x)
        for i, s in enumerate(halves_at)
    ]
    steps_h = []

    def down_step(i):
        s = halves_at[i]
        steps_x[i].wait_recv()
        take = pltpu.make_async_copy(down_came.at[:, s], down_stage, more_sems.at[2, i])
        take.start()
        take.wait()
        total = down_own[:, s].astype(wide) + down_stage[...].astype(wide)
        down_own[:, s] = total.astype(low)
        part_rows = came_h.shape[0]
        theirs = down_own.at[pl.ds(pl.multiple_of(other(at_h) * part_rows, 16), part_rows), s]
        copy = remote(theirs, came_h.at[:, s], more_sems.at[0, 2 + i], more_sems.at[1, 2 + i], over_h)
        copy.start()
        steps_h.append(copy)

    c, l, y, near, side, twin = row_peers(even)
    rows = out_ref.shape[0] // chunks
    columns, width = wd.shape
    used = 4 * downs[0].shape[0]
    me = l * 2 + y
    near_at, side_at = near["l"] * 2 + near["y"], side["l"] * 2 + side["y"]
    far_at = other(l) * 2 + other(y)
    own_order = (far_at, side_at, near_at, me)
    twin_order = (far_at, near_at, side_at, me) if even else own_order
    pairs = []
    for p, q in zip(twin_order, own_order):
        pairs += [(other(c) * 4 + p, p, True), (c * 4 + q, q, False)]
    downs = load_rows((downs[:4], downs[4:]), wd, down_sems)
    blocks = []
    for i, (place, _, _) in enumerate(pairs):
        loads = [
            pltpu.make_async_copy(source.at[place], buf.at[i], block_sems.at[i, j])
            for j, (source, buf) in enumerate(
                ((grad_ref, gx), (a_ref, a_s), (b_ref, b_s), (inner_ref, inner_s))
            )
        ]
        for load in loads:
            load.start()
        blocks.append(loads)
    weights = load_columns(gates, wg, weight_sems, 0) + load_columns(ups, wu, weight_sems, 8)
    for load in weights:
        load.start()
    wd[used:, :] = jnp.zeros((columns - used, width), low)
    greet([near, side, twin, over_x, over_h])
    copies = []

    def start(source, target, slot, k, peer):
        copy = remote(source, target, sends.at[slot, k], recvs.at[slot, k], peer)
        copy.start()
        copies.append(copy)

    def arrived(slot, k):
        span = far_in.at[pl.ds(k * rows, rows)]
        remote(span, span, sends.at[slot, k], recvs.at[slot, k], twin).wait_recv()

    def block_arrived(slot):
        remote(
            own_buf.at[0], twin_buf.at[0], sends.at[slot, 0], recvs.at[slot, 0], twin
        ).wait_recv()

    def term(pair, twin_target, own_target):
        span = pl.ds(2 * pair, 2)
        grads = gx[span].reshape(-1, width)

        dinner = contract(grads, wd[...], ((1,), (1,))).reshape(2, -1, columns)
        a_s[span] = (dinner * a_s[span].astype(wide)).astype(low)
        b_s[span] = (dinner * b_s[span].astype(wide)).astype(low)
        if pair == 0:
            wait_all(weights)
        dgate = a_s[span].reshape(-1, columns)
        dup = b_s[span].reshape(-1, columns)

        def second(cols):
            part = contract(dgate, wg[cols, :], ((1,), (1,)))
            part = (part + contract(dup, wu[cols, :], ((1,), (1,)))).astype(low)
            half = part.shape[0] // 2
            twin_target[:, cols] = part[:half]
            own_target[:, cols] = part[half:]

        for_tiles(width, width // 2, second)

    def both(place, span):
        return own_buf[place, span, :].astype(wide) + twin_buf[place, span, :].astype(wide)

    spans = [(k, pl.ds(k * rows, rows)) for k in range(chunks)]
    for loads in blocks:
        wait_all(loads)
    inners = inner_s[...].reshape(-1, columns)
    x_at = lax.axis_index("x")
    down_rows = down_own.shape[0]

    def down_tile(j):
        span = slice(j * (width // 4), (j + 1) * (width // 4))
        part = contract(inners, gx[:, :, span].reshape(-1, width // 4), ((0,), (0,))).astype(low)
        down_s[...] = part
        at = pl.multiple_of(x_at * down_rows, 16)
        down_own[:, span] = down_s[pl.ds(at, down_rows), :]
        at = pl.multiple_of(other(x_at) * down_rows, 16)
        down_across[:, span] = down_s[pl.ds(at, down_rows), :]

    for j in range(4):
        down_tile(j)
        if j % 2:
            steps_x[j // 2].start()
    wait_all(downs)
    for i in range(4):
        twin_place, own_place = pairs[2 * i][1], pairs[2 * i + 1][1]
        term(i, twin_out.at[i], own_buf.at[own_place])
        start(twin_out.at[i], twin_buf.at[twin_place], 3 + i, 0, twin)
        if i >= 1:
            block_arrived(2 + i)
        if i == 1:
            for k, span in spans:
                far_out[span, :] = both(far_at, span).astype(low)
                start(far_out.at[span], far_in.at[span], 0, k, side)
        if i == 2:
            down_step(0)
            for k, span in spans:
                side_out[span, :] = both(side_at, span).astype(low)
                start(side_out.at[span], side_in.at[span], 1, k, side)
    block_arrived(6)
    all_loads = [
        pltpu.make_async_copy(all_ref.at[pairs[i][0]], gx.at[i], all_sems.at[i]) for i in range(8)
    ]
    for load in all_loads:
        load.start()
    stores = []

    def output_term(pair):
        span = pl.ds(2 * pair, 2)
        if pair:
            wait_all(stores[2 * pair - 2 :])
        inner = inner_s[span].reshape(-1, columns)

        def tile(cols):
            part = jnp.dot(inner, wd[:, cols], preferred_element_type=wide)
            terms_s[:, :, cols] = part.astype(low).reshape(2, -1, width // 2)

        for_tiles(width, width // 2, tile)
        for i in range(2):
            _, place, is_twin = pairs[2 * pair + i]
            store = pltpu.make_async_copy(
                terms_s.at[i],
                (terms_twin if is_twin else terms_own).at[place],
                terms_sems.at[2 * pair + i],
            )
            store.start()
            stores.append(store)

    for i in range(2):
        output_term(i)
    for k, span in spans:
        arrived(0, k)
        near_out[span, :] = (both(near_at, span) + far_in[span, :].astype(wide)).astype(low)
        start(near_out.at[span], near_in.at[span], 2, k, near)
    down_step(1)
    for i in range(2, 4):
        output_term(i)
    wait_all(all_loads)
    dgates = a_s[...].reshape(-1, columns)
    dups = b_s[...].reshape(-1, columns)

    half = width // 2
    for gate_ref, up_ref, at in ((gate_across, up_across, other(x_at)), (gate_own, up_own, x_at)):
        for j in range(2):
            cols = pl.ds(pl.multiple_of(at * half + j * (half // 2), 128), half // 2)
            rows_out = slice(j * (half // 2), (j + 1) * (half // 2))
            x = gx[:, :, cols].reshape(-1, half // 2)
            gate_ref[rows_out, :] = contract(x, dgates, ((0,), (0,))).astype(low)
            up_ref[rows_out, :] = contract(x, dups, ((0,), (0,))).astype(low)
    for k, span in spans:
        arrived(1, k)
        arrived(2, k)
        out_ref[span, :] = (
            both(me, span) + side_in[span, :].astype(wide) + near_in[span, :].astype(wide)
        )
    wait_all(stores[6:])
    for copy in steps_h:
        copy.wait()
    part_rows = came_h.shape[0]
    mine = down_own[pl.ds(pl.multiple_of(at_h * part_rows, 16), part_rows), :]
    down_sum[...] = mine.astype(wide) + came_h[...].astype(wide)
    for copy in copies + steps_x:
        copy.wait_send()


def feed_back(grad_all, a, b, inner, all_two, gate_pieces, up_pieces, down_parts, number):
    count, width = a.shape[1], all_two.shape[2]
    columns = a.shape[2]
    chunks = 4 if count % 64 == 0 else 1
    row, part = (8, count, width), (8, count, columns)
    sem = pltpu.SemaphoreType.DMA
    block = pltpu.VMEM((count, width), low)
    vmem = pl.BlockSpec(memory_space=pltpu.VMEM)
    flops = 2 * 8 * count * width * columns * 6
    args = [grad_all.reshape(row), a, b, inner, all_two, *gate_pieces, *up_pieces]
    args += [piece for parts in down_parts for piece in parts]
    own_rows = down_parts[0][0].shape[0]
    return pl.pallas_call(
        functools.partial(feed_back_kernel, True, chunks),
        in_specs=[in_hbm()] * len(args),
        out_specs=[vmem, in_hbm(), in_hbm()] + [vmem] * 6 + [in_hbm()],
        out_shape=[jax.ShapeDtypeStruct((count, width), wide)]
        + [jax.ShapeDtypeStruct((4, count, width), low)] * 2
        + [jax.ShapeDtypeStruct((width // 2, columns), low)] * 4
        + [jax.ShapeDtypeStruct((own_rows, width), wide)]
        + [jax.ShapeDtypeStruct((2 * own_rows, width), low)] * 2,
        scratch_shapes=[
            pltpu.VMEM((2 * own_rows, width), low),
            pltpu.VMEM((2 * own_rows, width // 2), low),
            pltpu.VMEM((own_rows, width), low),
            pltpu.VMEM(row, low),
            pltpu.VMEM((width, columns), low),
            pltpu.VMEM((width, columns), low),
            pltpu.VMEM((columns, width), low),
            pltpu.VMEM(part, low),
            pltpu.VMEM(part, low),
            pltpu.VMEM(part, low),
            pltpu.VMEM((2, count, width), low),
            pltpu.VMEM((4, count, width), low),
            pltpu.VMEM((4, count, width), low),
            pltpu.VMEM((4, count, width), low),
            pltpu.VMEM((columns, width // 4), low),
        ]
        + [block] * 6
        + [
            sem((7, chunks)),
            sem((7, chunks)),
            sem((16,)),
            sem((8,)),
            sem((8, 4)),
            sem((8,)),
            sem((8,)),
            sem((3, 4)),
        ],
        compiler_params=pltpu.CompilerParams(
            collective_id=number, has_side_effects=True, vmem_limit_bytes=60 * 1024 * 1024
        ),
        cost_estimate=pl.CostEstimate(
            flops=flops, bytes_accessed=100 * 1024 * 1024, transcendentals=0
        ),
        name="feed_back",
    )(*args)


def scatter_kernel(even, chunks, n, kinds, *refs):
    m = len(kinds)
    terms, more, refs = refs[:n], refs[n : n + m], refs[n + m :]
    outs, more_out, refs = refs[:n], refs[n : n + m], refs[n + m :]
    bufs, (sends, recvs, local_sems, more_sems) = refs[: 8 * n], refs[8 * n :]
    beside = Beside(kinds, more, more_out, more_sems)
    bufs = [bufs[8 * a : 8 * a + 8] for a in range(n)]
    c, l, y, near, side, twin = row_peers(even)
    rows = outs[0].shape[0] // chunks
    me = l * 2 + y
    near_at, side_at = near["l"] * 2 + near["y"], side["l"] * 2 + side["y"]
    far_at = other(l) * 2 + other(y)
    greet([near, side, twin] + beside.peers)
    beside.start()
    copies = []

    def start(source, target, a, slot, k, peer):
        copy = remote(source, target, sends.at[a, slot, k], recvs.at[a, slot, k], peer)
        copy.start()
        copies.append(copy)

    parts = [(a, k, pl.ds(k * rows, rows)) for k in range(chunks) for a in range(n)]
    twin_side, twin_near = (near_at, side_at) if even else (side_at, near_at)
    for slot, place in ((3, far_at), (4, twin_side), (5, twin_near), (6, me)):
        for a, k, span in parts:
            start(
                terms[a].at[other(c) * 4 + place, span], bufs[a][1].at[place, span], a, slot, k, twin
            )
    loads = []
    for slot, place in ((0, far_at), (1, side_at), (2, near_at), (3, me)):
        for a in range(n):
            load = pltpu.make_async_copy(
                terms[a].at[c * 4 + place], bufs[a][0].at[place], local_sems.at[a, slot]
            )
            load.start()
            loads.append(load)

    def arrived(a, slot, k):
        span = bufs[a][5].at[pl.ds(k * rows, rows)]
        remote(span, span, sends.at[a, slot, k], recvs.at[a, slot, k], twin).wait_recv()

    def both(a, place, span):
        own, came = bufs[a][0], bufs[a][1]
        return own[place, span, :].astype(wide) + came[place, span, :].astype(wide)

    for load in loads[: 2 * n]:
        load.wait()
    for a, k, span in parts:
        far_out, far_in = bufs[a][2], bufs[a][5]
        arrived(a, 3, k)
        far_out[span, :] = both(a, far_at, span).astype(low)
        start(far_out.at[span], far_in.at[span], a, 0, k, side)
    for a, k, span in parts:
        side_out, side_in = bufs[a][3], bufs[a][6]
        arrived(a, 4, k)
        side_out[span, :] = both(a, side_at, span).astype(low)
        start(side_out.at[span], side_in.at[span], a, 1, k, side)
    for load in loads[2 * n :]:
        load.wait()
    for a, k, span in parts:
        near_out, far_in, near_in = bufs[a][4], bufs[a][5], bufs[a][7]
        arrived(a, 5, k)
        arrived(a, 0, k)
        near_out[span, :] = (both(a, near_at, span) + far_in[span, :].astype(wide)).astype(low)
        start(near_out.at[span], near_in.at[span], a, 2, k, near)
    for a, k, span in parts:
        arrived(a, 6, k)
        arrived(a, 1, k)
        outs[a][span, :] = both(a, me, span) + bufs[a][6][span, :].astype(wide)
    for a, k, span in parts:
        arrived(a, 2, k)
        outs[a][span, :] += bufs[a][7][span, :].astype(wide)
    for copy in copies:
        copy.wait_send()
    beside.wait()


def scatter_row(number, *terms, even=False, kinds=(), more=()):
    if lax.axis_size("l") != 2:
        return [
            lax.psum_scatter(t.astype(wide), group, scatter_dimension=0, tiled=True) for t in terms
        ]
    terms = [t.reshape(8, -1, t.shape[1]) for t in terms]
    n, count = len(terms), terms[0].shape[1]
    chunks = 4 if count % 64 == 0 else 1
    scratch = []
    for t in terms:
        scratch += [pltpu.VMEM((4, count, t.shape[2]), low)] * 2
        scratch += [pltpu.VMEM((count, t.shape[2]), low)] * 6
    return pl.pallas_call(
        functools.partial(scatter_kernel, even, chunks, n, kinds),
        in_specs=[in_hbm()] * (n + len(more)),
        out_specs=[pl.BlockSpec(memory_space=pltpu.VMEM)] * n + [in_hbm()] * len(more),
        out_shape=[jax.ShapeDtypeStruct((count, t.shape[2]), wide) for t in terms]
        + [jax.ShapeDtypeStruct(a.shape, low) for a in more],
        scratch_shapes=scratch
        + [
            pltpu.SemaphoreType.DMA((n, 7, chunks)),
            pltpu.SemaphoreType.DMA((n, 7, chunks)),
            pltpu.SemaphoreType.DMA((n, 4)),
            pltpu.SemaphoreType.DMA((2, max(1, len(more)))),
        ],
        compiler_params=pltpu.CompilerParams(
            collective_id=number, has_side_effects=True, vmem_limit_bytes=24 * 1024 * 1024
        ),
        cost_estimate=pl.CostEstimate(flops=0, bytes_accessed=80 * 1024 * 1024, transcendentals=0),
        name="scatter_row",
    )(*terms, *more)


class SumColumns:
    def __init__(self, mine_ref, across_ref, land_ref, out_ref, mine, stage, came_h, sems, local_sems):
        self.h = lax.axis_index("h")
        over_x, self.over_h = {"x": other(lax.axis_index("x"))}, {"h": other(self.h)}
        self.land_ref, self.out_ref = land_ref, out_ref
        self.mine, self.stage, self.came_h = mine, stage, came_h
        self.sems, self.local_sems = sems, local_sems
        rows = mine.shape[2] // 2
        self.parts = [(c, pl.ds(i * rows, rows)) for c in range(2) for i in range(2)]
        self.steps_x = [
            remote(
                across_ref.at[c, :, s], land_ref.at[c, :, s], sems.at[0, i], sems.at[1, i], over_x
            )
            for i, (c, s) in enumerate(self.parts)
        ]
        self.steps_h = []
        self.load = pltpu.make_async_copy(mine_ref, mine, local_sems.at[0])

    def start(self):
        for copy in self.steps_x:
            copy.start()
        self.load.start()

    def step(self, i):
        c, s = self.parts[i]
        if i == 0:
            self.load.wait()
        self.steps_x[i].wait_recv()
        take = pltpu.make_async_copy(self.land_ref.at[c, :, s], self.stage, self.local_sems.at[1])
        take.start()
        take.wait()
        total = self.mine[c, :, s].astype(wide) + self.stage[...].astype(wide)
        self.mine[c, :, s] = total.astype(low)
        copy = remote(
            self.mine.at[c, other(self.h), s], self.came_h.at[c, s], self.sems.at[0, 4 + i],
            self.sems.at[1, 4 + i], self.over_h,
        )
        copy.start()
        self.steps_h.append(copy)

    def end(self):
        for (c, s), copy in zip(self.parts, self.steps_h):
            copy.wait()
            total = self.mine[c, self.h, s].astype(wide) + self.came_h[c, s].astype(wide)
            self.out_ref[c, s] = total.astype(low)
        for copy in self.steps_x:
            copy.wait_send()


def middle_kernel(heads, tile, scale, chunks, *refs):
    ends_ref, branch_ref, gate_mine, gate_across, up_mine, up_across, terms_own, terms_twin = refs[:8]
    query_ref, mixed_ref, packed_ref, logs_ref, cos_in, sin_in, out_in, up_in = refs[8:16]
    resid_ref, refs = refs[16], refs[17:]
    dlow_out, dkv_out, gate_out, up_out, final_ref, by_h_ref, head_out = refs[:7]
    land_gate, land_up, land_twin, refs = *refs[7:10], refs[10:]
    xs, kv, q, o, logs, cos_ref, sin_ref, out_own, up_query, dq, dlow, dkv_sum, dkv = refs[:13]
    refs = refs[13:]
    scatter_bufs, refs = (refs[:7], refs[7:14]), refs[14:]
    stage_a, stage_b, stage_c, sp_far, sp_side, sp_near, sp_far_in, sp_side_in, sp_near_in = refs[:9]
    refs = refs[9:]
    gate_own, gate_h, up_own, up_h, column_stage, refs = *refs[:5], refs[5:]
    go, came_o, came_y, gh, came_hx, came_hh, refs = *refs[:6], refs[6:]
    sends, recvs, sc_sends, sc_recvs, sp_sems, gate_sems, up_sems = refs[:7]
    chain_sems, load_sems, block_sems, local_sems = refs[7:]
    x, h, y_at = [lax.axis_index(a) for a in ("x", "h", "y")]
    c, l, y, near, side, twin = row_peers(False)
    count = branch_ref.shape[0]
    rows = count // chunks
    width = up_query.shape[1] // heads
    half, low_width = width // 2, up_query.shape[0]
    over_x, over_h, over_y = {"x": other(x)}, {"h": other(h)}, {"y": other(y)}
    me = l * 2 + y
    near_at, side_at = near["l"] * 2 + near["y"], side["l"] * 2 + side["y"]
    far_at = other(l) * 2 + other(y)
    flow = RowGather(False, chunks, branch_ref, xs, sends, recvs)
    gate = SumColumns(
        gate_mine, gate_across, land_gate, gate_out, gate_own, column_stage, gate_h, gate_sems,
        local_sems.at[0],
    )
    up = SumColumns(
        up_mine, up_across, land_up, up_out, up_own, column_stage, up_h, up_sems, local_sems.at[1]
    )
    greet([near, side, twin, over_x, over_h])
    flow.begin(None)
    sp_twin = remote(terms_twin, land_twin, sp_sems.at[0, 0], sp_sems.at[1, 0], twin)
    sp_twin.start()
    gate.start()
    up.start()
    own_load = pltpu.make_async_copy(branch_ref, xs.at[flow.me], load_sems.at[0])
    own_load.start()
    loads = [
        pltpu.make_async_copy(source, target, load_sems.at[1 + i])
        for i, (source, target) in enumerate(
            (
                (packed_ref.at[:, pl.ds(low_width, 2 * width)], kv), (query_ref, q), (mixed_ref, o),
                (logs_ref, logs), (cos_in, cos_ref), (sin_in, sin_ref), (out_in, out_own),
                (up_in, up_query),
            )
        )
    ]
    for load in loads:
        load.start()

    sp_copies = [sp_twin]

    def sp_pair(place):
        first = pltpu.make_async_copy(terms_own.at[place], stage_a, local_sems.at[2, 0])
        second = pltpu.make_async_copy(land_twin.at[place], stage_b, local_sems.at[2, 1])
        first.start()
        second.start()
        first.wait()
        second.wait()
        return stage_a[...].astype(wide) + stage_b[...].astype(wide)

    def sp_send(total, buf, target, slot, peer):
        buf[...] = total.astype(low)
        copy = remote(buf, target, sp_sems.at[0, slot], sp_sems.at[1, slot], peer)
        copy.start()
        sp_copies.append(copy)

    def sp_arrived(slot):
        remote(sp_far, sp_far_in, sp_sems.at[0, slot], sp_sems.at[1, slot], twin).wait_recv()

    dkv_sum[...] = jnp.zeros_like(dkv_sum)
    flow.take_near()
    gate.step(0)
    flow.take_side()
    sp_twin.wait_recv()
    sp_send(sp_pair(far_at), sp_far, sp_far_in, 1, side)
    sp_send(sp_pair(side_at), sp_side, sp_side_in, 2, side)
    gate.step(1)
    flow.take(3)
    flow.take(4)
    gate.step(2)
    flow.take_far()
    flow.take(5)
    gate.step(3)
    flow.take(6)
    own_load.wait()
    wait_all(loads)

    def grad_out(at):
        cols = pl.ds(pl.multiple_of(at * 256, 256), 256)
        for j in range(2):
            span = slice(j * 1024, (j + 1) * 1024)
            branch = xs[:, :, span].reshape(-1, 1024)
            go[at, :, span] = contract(o[:, cols], branch, ((0,), (0,))).astype(low)

    grad_out(other(x))
    out_x = remote(go.at[other(x)], came_o, chain_sems.at[0, 0], chain_sems.at[1, 0], over_x)
    out_x.start()
    grad_out(x)

    def block_rows(begin, size):
        first, offset = begin // count, begin % count
        got = min(size, count - offset)
        parts = [xs[first, offset : offset + got, :]]
        if got < size:
            parts.append(xs[first + 1, : size - got, :])
        return jnp.concatenate(parts, axis=0) if len(parts) > 1 else parts[0]

    def attention(i):
        span, length = slice(i * tile, (i + 1) * tile), (i + 1) * tile
        mask = tile_mask(ends_ref, i * tile, tile, length, heads)
        queries = stacked(q, span, heads, width)
        dmixed = contract(block_rows(i * tile, tile), out_own[...], ((1,), (1,))).astype(low)
        grads = jnp.concatenate(
            [dmixed[:, j * width : (j + 1) * width] for j in range(heads)], axis=0
        )
        outs = stacked(o, span, heads, width)
        delta = jnp.sum(grads.astype(wide) * outs.astype(wide), axis=1, keepdims=True)
        log = jnp.concatenate([logs[j, span, :1] for j in range(heads)], axis=0)
        keys, values = kv[:length, :width], kv[:length, width:]
        scores = contract(queries, keys, ((1,), (1,)))
        weights = jnp.where(mask, jnp.exp(scores - log), 0.0)
        dprob = contract(grads, values, ((1,), (1,)))
        dscore = (weights * (dprob - delta)).astype(low)
        dkv_sum[:length, width:] += contract(weights.astype(low), grads, ((0,), (0,)))
        dkv_sum[:length, :width] += contract(dscore, queries, ((0,), (0,)))
        dquery = contract(dscore, keys, ((1,), (0,))) * scale
        cosine, sine = cos_ref[span, :], sin_ref[span, :]
        for j in range(heads):
            a = dquery[j * tile : (j + 1) * tile, :half]
            b = dquery[j * tile : (j + 1) * tile, half:]
            at = j * width
            dq[span, at : at + half] = (a * cosine + b * sine).astype(low)
            dq[span, at + half : at + width] = (b * cosine - a * sine).astype(low)
        dlow[span, :] = contract(dq[span, :], up_query[...], ((1,), (1,))).astype(low)

    for i in range(q.shape[0] // tile):
        attention(i)
        if i == 0:
            up.step(0)
        if i == 2:
            up.step(1)
        if i == 4:
            up.step(2)
            sp_arrived(1)
            sp_send(
                sp_pair(near_at) + sp_far_in[...].astype(wide), sp_near, sp_near_in, 3, near
            )
    dkv[...] = dkv_sum[...].astype(low)
    flow.end()
    latents = [
        pltpu.make_async_copy(
            packed_ref.at[pl.ds(i * count, count), pl.ds(0, low_width)],
            xs.at[i, :, pl.ds(0, low_width)],
            block_sems.at[i],
        )
        for i in range(8)
    ]
    for load in latents:
        load.start()

    sc_copies = []
    terms = (dlow, dkv)
    sc_parts = [(a, k, pl.ds(k * rows, rows)) for k in range(chunks) for a in range(2)]

    def sc_start(source, target, a, slot, k, peer):
        copy = remote(source, target, sc_sends.at[a, slot, k], sc_recvs.at[a, slot, k], peer)
        copy.start()
        sc_copies.append(copy)

    def sc_arrived(a, slot, k):
        span = scatter_bufs[a][4].at[pl.ds(k * rows, rows)]
        remote(span, span, sc_sends.at[a, slot, k], sc_recvs.at[a, slot, k], twin).wait_recv()

    def term_rows(core, place, k):
        return pl.ds(pl.multiple_of((core * 4 + place) * count + k * rows, 16), rows)

    for slot, place in ((3, far_at), (4, side_at), (5, near_at), (6, me)):
        for a, k, span in sc_parts:
            sc_start(
                terms[a].at[term_rows(other(c), place, k)], scatter_bufs[a][0].at[place, span], a,
                slot, k, twin,
            )

    def both(a, place, k, span):
        own = terms[a][term_rows(c, place, k), :]
        return own.astype(wide) + scatter_bufs[a][0][place, span, :].astype(wide)

    for a, k, span in sc_parts:
        far_out, far_in = scatter_bufs[a][1], scatter_bufs[a][4]
        sc_arrived(a, 3, k)
        far_out[span, :] = both(a, far_at, k, span).astype(low)
        sc_start(far_out.at[span], far_in.at[span], a, 0, k, side)
    for a, k, span in sc_parts:
        side_out, side_in = scatter_bufs[a][2], scatter_bufs[a][5]
        sc_arrived(a, 4, k)
        side_out[span, :] = both(a, side_at, k, span).astype(low)
        sc_start(side_out.at[span], side_in.at[span], a, 1, k, side)
    wait_all(latents)
    dqs = dq[...]

    def grad_heads(at):
        cols = pl.ds(pl.multiple_of(at * (low_width // 2), 128), low_width // 2)
        latent = xs[:, :, cols].reshape(-1, low_width // 2)
        gh[at] = contract(latent, dqs, ((0,), (0,))).astype(low).reshape(gh.shape[1:])

    grad_heads(other(x))
    head_x = remote(gh.at[other(x)], came_hx, chain_sems.at[0, 1], chain_sems.at[1, 1], over_x)
    head_x.start()
    grad_heads(x)
    up.step(3)
    for a, k, span in sc_parts:
        near_out, far_in, near_in = scatter_bufs[a][3], scatter_bufs[a][4], scatter_bufs[a][6]
        sc_arrived(a, 5, k)
        sc_arrived(a, 0, k)
        near_out[span, :] = (both(a, near_at, k, span) + far_in[span, :].astype(wide)).astype(low)
        sc_start(near_out.at[span], near_in.at[span], a, 2, k, near)
    out_x.wait_recv()
    total = go[x].astype(wide) + came_o[...].astype(wide)
    go[x] = total.astype(low)
    part = by_h_ref.shape[1]
    mine_rows = pl.ds(pl.multiple_of(y * part, part), part)
    their_rows = pl.ds(pl.multiple_of(other(y) * part, part), part)
    out_y = remote(
        go.at[x, their_rows], came_y, chain_sems.at[0, 2], chain_sems.at[1, 2], over_y
    )
    out_y.start()
    head_x.wait_recv()
    gh[x] = (gh[x].astype(wide) + came_hx[...].astype(wide)).astype(low)
    head_h = remote(
        gh.at[x, :, other(h)], came_hh, chain_sems.at[0, 3], chain_sems.at[1, 3], over_h
    )
    head_h.start()
    sp_arrived(2)
    sp_arrived(3)
    resid_load = pltpu.make_async_copy(resid_ref, stage_c, local_sems.at[2, 0])
    resid_load.start()
    resid_load.wait()
    total = sp_pair(me) + sp_side_in[...].astype(wide) + sp_near_in[...].astype(wide)
    final_ref[...] = (stage_c[...] + total).astype(low)
    gate.end()
    outs = (dlow_out, dkv_out)
    for a, k, span in sc_parts:
        sc_arrived(a, 6, k)
        sc_arrived(a, 1, k)
        outs[a][span, :] = both(a, me, k, span) + scatter_bufs[a][5][span, :].astype(wide)
    for a, k, span in sc_parts:
        sc_arrived(a, 2, k)
        outs[a][span, :] += scatter_bufs[a][6][span, :].astype(wide)
    by_h_ref[y] = go[x, mine_rows, :]
    out_y.wait_recv()
    by_h_ref[other(y)] = came_y[...]
    head_h.wait_recv()
    head_out[...] = (gh[x, :, h].astype(wide) + came_hh[...].astype(wide)).astype(low)
    up.end()
    for copy in sp_copies + sc_copies + [out_x, out_y, head_x, head_h]:
        copy.wait_send()


def middle(
    ends, branch, gate_terms, up_terms, spread, query, mixed, packed, logs, cosine, sine, out_own,
    up_query, resid, heads, scale, number,
):
    count, width = branch.shape
    length, columns = query.shape
    low_width = up_query.shape[0]
    chunks = 4
    args = [
        ends, branch, *gate_terms, *up_terms, *spread, query, mixed, packed, logs, cosine, sine,
        out_own, up_query, resid,
    ]
    kept = (2,) + gate_terms[0].shape[2:]
    part = columns // 4
    rows_up = low_width // 8
    vmem, sem = pl.BlockSpec(memory_space=pltpu.VMEM), pltpu.SemaphoreType.DMA
    shapes = [
        ((count, low_width), wide),
        ((count, columns), wide),
        (kept, low),
        (kept, low),
        ((count, width), low),
        ((2, part, width), low),
        ((2, rows_up, columns), low),
        (gate_terms[0].shape, low),
        (up_terms[0].shape, low),
        (spread[0].shape, low),
    ]
    block = pltpu.VMEM((count, width), low)

    def scatter_scratch(w):
        return [pltpu.VMEM((4, count, w), low)] + [pltpu.VMEM((count, w), low)] * 6

    return pl.pallas_call(
        functools.partial(middle_kernel, heads, tile_of(length), scale, chunks),
        in_specs=[pl.BlockSpec(memory_space=pltpu.SMEM)] + [in_hbm()] * (len(args) - 1),
        out_specs=[vmem] * 7 + [in_hbm()] * 3,
        out_shape=[jax.ShapeDtypeStruct(*s) for s in shapes],
        scratch_shapes=[
            pltpu.VMEM((8, count, width), low),
            pltpu.VMEM((length, columns), low),
            pltpu.VMEM((length, columns), low),
            pltpu.VMEM((length, columns), low),
            pltpu.VMEM(logs.shape, wide),
            pltpu.VMEM(cosine.shape, wide),
            pltpu.VMEM(sine.shape, wide),
            pltpu.VMEM(out_own.shape, low),
            pltpu.VMEM(up_query.shape, low),
            pltpu.VMEM((length, columns), low),
            pltpu.VMEM((length, low_width), low),
            pltpu.VMEM((length, columns), wide),
            pltpu.VMEM((length, columns), low),
            *scatter_scratch(low_width),
            *scatter_scratch(columns),
            block,
            block,
            pltpu.VMEM((count, width), wide),
            *[block] * 6,
            pltpu.VMEM(gate_terms[0].shape, low),
            pltpu.VMEM(kept, low),
            pltpu.VMEM(up_terms[0].shape, low),
            pltpu.VMEM(kept, low),
            pltpu.VMEM((2, kept[1] // 2, kept[2]), low),
            pltpu.VMEM((2, columns // 2, width), low),
            pltpu.VMEM((columns // 2, width), low),
            pltpu.VMEM((part, width), low),
            pltpu.VMEM((2, 2, 2, rows_up, columns), low),
            pltpu.VMEM((2, 2, rows_up, columns), low),
            pltpu.VMEM((2, rows_up, columns), low),
            sem((7, chunks)),
            sem((7, chunks)),
            sem((2, 7, chunks)),
            sem((2, 7, chunks)),
            sem((2, 4)),
            sem((2, 8)),
            sem((2, 8)),
            sem((2, 4)),
            sem((9,)),
            sem((8,)),
            sem((3, 2)),
        ],
        compiler_params=pltpu.CompilerParams(
            collective_id=number, has_side_effects=True, vmem_limit_bytes=63 * 1024 * 1024
        ),
        cost_estimate=pl.CostEstimate(
            flops=18 * length * length * columns,
            bytes_accessed=200 * 1024 * 1024,
            transcendentals=length * length * heads // 2,
        ),
        name="middle",
    )(*args)


def norm_back_rows(incoming, source, gain):
    scale = rms_scale(source)
    weighted = incoming * gain
    mean = jnp.mean(weighted * source, axis=-1, keepdims=True)
    grad = scale * weighted - source * (scale * scale * scale) * mean
    return grad, jnp.sum(incoming * source * scale, axis=0, keepdims=True)


def shut_kernel(part, head_dim, order, n_in, n_out, *refs):
    ins, outs, refs = refs[:n_in], refs[n_in : n_in + n_out], refs[n_in + n_out :]
    (
        dlow_ref, dkv_ref, latent_ref, gain_latent_ref, cos_ref, sin_ref, hidden_ref, in_full_ref,
        home_ref, gain_one_ref, dresid_ref, gain_two_ref, gate_ref, up_ref, heads_ref, final_ref,
        kept_ref, across_ref,
    ) = ins
    sum_ref, tokens_ref, output_ref, gate_out, up_out, heads_out, out_ref = outs
    full, mapped, terms, gains, twin_buf, held, came, moved, swap_buf = refs[:9]
    gate_in, up_in, heads_in, final_buf, across_in = refs[9:14]
    sends, recvs, set_sends, set_recvs, swap_sems, local_sems = refs[14:]
    x, c, h, l, y = [lax.axis_index(a) for a in every]
    hops = {
        1: {"h": other(h)},
        2: {"l": other(l)},
        4: {"y": other(y)},
        8: {"x": other(x)},
    }
    twin = {"c": other(c)}
    cross = {"c": other(c), "h": other(h)}
    me = (c * 2 + l) * 2 + y

    def group_peer(k):
        return {"c": other(c, k // 4), "l": other(l, k // 2 % 2), "y": other(y, k % 2)}

    def group_index(k):
        peer = group_peer(k)
        return (peer["c"] * 2 + peer["l"]) * 2 + peer["y"]

    def index(code, core):
        at_x, at_l = other(x, code // 8 % 2), other(l, code // 2 % 2)
        return (((at_x * 2 + core) * 2 + other(h, code % 2)) * 2 + at_l) * 2 + other(y, code // 4 % 2)

    load = pltpu.make_async_copy(in_full_ref, full, local_sems.at[0])
    load.start()
    greet([hops[1], hops[8], cross] + [group_peer(k) for k in range(1, 8)])
    set_copies = []
    for i, (source, target) in enumerate(
        ((heads_ref, heads_in), (gate_ref, gate_in), (up_ref, up_in))
    ):
        for k in range(1, 8):
            copy = remote(
                source.at[group_index(k)], target.at[me], set_sends.at[i, k], set_recvs.at[i, k],
                group_peer(k),
            )
            copy.start()
            set_copies.append(copy)
    set_loads = [
        pltpu.make_async_copy(source.at[me], target.at[me], local_sems.at[1 + i])
        for i, (source, target) in enumerate(
            ((heads_ref, heads_in), (gate_ref, gate_in), (up_ref, up_in))
        )
    ]
    for copy in set_loads:
        copy.start()
    exchange = remote(across_ref, across_in, swap_sems.at[0], swap_sems.at[1], hops[1])
    output_move = remote(final_ref, output_ref, swap_sems.at[2], swap_sems.at[3], cross)
    tokens_move = remote(swap_buf, moved, swap_sems.at[4], swap_sems.at[5], cross)
    final_load = pltpu.make_async_copy(final_ref, final_buf, local_sems.at[4])
    final_store = pltpu.make_async_copy(final_buf, output_ref, local_sems.at[5])

    @pl.when(c != h)
    def _():
        output_move.start()

    @pl.when(c == h)
    def _():
        final_load.start()

    width, low_width = hidden_ref.shape[1], latent_ref.shape[1]
    half = head_dim // 2
    dlatent, dgain_latent = norm_back_rows(dlow_ref[...], latent_ref[...], gain_latent_ref[...])
    mapped[:, :low_width] = dlatent.astype(low)
    a, b = dkv_ref[:, :half], dkv_ref[:, half:head_dim]
    cosine, sine = cos_ref[...], sin_ref[...]
    mapped[:, low_width : low_width + half] = (a * cosine + b * sine).astype(low)
    mapped[:, low_width + half : low_width + head_dim] = (b * cosine - a * sine).astype(low)
    mapped[:, low_width + head_dim : low_width + 2 * head_dim] = dkv_ref[:, head_dim:].astype(low)
    mapped[:, low_width + 2 * head_dim :] = jnp.zeros((mapped.shape[0], 128), low)
    load.wait()
    dmapped = mapped[...]
    weights = full[...].reshape(width, -1)
    dhidden = contract(dmapped, weights, ((1,), (1,)))
    dinput, dgain_one = norm_back_rows(dhidden, home_ref[...].astype(wide), gain_one_ref[...])
    dtokens = dresid_ref[...] + dinput
    tokens_ref[...] = dtokens
    swap_buf[...] = dtokens.astype(low)

    gains[...] = jnp.zeros_like(gains)
    gains[0:1, :width] = dgain_one
    gains[1:2, :width] = gain_two_ref[...]
    gains[2:3, :low_width] = dgain_latent
    rows = terms.shape[1]
    low_part = low_width // 32
    used = low_width + 2 * head_dim
    for at in range(0, 32, 4):
        left = hidden_ref[:, at * rows : (at + 4) * rows]
        block = contract(left, dmapped[:, :used], ((0,), (0,))).astype(low)
        terms[at : at + 4, :, :used] = block.reshape(4, rows, used)
        for i in range(at, at + 4):
            tile = jnp.concatenate(
                [
                    gains[0:2, i * rows : i * rows + 128],
                    gains[2:3, i * low_part : i * low_part + 128],
                    jnp.zeros((rows - 3, 128), wide),
                ],
                axis=0,
            )
            terms[i, :, used:] = tile.astype(low)
    copies = []

    def start(source, target, slot, peer):
        copy = remote(source, target, sends.at[slot], recvs.at[slot], peer)
        copy.start()
        copies.append(copy)

    def arrived(slot):
        remote(came.at[0], came.at[0], sends.at[slot], recvs.at[slot], twin).wait_recv()

    for code in range(15, -1, -1):
        start(terms.at[index(code, 1 - c)], twin_buf.at[code], 16 + code, twin)
    for code in range(15, -1, -1):
        arrived(16 + code)
        total = terms[index(code, c)].astype(wide) + twin_buf[code].astype(wide)
        for hop in (8, 4, 2, 1):
            if code < hop:
                arrived(code + hop)
                total = total + came[code + hop].astype(wide)
        if code == 0:
            sum_ref[...] = total
        else:
            held[code] = total.astype(low)
            hop = 1 << (code.bit_length() - 1)
            start(held.at[code], came.at[code], code, hops[hop])
        if code == 8:

            @pl.when(c != h)
            def _():
                tokens_move.start()

            exchange.start()

        if code == 4:
            for copy in set_loads:
                copy.wait()
            for copy in set_copies:
                copy.wait()
            for source, target in ((gate_in, gate_out), (up_in, up_out)):
                for place, blocks in enumerate(order):
                    for j, block in enumerate(blocks):
                        target[:, block * part : (block + 1) * part] = source[
                            place, :, j * part : (j + 1) * part
                        ].astype(wide)
            for place in range(8):
                core, at_l, at_y = place // 4, place // 2 % 2, place % 2
                for j in range(2):
                    head = ((j * 2 + core) * 2 + at_y) * 2 + at_l
                    heads_out[:, head * head_dim : (head + 1) * head_dim] = heads_in[
                        place, :, j * head_dim : (j + 1) * head_dim
                    ].astype(wide)
    exchange.wait()
    out_ref[...] = kept_ref[...].astype(wide) + across_in[...].astype(wide)
    for copy in copies:
        copy.wait_send()

    @pl.when(c != h)
    def _():
        output_move.wait()
        tokens_move.wait()
        tokens_ref[...] = moved[...].astype(wide)

    @pl.when(c == h)
    def _():
        final_load.wait()
        final_store.start()
        final_store.wait()


def shut(
    dlow, dkv, latent, gain_latent, cosine, sine, hidden, in_full, home, gain_one, dresid, dgain_two,
    gate_terms, up_terms, head_terms, final, kept, across, part, order, number,
):
    count, width = hidden.shape
    head_dim = dkv.shape[1] // 2
    rows, columns = in_full.shape[1:]
    vmem, sem = pl.BlockSpec(memory_space=pltpu.VMEM), pltpu.SemaphoreType.DMA
    args = [
        dlow, dkv, latent, gain_latent, cosine, sine, hidden, in_full, home, gain_one, dresid,
        dgain_two, gate_terms, up_terms, head_terms, final, kept, across,
    ]
    hbm = {7, 12, 13, 14, 15, 17}
    ff = len(order) * len(order[0]) * part
    shapes = [
        ((rows, columns), wide),
        ((count, width), wide),
        ((count, width), low),
        ((gate_terms.shape[1], ff), wide),
        ((up_terms.shape[1], ff), wide),
        ((head_terms.shape[1], 8 * head_terms.shape[2]), wide),
        (kept.shape, wide),
    ]
    blocks = pltpu.VMEM((16, rows, columns), low)
    return pl.pallas_call(
        functools.partial(shut_kernel, part, head_dim, order, len(args), len(shapes)),
        in_specs=[in_hbm() if i in hbm else vmem for i in range(len(args))],
        out_specs=[in_hbm() if i == 2 else vmem for i in range(len(shapes))],
        out_shape=[jax.ShapeDtypeStruct(*s) for s in shapes],
        scratch_shapes=[
            pltpu.VMEM(in_full.shape, low),
            pltpu.VMEM((count, columns), low),
            pltpu.VMEM(in_full.shape, low),
            pltpu.VMEM((16, width + 128), wide),
            blocks,
            blocks,
            blocks,
            pltpu.VMEM((count, width), low),
            pltpu.VMEM((count, width), low),
            pltpu.VMEM(gate_terms.shape, low),
            pltpu.VMEM(up_terms.shape, low),
            pltpu.VMEM(head_terms.shape, low),
            pltpu.VMEM((count, width), low),
            pltpu.VMEM(across.shape, low),
            sem((32,)),
            sem((32,)),
            sem((3, 8)),
            sem((3, 8)),
            sem((6,)),
            sem((6,)),
        ],
        compiler_params=pltpu.CompilerParams(
            collective_id=number, has_side_effects=True, vmem_limit_bytes=60 * 1024 * 1024
        ),
        cost_estimate=pl.CostEstimate(flops=0, bytes_accessed=150 * 1024 * 1024, transcendentals=0),
        name="shut",
    )(*args)


def split_kernel(part, order, a_ref, b_ref, a_out, b_out):
    for source, target in ((a_ref, a_out), (b_ref, b_out)):
        used, total = len(order[0]) * part, target.shape[2]
        for place, blocks in enumerate(order):
            for j, block in enumerate(blocks):
                target[place, :, j * part : (j + 1) * part] = source[
                    :, block * part : (block + 1) * part
                ]
            if used < total:
                target[place, :, used:] = jnp.zeros((target.shape[1], total - used), target.dtype)


def join_kernel(part, order, a_ref, b_ref, a_out, b_out):
    for source, target in ((a_ref, a_out), (b_ref, b_out)):
        for place, blocks in enumerate(order):
            for j, block in enumerate(blocks):
                target[:, block * part : (block + 1) * part] = source[
                    place, :, j * part : (j + 1) * part
                ].astype(wide)


def column_order(n_x, n_l):
    return [
        [
            (((x * 2 + c) * 2 + h) * n_l + l) * 2 + y
            for x in range(n_x)
            for h in range(2)
        ]
        for c in range(2)
        for l in range(n_l)
        for y in range(2)
    ]


def split_columns(a, b, part, order, total):
    shape = jax.ShapeDtypeStruct((len(order), a.shape[0], total), a.dtype)
    return pl.pallas_call(
        functools.partial(split_kernel, part, order), out_shape=[shape] * 2, name="split_columns"
    )(a, b)


def join_columns(a, b, part, order):
    shape = jax.ShapeDtypeStruct((a.shape[1], len(order) * len(order[0]) * part), wide)
    return pl.pallas_call(
        functools.partial(join_kernel, part, order), out_shape=[shape] * 2, name="join_columns"
    )(a, b)


def first_allowed(ends_ref, count, places):
    start = jnp.zeros_like(places)
    for j in range(count):
        end = ends_ref[j]
        start = jnp.where(places >= end, end, start)
    return jnp.where(places >= ends_ref[count - 1], places, start)


def contract(left, right, dims):
    return lax.dot_general(left, right, (dims, ((), ())), preferred_element_type=wide)


def stacked(ref, span, heads, width):
    return jnp.concatenate(
        [ref[span, j * width : (j + 1) * width] for j in range(heads)], axis=0
    )


def tile_mask(ends_ref, begin, tile, length, heads):
    rows = begin + lax.broadcasted_iota(jnp.int32, (tile, 1), 0)
    lows = first_allowed(ends_ref, ends_ref.shape[0], rows)
    rows = jnp.concatenate([rows] * heads, axis=0)
    lows = jnp.concatenate([lows] * heads, axis=0)
    columns = lax.broadcasted_iota(jnp.int32, (heads * tile, length), 1)
    return (columns >= lows) & (columns <= rows)


def attend_kernel(heads, tile, ends_ref, q_ref, k_ref, v_ref, o_ref, log_ref):
    width = k_ref.shape[1]
    for i in range(q_ref.shape[0] // tile):
        span, length = slice(i * tile, (i + 1) * tile), (i + 1) * tile
        mask = tile_mask(ends_ref, i * tile, tile, length, heads)
        scores = contract(stacked(q_ref, span, heads, width), k_ref[:length, :], ((1,), (1,)))
        scores = jnp.where(mask, scores, masked_value)
        top = jnp.max(scores, axis=1, keepdims=True)
        weights = jnp.exp(scores - top)
        total = jnp.sum(weights, axis=1, keepdims=True)
        mixed = contract(weights.astype(low), v_ref[:length, :], ((1,), (0,))) / total
        log = jnp.broadcast_to(top + jnp.log(total), (heads * tile, 128))
        for j in range(heads):
            part = slice(j * tile, (j + 1) * tile)
            o_ref[span, j * width : (j + 1) * width] = mixed[part].astype(low)
            log_ref[j, span, :] = log[part]


def attend_back_kernel(
    heads, tile, scale, ends_ref, q_ref, g_ref, o_ref, k_ref, v_ref, log_ref, cos_ref, sin_ref,
    dq_ref, dkv_ref, sum_ref,
):
    width = k_ref.shape[1]
    half = width // 2
    sum_ref[...] = jnp.zeros_like(sum_ref)
    for i in range(q_ref.shape[0] // tile):
        span, length = slice(i * tile, (i + 1) * tile), (i + 1) * tile
        mask = tile_mask(ends_ref, i * tile, tile, length, heads)
        queries = stacked(q_ref, span, heads, width)
        grads = stacked(g_ref, span, heads, width)
        outs = stacked(o_ref, span, heads, width)
        delta = jnp.sum(grads.astype(wide) * outs.astype(wide), axis=1, keepdims=True)
        log = jnp.concatenate([log_ref[j, span, :1] for j in range(heads)], axis=0)
        keys, values = k_ref[:length, :], v_ref[:length, :]
        scores = contract(queries, keys, ((1,), (1,)))
        weights = jnp.where(mask, jnp.exp(scores - log), 0.0)
        dprob = contract(grads, values, ((1,), (1,)))
        dscore = (weights * (dprob - delta)).astype(low)
        sum_ref[:length, width:] += contract(weights.astype(low), grads, ((0,), (0,)))
        sum_ref[:length, :width] += contract(dscore, queries, ((0,), (0,)))
        dquery = contract(dscore, keys, ((1,), (0,))) * scale
        cosine, sine = cos_ref[span, :], sin_ref[span, :]
        for j in range(heads):
            a = dquery[j * tile : (j + 1) * tile, :half]
            b = dquery[j * tile : (j + 1) * tile, half:]
            at = j * width
            dq_ref[span, at : at + half] = (a * cosine + b * sine).astype(low)
            dq_ref[span, at + half : at + width] = (b * cosine - a * sine).astype(low)
    dkv_ref[...] = sum_ref[...].astype(low)


def attend_whole_kernel(
    heads, tile, scale, ends_ref, packed_ref, up_ref, cos_ref, sin_ref, own_ref, other_ref,
    q_ref, o_ref, log_ref, terms_ref, out_ref,
):
    x = lax.axis_index("x")
    width = up_ref.shape[1] // heads
    half, low_width = width // 2, up_ref.shape[0]
    rows = own_ref.shape[0]
    out_ref[pl.ds(pl.multiple_of(x * rows, rows), rows), :] = own_ref[...]
    out_ref[pl.ds(pl.multiple_of(other(x) * rows, rows), rows), :] = other_ref[...]
    for i in range(q_ref.shape[0] // tile):
        span, length = slice(i * tile, (i + 1) * tile), (i + 1) * tile
        raw = jnp.dot(packed_ref[span, :low_width], up_ref[...], preferred_element_type=wide)
        cosine, sine = cos_ref[span, :] * scale, sin_ref[span, :] * scale
        queries = []
        for j in range(heads):
            a, b = turn(raw[:, j * width : (j + 1) * width], cosine, sine)
            q_ref[span, j * width : j * width + half] = a.astype(low)
            q_ref[span, j * width + half : (j + 1) * width] = b.astype(low)
        mask = tile_mask(ends_ref, i * tile, tile, length, heads)
        keys = packed_ref[:length, low_width : low_width + width]
        values = packed_ref[:length, low_width + width :]
        scores = contract(stacked(q_ref, span, heads, width), keys, ((1,), (1,)))
        scores = jnp.where(mask, scores, masked_value)
        top = jnp.max(scores, axis=1, keepdims=True)
        weights = jnp.exp(scores - top)
        total = jnp.sum(weights, axis=1, keepdims=True)
        mixed = contract(weights.astype(low), values, ((1,), (0,))) / total
        log = jnp.broadcast_to(top + jnp.log(total), (heads * tile, 128))
        for j in range(heads):
            part = slice(j * tile, (j + 1) * tile)
            o_ref[span, j * width : (j + 1) * width] = mixed[part].astype(low)
            log_ref[j, span, :] = log[part]
        terms_ref[span, :] = jnp.dot(
            o_ref[span, :], out_ref[...], preferred_element_type=wide
        ).astype(low)


def attend_whole(ends, packed, up_query, cosine, sine, own_heads, other_heads, heads, scale):
    length, width = packed.shape[0], own_heads.shape[1]
    columns = up_query.shape[1]
    vmem = pl.BlockSpec(memory_space=pltpu.VMEM)
    return pl.pallas_call(
        functools.partial(attend_whole_kernel, heads, tile_of(length), scale),
        in_specs=[pl.BlockSpec(memory_space=pltpu.SMEM)] + [vmem] * 6,
        out_specs=[vmem] * 5,
        out_shape=[
            jax.ShapeDtypeStruct((length, columns), low),
            jax.ShapeDtypeStruct((length, columns), low),
            jax.ShapeDtypeStruct((heads, length, 128), wide),
            jax.ShapeDtypeStruct((length, width), low),
            jax.ShapeDtypeStruct((columns, width), low),
        ],
        compiler_params=pltpu.CompilerParams(vmem_limit_bytes=56 * 1024 * 1024),
        cost_estimate=pl.CostEstimate(
            flops=12 * length * length * columns,
            bytes_accessed=16 * length * columns,
            transcendentals=length * length * heads // 2,
        ),
        name="attend",
    )(ends, packed, up_query, cosine, sine, own_heads, other_heads)


def tile_of(length):
    return next(t for t in (256, 128, 64, 32, 16, 8) if length % t == 0)


def attend(ends, query, packed, heads):
    length, width = query.shape[0], query.shape[1] // heads
    tile = tile_of(length)
    first = packed.shape[1] // width - 2
    return pl.pallas_call(
        functools.partial(attend_kernel, heads, tile),
        grid=(1,),
        in_specs=[
            pl.BlockSpec(memory_space=pltpu.SMEM),
            pl.BlockSpec((length, heads * width), lambda i: (0, 0)),
            pl.BlockSpec((length, width), lambda i: (0, first)),
            pl.BlockSpec((length, width), lambda i: (0, first + 1)),
        ],
        out_specs=[
            pl.BlockSpec((length, heads * width), lambda i: (0, 0)),
            pl.BlockSpec((heads, length, 128), lambda i: (0, 0, 0)),
        ],
        out_shape=[
            jax.ShapeDtypeStruct((length, heads * width), low),
            jax.ShapeDtypeStruct((heads, length, 128), wide),
        ],
        compiler_params=pltpu.CompilerParams(vmem_limit_bytes=56 * 1024 * 1024),
        cost_estimate=pl.CostEstimate(
            flops=6 * length * length * width * heads,
            bytes_accessed=8 * length * width * heads,
            transcendentals=length * length * heads // 2,
        ),
        name="attend",
    )(ends, query, packed, packed)


def attend_back(ends, query, grad, mixed, packed, logs, cosine, sine, heads, scale):
    length, width = query.shape[0], query.shape[1] // heads
    tile = tile_of(length)
    first = packed.shape[1] // width - 2
    rows = pl.BlockSpec((length, heads * width), lambda i: (0, 0))
    angle = pl.BlockSpec((length, width // 2), lambda i: (0, 0))
    return pl.pallas_call(
        functools.partial(attend_back_kernel, heads, tile, scale),
        grid=(1,),
        in_specs=[
            pl.BlockSpec(memory_space=pltpu.SMEM),
            rows,
            rows,
            rows,
            pl.BlockSpec((length, width), lambda i: (0, first)),
            pl.BlockSpec((length, width), lambda i: (0, first + 1)),
            pl.BlockSpec((heads, length, 128), lambda i: (0, 0, 0)),
            angle,
            angle,
        ],
        out_specs=[rows, pl.BlockSpec((length, 2 * width), lambda i: (0, 0))],
        out_shape=[
            jax.ShapeDtypeStruct((length, heads * width), low),
            jax.ShapeDtypeStruct((length, 2 * width), low),
        ],
        scratch_shapes=[pltpu.VMEM((length, 2 * width), wide)],
        compiler_params=pltpu.CompilerParams(vmem_limit_bytes=56 * 1024 * 1024),
        cost_estimate=pl.CostEstimate(
            flops=10 * length * length * width * heads,
            bytes_accessed=16 * length * width * heads,
            transcendentals=length * length * heads // 2,
        ),
        name="attend_back",
    )(ends, query, grad, mixed, packed, packed, logs, cosine, sine)


def on_device(
    tokens,
    lengths,
    cotangent,
    norm_one,
    query_down,
    query_gain,
    query_up,
    key_proj,
    value_proj,
    out_proj,
    norm_two,
    gate_proj,
    up_proj,
    down_proj,
):
    n_x, n_l = lax.axis_size("x"), lax.axis_size("l")
    x, c, h, l, y = [lax.axis_index(a) for a in every]
    n_dev = n_x * 8 * n_l
    n_group = 4 * n_l
    me = group_place()
    count, width = tokens.shape
    row_len = count * n_group
    latent_width = query_down.shape[1]
    head_dim = key_proj.shape[1]
    shard = query_down.shape[0]
    heads = query_up.shape[1] // head_dim // n_group
    ff_part = down_proj.shape[0]
    ff_own = ff_part * n_x * 2
    ff_pad = -(-ff_own // 128) * 128
    natural = n_x == 2 and n_l == 2
    scale = 1.0 / math.sqrt(head_dim)
    order = column_order(n_x, n_l)
    mapped_width = latent_width + 2 * head_dim

    gains = jnp.zeros((shard, 128), low)
    gains = gains.at[0, :shard].set(norm_one).at[1, :shard].set(norm_two)
    gains = gains.at[2, : query_gain.shape[0]].set(query_gain)
    small = jnp.concatenate([query_down, key_proj, value_proj, gains], axis=1)
    rows_up = query_up.shape[0]
    if natural:
        head_cols = query_up.reshape(rows_up, 2, 2, 2, 2, head_dim)
        head_cols = head_cols.transpose(2, 4, 3, 0, 1, 5)
    else:
        head_cols = query_up.reshape(rows_up, n_group, -1).transpose(1, 0, 2)
    head_cols = head_cols.reshape(n_group, rows_up, heads * head_dim)
    gate_cols, up_cols = split_columns(gate_proj, up_proj, ff_part, order, ff_pad)
    if natural:
        lens = jnp.pad(lengths, ((0, 7), (0, 128 - lengths.shape[1])))
        in_full, own_heads, (up_query, gate_rows, up_rows), (home, lens) = open_exchange(
            small, out_proj, [head_cols, gate_cols, up_cols], [tokens, lens]
        )
        row_lengths = lens[0, : lengths.shape[1]]
    else:
        in_full = lax.all_gather(small, every, axis=0)
        home, grad_home, row_lengths = [swap_home(a) for a in (tokens, cotangent, lengths)]
        row_lengths = row_lengths[0]
        up_query, gate_rows, up_rows = [
            all_to_all_row(a) for a in (head_cols, gate_cols, up_cols)
        ]
        up_query = up_query.reshape((2, -1) + up_query.shape[1:])
        up_query = lax.all_gather(lax.all_gather(up_query, "h", axis=1), "x", axis=0)
    up_query = up_query.reshape(latent_width, -1)
    gate_rows = gate_rows.reshape(2, -1, ff_pad)
    up_rows = up_rows.reshape(2, -1, ff_pad)
    gain_one = in_full[:, 0, mapped_width : mapped_width + shard].reshape(width).astype(wide)
    gain_two = in_full[:, 1, mapped_width : mapped_width + shard].reshape(width).astype(wide)
    gain_latent = in_full[:, 2, mapped_width : mapped_width + query_gain.shape[0]]
    gain_latent = gain_latent.reshape(latent_width).astype(wide)
    in_full = in_full.reshape(width, -1)

    inputs = home.astype(wide)
    mapped_rates = jnp.exp(
        jnp.arange(head_dim // 2, dtype=wide) * (-math.log(10000.0) / (head_dim // 2))
    )
    ends = jnp.cumsum(row_lengths, dtype=jnp.int32)
    places = jnp.arange(row_len, dtype=jnp.int32)
    begins = jnp.max(jnp.where(places[:, None] >= ends[None, :], ends[None, :], 0), axis=1)
    if not natural:
        phases = (places - begins).astype(wide)[:, None] * mapped_rates
        cosine, sine = jnp.cos(phases), jnp.sin(phases)
        own_cos = lax.dynamic_slice_in_dim(cosine, me * count, count)
        own_sin = lax.dynamic_slice_in_dim(sine, me * count, count)

    if natural:
        own_heads = own_heads.reshape(-1, width)
        gate_a, gate_b, up_a, up_b = gate_rows[0], gate_rows[1], up_rows[0], up_rows[1]
        down_a, down_b = down_proj[:, : width // 2], down_proj[:, width // 2 :]
        heads_x = flip(own_heads, "x")
    else:
        out_full = lax.all_gather(out_proj, every, axis=0, tiled=True)
        out_own = lax.dynamic_slice_in_dim(out_full, me * heads * head_dim, heads * head_dim)
        gate_own, up_own = [
            lax.all_gather(lax.all_gather(a, "h", axis=1), "x", axis=0).reshape(width, -1)
            for a in (gate_rows, up_rows)
        ]
        down_own = lax.all_gather(lax.all_gather(down_proj, "h", axis=0), "x", axis=0)
        down_own = jnp.pad(down_own.reshape(-1, width), ((0, ff_pad - ff_own), (0, 0)))

    scale_one = rms_scale(inputs)
    if natural:
        packed, hidden, latent, cosine, sine, gate_a_h, gate_b_h = front(
            ends, home, in_full, gain_one[None], gain_latent[None], mapped_rates[None], row_len, 2,
            ("h", "h"), (gate_a, gate_b),
        )
        own_cos = lax.dynamic_slice_in_dim(cosine, me * count, count)
        own_sin = lax.dynamic_slice_in_dim(sine, me * count, count)
        packed, heads_x, up_a = together(packed, heads_x, up_a)
        up_a_h, up_b_h = flip(up_a, "h"), flip(after(up_b, packed), "h")
        gate_x = [flip(a, "x") for a in (gate_a, gate_b, gate_a_h, gate_b_h)]
        all_latent = packed[:, :latent_width]
        query, mixed, logs, terms, out_own = attend_whole(
            ends, packed, up_query, cosine, sine, own_heads, heads_x, heads, scale
        )
        terms, up_a_h, up_b_h = together(terms, up_a_h, up_b_h)
        up_x = [flip(a, "x") for a in (up_a, up_b, up_a_h, up_b_h)]
        attended, down_a_h, down_b_h = scatter_row(3, terms, kinds=("h", "h"), more=(down_a, down_b))
        attended, gate_x, up_x = together(attended, gate_x, up_x)
    else:
        hidden = (inputs * scale_one * gain_one).astype(low)
        mapped = dot(hidden, in_full)
        latent = mapped[:, :latent_width]
        scale_latent = rms_scale(latent)
        latent_low = (latent * scale_latent * gain_latent).astype(low)
        keys = mapped[:, latent_width : latent_width + head_dim]
        keys = rotate(keys, own_cos, own_sin).astype(low)
        values = mapped[:, latent_width + head_dim : mapped_width].astype(low)
        packed = gather_row(jnp.concatenate([latent_low, keys, values], axis=1), 2)
        grad_all = lax.all_gather(grad_home, group, axis=0, tiled=True)
        all_latent = packed[:, :latent_width]
        query_raw = dot(all_latent, up_query)
        query = jnp.concatenate(
            [
                rotate(query_raw[:, j * head_dim : (j + 1) * head_dim], cosine, sine)
                for j in range(heads)
            ],
            axis=1,
        ).astype(low) * jnp.asarray(scale, low)
        mixed, logs = attend(ends, query, packed, heads)
        attended = scatter_row(3, dot(mixed, out_own, low))[0]
    resid = inputs + attended
    scale_two = rms_scale(resid)
    hidden_two = (resid * scale_two * gain_two).astype(low)
    if natural:
        gate_parts = [gate_a, gate_b, gate_a_h, gate_b_h] + list(gate_x)
        up_parts = [up_a, up_b, up_a_h, up_b_h] + list(up_x)
        (
            all_two, inner, gate_factor, up_factor, down_a_x, down_a_xh, down_b_x, down_b_xh,
            grad_home, grad_all,
        ) = feed_forward(
            hidden_two, gate_parts, up_parts, (down_a, down_a_h, down_b, down_b_h), cotangent, 4
        )
    else:
        all_two = gather_row(hidden_two, 4)
        gate = dot(all_two, gate_own)
        upward = dot(all_two, up_own)
        sigma = jax.nn.sigmoid(gate)
        inner = (gate * sigma * upward).astype(low)
        grad_down = outer_sum(inner, grad_all, low)

    if natural:
        (
            dhidden_two, *spread, gate_terms, gate_x, up_terms, up_x, grad_down, _, _
        ) = feed_back(
            grad_all,
            gate_factor,
            up_factor,
            inner,
            all_two,
            gate_parts,
            up_parts,
            [
                (down_a, down_a_h, down_a_x, down_a_xh),
                (down_b, down_b_h, down_b_x, down_b_xh),
            ],
            5,
        )
    else:
        dinner = times_transposed(grad_all, down_own)
        dgate = (dinner * upward * sigma * (1.0 + gate * (1.0 - sigma))).astype(low)
        dupward = (dinner * gate * sigma).astype(low)
        grad_gate, grad_upward = outer_sum(all_two, dgate, low), outer_sum(all_two, dupward, low)
        dhidden_two = times_transposed(dgate, gate_own) + times_transposed(dupward, up_own)
        dhidden_two = scatter_row(5, dhidden_two.astype(low))[0]
        spread = scatter_row(6, dot(inner, down_own, low))[0]
        grad_down = sum_columns(grad_down[:ff_own].reshape(n_x, 2, ff_part, width), 0).astype(wide)
        gate_terms, up_terms = [
            sum_columns(a.reshape(n_x, 2, 2, -1, ff_pad), 1) for a in (grad_gate, grad_upward)
        ]

    dresid_part, dgain_two = norm_back(dhidden_two, resid, scale_two, gain_two)
    dresid = grad_home.astype(wide) + dresid_part
    branch = dresid.astype(low)
    if natural:
        by_h = (2, 2, -1, ff_pad)
        dlow, dkv, gate_terms, up_terms, final, out_terms, head_terms, *_ = middle(
            ends, branch, (gate_terms.reshape(by_h), gate_x.reshape(by_h)),
            (up_terms.reshape(by_h), up_x.reshape(by_h)), spread, query, mixed, packed, logs, cosine,
            sine, out_own, up_query, resid, heads, scale, 7,
        )
        gate_terms, up_terms = [a.reshape(n_group, shard, ff_pad) for a in (gate_terms, up_terms)]
        head_terms = head_terms.reshape(n_group, rows_up, heads * head_dim)
        summed, grad_tokens, output, grad_gate, grad_upward, grad_uquery, grad_out = shut(
            dlow, dkv, latent, gain_latent[None], own_cos, own_sin, hidden,
            in_full.reshape(n_dev, shard, -1), home, gain_one[None], dresid, dgain_two[None],
            gate_terms, up_terms, head_terms, final, pick(out_terms, h), pick(out_terms, 1 - h),
            ff_part, order, 9,
        )
    else:
        branch_all = gather_row(branch, 7)
        grad_out = outer_sum(mixed, branch_all, low)
        dmixed = times_transposed(branch_all, out_own, low)
        dquery, dkv = attend_back(
            ends, query, dmixed, mixed, packed, logs, cosine, sine, heads, scale
        )
        dlow = times_transposed(dquery, up_query, low)
        head_terms = outer_sum(all_latent, dquery, low).reshape(n_x, 2, 2, -1, heads * head_dim)
        dlow, dkv = scatter_row(8, dlow, dkv)
        whole = jnp.zeros((n_group * heads * head_dim, width), wide)
        whole = lax.dynamic_update_slice_in_dim(
            whole, grad_out.astype(wide), me * heads * head_dim, 0
        )
        grad_out = lax.psum_scatter(whole, every, scatter_dimension=0, tiled=True)
        final = (resid + spread).astype(low)
        dkeys = rotate_back(dkv[:, :head_dim], own_cos, own_sin).astype(low)
        dvalues = dkv[:, head_dim:].astype(low)
        dlatent, dgain_latent = norm_back(dlow, latent, scale_latent, gain_latent)
        nothing = jnp.zeros((count, 128), low)
        dmapped = jnp.concatenate([dlatent.astype(low), dkeys, dvalues, nothing], axis=1)
        dhidden = times_transposed(dmapped, in_full)
        dinput_part, dgain_one = norm_back(dhidden, inputs, scale_one, gain_one)
        grad_tokens = (dresid + dinput_part).astype(low)
        grad_in = outer_sum(hidden, dmapped[:, :mapped_width], low).reshape(n_dev, shard, -1)
        gain_terms = jnp.zeros((n_dev, shard, 128), low)
        gain_terms = gain_terms.at[:, 0, :shard].set(dgain_one.reshape(n_dev, -1).astype(low))
        gain_terms = gain_terms.at[:, 1, :shard].set(dgain_two.reshape(n_dev, -1).astype(low))
        gain_terms = gain_terms.at[:, 2, : query_gain.shape[0]].set(
            dgain_latent.reshape(n_dev, -1).astype(low)
        )
        terms = jnp.concatenate([grad_in, gain_terms], axis=2)
        summed = lax.psum_scatter(terms.astype(wide), every, scatter_dimension=0, tiled=False)
        grad_tokens, output = swap_home(grad_tokens), swap_home(final)
        head_terms = all_to_all_row(
            sum_columns(head_terms, 1).reshape(n_group, rows_up, heads * head_dim)
        )
        gate_terms, up_terms = [
            all_to_all_row(a.reshape(n_group, shard, ff_pad)) for a in (gate_terms, up_terms)
        ]
        grad_gate, grad_upward = join_columns(gate_terms, up_terms, ff_part, order)
        grad_uquery = head_terms.transpose(1, 0, 2).reshape(rows_up, -1).astype(wide)
    return (
        output,
        grad_tokens.astype(wide),
        summed[0, mapped_width : mapped_width + shard],
        summed[:, :latent_width],
        summed[2, mapped_width : mapped_width + query_gain.shape[0]],
        grad_uquery,
        summed[:, latent_width : latent_width + head_dim],
        summed[:, latent_width + head_dim : mapped_width],
        grad_out,
        summed[1, mapped_width : mapped_width + shard],
        grad_gate,
        grad_upward,
        grad_down,
    )


def solution(mesh):
    n_dp, n_seq = mesh.shape["dp"], mesh.shape["seq"]
    fine = Mesh(mesh.devices.reshape(n_dp // 2, 2, 2, n_seq // 4, 2), every)
    rows, flat = P(every, None), P(every)
    placed = (rows, P(("x", "c"), None), rows, flat, rows, flat) + (rows,) * 4 + (flat,) + (rows,) * 3
    return jax.shard_map(
        on_device,
        mesh=fine,
        in_specs=placed,
        out_specs=(rows, rows, flat, rows, flat) + (rows,) * 4 + (flat,) + (rows,) * 3,
        check_vma=False,
    )
```

```python
import functools
import math

import jax
import jax.numpy as jnp
from jax import lax
from jax.experimental import pallas as pl
from jax.experimental.pallas import tpu as pltpu
from jax.sharding import Mesh, PartitionSpec as P

norm_eps = 1e-05
masked_value = -1e30
every = ("x", "c", "h", "l", "y")
group = ("c", "l", "y")
low = jnp.bfloat16
wide = jnp.float32


def rms_scale(values):
    return lax.rsqrt(jnp.mean(values * values, axis=-1, keepdims=True) + norm_eps)


def rotate(values, cosine, sine):
    half = values.shape[-1] // 2
    a, b = values[..., :half], values[..., half:]
    return jnp.concatenate([a * cosine - b * sine, b * cosine + a * sine], axis=-1)


def rotate_back(values, cosine, sine):
    half = values.shape[-1] // 2
    a, b = values[..., :half], values[..., half:]
    return jnp.concatenate([a * cosine + b * sine, b * cosine - a * sine], axis=-1)


def norm_back(incoming, source, scale, gain):
    weighted = incoming * gain
    source_grad = scale * weighted - source * (scale * scale * scale) * jnp.mean(
        weighted * source, axis=-1, keepdims=True
    )
    return source_grad, jnp.sum(incoming * source * scale, axis=0)


def dot(left, right, out=wide):
    return jnp.dot(left, right, preferred_element_type=wide).astype(out)


def outer_sum(left, right, out=wide):
    return lax.dot_general(
        left, right, (((0,), (0,)), ((), ())), preferred_element_type=wide
    ).astype(out)


def times_transposed(left, right, out=wide):
    return lax.dot_general(
        left, right, (((1,), (1,)), ((), ())), preferred_element_type=wide
    ).astype(out)


def pick(array, index, axis=0):
    return lax.dynamic_index_in_dim(array, index, axis, keepdims=False)


def after(value, *done):
    return lax.optimization_barrier((value,) + done)[0]


def together(*values):
    return lax.optimization_barrier(values)


def flip(value, axis):
    return lax.ppermute(value, axis, [(0, 1), (1, 0)])


def flip_cross(value):
    return lax.ppermute(value, ("c", "h"), [(1, 2), (2, 1)])


def choose_home(value, moved):
    return jnp.where(lax.axis_index("c") == lax.axis_index("h"), value, moved)


def swap_home(value):
    return choose_home(value, flip_cross(value))


def group_place():
    return (
        lax.axis_index("c") * lax.axis_size("l") + lax.axis_index("l")
    ) * 2 + lax.axis_index("y")


def all_to_all_row(blocks):
    return lax.all_to_all(blocks, group, 0, 0, tiled=True)


def send(value, offsets):
    return lax.ppermute(value, group, [(i, i ^ offsets[i // 4]) for i in range(8)])


def scatter_row_async(state, stage):
    core = lax.axis_index("c")
    me = lax.axis_index("l") * 2 + lax.axis_index("y")
    first, second = 1 + core, 2 - core
    if stage == 0:
        return state[0], flip(state[1], "c")
    own, moved = state[:2]

    def block(index):
        return pick(own, index).astype(wide) + pick(moved, index).astype(wide)

    if stage == 1:
        far = send(block(me ^ 3).astype(low), (2, 1))
        return own, moved, far, send(block(me ^ second).astype(low), (2, 1))
    far, side = state[2:4]
    if stage == 2:
        return state + (send((block(me ^ first) + far.astype(wide)).astype(low), (1, 2)),)
    return block(me) + side.astype(wide) + state[4].astype(wide)


def sum_columns(terms, h_dim):
    for axis, dim in (("x", 0), ("h", h_dim)):
        terms = jnp.moveaxis(terms, dim, 0).astype(wide)
        terms = lax.psum_scatter(terms, axis, scatter_dimension=0, tiled=False).astype(low)
    return terms


def halves(terms, axis, dim):
    me = lax.axis_index(axis)
    return pick(terms, me, dim), flip(pick(terms, 1 - me, dim), axis)


def add(own, came):
    return (own.astype(wide) + came.astype(wide)).astype(low)


def other(value, flag=1):
    return value + flag * (1 - 2 * value)


def greet(peers):
    barrier = pltpu.get_barrier_semaphore()
    for peer in peers:
        pl.semaphore_signal(barrier, inc=1, device_id=peer, device_id_type=pl.DeviceIdType.MESH)
    pl.semaphore_wait(barrier, len(peers))


def remote(source, target, send_sem, recv_sem, peer):
    return pltpu.make_async_remote_copy(
        src_ref=source,
        dst_ref=target,
        send_sem=send_sem,
        recv_sem=recv_sem,
        device_id=peer,
        device_id_type=pl.DeviceIdType.MESH,
    )


def in_hbm():
    return pl.BlockSpec(memory_space=pl.ANY)


def open_kernel(n_swaps, part, order, small_ref, out_ref, heads_in, gate_in, up_in, *refs):
    n_sets = 3
    swaps, refs = refs[:n_swaps], refs[n_swaps:]
    (full_ref, heads_ref), refs = refs[:2], refs[2:]
    set_outs, refs = refs[:n_sets], refs[n_sets:]
    swap_outs, refs = refs[:n_swaps], refs[n_swaps:]
    (small_buf, out_buf), refs = refs[:2], refs[2:]
    raws, set_bufs, refs = refs[:2], refs[2:5], refs[5:]
    heads_buf, splits = set_bufs[0], set_bufs[1:]
    sets = [heads_in, *splits]
    swap_bufs, refs = refs[:n_swaps], refs[n_swaps:]
    sends, recvs, swap_sends, swap_recvs, set_sends, set_recvs, out_sems, head_sems, loads_sem, stores_sem, split_sem = refs
    x, c, h, l, y = [lax.axis_index(a) for a in every]
    hops = {
        1: {"h": other(h)},
        2: {"l": other(l)},
        4: {"y": other(y)},
        8: {"x": other(x)},
        16: {"c": other(c)},
    }
    cross = {"c": other(c), "h": other(h)}
    me = (c * 2 + l) * 2 + y

    def group_peer(k):
        return {"c": other(c, k // 4), "l": other(l, k // 2 % 2), "y": other(y, k % 2)}

    def group_index(k):
        peer = group_peer(k)
        return (peer["c"] * 2 + peer["l"]) * 2 + peer["y"]

    def index(code):
        at_x, at_l = other(x, code // 8 % 2), other(l, code // 2 % 2)
        return (((at_x * 2 + c) * 2 + other(h, code % 2)) * 2 + at_l) * 2 + other(y, code // 4 % 2)

    beside, corner = {"y": other(y)}, {"h": other(h), "y": h}
    greet(
        [hops[1], hops[8], cross, {"h": other(h), "y": other(y)}]
        + [group_peer(k) for k in range(1, 8)]
    )
    copies = []
    half = heads_ref.at[y]
    to_beside = remote(out_ref, half, out_sems.at[0], out_sems.at[1], beside)
    differ = y + h - 2 * y * h
    to_corner = remote(out_ref, half, out_sems.at[2], out_sems.at[3 + differ], corner)

    def push(code):
        block = full_ref.at[index(code)]
        source = small_ref if code == 0 else block
        for hop in (1, 2, 4, 8, 16):
            if code < hop:
                name = code + hop
                copy = remote(source, block, sends.at[name], recvs.at[name], hops[hop])
                copy.start()
                copies.append(copy)

    def set_slot(i):
        return set_outs[0].at[x, c, h, l * 2 + y] if i == 0 else set_outs[i].at[me]

    set_copies = []

    def set_push(i):
        for k in range(1, 8):
            copy = remote(
                sets[i].at[group_index(k)], set_slot(i), set_sends.at[i, k], set_recvs.at[i, k],
                group_peer(k),
            )
            copy.start()
            set_copies.append(copy)

    push(0)
    set_push(0)
    moving = [
        remote(source, target, swap_sends.at[i], swap_recvs.at[i], cross)
        for i, (source, target) in enumerate(zip(swaps, swap_outs))
    ]

    def push_moves():
        @pl.when(c != h)
        def _():
            for copy in moving:
                copy.start()

        @pl.when(y != h)
        def _():
            to_beside.start()

        to_corner.start()

    loads, stores = [], []
    raw_loads = [
        pltpu.make_async_copy(source, raw, stores_sem.at[3 + n_swaps + i])
        for i, (source, raw) in enumerate(((gate_in, raws[0]), (up_in, raws[1])))
    ]
    for load in raw_loads:
        load.start()
    locals_in = [small_ref, out_ref, heads_in.at[me]] + list(swaps)
    locals_buf = [small_buf, out_buf, heads_buf] + list(swap_bufs)
    locals_out = [full_ref.at[index(0)], half, set_slot(0)]
    for i, (source, buf) in enumerate(zip(locals_in, locals_buf)):
        loads.append(pltpu.make_async_copy(source, buf, loads_sem.at[i]))
        loads[-1].start()
    for load in loads:
        load.wait()
    for i, (buf, target) in enumerate(zip(locals_buf, locals_out)):
        stores.append(pltpu.make_async_copy(buf, target, stores_sem.at[i]))
    keep_out = stores.pop(1)
    for store in stores:
        store.start()

    @pl.when(y == h)
    def _():
        keep_out.start()

    keeps = [
        pltpu.make_async_copy(buf, target, stores_sem.at[3 + i])
        for i, (buf, target) in enumerate(zip(swap_bufs, swap_outs))
    ]

    @pl.when(c == h)
    def _():
        for keep in keeps:
            keep.start()

    def arrived(name):
        remote(small_ref, small_ref, sends.at[name], recvs.at[name], hops[16]).wait_recv()

    def head_copy(at_h, slot, peer):
        part = set_outs[0].at[x, :, at_h]
        copy = remote(part, part, head_sems.at[slot], head_sems.at[3 + slot], peer)
        copy.start()
        return copy

    head_copies, split_keeps = [], []
    for n, code in enumerate((2, 4, 1, 6, 3, 5, 7, 8, 9, 10, 11, 12, 13, 14, 15)):
        arrived(code)
        push(code)
        if n == 2:
            for copy in set_copies:
                copy.wait()
            for store in stores:
                store.wait()
            done = len(set_copies)
            for load in raw_loads:
                load.wait()
            split_kernel(part, order, *raws, *splits)
            for i in range(1, n_sets):
                set_push(i)
                keep = pltpu.make_async_copy(splits[i - 1].at[me], set_slot(i), split_sem.at[i - 1])
                keep.start()
                split_keeps.append(keep)
            head_copies.append(head_copy(h, 0, hops[1]))
            head_copies.append(head_copy(h, 1, hops[8]))
            push_moves()
        if n == 9:
            head_copies[0].wait_recv()
            head_copies.append(head_copy(other(h), 2, hops[8]))
    for code in range(16):
        arrived(16 + code)
    for copy in copies:
        copy.wait_send()
    for copy in set_copies[done:] + split_keeps:
        copy.wait()
    head_copies[0].wait_send()
    for copy in head_copies[1:]:
        copy.wait()
    to_corner.wait_send()

    @pl.when(y != h)
    def _():
        to_beside.wait_send()
        remote(out_ref, half, out_sems.at[2], out_sems.at[3], corner).wait_recv()
        remote(out_ref, half, out_sems.at[2], out_sems.at[4], corner).wait_recv()

    @pl.when(y == h)
    def _():
        keep_out.wait()
        to_beside.wait_recv()

    @pl.when(c != h)
    def _():
        for copy in moving:
            copy.wait()

    @pl.when(c == h)
    def _():
        for keep in keeps:
            keep.wait()


def open_exchange(small, out_rows, heads, gate, up, swaps, part, order, total):
    n_swaps = len(swaps)
    args = [small, out_rows, heads, gate, up] + swaps
    split = (len(order), gate.shape[0], total)
    shapes = [(32,) + small.shape, (2,) + out_rows.shape, (2, 2, 2, 4) + heads.shape[1:], split, split]
    out_shape = [jax.ShapeDtypeStruct(s, low) for s in shapes]
    out_shape += [jax.ShapeDtypeStruct(a.shape, a.dtype) for a in swaps]
    sem = pltpu.SemaphoreType.DMA
    out = pl.pallas_call(
        functools.partial(open_kernel, n_swaps, part, order),
        in_specs=[in_hbm()] * len(args),
        out_specs=[in_hbm()] * len(out_shape),
        out_shape=out_shape,
        scratch_shapes=[pltpu.VMEM(a.shape, low) for a in (small, out_rows, gate, up)]
        + [pltpu.VMEM(s, low) for s in (heads.shape[1:], split, split)]
        + [pltpu.VMEM(a.shape, a.dtype) for a in swaps]
        + [sem((32,)), sem((32,)), sem((n_swaps,)), sem((n_swaps,))]
        + [sem((3, 8)), sem((3, 8)), sem((5,)), sem((6,))]
        + [sem((3 + n_swaps,)), sem((5 + n_swaps,)), sem((2,))],
        compiler_params=pltpu.CompilerParams(
            collective_id=1, has_side_effects=True, vmem_limit_bytes=16 * 1024 * 1024
        ),
        cost_estimate=pl.CostEstimate(flops=0, bytes_accessed=150 * 1024 * 1024, transcendentals=0),
        name="open_exchange",
    )(*args)
    return out[0], out[1], out[2:5], out[5:]


def row_peers(even):
    c, l, y = [lax.axis_index(a) for a in group]
    if even == "l":
        near = {"l": l, "y": other(y)}
        side = {"l": other(l), "y": y}
    elif even:
        near = {"l": other(l, c), "y": other(y, 1 - c)}
        side = {"l": other(l, 1 - c), "y": other(y, c)}
    else:
        near = {"l": other(l), "y": y}
        side = {"l": l, "y": other(y)}
    return c, l, y, near, side, {"c": other(c)}


def turn(values, cosine, sine):
    half = values.shape[1] // 2
    a, b = values[:, :half], values[:, half:]
    return a * cosine - b * sine, b * cosine + a * sine


def angles(ends_ref, rates, begin, count):
    places = begin + lax.broadcasted_iota(jnp.int32, (count, 1), 0)
    start = jnp.zeros_like(places)
    for j in range(ends_ref.shape[0]):
        end = ends_ref[j]
        start = jnp.where(places >= end, end, start)
    phases = (places - start).astype(wide) * rates
    return jnp.cos(phases), jnp.sin(phases)


def front_kernel(kinds, ends_ref, home_ref, full_ref, gain_ref, low_gain_ref, rates_ref, *refs):
    n = len(kinds)
    more, refs = refs[:n], refs[n:]
    out_ref, hidden_ref, latent_ref, cos_ref, sin_ref, refs = *refs[:5], refs[5:]
    more_out, refs = refs[:n], refs[n:]
    full, own, sends, recvs, load_sem, store_sem, more_sems = refs
    beside = Beside(kinds, more, more_out, more_sems)
    flow = RowGather(False, sends.shape[1], own, out_ref, sends, recvs)
    load = pltpu.make_async_copy(full_ref, full, load_sem)
    load.start()
    near, side, twin = flow.peers
    greet([near, side, twin, *beside.peers])
    count = home_ref.shape[0]
    low_width, head_dim = latent_ref.shape[1], 2 * cos_ref.shape[1]
    half = head_dim // 2
    values = home_ref[...].astype(wide)
    hidden = (values * rms_scale(values) * gain_ref[...]).astype(low)
    hidden_ref[...] = hidden
    cosine, sine = angles(ends_ref, rates_ref[...], flow.me * count, count)
    load.wait()
    mapped = jnp.dot(hidden, full[...], preferred_element_type=wide)
    latent = mapped[:, :low_width]
    latent_ref[...] = latent
    own[:, :low_width] = (latent * rms_scale(latent) * low_gain_ref[...]).astype(low)
    a, b = turn(mapped[:, low_width : low_width + head_dim], cosine, sine)
    own[:, low_width : low_width + half] = a.astype(low)
    own[:, low_width + half : low_width + head_dim] = b.astype(low)
    end = low_width + 2 * head_dim
    own[:, low_width + head_dim :] = mapped[:, low_width + head_dim : end].astype(low)
    flow.begin(None)
    beside.start()
    store = pltpu.make_async_copy(own, out_ref.at[flow.me], store_sem)
    store.start()

    def tables(begin, rows):
        cos_ref[begin : begin + rows, :], sin_ref[begin : begin + rows, :] = angles(
            ends_ref, rates_ref[...], begin, rows
        )

    quarter = cos_ref.shape[0] // 4
    tables(0, quarter)
    tables(quarter, quarter)
    flow.take_near()
    tables(2 * quarter, quarter)
    flow.take_side()
    tables(3 * quarter, quarter)
    flow.take_far()
    for slot in (3, 4, 5, 6):
        flow.take(slot)
    flow.end()
    store.wait()
    beside.wait()


def front(ends, home, in_full, gain_one, gain_latent, rates, row_len, number, kinds, more):
    count, width = home.shape
    low_width = gain_latent.shape[1]
    half = rates.shape[1]
    packed = (count, low_width + 4 * half)
    vmem, sem = pl.BlockSpec(memory_space=pltpu.VMEM), pltpu.SemaphoreType.DMA
    out = pl.pallas_call(
        functools.partial(front_kernel, kinds),
        in_specs=[pl.BlockSpec(memory_space=pltpu.SMEM), vmem, in_hbm(), vmem, vmem, vmem]
        + [in_hbm()] * len(more),
        out_specs=[in_hbm()] + [vmem] * 4 + [in_hbm()] * len(more),
        out_shape=[
            jax.ShapeDtypeStruct((8,) + packed, low),
            jax.ShapeDtypeStruct((count, width), low),
            jax.ShapeDtypeStruct((count, low_width), wide),
            jax.ShapeDtypeStruct((row_len, half), wide),
            jax.ShapeDtypeStruct((row_len, half), wide),
        ]
        + [jax.ShapeDtypeStruct(a.shape, low) for a in more],
        scratch_shapes=[
            pltpu.VMEM(in_full.shape, low),
            pltpu.VMEM(packed, low),
            sem((7, 4)),
            sem((7, 4)),
            sem,
            sem,
            sem((2, len(more))),
        ],
        compiler_params=pltpu.CompilerParams(
            collective_id=number, has_side_effects=True, vmem_limit_bytes=32 * 1024 * 1024
        ),
        cost_estimate=pl.CostEstimate(flops=0, bytes_accessed=100 * 1024 * 1024, transcendentals=0),
        name="front",
    )(ends, home, in_full, gain_one, gain_latent, rates, *more)
    return (out[0].reshape(-1, packed[1]), *out[1:])


def gather_kernel(even, chunks, kinds, own_ref, *refs):
    n = len(kinds)
    more, out_ref, more_out = refs[:n], refs[n], refs[n + 1 : 2 * n + 1]
    buf, sends, recvs, local_sems = refs[2 * n + 1 : 2 * n + 5]
    beside = Beside(kinds, more, more_out, refs[-1])
    flow = RowGather(even, chunks, own_ref, out_ref, sends, recvs)
    flow.begin(beside.peers)
    beside.start()
    load = pltpu.make_async_copy(own_ref, buf, local_sems.at[0])
    load.start()
    load.wait()
    store = pltpu.make_async_copy(buf, out_ref.at[flow.me], local_sems.at[1])
    store.start()
    flow.take_near()
    flow.take_side()
    flow.take_far()
    for slot in (3, 4, 5, 6):
        flow.take(slot)
    flow.end()
    store.wait()
    beside.wait()


class Beside:
    def __init__(self, kinds, sources, targets, sems):
        x, c, h = [lax.axis_index(a) for a in ("x", "c", "h")]
        ways = {"x": {"x": other(x)}, "h": {"h": other(h)}, "cross": {"c": other(c), "h": other(h)}}
        self.peers = [ways[k] for k in sorted(set(kinds))]
        self.moves = c != h
        self.copies = [
            (kind, remote(source, target, sems.at[0, i], sems.at[1, i], ways[kind]))
            for i, (kind, source, target) in enumerate(zip(kinds, sources, targets))
        ]

    def start(self, span=slice(None)):
        for kind, copy in self.copies[span]:
            if kind == "cross":
                pl.when(self.moves)(copy.start)
            else:
                copy.start()

    def wait(self, span=slice(None)):
        for kind, copy in self.copies[span]:
            if kind == "cross":
                pl.when(self.moves)(copy.wait)
            else:
                copy.wait()


class RowGather:
    def __init__(self, even, chunks, own_ref, out_ref, sends, recvs, in_slots=False):
        c, l, y, near, side, twin = row_peers(even)
        self.peers = near, side, twin
        self.chunks, self.rows = chunks, own_ref.shape[0] // chunks
        self.own_ref, self.out_ref, self.sends, self.recvs = own_ref, out_ref, sends, recvs
        at = l * 2 + y
        near_at, side_at = near["l"] * 2 + near["y"], side["l"] * 2 + side["y"]
        far_at = other(l) * 2 + other(y)
        self.me = c * 4 + at
        self.places = [c * 4 + p for p in (near_at, side_at, far_at)]
        swapped = even is True
        twins = (at, side_at, near_at, far_at) if swapped else (at, near_at, side_at, far_at)
        self.places += [other(c) * 4 + p for p in twins]
        self.copies = []
        self.lands = (2, 3, 6, 1, 4, 5, 7) if in_slots else None

    def land(self, slot):
        return self.lands[slot] if self.lands else self.places[slot]

    def start(self, held, k, slot, peer):
        span = pl.ds(k * self.rows, self.rows)
        source = self.own_ref.at[span] if held is None else self.out_ref.at[self.land(held), span]
        if self.lands:
            target = self.out_ref.at[self.lands[slot], span]
        else:
            target = self.out_ref.at[self.me if held is None else self.places[held], span]
        copy = remote(source, target, self.sends.at[slot, k], self.recvs.at[slot, k], peer)
        copy.start()
        self.copies.append(copy)

    def begin(self, more_peers=()):
        near, side, twin = self.peers
        if more_peers is not None:
            greet([near, side, twin, *more_peers])
        for k in range(self.chunks):
            self.start(None, k, 0, near)
            self.start(None, k, 1, side)
            self.start(None, k, 3, twin)

    def arrived(self, slot, k):
        span = self.own_ref.at[pl.ds(k * self.rows, self.rows)]
        target = self.out_ref.at[self.land(slot), pl.ds(k * self.rows, self.rows)]
        remote(
            span, target, self.sends.at[slot, k], self.recvs.at[slot, k], self.peers[2]
        ).wait_recv()

    def take(self, slot):
        for k in range(self.chunks):
            self.arrived(slot, k)

    def take_near(self):
        near, side, twin = self.peers
        for k in range(self.chunks):
            self.arrived(0, k)
            self.start(0, k, 2, side)
            self.start(0, k, 4, twin)

    def take_side(self):
        for k in range(self.chunks):
            self.arrived(1, k)
            self.start(1, k, 5, self.peers[2])

    def take_far(self):
        for k in range(self.chunks):
            self.arrived(2, k)
            self.start(2, k, 6, self.peers[2])

    def end(self):
        for copy in self.copies:
            copy.wait_send()


def gather_row(value, number, even=False, kinds=(), more=()):
    if lax.axis_size("l") != 2:
        return lax.all_gather(value, group, axis=0, tiled=True)
    chunks = 4 if value.shape[0] % 64 == 0 else 1
    args = [value, *more]
    out_shape = [jax.ShapeDtypeStruct((8,) + value.shape, low)]
    out_shape += [jax.ShapeDtypeStruct(a.shape, low) for a in more]
    out = pl.pallas_call(
        functools.partial(gather_kernel, even, chunks, kinds),
        in_specs=[in_hbm()] * len(args),
        out_specs=[in_hbm()] * len(args),
        out_shape=out_shape,
        scratch_shapes=[
            pltpu.VMEM(value.shape, low),
            pltpu.SemaphoreType.DMA((7, chunks)),
            pltpu.SemaphoreType.DMA((7, chunks)),
            pltpu.SemaphoreType.DMA((2,)),
            pltpu.SemaphoreType.DMA((2, max(1, len(more)))),
        ],
        compiler_params=pltpu.CompilerParams(
            collective_id=number, has_side_effects=True, vmem_limit_bytes=16 * 1024 * 1024
        ),
        cost_estimate=pl.CostEstimate(flops=0, bytes_accessed=80 * 1024 * 1024, transcendentals=0),
        name="gather_row",
    )(*args)
    rows = out[0].reshape(-1, value.shape[1])
    return (rows, *out[1:]) if kinds else rows


def load_columns(pieces, target, sem, first):
    x, h = lax.axis_index("x"), lax.axis_index("h")
    rows = pieces[0].shape[0]
    loads = []
    for i, piece in enumerate(pieces):
        at_x = x if i < 4 else other(x)
        at_h = h if i // 2 % 2 == 0 else other(h)
        at = pl.multiple_of(((at_x * 2 + i % 2) * 2 + at_h) * rows, rows)
        loads.append(
            pltpu.make_async_copy(piece, target.at[pl.ds(at, rows)], sem.at[first + i])
        )
    return loads


def load_rows(parts, target, sem):
    x, h = lax.axis_index("x"), lax.axis_index("h")
    rows, width = parts[0][0].shape
    loads = []
    for s, part in enumerate(parts):
        for i, (at_x, at_h) in enumerate(
            ((x, h), (x, other(h)), (other(x), h), (other(x), other(h)))
        ):
            at = pl.multiple_of((at_x * 2 + at_h) * rows, 16)
            loads.append(
                pltpu.make_async_copy(
                    part[i],
                    target.at[pl.ds(at, rows), pl.ds(s * width, width)],
                    sem.at[len(loads)],
                )
            )
            loads[-1].start()
    return loads


def wait_all(copies):
    for copy in copies:
        copy.wait()


def for_tiles(total, tile, body):
    def step(j, carry):
        body(pl.ds(pl.multiple_of(j * tile, tile), tile))
        return carry

    lax.fori_loop(0, total // tile, step, 0)


def feed_kernel(even, chunks, *refs):
    own_ref, gates, ups = refs[0], refs[1:9], refs[9:17]
    downs, grad_ref, refs = refs[17:21], refs[21], refs[22:]
    all_ref, inner_ref, a_ref, b_ref = refs[:4]
    downs_x, home_ref, grads_ref, refs = refs[4:8], refs[8], refs[9], refs[10:]
    xs, wg, wu, inner_s, a_s, b_s, grad_buf, sends, recvs, grad_sends, grad_recvs = refs[:11]
    weight_sems, store_sems, own_sem, more_sems, grad_sems = refs[11:]
    flow = RowGather(even, chunks, own_ref, xs, sends, recvs, in_slots=True)
    beside = Beside(
        ("cross", "x", "x", "x", "x"),
        (grad_ref, *downs),
        (home_ref, *downs_x),
        more_sems,
    )
    away = lax.axis_index("c") != lax.axis_index("h")
    grad_flow = RowGather(True, chunks, home_ref, grads_ref, grad_sends, grad_recvs)
    flow.begin(beside.peers)
    beside.start()
    grad_load = pltpu.make_async_copy(grad_ref, grad_buf, grad_sems.at[0])
    grad_load.start()
    own_load = pltpu.make_async_copy(own_ref, xs.at[0], own_sem)
    own_load.start()
    weights = load_columns(gates, wg, weight_sems, 0) + load_columns(ups, wu, weight_sems, 8)
    for load in weights:
        load.start()
    grad_load.wait()
    to_home = pltpu.make_async_copy(grad_buf, home_ref, grad_sems.at[1])

    @pl.when(jnp.logical_not(away))
    def _():
        to_home.start()
        to_home.wait()

    order = [flow.me] + [flow.places[s] for s in (3, 0, 1, 4, 5, 2, 6)]
    stores = []
    columns, width = wg.shape[1], wg.shape[0]

    def work(pair):
        both = pl.ds(2 * pair, 2)
        x = xs[both].reshape(-1, width)

        def tile(cols):
            gate = jnp.dot(x, wg[:, cols], preferred_element_type=wide)
            upward = jnp.dot(x, wu[:, cols], preferred_element_type=wide)
            sigma = jax.nn.sigmoid(gate)
            swish = gate * sigma
            shape = (2, -1, upward.shape[1])
            inner_s[both, :, cols] = (swish * upward).astype(low).reshape(shape)
            b_s[both, :, cols] = swish.astype(low).reshape(shape)
            factor = upward * sigma * (1.0 + gate * (1.0 - sigma))
            a_s[both, :, cols] = factor.astype(low).reshape(shape)

        tile(slice(None))
        for i in (2 * pair, 2 * pair + 1):
            place = order[i]
            for j, (buf, target) in enumerate(
                ((xs, all_ref), (inner_s, inner_ref), (a_s, a_ref), (b_s, b_ref))
            ):
                store = pltpu.make_async_copy(buf.at[i], target.at[place], store_sems.at[i, j])
                store.start()
                stores.append(store)

    own_load.wait()
    flow.take(3)
    wait_all(weights)
    work(0)
    flow.take_near()
    flow.take_side()
    beside.wait(slice(0, 1))
    grad_flow.begin(None)
    home_load = pltpu.make_async_copy(home_ref, grad_buf, grad_sems.at[2])
    home_load.start()
    work(1)
    home_load.wait()
    own_store = pltpu.make_async_copy(grad_buf, grads_ref.at[grad_flow.me], grad_sems.at[3])
    own_store.start()
    flow.take(4)
    flow.take(5)
    work(2)
    flow.take_far()
    grad_flow.take_near()
    grad_flow.take_side()
    flow.take(6)
    work(3)
    grad_flow.take_far()
    for slot in (3, 4, 5, 6):
        grad_flow.take(slot)
    flow.end()
    grad_flow.end()
    wait_all(stores + [own_store])
    beside.wait(slice(1, 5))


def feed_forward(own, gates, ups, downs, grad, number):
    count, width = own.shape
    columns = gates[0].shape[1]
    chunks = 4 if count % 64 == 0 else 1
    row, part = (8, count, width), (8, count, columns)
    sem = pltpu.SemaphoreType.DMA
    flops = 2 * 8 * count * width * columns * 2
    args = [own, *gates, *ups, *downs, grad]
    shapes = [row, part, part, part] + [a.shape for a in downs] + [grad.shape, row]
    return pl.pallas_call(
        functools.partial(feed_kernel, False, chunks),
        in_specs=[in_hbm()] * len(args),
        out_specs=[in_hbm()] * len(shapes),
        out_shape=[jax.ShapeDtypeStruct(s, low) for s in shapes],
        scratch_shapes=[
            pltpu.VMEM(row, low),
            pltpu.VMEM((width, columns), low),
            pltpu.VMEM((width, columns), low),
            pltpu.VMEM(part, low),
            pltpu.VMEM(part, low),
            pltpu.VMEM(part, low),
            pltpu.VMEM(grad.shape, low),
            sem((7, chunks)),
            sem((7, chunks)),
            sem((7, chunks)),
            sem((7, chunks)),
            sem((16,)),
            sem((8, 4)),
            sem,
            sem((2, 5)),
            sem((4,)),
        ],
        compiler_params=pltpu.CompilerParams(
            collective_id=number, has_side_effects=True, vmem_limit_bytes=56 * 1024 * 1024
        ),
        cost_estimate=pl.CostEstimate(
            flops=flops, bytes_accessed=100 * 1024 * 1024, transcendentals=0
        ),
        name="feed_forward",
    )(*args)


def feed_back_kernel(
    even, chunks, *refs,
):
    grad_ref, a_ref, b_ref, inner_ref, all_ref = refs[:5]
    gates, ups, downs, refs = refs[5:13], refs[13:21], refs[21:29], refs[29:]
    out_ref, terms_own, terms_twin, gate_own, gate_across, up_own, up_across = refs[:7]
    down_sum, down_across, down_came, refs = refs[7], refs[8], refs[9], refs[10:]
    down_own, down_stage, came_h, refs = refs[0], refs[1], refs[2], refs[3:]
    gx, wg, wu, wd, a_s, b_s, inner_s, terms_s, own_buf, twin_buf, twin_out, down_s = refs[:12]
    far_out, side_out, near_out, far_in, side_in, near_in = refs[12:18]
    sends, recvs, weight_sems, down_sems, block_sems, all_sems, terms_sems, more_sems = refs[18:]
    over_x, over_h = {"x": other(lax.axis_index("x"))}, {"h": other(lax.axis_index("h"))}
    at_h = lax.axis_index("h")
    halves_at = [pl.ds(0, grad_ref.shape[2] // 2), pl.ds(grad_ref.shape[2] // 2, grad_ref.shape[2] // 2)]
    steps_x = [
        remote(down_across.at[:, s], down_came.at[:, s], more_sems.at[0, i], more_sems.at[1, i], over_x)
        for i, s in enumerate(halves_at)
    ]
    steps_h = []

    def down_step(i):
        s = halves_at[i]
        steps_x[i].wait_recv()
        take = pltpu.make_async_copy(down_came.at[:, s], down_stage, more_sems.at[2, i])
        take.start()
        take.wait()
        total = down_own[:, s].astype(wide) + down_stage[...].astype(wide)
        down_own[:, s] = total.astype(low)
        part_rows = came_h.shape[0]
        theirs = down_own.at[pl.ds(pl.multiple_of(other(at_h) * part_rows, 16), part_rows), s]
        copy = remote(theirs, came_h.at[:, s], more_sems.at[0, 2 + i], more_sems.at[1, 2 + i], over_h)
        copy.start()
        steps_h.append(copy)

    c, l, y, near, side, twin = row_peers(even)
    rows = out_ref.shape[0] // chunks
    columns, width = wd.shape
    used = 4 * downs[0].shape[0]
    me = l * 2 + y
    near_at, side_at = near["l"] * 2 + near["y"], side["l"] * 2 + side["y"]
    far_at = other(l) * 2 + other(y)
    own_order = (far_at, side_at, near_at, me)
    twin_order = (far_at, near_at, side_at, me) if even else own_order
    pairs = []
    for p, q in zip(twin_order, own_order):
        pairs += [(other(c) * 4 + p, p, True), (c * 4 + q, q, False)]
    downs = load_rows((downs[:4], downs[4:]), wd, down_sems)
    blocks = []
    for i, (place, _, _) in enumerate(pairs):
        loads = [
            pltpu.make_async_copy(source.at[place], buf.at[i], block_sems.at[i, j])
            for j, (source, buf) in enumerate(
                ((grad_ref, gx), (a_ref, a_s), (b_ref, b_s), (inner_ref, inner_s))
            )
        ]
        for load in loads:
            load.start()
        blocks.append(loads)
    weights = load_columns(gates, wg, weight_sems, 0) + load_columns(ups, wu, weight_sems, 8)
    for load in weights:
        load.start()
    wd[used:, :] = jnp.zeros((columns - used, width), low)
    greet([near, side, twin, over_x, over_h])
    copies = []

    def start(source, target, slot, k, peer):
        copy = remote(source, target, sends.at[slot, k], recvs.at[slot, k], peer)
        copy.start()
        copies.append(copy)

    def arrived(slot, k):
        span = far_in.at[pl.ds(k * rows, rows)]
        remote(span, span, sends.at[slot, k], recvs.at[slot, k], twin).wait_recv()

    def block_arrived(slot):
        remote(
            own_buf.at[0], twin_buf.at[0], sends.at[slot, 0], recvs.at[slot, 0], twin
        ).wait_recv()

    def term(pair, twin_target, own_target):
        span = pl.ds(2 * pair, 2)
        grads = gx[span].reshape(-1, width)

        dinner = contract(grads, wd[...], ((1,), (1,))).reshape(2, -1, columns)
        a_s[span] = (dinner * a_s[span].astype(wide)).astype(low)
        b_s[span] = (dinner * b_s[span].astype(wide)).astype(low)
        if pair == 0:
            wait_all(weights)
        dgate = a_s[span].reshape(-1, columns)
        dup = b_s[span].reshape(-1, columns)

        def second(cols):
            part = contract(dgate, wg[cols, :], ((1,), (1,)))
            part = (part + contract(dup, wu[cols, :], ((1,), (1,)))).astype(low)
            half = part.shape[0] // 2
            twin_target[:, cols] = part[:half]
            own_target[:, cols] = part[half:]

        for_tiles(width, width // 2, second)

    def both(place, span):
        return own_buf[place, span, :].astype(wide) + twin_buf[place, span, :].astype(wide)

    spans = [(k, pl.ds(k * rows, rows)) for k in range(chunks)]
    for loads in blocks:
        wait_all(loads)
    inners = inner_s[...].reshape(-1, columns)
    x_at = lax.axis_index("x")
    down_rows = down_own.shape[0]

    def down_tile(j):
        span = slice(j * (width // 4), (j + 1) * (width // 4))
        part = contract(inners, gx[:, :, span].reshape(-1, width // 4), ((0,), (0,))).astype(low)
        down_s[...] = part
        at = pl.multiple_of(x_at * down_rows, 16)
        down_own[:, span] = down_s[pl.ds(at, down_rows), :]
        at = pl.multiple_of(other(x_at) * down_rows, 16)
        down_across[:, span] = down_s[pl.ds(at, down_rows), :]

    for j in range(4):
        down_tile(j)
        if j % 2:
            steps_x[j // 2].start()
    wait_all(downs)
    for i in range(4):
        twin_place, own_place = pairs[2 * i][1], pairs[2 * i + 1][1]
        term(i, twin_out.at[i], own_buf.at[own_place])
        start(twin_out.at[i], twin_buf.at[twin_place], 3 + i, 0, twin)
        if i >= 1:
            block_arrived(2 + i)
        if i == 1:
            for k, span in spans:
                far_out[span, :] = both(far_at, span).astype(low)
                start(far_out.at[span], far_in.at[span], 0, k, side)
        if i == 2:
            down_step(0)
            for k, span in spans:
                side_out[span, :] = both(side_at, span).astype(low)
                start(side_out.at[span], side_in.at[span], 1, k, side)
    block_arrived(6)
    all_loads = [
        pltpu.make_async_copy(all_ref.at[pairs[i][0]], gx.at[i], all_sems.at[i]) for i in range(8)
    ]
    for load in all_loads:
        load.start()
    stores = []

    def output_term(pair):
        span = pl.ds(2 * pair, 2)
        if pair:
            wait_all(stores[2 * pair - 2 :])
        inner = inner_s[span].reshape(-1, columns)

        def tile(cols):
            part = jnp.dot(inner, wd[:, cols], preferred_element_type=wide)
            terms_s[:, :, cols] = part.astype(low).reshape(2, -1, width // 2)

        for_tiles(width, width // 2, tile)
        for i in range(2):
            _, place, is_twin = pairs[2 * pair + i]
            store = pltpu.make_async_copy(
                terms_s.at[i],
                (terms_twin if is_twin else terms_own).at[place],
                terms_sems.at[2 * pair + i],
            )
            store.start()
            stores.append(store)

    for i in range(2):
        output_term(i)
    for k, span in spans:
        arrived(0, k)
        near_out[span, :] = (both(near_at, span) + far_in[span, :].astype(wide)).astype(low)
        start(near_out.at[span], near_in.at[span], 2, k, near)
    down_step(1)
    for i in range(2, 4):
        output_term(i)
    wait_all(all_loads)
    dgates = a_s[...].reshape(-1, columns)
    dups = b_s[...].reshape(-1, columns)

    half = width // 2
    for gate_ref, up_ref, at in ((gate_across, up_across, other(x_at)), (gate_own, up_own, x_at)):
        for j in range(2):
            cols = pl.ds(pl.multiple_of(at * half + j * (half // 2), 128), half // 2)
            rows_out = slice(j * (half // 2), (j + 1) * (half // 2))
            x = gx[:, :, cols].reshape(-1, half // 2)
            gate_ref[rows_out, :] = contract(x, dgates, ((0,), (0,))).astype(low)
            up_ref[rows_out, :] = contract(x, dups, ((0,), (0,))).astype(low)
    for k, span in spans:
        arrived(1, k)
        arrived(2, k)
        out_ref[span, :] = (
            both(me, span) + side_in[span, :].astype(wide) + near_in[span, :].astype(wide)
        )
    wait_all(stores[6:])
    for copy in steps_h:
        copy.wait()
    part_rows = came_h.shape[0]
    mine = down_own[pl.ds(pl.multiple_of(at_h * part_rows, 16), part_rows), :]
    down_sum[...] = mine.astype(wide) + came_h[...].astype(wide)
    for copy in copies + steps_x:
        copy.wait_send()


def feed_back(grad_all, a, b, inner, all_two, gate_pieces, up_pieces, down_parts, number):
    count, width = a.shape[1], all_two.shape[2]
    columns = a.shape[2]
    chunks = 4 if count % 64 == 0 else 1
    row, part = (8, count, width), (8, count, columns)
    sem = pltpu.SemaphoreType.DMA
    block = pltpu.VMEM((count, width), low)
    vmem = pl.BlockSpec(memory_space=pltpu.VMEM)
    flops = 2 * 8 * count * width * columns * 6
    args = [grad_all.reshape(row), a, b, inner, all_two, *gate_pieces, *up_pieces]
    args += [piece for parts in down_parts for piece in parts]
    own_rows = down_parts[0][0].shape[0]
    return pl.pallas_call(
        functools.partial(feed_back_kernel, True, chunks),
        in_specs=[in_hbm()] * len(args),
        out_specs=[vmem, in_hbm(), in_hbm()] + [vmem] * 6 + [in_hbm()],
        out_shape=[jax.ShapeDtypeStruct((count, width), wide)]
        + [jax.ShapeDtypeStruct((4, count, width), low)] * 2
        + [jax.ShapeDtypeStruct((width // 2, columns), low)] * 4
        + [jax.ShapeDtypeStruct((own_rows, width), wide)]
        + [jax.ShapeDtypeStruct((2 * own_rows, width), low)] * 2,
        scratch_shapes=[
            pltpu.VMEM((2 * own_rows, width), low),
            pltpu.VMEM((2 * own_rows, width // 2), low),
            pltpu.VMEM((own_rows, width), low),
            pltpu.VMEM(row, low),
            pltpu.VMEM((width, columns), low),
            pltpu.VMEM((width, columns), low),
            pltpu.VMEM((columns, width), low),
            pltpu.VMEM(part, low),
            pltpu.VMEM(part, low),
            pltpu.VMEM(part, low),
            pltpu.VMEM((2, count, width), low),
            pltpu.VMEM((4, count, width), low),
            pltpu.VMEM((4, count, width), low),
            pltpu.VMEM((4, count, width), low),
            pltpu.VMEM((columns, width // 4), low),
        ]
        + [block] * 6
        + [
            sem((7, chunks)),
            sem((7, chunks)),
            sem((16,)),
            sem((8,)),
            sem((8, 4)),
            sem((8,)),
            sem((8,)),
            sem((3, 4)),
        ],
        compiler_params=pltpu.CompilerParams(
            collective_id=number, has_side_effects=True, vmem_limit_bytes=60 * 1024 * 1024
        ),
        cost_estimate=pl.CostEstimate(
            flops=flops, bytes_accessed=100 * 1024 * 1024, transcendentals=0
        ),
        name="feed_back",
    )(*args)


def scatter_kernel(even, chunks, n, kinds, *refs):
    m = len(kinds)
    terms, more, refs = refs[:n], refs[n : n + m], refs[n + m :]
    outs, more_out, refs = refs[:n], refs[n : n + m], refs[n + m :]
    bufs, (sends, recvs, local_sems, more_sems) = refs[: 8 * n], refs[8 * n :]
    beside = Beside(kinds, more, more_out, more_sems)
    bufs = [bufs[8 * a : 8 * a + 8] for a in range(n)]
    c, l, y, near, side, twin = row_peers(even)
    rows = outs[0].shape[0] // chunks
    me = l * 2 + y
    near_at, side_at = near["l"] * 2 + near["y"], side["l"] * 2 + side["y"]
    far_at = other(l) * 2 + other(y)
    greet([near, side, twin] + beside.peers)
    beside.start()
    copies = []

    def start(source, target, a, slot, k, peer):
        copy = remote(source, target, sends.at[a, slot, k], recvs.at[a, slot, k], peer)
        copy.start()
        copies.append(copy)

    parts = [(a, k, pl.ds(k * rows, rows)) for k in range(chunks) for a in range(n)]
    twin_side, twin_near = (near_at, side_at) if even else (side_at, near_at)
    for slot, place in ((3, far_at), (4, twin_side), (5, twin_near), (6, me)):
        for a, k, span in parts:
            start(
                terms[a].at[other(c) * 4 + place, span], bufs[a][1].at[place, span], a, slot, k, twin
            )
    loads = []
    for slot, place in ((0, far_at), (1, side_at), (2, near_at), (3, me)):
        for a in range(n):
            load = pltpu.make_async_copy(
                terms[a].at[c * 4 + place], bufs[a][0].at[place], local_sems.at[a, slot]
            )
            load.start()
            loads.append(load)

    def arrived(a, slot, k):
        span = bufs[a][5].at[pl.ds(k * rows, rows)]
        remote(span, span, sends.at[a, slot, k], recvs.at[a, slot, k], twin).wait_recv()

    def both(a, place, span):
        own, came = bufs[a][0], bufs[a][1]
        return own[place, span, :].astype(wide) + came[place, span, :].astype(wide)

    for load in loads[: 2 * n]:
        load.wait()
    for a, k, span in parts:
        far_out, far_in = bufs[a][2], bufs[a][5]
        arrived(a, 3, k)
        far_out[span, :] = both(a, far_at, span).astype(low)
        start(far_out.at[span], far_in.at[span], a, 0, k, side)
    for a, k, span in parts:
        side_out, side_in = bufs[a][3], bufs[a][6]
        arrived(a, 4, k)
        side_out[span, :] = both(a, side_at, span).astype(low)
        start(side_out.at[span], side_in.at[span], a, 1, k, side)
    for load in loads[2 * n :]:
        load.wait()
    for a, k, span in parts:
        near_out, far_in, near_in = bufs[a][4], bufs[a][5], bufs[a][7]
        arrived(a, 5, k)
        arrived(a, 0, k)
        near_out[span, :] = (both(a, near_at, span) + far_in[span, :].astype(wide)).astype(low)
        start(near_out.at[span], near_in.at[span], a, 2, k, near)
    for a, k, span in parts:
        arrived(a, 6, k)
        arrived(a, 1, k)
        outs[a][span, :] = both(a, me, span) + bufs[a][6][span, :].astype(wide)
    for a, k, span in parts:
        arrived(a, 2, k)
        outs[a][span, :] += bufs[a][7][span, :].astype(wide)
    for copy in copies:
        copy.wait_send()
    beside.wait()


def scatter_row(number, *terms, even=False, kinds=(), more=()):
    if lax.axis_size("l") != 2:
        return [
            lax.psum_scatter(t.astype(wide), group, scatter_dimension=0, tiled=True) for t in terms
        ]
    terms = [t.reshape(8, -1, t.shape[1]) for t in terms]
    n, count = len(terms), terms[0].shape[1]
    chunks = 4 if count % 64 == 0 else 1
    scratch = []
    for t in terms:
        scratch += [pltpu.VMEM((4, count, t.shape[2]), low)] * 2
        scratch += [pltpu.VMEM((count, t.shape[2]), low)] * 6
    return pl.pallas_call(
        functools.partial(scatter_kernel, even, chunks, n, kinds),
        in_specs=[in_hbm()] * (n + len(more)),
        out_specs=[pl.BlockSpec(memory_space=pltpu.VMEM)] * n + [in_hbm()] * len(more),
        out_shape=[jax.ShapeDtypeStruct((count, t.shape[2]), wide) for t in terms]
        + [jax.ShapeDtypeStruct(a.shape, low) for a in more],
        scratch_shapes=scratch
        + [
            pltpu.SemaphoreType.DMA((n, 7, chunks)),
            pltpu.SemaphoreType.DMA((n, 7, chunks)),
            pltpu.SemaphoreType.DMA((n, 4)),
            pltpu.SemaphoreType.DMA((2, max(1, len(more)))),
        ],
        compiler_params=pltpu.CompilerParams(
            collective_id=number, has_side_effects=True, vmem_limit_bytes=24 * 1024 * 1024
        ),
        cost_estimate=pl.CostEstimate(flops=0, bytes_accessed=80 * 1024 * 1024, transcendentals=0),
        name="scatter_row",
    )(*terms, *more)


class SumColumns:
    def __init__(self, mine_ref, across_ref, land_ref, out_ref, mine, stage, came_h, sems, local_sems):
        self.h = lax.axis_index("h")
        over_x, self.over_h = {"x": other(lax.axis_index("x"))}, {"h": other(self.h)}
        self.land_ref, self.out_ref = land_ref, out_ref
        self.mine, self.stage, self.came_h = mine, stage, came_h
        self.sems, self.local_sems = sems, local_sems
        rows = mine.shape[2] // 2
        self.parts = [(c, pl.ds(i * rows, rows)) for c in range(2) for i in range(2)]
        self.steps_x = [
            remote(
                across_ref.at[c, :, s], land_ref.at[c, :, s], sems.at[0, i], sems.at[1, i], over_x
            )
            for i, (c, s) in enumerate(self.parts)
        ]
        self.steps_h = []
        self.load = pltpu.make_async_copy(mine_ref, mine, local_sems.at[0])

    def start(self):
        for copy in self.steps_x:
            copy.start()
        self.load.start()

    def step(self, i):
        c, s = self.parts[i]
        if i == 0:
            self.load.wait()
        self.steps_x[i].wait_recv()
        take = pltpu.make_async_copy(self.land_ref.at[c, :, s], self.stage, self.local_sems.at[1])
        take.start()
        take.wait()
        total = self.mine[c, :, s].astype(wide) + self.stage[...].astype(wide)
        self.mine[c, :, s] = total.astype(low)
        copy = remote(
            self.mine.at[c, other(self.h), s], self.came_h.at[c, s], self.sems.at[0, 4 + i],
            self.sems.at[1, 4 + i], self.over_h,
        )
        copy.start()
        self.steps_h.append(copy)

    def end(self):
        for (c, s), copy in zip(self.parts, self.steps_h):
            copy.wait()
            total = self.mine[c, self.h, s].astype(wide) + self.came_h[c, s].astype(wide)
            self.out_ref[c, s] = total.astype(low)
        for copy in self.steps_x:
            copy.wait_send()


def middle_kernel(heads, tile, scale, chunks, *refs):
    ends_ref, branch_ref, gate_mine, gate_across, up_mine, up_across, terms_own, terms_twin = refs[:8]
    query_ref, mixed_ref, packed_ref, logs_ref, cos_in, sin_in, out_in, up_in = refs[8:16]
    resid_ref, refs = refs[16], refs[17:]
    dlow_out, dkv_out, gate_out, up_out, final_ref, by_h_ref, head_out = refs[:7]
    land_gate, land_up, land_twin, refs = *refs[7:10], refs[10:]
    xs, kv, q, o, logs, cos_ref, sin_ref, out_own, up_query, dq, dlow, dkv_sum, dkv = refs[:13]
    refs = refs[13:]
    scatter_bufs, refs = (refs[:7], refs[7:14]), refs[14:]
    stage_a, stage_b, stage_c, sp_far, sp_side, sp_near, sp_far_in, sp_side_in, sp_near_in = refs[:9]
    refs = refs[9:]
    gate_own, gate_h, up_own, up_h, column_stage, refs = *refs[:5], refs[5:]
    go, came_o, came_y, gh, came_hx, came_hh, refs = *refs[:6], refs[6:]
    sends, recvs, sc_sends, sc_recvs, sp_sems, gate_sems, up_sems = refs[:7]
    chain_sems, load_sems, block_sems, local_sems = refs[7:]
    x, h, y_at = [lax.axis_index(a) for a in ("x", "h", "y")]
    c, l, y, near, side, twin = row_peers(False)
    count = branch_ref.shape[0]
    rows = count // chunks
    width = up_query.shape[1] // heads
    half, low_width = width // 2, up_query.shape[0]
    over_x, over_h, over_y = {"x": other(x)}, {"h": other(h)}, {"y": other(y)}
    me = l * 2 + y
    near_at, side_at = near["l"] * 2 + near["y"], side["l"] * 2 + side["y"]
    far_at = other(l) * 2 + other(y)
    flow = RowGather(True, chunks, branch_ref, xs, sends, recvs)
    gate = SumColumns(
        gate_mine, gate_across, land_gate, gate_out, gate_own, column_stage, gate_h, gate_sems,
        local_sems.at[0],
    )
    up = SumColumns(
        up_mine, up_across, land_up, up_out, up_own, column_stage, up_h, up_sems, local_sems.at[1]
    )
    greet([near, side, twin, over_x, over_h])
    flow.begin(None)
    sp_twin = remote(terms_twin, land_twin, sp_sems.at[0, 0], sp_sems.at[1, 0], twin)
    sp_twin.start()
    gate.start()
    up.start()
    own_load = pltpu.make_async_copy(branch_ref, xs.at[flow.me], load_sems.at[0])
    own_load.start()
    loads = [
        pltpu.make_async_copy(source, target, load_sems.at[1 + i])
        for i, (source, target) in enumerate(
            (
                (packed_ref.at[:, pl.ds(low_width, 2 * width)], kv), (query_ref, q), (mixed_ref, o),
                (logs_ref, logs), (cos_in, cos_ref), (sin_in, sin_ref), (out_in, out_own),
                (up_in, up_query),
            )
        )
    ]
    for load in loads:
        load.start()

    sp_copies = [sp_twin]

    def sp_pair(place):
        first = pltpu.make_async_copy(terms_own.at[place], stage_a, local_sems.at[2, 0])
        second = pltpu.make_async_copy(land_twin.at[place], stage_b, local_sems.at[2, 1])
        first.start()
        second.start()
        first.wait()
        second.wait()
        return stage_a[...].astype(wide) + stage_b[...].astype(wide)

    def sp_send(total, buf, target, slot, peer):
        buf[...] = total.astype(low)
        copy = remote(buf, target, sp_sems.at[0, slot], sp_sems.at[1, slot], peer)
        copy.start()
        sp_copies.append(copy)

    def sp_arrived(slot):
        remote(sp_far, sp_far_in, sp_sems.at[0, slot], sp_sems.at[1, slot], twin).wait_recv()

    dkv_sum[...] = jnp.zeros_like(dkv_sum)
    flow.take_near()
    gate.step(0)
    flow.take_side()
    sp_twin.wait_recv()
    sp_send(sp_pair(far_at), sp_far, sp_far_in, 1, side)
    sp_send(sp_pair(side_at), sp_side, sp_side_in, 2, side)
    gate.step(1)
    flow.take(3)
    flow.take(4)
    gate.step(2)
    flow.take_far()
    flow.take(5)
    gate.step(3)
    flow.take(6)
    own_load.wait()
    wait_all(loads)

    def grad_out(at):
        cols = pl.ds(pl.multiple_of(at * 256, 256), 256)
        for j in range(2):
            span = slice(j * 1024, (j + 1) * 1024)
            branch = xs[:, :, span].reshape(-1, 1024)
            go[at, :, span] = contract(o[:, cols], branch, ((0,), (0,))).astype(low)

    grad_out(other(x))
    out_x = remote(go.at[other(x)], came_o, chain_sems.at[0, 0], chain_sems.at[1, 0], over_x)
    out_x.start()
    grad_out(x)

    def block_rows(begin, size):
        first, offset = begin // count, begin % count
        got = min(size, count - offset)
        parts = [xs[first, offset : offset + got, :]]
        if got < size:
            parts.append(xs[first + 1, : size - got, :])
        return jnp.concatenate(parts, axis=0) if len(parts) > 1 else parts[0]

    def attention(i):
        span, length = slice(i * tile, (i + 1) * tile), (i + 1) * tile
        mask = tile_mask(ends_ref, i * tile, tile, length, heads)
        queries = stacked(q, span, heads, width)
        dmixed = contract(block_rows(i * tile, tile), out_own[...], ((1,), (1,))).astype(low)
        grads = jnp.concatenate(
            [dmixed[:, j * width : (j + 1) * width] for j in range(heads)], axis=0
        )
        outs = stacked(o, span, heads, width)
        delta = jnp.sum(grads.astype(wide) * outs.astype(wide), axis=1, keepdims=True)
        log = jnp.concatenate([logs[j, span, :1] for j in range(heads)], axis=0)
        keys, values = kv[:length, :width], kv[:length, width:]
        scores = contract(queries, keys, ((1,), (1,)))
        weights = jnp.where(mask, jnp.exp(scores - log), 0.0)
        dprob = contract(grads, values, ((1,), (1,)))
        dscore = (weights * (dprob - delta)).astype(low)
        dkv_sum[:length, width:] += contract(weights.astype(low), grads, ((0,), (0,)))
        dkv_sum[:length, :width] += contract(dscore, queries, ((0,), (0,)))
        dquery = contract(dscore, keys, ((1,), (0,))) * scale
        cosine, sine = cos_ref[span, :], sin_ref[span, :]
        for j in range(heads):
            a = dquery[j * tile : (j + 1) * tile, :half]
            b = dquery[j * tile : (j + 1) * tile, half:]
            at = j * width
            dq[span, at : at + half] = (a * cosine + b * sine).astype(low)
            dq[span, at + half : at + width] = (b * cosine - a * sine).astype(low)
        dlow[span, :] = contract(dq[span, :], up_query[...], ((1,), (1,))).astype(low)

    for i in range(q.shape[0] // tile):
        attention(i)
        if i == 3:
            up.step(0)
        if i == 4:
            sp_arrived(1)
            sp_send(
                sp_pair(near_at) + sp_far_in[...].astype(wide), sp_near, sp_near_in, 3, near
            )
    dkv[...] = dkv_sum[...].astype(low)
    flow.end()
    latents = [
        pltpu.make_async_copy(
            packed_ref.at[pl.ds(i * count, count), pl.ds(0, low_width)],
            xs.at[i, :, pl.ds(0, low_width)],
            block_sems.at[i],
        )
        for i in range(8)
    ]
    for load in latents:
        load.start()

    sc_copies = []
    terms = (dlow, dkv)
    sc_parts = [(a, k, pl.ds(k * rows, rows)) for k in range(chunks) for a in range(2)]

    def sc_start(source, target, a, slot, k, peer):
        copy = remote(source, target, sc_sends.at[a, slot, k], sc_recvs.at[a, slot, k], peer)
        copy.start()
        sc_copies.append(copy)

    def sc_arrived(a, slot, k):
        span = scatter_bufs[a][4].at[pl.ds(k * rows, rows)]
        remote(span, span, sc_sends.at[a, slot, k], sc_recvs.at[a, slot, k], twin).wait_recv()

    def term_rows(core, place, k):
        return pl.ds(pl.multiple_of((core * 4 + place) * count + k * rows, 16), rows)

    for slot, place in ((3, far_at), (4, side_at), (5, near_at), (6, me)):
        for a, k, span in sc_parts:
            sc_start(
                terms[a].at[term_rows(other(c), place, k)], scatter_bufs[a][0].at[place, span], a,
                slot, k, twin,
            )

    up.step(1)

    def both(a, place, k, span):
        own = terms[a][term_rows(c, place, k), :]
        return own.astype(wide) + scatter_bufs[a][0][place, span, :].astype(wide)

    for a, k, span in sc_parts:
        far_out, far_in = scatter_bufs[a][1], scatter_bufs[a][4]
        sc_arrived(a, 3, k)
        far_out[span, :] = both(a, far_at, k, span).astype(low)
        sc_start(far_out.at[span], far_in.at[span], a, 0, k, side)
    up.step(2)
    for a, k, span in sc_parts:
        side_out, side_in = scatter_bufs[a][2], scatter_bufs[a][5]
        sc_arrived(a, 4, k)
        side_out[span, :] = both(a, side_at, k, span).astype(low)
        sc_start(side_out.at[span], side_in.at[span], a, 1, k, side)
    wait_all(latents)
    dqs = dq[...]

    def grad_heads(at):
        cols = pl.ds(pl.multiple_of(at * (low_width // 2), 128), low_width // 2)
        latent = xs[:, :, cols].reshape(-1, low_width // 2)
        gh[at] = contract(latent, dqs, ((0,), (0,))).astype(low).reshape(gh.shape[1:])

    grad_heads(other(x))
    head_x = remote(gh.at[other(x)], came_hx, chain_sems.at[0, 1], chain_sems.at[1, 1], over_x)
    head_x.start()
    grad_heads(x)
    up.step(3)
    for a, k, span in sc_parts:
        near_out, far_in, near_in = scatter_bufs[a][3], scatter_bufs[a][4], scatter_bufs[a][6]
        sc_arrived(a, 5, k)
        sc_arrived(a, 0, k)
        near_out[span, :] = (both(a, near_at, k, span) + far_in[span, :].astype(wide)).astype(low)
        sc_start(near_out.at[span], near_in.at[span], a, 2, k, near)
    out_x.wait_recv()
    total = go[x].astype(wide) + came_o[...].astype(wide)
    go[x] = total.astype(low)
    part = by_h_ref.shape[1]
    mine_rows = pl.ds(pl.multiple_of(y * part, part), part)
    their_rows = pl.ds(pl.multiple_of(other(y) * part, part), part)
    out_y = remote(
        go.at[x, their_rows], came_y, chain_sems.at[0, 2], chain_sems.at[1, 2], over_y
    )
    out_y.start()
    head_x.wait_recv()
    gh[x] = (gh[x].astype(wide) + came_hx[...].astype(wide)).astype(low)
    head_h = remote(
        gh.at[x, :, other(h)], came_hh, chain_sems.at[0, 3], chain_sems.at[1, 3], over_h
    )
    head_h.start()
    sp_arrived(2)
    sp_arrived(3)
    resid_load = pltpu.make_async_copy(resid_ref, stage_c, local_sems.at[2, 0])
    resid_load.start()
    resid_load.wait()
    total = sp_pair(me) + sp_side_in[...].astype(wide) + sp_near_in[...].astype(wide)
    final_ref[...] = (stage_c[...] + total).astype(low)
    gate.end()
    outs = (dlow_out, dkv_out)
    for a, k, span in sc_parts:
        sc_arrived(a, 6, k)
        sc_arrived(a, 1, k)
        outs[a][span, :] = both(a, me, k, span) + scatter_bufs[a][5][span, :].astype(wide)
    for a, k, span in sc_parts:
        sc_arrived(a, 2, k)
        outs[a][span, :] += scatter_bufs[a][6][span, :].astype(wide)
    by_h_ref[y] = go[x, mine_rows, :]
    out_y.wait_recv()
    by_h_ref[other(y)] = came_y[...]
    head_h.wait_recv()
    head_out[...] = (gh[x, :, h].astype(wide) + came_hh[...].astype(wide)).astype(low)
    up.end()
    for copy in sp_copies + sc_copies + [out_x, out_y, head_x, head_h]:
        copy.wait_send()


def middle(
    ends, branch, gate_terms, up_terms, spread, query, mixed, packed, logs, cosine, sine, out_own,
    up_query, resid, heads, scale, number,
):
    count, width = branch.shape
    length, columns = query.shape
    low_width = up_query.shape[0]
    chunks = 4
    args = [
        ends, branch, *gate_terms, *up_terms, *spread, query, mixed, packed, logs, cosine, sine,
        out_own, up_query, resid,
    ]
    kept = (2,) + gate_terms[0].shape[2:]
    part = columns // 4
    rows_up = low_width // 8
    vmem, sem = pl.BlockSpec(memory_space=pltpu.VMEM), pltpu.SemaphoreType.DMA
    shapes = [
        ((count, low_width), wide),
        ((count, columns), wide),
        (kept, low),
        (kept, low),
        ((count, width), low),
        ((2, part, width), low),
        ((2, rows_up, columns), low),
        (gate_terms[0].shape, low),
        (up_terms[0].shape, low),
        (spread[0].shape, low),
    ]
    block = pltpu.VMEM((count, width), low)

    def scatter_scratch(w):
        return [pltpu.VMEM((4, count, w), low)] + [pltpu.VMEM((count, w), low)] * 6

    return pl.pallas_call(
        functools.partial(middle_kernel, heads, tile_of(length), scale, chunks),
        in_specs=[pl.BlockSpec(memory_space=pltpu.SMEM)] + [in_hbm()] * (len(args) - 1),
        out_specs=[vmem] * 7 + [in_hbm()] * 3,
        out_shape=[jax.ShapeDtypeStruct(*s) for s in shapes],
        scratch_shapes=[
            pltpu.VMEM((8, count, width), low),
            pltpu.VMEM((length, columns), low),
            pltpu.VMEM((length, columns), low),
            pltpu.VMEM((length, columns), low),
            pltpu.VMEM(logs.shape, wide),
            pltpu.VMEM(cosine.shape, wide),
            pltpu.VMEM(sine.shape, wide),
            pltpu.VMEM(out_own.shape, low),
            pltpu.VMEM(up_query.shape, low),
            pltpu.VMEM((length, columns), low),
            pltpu.VMEM((length, low_width), low),
            pltpu.VMEM((length, columns), wide),
            pltpu.VMEM((length, columns), low),
            *scatter_scratch(low_width),
            *scatter_scratch(columns),
            block,
            block,
            pltpu.VMEM((count, width), wide),
            *[block] * 6,
            pltpu.VMEM(gate_terms[0].shape, low),
            pltpu.VMEM(kept, low),
            pltpu.VMEM(up_terms[0].shape, low),
            pltpu.VMEM(kept, low),
            pltpu.VMEM((2, kept[1] // 2, kept[2]), low),
            pltpu.VMEM((2, columns // 2, width), low),
            pltpu.VMEM((columns // 2, width), low),
            pltpu.VMEM((part, width), low),
            pltpu.VMEM((2, 2, 2, rows_up, columns), low),
            pltpu.VMEM((2, 2, rows_up, columns), low),
            pltpu.VMEM((2, rows_up, columns), low),
            sem((7, chunks)),
            sem((7, chunks)),
            sem((2, 7, chunks)),
            sem((2, 7, chunks)),
            sem((2, 4)),
            sem((2, 8)),
            sem((2, 8)),
            sem((2, 4)),
            sem((9,)),
            sem((8,)),
            sem((3, 2)),
        ],
        compiler_params=pltpu.CompilerParams(
            collective_id=number, has_side_effects=True, vmem_limit_bytes=63 * 1024 * 1024
        ),
        cost_estimate=pl.CostEstimate(
            flops=18 * length * length * columns,
            bytes_accessed=200 * 1024 * 1024,
            transcendentals=length * length * heads // 2,
        ),
        name="middle",
    )(*args)


def norm_back_rows(incoming, source, gain):
    scale = rms_scale(source)
    weighted = incoming * gain
    mean = jnp.mean(weighted * source, axis=-1, keepdims=True)
    grad = scale * weighted - source * (scale * scale * scale) * mean
    return grad, jnp.sum(incoming * source * scale, axis=0, keepdims=True)


def shut_kernel(part, head_dim, order, n_in, n_out, *refs):
    ins, outs, refs = refs[:n_in], refs[n_in : n_in + n_out], refs[n_in + n_out :]
    (
        dlow_ref, dkv_ref, latent_ref, gain_latent_ref, cos_ref, sin_ref, hidden_ref, in_full_ref,
        home_ref, gain_one_ref, dresid_ref, gain_two_ref, gate_ref, up_ref, heads_ref, final_ref,
        kept_ref, across_ref,
    ) = ins
    sum_ref, tokens_ref, output_ref, gate_out, up_out, heads_out, out_ref = outs
    full, mapped, terms, gains, twin_buf, held, came, moved, swap_buf = refs[:9]
    gate_in, up_in, heads_in, final_buf, across_in = refs[9:14]
    sends, recvs, set_sends, set_recvs, swap_sems, local_sems = refs[14:]
    x, c, h, l, y = [lax.axis_index(a) for a in every]
    hops = {
        1: {"h": other(h)},
        2: {"l": other(l)},
        4: {"y": other(y)},
        8: {"x": other(x)},
    }
    twin = {"c": other(c)}
    cross = {"c": other(c), "h": other(h)}
    me = (c * 2 + l) * 2 + y

    def group_peer(k):
        return {"c": other(c, k // 4), "l": other(l, k // 2 % 2), "y": other(y, k % 2)}

    def group_index(k):
        peer = group_peer(k)
        return (peer["c"] * 2 + peer["l"]) * 2 + peer["y"]

    def index(code, core):
        at_x, at_l = other(x, code // 8 % 2), other(l, code // 2 % 2)
        return (((at_x * 2 + core) * 2 + other(h, code % 2)) * 2 + at_l) * 2 + other(y, code // 4 % 2)

    load = pltpu.make_async_copy(in_full_ref, full, local_sems.at[0])
    load.start()
    greet([hops[1], hops[8], cross] + [group_peer(k) for k in range(1, 8)])
    set_copies = []
    for i, (source, target) in enumerate(
        ((heads_ref, heads_in), (gate_ref, gate_in), (up_ref, up_in))
    ):
        for k in range(1, 8):
            copy = remote(
                source.at[group_index(k)], target.at[me], set_sends.at[i, k], set_recvs.at[i, k],
                group_peer(k),
            )
            copy.start()
            set_copies.append(copy)
    set_loads = [
        pltpu.make_async_copy(source.at[me], target.at[me], local_sems.at[1 + i])
        for i, (source, target) in enumerate(
            ((heads_ref, heads_in), (gate_ref, gate_in), (up_ref, up_in))
        )
    ]
    for copy in set_loads:
        copy.start()
    exchange = remote(across_ref, across_in, swap_sems.at[0], swap_sems.at[1], hops[1])
    output_move = remote(final_ref, output_ref, swap_sems.at[2], swap_sems.at[3], cross)
    tokens_move = remote(swap_buf, moved, swap_sems.at[4], swap_sems.at[5], cross)
    final_load = pltpu.make_async_copy(final_ref, final_buf, local_sems.at[4])
    final_store = pltpu.make_async_copy(final_buf, output_ref, local_sems.at[5])

    @pl.when(c != h)
    def _():
        output_move.start()

    @pl.when(c == h)
    def _():
        final_load.start()

    width, low_width = hidden_ref.shape[1], latent_ref.shape[1]
    half = head_dim // 2
    dlatent, dgain_latent = norm_back_rows(dlow_ref[...], latent_ref[...], gain_latent_ref[...])
    mapped[:, :low_width] = dlatent.astype(low)
    a, b = dkv_ref[:, :half], dkv_ref[:, half:head_dim]
    cosine, sine = cos_ref[...], sin_ref[...]
    mapped[:, low_width : low_width + half] = (a * cosine + b * sine).astype(low)
    mapped[:, low_width + half : low_width + head_dim] = (b * cosine - a * sine).astype(low)
    mapped[:, low_width + head_dim : low_width + 2 * head_dim] = dkv_ref[:, head_dim:].astype(low)
    mapped[:, low_width + 2 * head_dim :] = jnp.zeros((mapped.shape[0], 128), low)
    load.wait()
    dmapped = mapped[...]
    weights = full[...].reshape(width, -1)
    dhidden = contract(dmapped, weights, ((1,), (1,)))
    dinput, dgain_one = norm_back_rows(dhidden, home_ref[...].astype(wide), gain_one_ref[...])
    dtokens = dresid_ref[...] + dinput
    tokens_ref[...] = dtokens
    swap_buf[...] = dtokens.astype(low)

    gains[...] = jnp.zeros_like(gains)
    gains[0:1, :width] = dgain_one
    gains[1:2, :width] = gain_two_ref[...]
    gains[2:3, :low_width] = dgain_latent
    rows = terms.shape[1]
    low_part = low_width // 32
    used = low_width + 2 * head_dim
    for at in range(0, 32, 4):
        left = hidden_ref[:, at * rows : (at + 4) * rows]
        block = contract(left, dmapped[:, :used], ((0,), (0,))).astype(low)
        terms[at : at + 4, :, :used] = block.reshape(4, rows, used)
        for i in range(at, at + 4):
            tile = jnp.concatenate(
                [
                    gains[0:2, i * rows : i * rows + 128],
                    gains[2:3, i * low_part : i * low_part + 128],
                    jnp.zeros((rows - 3, 128), wide),
                ],
                axis=0,
            )
            terms[i, :, used:] = tile.astype(low)
    copies = []

    def start(source, target, slot, peer):
        copy = remote(source, target, sends.at[slot], recvs.at[slot], peer)
        copy.start()
        copies.append(copy)

    def arrived(slot):
        remote(came.at[0], came.at[0], sends.at[slot], recvs.at[slot], twin).wait_recv()

    for code in range(15, -1, -1):
        start(terms.at[index(code, 1 - c)], twin_buf.at[code], 16 + code, twin)
    for code in range(15, -1, -1):
        arrived(16 + code)
        total = terms[index(code, c)].astype(wide) + twin_buf[code].astype(wide)
        for hop in (8, 4, 2, 1):
            if code < hop:
                arrived(code + hop)
                total = total + came[code + hop].astype(wide)
        if code == 0:
            sum_ref[...] = total
        else:
            held[code] = total.astype(low)
            hop = 1 << (code.bit_length() - 1)
            start(held.at[code], came.at[code], code, hops[hop])
        if code == 8:

            @pl.when(c != h)
            def _():
                tokens_move.start()

            exchange.start()

        if code == 4:
            for copy in set_loads:
                copy.wait()
            for copy in set_copies:
                copy.wait()
            for source, target in ((gate_in, gate_out), (up_in, up_out)):
                for place, blocks in enumerate(order):
                    for j, block in enumerate(blocks):
                        target[:, block * part : (block + 1) * part] = source[
                            place, :, j * part : (j + 1) * part
                        ].astype(wide)
            for place in range(8):
                core, at_l, at_y = place // 4, place // 2 % 2, place % 2
                for j in range(2):
                    head = ((j * 2 + core) * 2 + at_y) * 2 + at_l
                    heads_out[:, head * head_dim : (head + 1) * head_dim] = heads_in[
                        place, :, j * head_dim : (j + 1) * head_dim
                    ].astype(wide)
    exchange.wait()
    out_ref[...] = kept_ref[...].astype(wide) + across_in[...].astype(wide)
    for copy in copies:
        copy.wait_send()

    @pl.when(c != h)
    def _():
        output_move.wait()
        tokens_move.wait()
        tokens_ref[...] = moved[...].astype(wide)

    @pl.when(c == h)
    def _():
        final_load.wait()
        final_store.start()
        final_store.wait()


def shut(
    dlow, dkv, latent, gain_latent, cosine, sine, hidden, in_full, home, gain_one, dresid, dgain_two,
    gate_terms, up_terms, head_terms, final, kept, across, part, order, number,
):
    count, width = hidden.shape
    head_dim = dkv.shape[1] // 2
    rows, columns = in_full.shape[1:]
    vmem, sem = pl.BlockSpec(memory_space=pltpu.VMEM), pltpu.SemaphoreType.DMA
    args = [
        dlow, dkv, latent, gain_latent, cosine, sine, hidden, in_full, home, gain_one, dresid,
        dgain_two, gate_terms, up_terms, head_terms, final, kept, across,
    ]
    hbm = {7, 12, 13, 14, 15, 17}
    ff = len(order) * len(order[0]) * part
    shapes = [
        ((rows, columns), wide),
        ((count, width), wide),
        ((count, width), low),
        ((gate_terms.shape[1], ff), wide),
        ((up_terms.shape[1], ff), wide),
        ((head_terms.shape[1], 8 * head_terms.shape[2]), wide),
        (kept.shape, wide),
    ]
    blocks = pltpu.VMEM((16, rows, columns), low)
    return pl.pallas_call(
        functools.partial(shut_kernel, part, head_dim, order, len(args), len(shapes)),
        in_specs=[in_hbm() if i in hbm else vmem for i in range(len(args))],
        out_specs=[in_hbm() if i == 2 else vmem for i in range(len(shapes))],
        out_shape=[jax.ShapeDtypeStruct(*s) for s in shapes],
        scratch_shapes=[
            pltpu.VMEM(in_full.shape, low),
            pltpu.VMEM((count, columns), low),
            pltpu.VMEM(in_full.shape, low),
            pltpu.VMEM((16, width + 128), wide),
            blocks,
            blocks,
            blocks,
            pltpu.VMEM((count, width), low),
            pltpu.VMEM((count, width), low),
            pltpu.VMEM(gate_terms.shape, low),
            pltpu.VMEM(up_terms.shape, low),
            pltpu.VMEM(head_terms.shape, low),
            pltpu.VMEM((count, width), low),
            pltpu.VMEM(across.shape, low),
            sem((32,)),
            sem((32,)),
            sem((3, 8)),
            sem((3, 8)),
            sem((6,)),
            sem((6,)),
        ],
        compiler_params=pltpu.CompilerParams(
            collective_id=number, has_side_effects=True, vmem_limit_bytes=60 * 1024 * 1024
        ),
        cost_estimate=pl.CostEstimate(flops=0, bytes_accessed=150 * 1024 * 1024, transcendentals=0),
        name="shut",
    )(*args)


def split_kernel(part, order, a_ref, b_ref, a_out, b_out):
    for source, target in ((a_ref, a_out), (b_ref, b_out)):
        used, total = len(order[0]) * part, target.shape[2]
        for place, blocks in enumerate(order):
            for j, block in enumerate(blocks):
                target[place, :, j * part : (j + 1) * part] = source[
                    :, block * part : (block + 1) * part
                ]
            if used < total:
                target[place, :, used:] = jnp.zeros((target.shape[1], total - used), target.dtype)


def join_kernel(part, order, a_ref, b_ref, a_out, b_out):
    for source, target in ((a_ref, a_out), (b_ref, b_out)):
        for place, blocks in enumerate(order):
            for j, block in enumerate(blocks):
                target[:, block * part : (block + 1) * part] = source[
                    place, :, j * part : (j + 1) * part
                ].astype(wide)


def column_order(n_x, n_l):
    return [
        [
            (((x * 2 + c) * 2 + h) * n_l + l) * 2 + y
            for x in range(n_x)
            for h in range(2)
        ]
        for c in range(2)
        for l in range(n_l)
        for y in range(2)
    ]


def split_columns(a, b, part, order, total):
    shape = jax.ShapeDtypeStruct((len(order), a.shape[0], total), a.dtype)
    return pl.pallas_call(
        functools.partial(split_kernel, part, order), out_shape=[shape] * 2, name="split_columns"
    )(a, b)


def join_columns(a, b, part, order):
    shape = jax.ShapeDtypeStruct((a.shape[1], len(order) * len(order[0]) * part), wide)
    return pl.pallas_call(
        functools.partial(join_kernel, part, order), out_shape=[shape] * 2, name="join_columns"
    )(a, b)


def first_allowed(ends_ref, count, places):
    start = jnp.zeros_like(places)
    for j in range(count):
        end = ends_ref[j]
        start = jnp.where(places >= end, end, start)
    return jnp.where(places >= ends_ref[count - 1], places, start)


def contract(left, right, dims):
    return lax.dot_general(left, right, (dims, ((), ())), preferred_element_type=wide)


def stacked(ref, span, heads, width):
    return jnp.concatenate(
        [ref[span, j * width : (j + 1) * width] for j in range(heads)], axis=0
    )


def tile_mask(ends_ref, begin, tile, length, heads):
    rows = begin + lax.broadcasted_iota(jnp.int32, (tile, 1), 0)
    lows = first_allowed(ends_ref, ends_ref.shape[0], rows)
    rows = jnp.concatenate([rows] * heads, axis=0)
    lows = jnp.concatenate([lows] * heads, axis=0)
    columns = lax.broadcasted_iota(jnp.int32, (heads * tile, length), 1)
    return (columns >= lows) & (columns <= rows)


def attend_kernel(heads, tile, ends_ref, q_ref, k_ref, v_ref, o_ref, log_ref):
    width = k_ref.shape[1]
    for i in range(q_ref.shape[0] // tile):
        span, length = slice(i * tile, (i + 1) * tile), (i + 1) * tile
        mask = tile_mask(ends_ref, i * tile, tile, length, heads)
        scores = contract(stacked(q_ref, span, heads, width), k_ref[:length, :], ((1,), (1,)))
        scores = jnp.where(mask, scores, masked_value)
        top = jnp.max(scores, axis=1, keepdims=True)
        weights = jnp.exp(scores - top)
        total = jnp.sum(weights, axis=1, keepdims=True)
        mixed = contract(weights.astype(low), v_ref[:length, :], ((1,), (0,))) / total
        log = jnp.broadcast_to(top + jnp.log(total), (heads * tile, 128))
        for j in range(heads):
            part = slice(j * tile, (j + 1) * tile)
            o_ref[span, j * width : (j + 1) * width] = mixed[part].astype(low)
            log_ref[j, span, :] = log[part]


def attend_back_kernel(
    heads, tile, scale, ends_ref, q_ref, g_ref, o_ref, k_ref, v_ref, log_ref, cos_ref, sin_ref,
    dq_ref, dkv_ref, sum_ref,
):
    width = k_ref.shape[1]
    half = width // 2
    sum_ref[...] = jnp.zeros_like(sum_ref)
    for i in range(q_ref.shape[0] // tile):
        span, length = slice(i * tile, (i + 1) * tile), (i + 1) * tile
        mask = tile_mask(ends_ref, i * tile, tile, length, heads)
        queries = stacked(q_ref, span, heads, width)
        grads = stacked(g_ref, span, heads, width)
        outs = stacked(o_ref, span, heads, width)
        delta = jnp.sum(grads.astype(wide) * outs.astype(wide), axis=1, keepdims=True)
        log = jnp.concatenate([log_ref[j, span, :1] for j in range(heads)], axis=0)
        keys, values = k_ref[:length, :], v_ref[:length, :]
        scores = contract(queries, keys, ((1,), (1,)))
        weights = jnp.where(mask, jnp.exp(scores - log), 0.0)
        dprob = contract(grads, values, ((1,), (1,)))
        dscore = (weights * (dprob - delta)).astype(low)
        sum_ref[:length, width:] += contract(weights.astype(low), grads, ((0,), (0,)))
        sum_ref[:length, :width] += contract(dscore, queries, ((0,), (0,)))
        dquery = contract(dscore, keys, ((1,), (0,))) * scale
        cosine, sine = cos_ref[span, :], sin_ref[span, :]
        for j in range(heads):
            a = dquery[j * tile : (j + 1) * tile, :half]
            b = dquery[j * tile : (j + 1) * tile, half:]
            at = j * width
            dq_ref[span, at : at + half] = (a * cosine + b * sine).astype(low)
            dq_ref[span, at + half : at + width] = (b * cosine - a * sine).astype(low)
    dkv_ref[...] = sum_ref[...].astype(low)


def attend_whole_kernel(
    heads, tile, scale, ends_ref, packed_ref, up_ref, cos_ref, sin_ref, own_ref, other_ref,
    q_ref, o_ref, log_ref, terms_ref, out_ref,
):
    x = lax.axis_index("x")
    width = up_ref.shape[1] // heads
    half, low_width = width // 2, up_ref.shape[0]
    rows = own_ref.shape[0]
    out_ref[pl.ds(pl.multiple_of(x * rows, rows), rows), :] = own_ref[...]
    out_ref[pl.ds(pl.multiple_of(other(x) * rows, rows), rows), :] = other_ref[...]
    for i in range(q_ref.shape[0] // tile):
        span, length = slice(i * tile, (i + 1) * tile), (i + 1) * tile
        raw = jnp.dot(packed_ref[span, :low_width], up_ref[...], preferred_element_type=wide)
        cosine, sine = cos_ref[span, :] * scale, sin_ref[span, :] * scale
        queries = []
        for j in range(heads):
            a, b = turn(raw[:, j * width : (j + 1) * width], cosine, sine)
            q_ref[span, j * width : j * width + half] = a.astype(low)
            q_ref[span, j * width + half : (j + 1) * width] = b.astype(low)
        mask = tile_mask(ends_ref, i * tile, tile, length, heads)
        keys = packed_ref[:length, low_width : low_width + width]
        values = packed_ref[:length, low_width + width :]
        scores = contract(stacked(q_ref, span, heads, width), keys, ((1,), (1,)))
        scores = jnp.where(mask, scores, masked_value)
        top = jnp.max(scores, axis=1, keepdims=True)
        weights = jnp.exp(scores - top)
        total = jnp.sum(weights, axis=1, keepdims=True)
        mixed = contract(weights.astype(low), values, ((1,), (0,))) / total
        log = jnp.broadcast_to(top + jnp.log(total), (heads * tile, 128))
        for j in range(heads):
            part = slice(j * tile, (j + 1) * tile)
            o_ref[span, j * width : (j + 1) * width] = mixed[part].astype(low)
            log_ref[j, span, :] = log[part]
        terms_ref[span, :] = jnp.dot(
            o_ref[span, :], out_ref[...], preferred_element_type=wide
        ).astype(low)


def attend_whole(ends, packed, up_query, cosine, sine, own_heads, other_heads, heads, scale):
    length, width = packed.shape[0], own_heads.shape[1]
    columns = up_query.shape[1]
    vmem = pl.BlockSpec(memory_space=pltpu.VMEM)
    return pl.pallas_call(
        functools.partial(attend_whole_kernel, heads, tile_of(length), scale),
        in_specs=[pl.BlockSpec(memory_space=pltpu.SMEM)] + [vmem] * 6,
        out_specs=[vmem] * 5,
        out_shape=[
            jax.ShapeDtypeStruct((length, columns), low),
            jax.ShapeDtypeStruct((length, columns), low),
            jax.ShapeDtypeStruct((heads, length, 128), wide),
            jax.ShapeDtypeStruct((length, width), low),
            jax.ShapeDtypeStruct((columns, width), low),
        ],
        compiler_params=pltpu.CompilerParams(vmem_limit_bytes=56 * 1024 * 1024),
        cost_estimate=pl.CostEstimate(
            flops=12 * length * length * columns,
            bytes_accessed=16 * length * columns,
            transcendentals=length * length * heads // 2,
        ),
        name="attend",
    )(ends, packed, up_query, cosine, sine, own_heads, other_heads)


def tile_of(length):
    return next(t for t in (256, 128, 64, 32, 16, 8) if length % t == 0)


def attend(ends, query, packed, heads):
    length, width = query.shape[0], query.shape[1] // heads
    tile = tile_of(length)
    first = packed.shape[1] // width - 2
    return pl.pallas_call(
        functools.partial(attend_kernel, heads, tile),
        grid=(1,),
        in_specs=[
            pl.BlockSpec(memory_space=pltpu.SMEM),
            pl.BlockSpec((length, heads * width), lambda i: (0, 0)),
            pl.BlockSpec((length, width), lambda i: (0, first)),
            pl.BlockSpec((length, width), lambda i: (0, first + 1)),
        ],
        out_specs=[
            pl.BlockSpec((length, heads * width), lambda i: (0, 0)),
            pl.BlockSpec((heads, length, 128), lambda i: (0, 0, 0)),
        ],
        out_shape=[
            jax.ShapeDtypeStruct((length, heads * width), low),
            jax.ShapeDtypeStruct((heads, length, 128), wide),
        ],
        compiler_params=pltpu.CompilerParams(vmem_limit_bytes=56 * 1024 * 1024),
        cost_estimate=pl.CostEstimate(
            flops=6 * length * length * width * heads,
            bytes_accessed=8 * length * width * heads,
            transcendentals=length * length * heads // 2,
        ),
        name="attend",
    )(ends, query, packed, packed)


def attend_back(ends, query, grad, mixed, packed, logs, cosine, sine, heads, scale):
    length, width = query.shape[0], query.shape[1] // heads
    tile = tile_of(length)
    first = packed.shape[1] // width - 2
    rows = pl.BlockSpec((length, heads * width), lambda i: (0, 0))
    angle = pl.BlockSpec((length, width // 2), lambda i: (0, 0))
    return pl.pallas_call(
        functools.partial(attend_back_kernel, heads, tile, scale),
        grid=(1,),
        in_specs=[
            pl.BlockSpec(memory_space=pltpu.SMEM),
            rows,
            rows,
            rows,
            pl.BlockSpec((length, width), lambda i: (0, first)),
            pl.BlockSpec((length, width), lambda i: (0, first + 1)),
            pl.BlockSpec((heads, length, 128), lambda i: (0, 0, 0)),
            angle,
            angle,
        ],
        out_specs=[rows, pl.BlockSpec((length, 2 * width), lambda i: (0, 0))],
        out_shape=[
            jax.ShapeDtypeStruct((length, heads * width), low),
            jax.ShapeDtypeStruct((length, 2 * width), low),
        ],
        scratch_shapes=[pltpu.VMEM((length, 2 * width), wide)],
        compiler_params=pltpu.CompilerParams(vmem_limit_bytes=56 * 1024 * 1024),
        cost_estimate=pl.CostEstimate(
            flops=10 * length * length * width * heads,
            bytes_accessed=16 * length * width * heads,
            transcendentals=length * length * heads // 2,
        ),
        name="attend_back",
    )(ends, query, grad, mixed, packed, packed, logs, cosine, sine)


def on_device(
    tokens,
    lengths,
    cotangent,
    norm_one,
    query_down,
    query_gain,
    query_up,
    key_proj,
    value_proj,
    out_proj,
    norm_two,
    gate_proj,
    up_proj,
    down_proj,
):
    n_x, n_l = lax.axis_size("x"), lax.axis_size("l")
    x, c, h, l, y = [lax.axis_index(a) for a in every]
    n_dev = n_x * 8 * n_l
    n_group = 4 * n_l
    me = group_place()
    count, width = tokens.shape
    row_len = count * n_group
    latent_width = query_down.shape[1]
    head_dim = key_proj.shape[1]
    shard = query_down.shape[0]
    heads = query_up.shape[1] // head_dim // n_group
    ff_part = down_proj.shape[0]
    ff_own = ff_part * n_x * 2
    ff_pad = -(-ff_own // 128) * 128
    natural = n_x == 2 and n_l == 2
    scale = 1.0 / math.sqrt(head_dim)
    order = column_order(n_x, n_l)
    mapped_width = latent_width + 2 * head_dim

    gains = jnp.zeros((shard, 128), low)
    gains = gains.at[0, :shard].set(norm_one).at[1, :shard].set(norm_two)
    gains = gains.at[2, : query_gain.shape[0]].set(query_gain)
    small = jnp.concatenate([query_down, key_proj, value_proj, gains], axis=1)
    rows_up = query_up.shape[0]
    if natural:
        head_cols = query_up.reshape(rows_up, 2, 2, 2, 2, head_dim)
        head_cols = head_cols.transpose(2, 4, 3, 0, 1, 5)
    else:
        head_cols = query_up.reshape(rows_up, n_group, -1).transpose(1, 0, 2)
    head_cols = head_cols.reshape(n_group, rows_up, heads * head_dim)
    if natural:
        lens = jnp.pad(lengths, ((0, 7), (0, 128 - lengths.shape[1])))
        in_full, own_heads, (up_query, gate_rows, up_rows), (home, lens) = open_exchange(
            small, out_proj, head_cols, gate_proj, up_proj, [tokens, lens], ff_part, order, ff_pad
        )
        row_lengths = lens[0, : lengths.shape[1]]
    else:
        in_full = lax.all_gather(small, every, axis=0)
        home, grad_home, row_lengths = [swap_home(a) for a in (tokens, cotangent, lengths)]
        row_lengths = row_lengths[0]
        gate_cols, up_cols = split_columns(gate_proj, up_proj, ff_part, order, ff_pad)
        up_query, gate_rows, up_rows = [
            all_to_all_row(a) for a in (head_cols, gate_cols, up_cols)
        ]
        up_query = up_query.reshape((2, -1) + up_query.shape[1:])
        up_query = lax.all_gather(lax.all_gather(up_query, "h", axis=1), "x", axis=0)
    up_query = up_query.reshape(latent_width, -1)
    gate_rows = gate_rows.reshape(2, -1, ff_pad)
    up_rows = up_rows.reshape(2, -1, ff_pad)
    gain_one = in_full[:, 0, mapped_width : mapped_width + shard].reshape(width).astype(wide)
    gain_two = in_full[:, 1, mapped_width : mapped_width + shard].reshape(width).astype(wide)
    gain_latent = in_full[:, 2, mapped_width : mapped_width + query_gain.shape[0]]
    gain_latent = gain_latent.reshape(latent_width).astype(wide)
    in_full = in_full.reshape(width, -1)

    inputs = home.astype(wide)
    mapped_rates = jnp.exp(
        jnp.arange(head_dim // 2, dtype=wide) * (-math.log(10000.0) / (head_dim // 2))
    )
    ends = jnp.cumsum(row_lengths, dtype=jnp.int32)
    places = jnp.arange(row_len, dtype=jnp.int32)
    begins = jnp.max(jnp.where(places[:, None] >= ends[None, :], ends[None, :], 0), axis=1)
    if not natural:
        phases = (places - begins).astype(wide)[:, None] * mapped_rates
        cosine, sine = jnp.cos(phases), jnp.sin(phases)
        own_cos = lax.dynamic_slice_in_dim(cosine, me * count, count)
        own_sin = lax.dynamic_slice_in_dim(sine, me * count, count)

    if natural:
        own_heads = own_heads.reshape(-1, width)
        gate_a, gate_b, up_a, up_b = gate_rows[0], gate_rows[1], up_rows[0], up_rows[1]
        down_a, down_b = down_proj[:, : width // 2], down_proj[:, width // 2 :]
        heads_x = flip(own_heads, "x")
    else:
        out_full = lax.all_gather(out_proj, every, axis=0, tiled=True)
        out_own = lax.dynamic_slice_in_dim(out_full, me * heads * head_dim, heads * head_dim)
        gate_own, up_own = [
            lax.all_gather(lax.all_gather(a, "h", axis=1), "x", axis=0).reshape(width, -1)
            for a in (gate_rows, up_rows)
        ]
        down_own = lax.all_gather(lax.all_gather(down_proj, "h", axis=0), "x", axis=0)
        down_own = jnp.pad(down_own.reshape(-1, width), ((0, ff_pad - ff_own), (0, 0)))

    scale_one = rms_scale(inputs)
    if natural:
        packed, hidden, latent, cosine, sine, gate_a_h, gate_b_h = front(
            ends, home, in_full, gain_one[None], gain_latent[None], mapped_rates[None], row_len, 2,
            ("h", "h"), (gate_a, gate_b),
        )
        own_cos = lax.dynamic_slice_in_dim(cosine, me * count, count)
        own_sin = lax.dynamic_slice_in_dim(sine, me * count, count)
        packed, heads_x, up_a = together(packed, heads_x, up_a)
        up_a_h, up_b_h = flip(up_a, "h"), flip(after(up_b, packed), "h")
        gate_x = [flip(a, "x") for a in (gate_a, gate_b, gate_a_h, gate_b_h)]
        all_latent = packed[:, :latent_width]
        query, mixed, logs, terms, out_own = attend_whole(
            ends, packed, up_query, cosine, sine, own_heads, heads_x, heads, scale
        )
        terms, up_a_h, up_b_h = together(terms, up_a_h, up_b_h)
        up_x = [flip(a, "x") for a in (up_a, up_b, up_a_h, up_b_h)]
        attended, down_a_h, down_b_h = scatter_row(3, terms, kinds=("h", "h"), more=(down_a, down_b))
        attended, gate_x, up_x = together(attended, gate_x, up_x)
    else:
        hidden = (inputs * scale_one * gain_one).astype(low)
        mapped = dot(hidden, in_full)
        latent = mapped[:, :latent_width]
        scale_latent = rms_scale(latent)
        latent_low = (latent * scale_latent * gain_latent).astype(low)
        keys = mapped[:, latent_width : latent_width + head_dim]
        keys = rotate(keys, own_cos, own_sin).astype(low)
        values = mapped[:, latent_width + head_dim : mapped_width].astype(low)
        packed = gather_row(jnp.concatenate([latent_low, keys, values], axis=1), 2)
        grad_all = lax.all_gather(grad_home, group, axis=0, tiled=True)
        all_latent = packed[:, :latent_width]
        query_raw = dot(all_latent, up_query)
        query = jnp.concatenate(
            [
                rotate(query_raw[:, j * head_dim : (j + 1) * head_dim], cosine, sine)
                for j in range(heads)
            ],
            axis=1,
        ).astype(low) * jnp.asarray(scale, low)
        mixed, logs = attend(ends, query, packed, heads)
        attended = scatter_row(3, dot(mixed, out_own, low))[0]
    resid = inputs + attended
    scale_two = rms_scale(resid)
    hidden_two = (resid * scale_two * gain_two).astype(low)
    if natural:
        gate_parts = [gate_a, gate_b, gate_a_h, gate_b_h] + list(gate_x)
        up_parts = [up_a, up_b, up_a_h, up_b_h] + list(up_x)
        (
            all_two, inner, gate_factor, up_factor, down_a_x, down_a_xh, down_b_x, down_b_xh,
            grad_home, grad_all,
        ) = feed_forward(
            hidden_two, gate_parts, up_parts, (down_a, down_a_h, down_b, down_b_h), cotangent, 4
        )
    else:
        all_two = gather_row(hidden_two, 4)
        gate = dot(all_two, gate_own)
        upward = dot(all_two, up_own)
        sigma = jax.nn.sigmoid(gate)
        inner = (gate * sigma * upward).astype(low)
        grad_down = outer_sum(inner, grad_all, low)

    if natural:
        (
            dhidden_two, *spread, gate_terms, gate_x, up_terms, up_x, grad_down, _, _
        ) = feed_back(
            grad_all,
            gate_factor,
            up_factor,
            inner,
            all_two,
            gate_parts,
            up_parts,
            [
                (down_a, down_a_h, down_a_x, down_a_xh),
                (down_b, down_b_h, down_b_x, down_b_xh),
            ],
            5,
        )
    else:
        dinner = times_transposed(grad_all, down_own)
        dgate = (dinner * upward * sigma * (1.0 + gate * (1.0 - sigma))).astype(low)
        dupward = (dinner * gate * sigma).astype(low)
        grad_gate, grad_upward = outer_sum(all_two, dgate, low), outer_sum(all_two, dupward, low)
        dhidden_two = times_transposed(dgate, gate_own) + times_transposed(dupward, up_own)
        dhidden_two = scatter_row(5, dhidden_two.astype(low))[0]
        spread = scatter_row(6, dot(inner, down_own, low))[0]
        grad_down = sum_columns(grad_down[:ff_own].reshape(n_x, 2, ff_part, width), 0).astype(wide)
        gate_terms, up_terms = [
            sum_columns(a.reshape(n_x, 2, 2, -1, ff_pad), 1) for a in (grad_gate, grad_upward)
        ]

    dresid_part, dgain_two = norm_back(dhidden_two, resid, scale_two, gain_two)
    dresid = grad_home.astype(wide) + dresid_part
    branch = dresid.astype(low)
    if natural:
        by_h = (2, 2, -1, ff_pad)
        dlow, dkv, gate_terms, up_terms, final, out_terms, head_terms, *_ = middle(
            ends, branch, (gate_terms.reshape(by_h), gate_x.reshape(by_h)),
            (up_terms.reshape(by_h), up_x.reshape(by_h)), spread, query, mixed, packed, logs, cosine,
            sine, out_own, up_query, resid, heads, scale, 7,
        )
        gate_terms, up_terms = [a.reshape(n_group, shard, ff_pad) for a in (gate_terms, up_terms)]
        head_terms = head_terms.reshape(n_group, rows_up, heads * head_dim)
        summed, grad_tokens, output, grad_gate, grad_upward, grad_uquery, grad_out = shut(
            dlow, dkv, latent, gain_latent[None], own_cos, own_sin, hidden,
            in_full.reshape(n_dev, shard, -1), home, gain_one[None], dresid, dgain_two[None],
            gate_terms, up_terms, head_terms, final, pick(out_terms, h), pick(out_terms, 1 - h),
            ff_part, order, 9,
        )
    else:
        branch_all = gather_row(branch, 7)
        grad_out = outer_sum(mixed, branch_all, low)
        dmixed = times_transposed(branch_all, out_own, low)
        dquery, dkv = attend_back(
            ends, query, dmixed, mixed, packed, logs, cosine, sine, heads, scale
        )
        dlow = times_transposed(dquery, up_query, low)
        head_terms = outer_sum(all_latent, dquery, low).reshape(n_x, 2, 2, -1, heads * head_dim)
        dlow, dkv = scatter_row(8, dlow, dkv)
        whole = jnp.zeros((n_group * heads * head_dim, width), wide)
        whole = lax.dynamic_update_slice_in_dim(
            whole, grad_out.astype(wide), me * heads * head_dim, 0
        )
        grad_out = lax.psum_scatter(whole, every, scatter_dimension=0, tiled=True)
        final = (resid + spread).astype(low)
        dkeys = rotate_back(dkv[:, :head_dim], own_cos, own_sin).astype(low)
        dvalues = dkv[:, head_dim:].astype(low)
        dlatent, dgain_latent = norm_back(dlow, latent, scale_latent, gain_latent)
        nothing = jnp.zeros((count, 128), low)
        dmapped = jnp.concatenate([dlatent.astype(low), dkeys, dvalues, nothing], axis=1)
        dhidden = times_transposed(dmapped, in_full)
        dinput_part, dgain_one = norm_back(dhidden, inputs, scale_one, gain_one)
        grad_tokens = (dresid + dinput_part).astype(low)
        grad_in = outer_sum(hidden, dmapped[:, :mapped_width], low).reshape(n_dev, shard, -1)
        gain_terms = jnp.zeros((n_dev, shard, 128), low)
        gain_terms = gain_terms.at[:, 0, :shard].set(dgain_one.reshape(n_dev, -1).astype(low))
        gain_terms = gain_terms.at[:, 1, :shard].set(dgain_two.reshape(n_dev, -1).astype(low))
        gain_terms = gain_terms.at[:, 2, : query_gain.shape[0]].set(
            dgain_latent.reshape(n_dev, -1).astype(low)
        )
        terms = jnp.concatenate([grad_in, gain_terms], axis=2)
        summed = lax.psum_scatter(terms.astype(wide), every, scatter_dimension=0, tiled=False)
        grad_tokens, output = swap_home(grad_tokens), swap_home(final)
        head_terms = all_to_all_row(
            sum_columns(head_terms, 1).reshape(n_group, rows_up, heads * head_dim)
        )
        gate_terms, up_terms = [
            all_to_all_row(a.reshape(n_group, shard, ff_pad)) for a in (gate_terms, up_terms)
        ]
        grad_gate, grad_upward = join_columns(gate_terms, up_terms, ff_part, order)
        grad_uquery = head_terms.transpose(1, 0, 2).reshape(rows_up, -1).astype(wide)
    return (
        output,
        grad_tokens.astype(wide),
        summed[0, mapped_width : mapped_width + shard],
        summed[:, :latent_width],
        summed[2, mapped_width : mapped_width + query_gain.shape[0]],
        grad_uquery,
        summed[:, latent_width : latent_width + head_dim],
        summed[:, latent_width + head_dim : mapped_width],
        grad_out,
        summed[1, mapped_width : mapped_width + shard],
        grad_gate,
        grad_upward,
        grad_down,
    )


def solution(mesh):
    n_dp, n_seq = mesh.shape["dp"], mesh.shape["seq"]
    fine = Mesh(mesh.devices.reshape(n_dp // 2, 2, 2, n_seq // 4, 2), every)
    rows, flat = P(every, None), P(every)
    placed = (rows, P(("x", "c"), None), rows, flat, rows, flat) + (rows,) * 4 + (flat,) + (rows,) * 3
    return jax.shard_map(
        on_device,
        mesh=fine,
        in_specs=placed,
        out_specs=(rows, rows, flat, rows, flat) + (rows,) * 4 + (flat,) + (rows,) * 3,
        check_vma=False,
    )
```

```python
import functools
import math

import jax
import jax.numpy as jnp
from jax import lax
from jax.experimental import pallas as pl
from jax.experimental.pallas import tpu as pltpu
from jax.sharding import Mesh, PartitionSpec as P

norm_eps = 1e-05
masked_value = -1e30
every = ("x", "c", "h", "l", "y")
group = ("c", "l", "y")
low = jnp.bfloat16
wide = jnp.float32


def rms_scale(values):
    return lax.rsqrt(jnp.mean(values * values, axis=-1, keepdims=True) + norm_eps)


def rotate(values, cosine, sine):
    half = values.shape[-1] // 2
    a, b = values[..., :half], values[..., half:]
    return jnp.concatenate([a * cosine - b * sine, b * cosine + a * sine], axis=-1)


def rotate_back(values, cosine, sine):
    half = values.shape[-1] // 2
    a, b = values[..., :half], values[..., half:]
    return jnp.concatenate([a * cosine + b * sine, b * cosine - a * sine], axis=-1)


def norm_back(incoming, source, scale, gain):
    weighted = incoming * gain
    source_grad = scale * weighted - source * (scale * scale * scale) * jnp.mean(
        weighted * source, axis=-1, keepdims=True
    )
    return source_grad, jnp.sum(incoming * source * scale, axis=0)


def dot(left, right, out=wide):
    return jnp.dot(left, right, preferred_element_type=wide).astype(out)


def outer_sum(left, right, out=wide):
    return lax.dot_general(
        left, right, (((0,), (0,)), ((), ())), preferred_element_type=wide
    ).astype(out)


def times_transposed(left, right, out=wide):
    return lax.dot_general(
        left, right, (((1,), (1,)), ((), ())), preferred_element_type=wide
    ).astype(out)


def pick(array, index, axis=0):
    return lax.dynamic_index_in_dim(array, index, axis, keepdims=False)


def after(value, *done):
    return lax.optimization_barrier((value,) + done)[0]


def together(*values):
    return lax.optimization_barrier(values)


def flip(value, axis):
    return lax.ppermute(value, axis, [(0, 1), (1, 0)])


def flip_cross(value):
    return lax.ppermute(value, ("c", "h"), [(1, 2), (2, 1)])


def choose_home(value, moved):
    return jnp.where(lax.axis_index("c") == lax.axis_index("h"), value, moved)


def swap_home(value):
    return choose_home(value, flip_cross(value))


def group_place():
    return (
        lax.axis_index("c") * lax.axis_size("l") + lax.axis_index("l")
    ) * 2 + lax.axis_index("y")


def all_to_all_row(blocks):
    return lax.all_to_all(blocks, group, 0, 0, tiled=True)


def send(value, offsets):
    return lax.ppermute(value, group, [(i, i ^ offsets[i // 4]) for i in range(8)])


def scatter_row_async(state, stage):
    core = lax.axis_index("c")
    me = lax.axis_index("l") * 2 + lax.axis_index("y")
    first, second = 1 + core, 2 - core
    if stage == 0:
        return state[0], flip(state[1], "c")
    own, moved = state[:2]

    def block(index):
        return pick(own, index).astype(wide) + pick(moved, index).astype(wide)

    if stage == 1:
        far = send(block(me ^ 3).astype(low), (2, 1))
        return own, moved, far, send(block(me ^ second).astype(low), (2, 1))
    far, side = state[2:4]
    if stage == 2:
        return state + (send((block(me ^ first) + far.astype(wide)).astype(low), (1, 2)),)
    return block(me) + side.astype(wide) + state[4].astype(wide)


def sum_columns(terms, h_dim):
    for axis, dim in (("x", 0), ("h", h_dim)):
        terms = jnp.moveaxis(terms, dim, 0).astype(wide)
        terms = lax.psum_scatter(terms, axis, scatter_dimension=0, tiled=False).astype(low)
    return terms


def halves(terms, axis, dim):
    me = lax.axis_index(axis)
    return pick(terms, me, dim), flip(pick(terms, 1 - me, dim), axis)


def add(own, came):
    return (own.astype(wide) + came.astype(wide)).astype(low)


def other(value, flag=1):
    return value + flag * (1 - 2 * value)


def greet(peers):
    barrier = pltpu.get_barrier_semaphore()
    for peer in peers:
        pl.semaphore_signal(barrier, inc=1, device_id=peer, device_id_type=pl.DeviceIdType.MESH)
    pl.semaphore_wait(barrier, len(peers))


def remote(source, target, send_sem, recv_sem, peer):
    return pltpu.make_async_remote_copy(
        src_ref=source,
        dst_ref=target,
        send_sem=send_sem,
        recv_sem=recv_sem,
        device_id=peer,
        device_id_type=pl.DeviceIdType.MESH,
    )


def in_hbm():
    return pl.BlockSpec(memory_space=pl.ANY)


def open_kernel(n_swaps, part, order, small_ref, out_ref, heads_in, gate_in, up_in, *refs):
    n_sets = 3
    swaps, refs = refs[:n_swaps], refs[n_swaps:]
    (full_ref, heads_ref), refs = refs[:2], refs[2:]
    set_outs, refs = refs[:n_sets], refs[n_sets:]
    swap_outs, refs = refs[:n_swaps], refs[n_swaps:]
    (small_buf, out_buf), refs = refs[:2], refs[2:]
    raws, set_bufs, refs = refs[:2], refs[2:5], refs[5:]
    heads_buf, splits = set_bufs[0], set_bufs[1:]
    sets = [heads_in, *splits]
    swap_bufs, refs = refs[:n_swaps], refs[n_swaps:]
    sends, recvs, swap_sends, swap_recvs, set_sends, set_recvs, out_sems, head_sems, loads_sem, stores_sem, split_sem = refs
    x, c, h, l, y = [lax.axis_index(a) for a in every]
    hops = {
        1: {"h": other(h)},
        2: {"l": other(l)},
        4: {"y": other(y)},
        8: {"x": other(x)},
        16: {"c": other(c)},
    }
    cross = {"c": other(c), "h": other(h)}
    me = (c * 2 + l) * 2 + y

    def group_peer(k):
        return {"c": other(c, k // 4), "l": other(l, k // 2 % 2), "y": other(y, k % 2)}

    def group_index(k):
        peer = group_peer(k)
        return (peer["c"] * 2 + peer["l"]) * 2 + peer["y"]

    def index(code):
        at_x, at_l = other(x, code // 8 % 2), other(l, code // 2 % 2)
        return (((at_x * 2 + c) * 2 + other(h, code % 2)) * 2 + at_l) * 2 + other(y, code // 4 % 2)

    beside, corner = {"y": other(y)}, {"h": other(h), "y": h}
    greet(
        [hops[1], hops[8], cross, {"h": other(h), "y": other(y)}]
        + [group_peer(k) for k in range(1, 8)]
    )
    copies = []
    half = heads_ref.at[y]
    to_beside = remote(out_ref, half, out_sems.at[0], out_sems.at[1], beside)
    differ = y + h - 2 * y * h
    to_corner = remote(out_ref, half, out_sems.at[2], out_sems.at[3 + differ], corner)

    def push(code):
        block = full_ref.at[index(code)]
        source = small_ref if code == 0 else block
        for hop in (1, 2, 4, 8, 16):
            if code < hop:
                name = code + hop
                copy = remote(source, block, sends.at[name], recvs.at[name], hops[hop])
                copy.start()
                copies.append(copy)

    def set_slot(i):
        return set_outs[0].at[x, c, h, l * 2 + y] if i == 0 else set_outs[i].at[me]

    set_copies = []

    def set_push(i):
        for k in range(1, 8):
            copy = remote(
                sets[i].at[group_index(k)], set_slot(i), set_sends.at[i, k], set_recvs.at[i, k],
                group_peer(k),
            )
            copy.start()
            set_copies.append(copy)

    push(0)
    set_push(0)
    moving = [
        remote(source, target, swap_sends.at[i], swap_recvs.at[i], cross)
        for i, (source, target) in enumerate(zip(swaps, swap_outs))
    ]

    def push_moves():
        @pl.when(c != h)
        def _():
            for copy in moving:
                copy.start()

        @pl.when(y != h)
        def _():
            to_beside.start()

        to_corner.start()

    loads, stores = [], []
    raw_loads = [
        pltpu.make_async_copy(source, raw, stores_sem.at[3 + n_swaps + i])
        for i, (source, raw) in enumerate(((gate_in, raws[0]), (up_in, raws[1])))
    ]
    for load in raw_loads:
        load.start()
    locals_in = [small_ref, out_ref, heads_in.at[me]] + list(swaps)
    locals_buf = [small_buf, out_buf, heads_buf] + list(swap_bufs)
    locals_out = [full_ref.at[index(0)], half, set_slot(0)]
    for i, (source, buf) in enumerate(zip(locals_in, locals_buf)):
        loads.append(pltpu.make_async_copy(source, buf, loads_sem.at[i]))
        loads[-1].start()
    for load in loads:
        load.wait()
    for i, (buf, target) in enumerate(zip(locals_buf, locals_out)):
        stores.append(pltpu.make_async_copy(buf, target, stores_sem.at[i]))
    keep_out = stores.pop(1)
    for store in stores:
        store.start()

    @pl.when(y == h)
    def _():
        keep_out.start()

    keeps = [
        pltpu.make_async_copy(buf, target, stores_sem.at[3 + i])
        for i, (buf, target) in enumerate(zip(swap_bufs, swap_outs))
    ]

    @pl.when(c == h)
    def _():
        for keep in keeps:
            keep.start()

    def arrived(name):
        remote(small_ref, small_ref, sends.at[name], recvs.at[name], hops[16]).wait_recv()

    def head_copy(at_h, slot, peer):
        part = set_outs[0].at[x, :, at_h]
        copy = remote(part, part, head_sems.at[slot], head_sems.at[3 + slot], peer)
        copy.start()
        return copy

    head_copies, split_keeps = [], []
    for n, code in enumerate((2, 4, 1, 6, 3, 5, 7, 8, 9, 10, 11, 12, 13, 14, 15)):
        arrived(code)
        push(code)
        if n == 2:
            for copy in set_copies:
                copy.wait()
            for store in stores:
                store.wait()
            done = len(set_copies)
            for load in raw_loads:
                load.wait()
            split_kernel(part, order, *raws, *splits)
            for i in range(1, n_sets):
                set_push(i)
                keep = pltpu.make_async_copy(splits[i - 1].at[me], set_slot(i), split_sem.at[i - 1])
                keep.start()
                split_keeps.append(keep)
            head_copies.append(head_copy(h, 0, hops[1]))
            head_copies.append(head_copy(h, 1, hops[8]))
            push_moves()
        if n == 9:
            head_copies[0].wait_recv()
            head_copies.append(head_copy(other(h), 2, hops[8]))
    for code in range(16):
        arrived(16 + code)
    for copy in copies:
        copy.wait_send()
    for copy in set_copies[done:] + split_keeps:
        copy.wait()
    head_copies[0].wait_send()
    for copy in head_copies[1:]:
        copy.wait()
    to_corner.wait_send()

    @pl.when(y != h)
    def _():
        to_beside.wait_send()
        remote(out_ref, half, out_sems.at[2], out_sems.at[3], corner).wait_recv()
        remote(out_ref, half, out_sems.at[2], out_sems.at[4], corner).wait_recv()

    @pl.when(y == h)
    def _():
        keep_out.wait()
        to_beside.wait_recv()

    @pl.when(c != h)
    def _():
        for copy in moving:
            copy.wait()

    @pl.when(c == h)
    def _():
        for keep in keeps:
            keep.wait()


def open_exchange(small, out_rows, heads, gate, up, swaps, part, order, total):
    n_swaps = len(swaps)
    args = [small, out_rows, heads, gate, up] + swaps
    split = (len(order), gate.shape[0], total)
    shapes = [(32,) + small.shape, (2,) + out_rows.shape, (2, 2, 2, 4) + heads.shape[1:], split, split]
    out_shape = [jax.ShapeDtypeStruct(s, low) for s in shapes]
    out_shape += [jax.ShapeDtypeStruct(a.shape, a.dtype) for a in swaps]
    sem = pltpu.SemaphoreType.DMA
    out = pl.pallas_call(
        functools.partial(open_kernel, n_swaps, part, order),
        in_specs=[in_hbm()] * len(args),
        out_specs=[in_hbm()] * len(out_shape),
        out_shape=out_shape,
        scratch_shapes=[pltpu.VMEM(a.shape, low) for a in (small, out_rows, gate, up)]
        + [pltpu.VMEM(s, low) for s in (heads.shape[1:], split, split)]
        + [pltpu.VMEM(a.shape, a.dtype) for a in swaps]
        + [sem((32,)), sem((32,)), sem((n_swaps,)), sem((n_swaps,))]
        + [sem((3, 8)), sem((3, 8)), sem((5,)), sem((6,))]
        + [sem((3 + n_swaps,)), sem((5 + n_swaps,)), sem((2,))],
        compiler_params=pltpu.CompilerParams(
            collective_id=1, has_side_effects=True, vmem_limit_bytes=16 * 1024 * 1024
        ),
        cost_estimate=pl.CostEstimate(flops=0, bytes_accessed=150 * 1024 * 1024, transcendentals=0),
        name="open_exchange",
    )(*args)
    return out[0], out[1], out[2:5], out[5:]


def row_peers(even):
    c, l, y = [lax.axis_index(a) for a in group]
    if even == "l":
        near = {"l": l, "y": other(y)}
        side = {"l": other(l), "y": y}
    elif even:
        near = {"l": other(l, c), "y": other(y, 1 - c)}
        side = {"l": other(l, 1 - c), "y": other(y, c)}
    else:
        near = {"l": other(l), "y": y}
        side = {"l": l, "y": other(y)}
    return c, l, y, near, side, {"c": other(c)}


def turn(values, cosine, sine):
    half = values.shape[1] // 2
    a, b = values[:, :half], values[:, half:]
    return a * cosine - b * sine, b * cosine + a * sine


def angles(ends_ref, rates, begin, count):
    places = begin + lax.broadcasted_iota(jnp.int32, (count, 1), 0)
    start = jnp.zeros_like(places)
    for j in range(ends_ref.shape[0]):
        end = ends_ref[j]
        start = jnp.where(places >= end, end, start)
    phases = (places - start).astype(wide) * rates
    return jnp.cos(phases), jnp.sin(phases)


def front_kernel(kinds, ends_ref, home_ref, full_ref, gain_ref, low_gain_ref, rates_ref, *refs):
    n = len(kinds)
    more, refs = refs[:n], refs[n:]
    out_ref, hidden_ref, latent_ref, cos_ref, sin_ref, own_cos, own_sin, refs = *refs[:7], refs[7:]
    more_out, refs = refs[:n], refs[n:]
    full, own, sends, recvs, load_sem, store_sem, more_sems = refs
    beside = Beside(kinds, more, more_out, more_sems)
    flow = RowGather(False, sends.shape[1], own, out_ref, sends, recvs)
    load = pltpu.make_async_copy(full_ref, full, load_sem)
    load.start()
    near, side, twin = flow.peers
    greet([near, side, twin, *beside.peers])
    count = home_ref.shape[0]
    low_width, head_dim = latent_ref.shape[1], 2 * cos_ref.shape[1]
    half = head_dim // 2
    values = home_ref[...].astype(wide)
    hidden = (values * rms_scale(values) * gain_ref[...]).astype(low)
    hidden_ref[...] = hidden
    cosine, sine = angles(ends_ref, rates_ref[...], flow.me * count, count)
    own_cos[...] = cosine
    own_sin[...] = sine
    load.wait()
    mapped = jnp.dot(hidden, full[...], preferred_element_type=wide)
    latent = mapped[:, :low_width]
    latent_ref[...] = latent
    own[:, :low_width] = (latent * rms_scale(latent) * low_gain_ref[...]).astype(low)
    a, b = turn(mapped[:, low_width : low_width + head_dim], cosine, sine)
    own[:, low_width : low_width + half] = a.astype(low)
    own[:, low_width + half : low_width + head_dim] = b.astype(low)
    end = low_width + 2 * head_dim
    own[:, low_width + head_dim :] = mapped[:, low_width + head_dim : end].astype(low)
    flow.begin(None)
    beside.start()
    store = pltpu.make_async_copy(own, out_ref.at[flow.me], store_sem)
    store.start()

    def tables(begin, rows):
        cos_ref[begin : begin + rows, :], sin_ref[begin : begin + rows, :] = angles(
            ends_ref, rates_ref[...], begin, rows
        )

    quarter = cos_ref.shape[0] // 4
    tables(0, quarter)
    tables(quarter, quarter)
    flow.take_near()
    tables(2 * quarter, quarter)
    flow.take_side()
    tables(3 * quarter, quarter)
    flow.take_far()
    for slot in (3, 4, 5, 6):
        flow.take(slot)
    flow.end()
    store.wait()
    beside.wait()


def front(ends, home, in_full, gain_one, gain_latent, rates, row_len, number, kinds, more):
    count, width = home.shape
    low_width = gain_latent.shape[1]
    half = rates.shape[1]
    packed = (count, low_width + 4 * half)
    vmem, sem = pl.BlockSpec(memory_space=pltpu.VMEM), pltpu.SemaphoreType.DMA
    out = pl.pallas_call(
        functools.partial(front_kernel, kinds),
        in_specs=[pl.BlockSpec(memory_space=pltpu.SMEM), vmem, in_hbm(), vmem, vmem, vmem]
        + [in_hbm()] * len(more),
        out_specs=[in_hbm()] + [vmem] * 6 + [in_hbm()] * len(more),
        out_shape=[
            jax.ShapeDtypeStruct((8,) + packed, low),
            jax.ShapeDtypeStruct((count, width), low),
            jax.ShapeDtypeStruct((count, low_width), wide),
            jax.ShapeDtypeStruct((row_len, half), wide),
            jax.ShapeDtypeStruct((row_len, half), wide),
            jax.ShapeDtypeStruct((count, half), wide),
            jax.ShapeDtypeStruct((count, half), wide),
        ]
        + [jax.ShapeDtypeStruct(a.shape, low) for a in more],
        scratch_shapes=[
            pltpu.VMEM(in_full.shape, low),
            pltpu.VMEM(packed, low),
            sem((7, 4)),
            sem((7, 4)),
            sem,
            sem,
            sem((2, len(more))),
        ],
        compiler_params=pltpu.CompilerParams(
            collective_id=number, has_side_effects=True, vmem_limit_bytes=32 * 1024 * 1024
        ),
        cost_estimate=pl.CostEstimate(flops=0, bytes_accessed=100 * 1024 * 1024, transcendentals=0),
        name="front",
    )(ends, home, in_full, gain_one, gain_latent, rates, *more)
    return (out[0].reshape(-1, packed[1]), *out[1:])


def gather_kernel(even, chunks, kinds, own_ref, *refs):
    n = len(kinds)
    more, out_ref, more_out = refs[:n], refs[n], refs[n + 1 : 2 * n + 1]
    buf, sends, recvs, local_sems = refs[2 * n + 1 : 2 * n + 5]
    beside = Beside(kinds, more, more_out, refs[-1])
    flow = RowGather(even, chunks, own_ref, out_ref, sends, recvs)
    flow.begin(beside.peers)
    beside.start()
    load = pltpu.make_async_copy(own_ref, buf, local_sems.at[0])
    load.start()
    load.wait()
    store = pltpu.make_async_copy(buf, out_ref.at[flow.me], local_sems.at[1])
    store.start()
    flow.take_near()
    flow.take_side()
    flow.take_far()
    for slot in (3, 4, 5, 6):
        flow.take(slot)
    flow.end()
    store.wait()
    beside.wait()


class Beside:
    def __init__(self, kinds, sources, targets, sems):
        x, c, h = [lax.axis_index(a) for a in ("x", "c", "h")]
        ways = {"x": {"x": other(x)}, "h": {"h": other(h)}, "cross": {"c": other(c), "h": other(h)}}
        self.peers = [ways[k] for k in sorted(set(kinds))]
        self.moves = c != h
        self.copies = [
            (kind, remote(source, target, sems.at[0, i], sems.at[1, i], ways[kind]))
            for i, (kind, source, target) in enumerate(zip(kinds, sources, targets))
        ]

    def start(self, span=slice(None)):
        for kind, copy in self.copies[span]:
            if kind == "cross":
                pl.when(self.moves)(copy.start)
            else:
                copy.start()

    def wait(self, span=slice(None)):
        for kind, copy in self.copies[span]:
            if kind == "cross":
                pl.when(self.moves)(copy.wait)
            else:
                copy.wait()


class RowGather:
    def __init__(self, even, chunks, own_ref, out_ref, sends, recvs, in_slots=False):
        c, l, y, near, side, twin = row_peers(even)
        self.peers = near, side, twin
        self.chunks, self.rows = chunks, own_ref.shape[0] // chunks
        self.own_ref, self.out_ref, self.sends, self.recvs = own_ref, out_ref, sends, recvs
        at = l * 2 + y
        near_at, side_at = near["l"] * 2 + near["y"], side["l"] * 2 + side["y"]
        far_at = other(l) * 2 + other(y)
        self.me = c * 4 + at
        self.places = [c * 4 + p for p in (near_at, side_at, far_at)]
        swapped = even is True
        twins = (at, side_at, near_at, far_at) if swapped else (at, near_at, side_at, far_at)
        self.places += [other(c) * 4 + p for p in twins]
        self.copies = []
        self.lands = (2, 3, 6, 1, 4, 5, 7) if in_slots else None

    def land(self, slot):
        return self.lands[slot] if self.lands else self.places[slot]

    def start(self, held, k, slot, peer):
        span = pl.ds(k * self.rows, self.rows)
        source = self.own_ref.at[span] if held is None else self.out_ref.at[self.land(held), span]
        if self.lands:
            target = self.out_ref.at[self.lands[slot], span]
        else:
            target = self.out_ref.at[self.me if held is None else self.places[held], span]
        copy = remote(source, target, self.sends.at[slot, k], self.recvs.at[slot, k], peer)
        copy.start()
        self.copies.append(copy)

    def begin(self, more_peers=()):
        near, side, twin = self.peers
        if more_peers is not None:
            greet([near, side, twin, *more_peers])
        for k in range(self.chunks):
            self.start(None, k, 0, near)
            self.start(None, k, 1, side)
            self.start(None, k, 3, twin)

    def arrived(self, slot, k):
        span = self.own_ref.at[pl.ds(k * self.rows, self.rows)]
        target = self.out_ref.at[self.land(slot), pl.ds(k * self.rows, self.rows)]
        remote(
            span, target, self.sends.at[slot, k], self.recvs.at[slot, k], self.peers[2]
        ).wait_recv()

    def take(self, slot):
        for k in range(self.chunks):
            self.arrived(slot, k)

    def take_near(self):
        near, side, twin = self.peers
        for k in range(self.chunks):
            self.arrived(0, k)
            self.start(0, k, 2, side)
            self.start(0, k, 4, twin)

    def take_side(self):
        for k in range(self.chunks):
            self.arrived(1, k)
            self.start(1, k, 5, self.peers[2])

    def take_far(self):
        for k in range(self.chunks):
            self.arrived(2, k)
            self.start(2, k, 6, self.peers[2])

    def end(self):
        for copy in self.copies:
            copy.wait_send()


def gather_row(value, number, even=False, kinds=(), more=()):
    if lax.axis_size("l") != 2:
        return lax.all_gather(value, group, axis=0, tiled=True)
    chunks = 4 if value.shape[0] % 64 == 0 else 1
    args = [value, *more]
    out_shape = [jax.ShapeDtypeStruct((8,) + value.shape, low)]
    out_shape += [jax.ShapeDtypeStruct(a.shape, low) for a in more]
    out = pl.pallas_call(
        functools.partial(gather_kernel, even, chunks, kinds),
        in_specs=[in_hbm()] * len(args),
        out_specs=[in_hbm()] * len(args),
        out_shape=out_shape,
        scratch_shapes=[
            pltpu.VMEM(value.shape, low),
            pltpu.SemaphoreType.DMA((7, chunks)),
            pltpu.SemaphoreType.DMA((7, chunks)),
            pltpu.SemaphoreType.DMA((2,)),
            pltpu.SemaphoreType.DMA((2, max(1, len(more)))),
        ],
        compiler_params=pltpu.CompilerParams(
            collective_id=number, has_side_effects=True, vmem_limit_bytes=16 * 1024 * 1024
        ),
        cost_estimate=pl.CostEstimate(flops=0, bytes_accessed=80 * 1024 * 1024, transcendentals=0),
        name="gather_row",
    )(*args)
    rows = out[0].reshape(-1, value.shape[1])
    return (rows, *out[1:]) if kinds else rows


def load_columns(pieces, target, sem, first):
    x, h = lax.axis_index("x"), lax.axis_index("h")
    rows = pieces[0].shape[0]
    loads = []
    for i, piece in enumerate(pieces):
        at_x = x if i < 4 else other(x)
        at_h = h if i // 2 % 2 == 0 else other(h)
        at = pl.multiple_of(((at_x * 2 + i % 2) * 2 + at_h) * rows, rows)
        loads.append(
            pltpu.make_async_copy(piece, target.at[pl.ds(at, rows)], sem.at[first + i])
        )
    return loads


def load_rows(parts, target, sem):
    x, h = lax.axis_index("x"), lax.axis_index("h")
    rows, width = parts[0][0].shape
    loads = []
    for s, part in enumerate(parts):
        for i, (at_x, at_h) in enumerate(
            ((x, h), (x, other(h)), (other(x), h), (other(x), other(h)))
        ):
            at = pl.multiple_of((at_x * 2 + at_h) * rows, 16)
            loads.append(
                pltpu.make_async_copy(
                    part[i],
                    target.at[pl.ds(at, rows), pl.ds(s * width, width)],
                    sem.at[len(loads)],
                )
            )
            loads[-1].start()
    return loads


def wait_all(copies):
    for copy in copies:
        copy.wait()


def for_tiles(total, tile, body):
    def step(j, carry):
        body(pl.ds(pl.multiple_of(j * tile, tile), tile))
        return carry

    lax.fori_loop(0, total // tile, step, 0)


def feed_kernel(even, chunks, *refs):
    own_ref, gates, ups = refs[0], refs[1:9], refs[9:17]
    downs, grad_ref, refs = refs[17:21], refs[21], refs[22:]
    all_ref, inner_ref, a_ref, b_ref = refs[:4]
    downs_x, home_ref, grads_ref, refs = refs[4:8], refs[8], refs[9], refs[10:]
    xs, wg, wu, inner_s, a_s, b_s, grad_buf, sends, recvs, grad_sends, grad_recvs = refs[:11]
    weight_sems, store_sems, own_sem, more_sems, grad_sems = refs[11:]
    flow = RowGather(even, chunks, own_ref, xs, sends, recvs, in_slots=True)
    beside = Beside(
        ("cross", "x", "x", "x", "x"),
        (grad_ref, *downs),
        (home_ref, *downs_x),
        more_sems,
    )
    away = lax.axis_index("c") != lax.axis_index("h")
    grad_flow = RowGather(True, chunks, home_ref, grads_ref, grad_sends, grad_recvs)
    flow.begin(beside.peers)
    beside.start()
    grad_load = pltpu.make_async_copy(grad_ref, grad_buf, grad_sems.at[0])
    grad_load.start()
    own_load = pltpu.make_async_copy(own_ref, xs.at[0], own_sem)
    own_load.start()
    weights = load_columns(gates, wg, weight_sems, 0) + load_columns(ups, wu, weight_sems, 8)
    for load in weights:
        load.start()
    grad_load.wait()
    to_home = pltpu.make_async_copy(grad_buf, home_ref, grad_sems.at[1])

    @pl.when(jnp.logical_not(away))
    def _():
        to_home.start()
        to_home.wait()

    order = [flow.me] + [flow.places[s] for s in (3, 0, 1, 4, 5, 2, 6)]
    stores = []
    columns, width = wg.shape[1], wg.shape[0]

    def work(pair):
        both = pl.ds(2 * pair, 2)
        x = xs[both].reshape(-1, width)

        def tile(cols):
            gate = jnp.dot(x, wg[:, cols], preferred_element_type=wide)
            upward = jnp.dot(x, wu[:, cols], preferred_element_type=wide)
            sigma = jax.nn.sigmoid(gate)
            swish = gate * sigma
            shape = (2, -1, upward.shape[1])
            inner_s[both, :, cols] = (swish * upward).astype(low).reshape(shape)
            b_s[both, :, cols] = swish.astype(low).reshape(shape)
            factor = upward * sigma * (1.0 + gate * (1.0 - sigma))
            a_s[both, :, cols] = factor.astype(low).reshape(shape)

        tile(slice(None))
        for i in (2 * pair, 2 * pair + 1):
            place = order[i]
            for j, (buf, target) in enumerate(
                ((xs, all_ref), (inner_s, inner_ref), (a_s, a_ref), (b_s, b_ref))
            ):
                store = pltpu.make_async_copy(buf.at[i], target.at[place], store_sems.at[i, j])
                store.start()
                stores.append(store)

    own_load.wait()
    flow.take(3)
    wait_all(weights)
    work(0)
    flow.take_near()
    flow.take_side()
    beside.wait(slice(0, 1))
    grad_flow.begin(None)
    home_load = pltpu.make_async_copy(home_ref, grad_buf, grad_sems.at[2])
    home_load.start()
    work(1)
    home_load.wait()
    own_store = pltpu.make_async_copy(grad_buf, grads_ref.at[grad_flow.me], grad_sems.at[3])
    own_store.start()
    flow.take(4)
    flow.take(5)
    work(2)
    flow.take_far()
    grad_flow.take_near()
    grad_flow.take_side()
    flow.take(6)
    work(3)
    grad_flow.take_far()
    for slot in (3, 4, 5, 6):
        grad_flow.take(slot)
    flow.end()
    grad_flow.end()
    wait_all(stores + [own_store])
    beside.wait(slice(1, 5))


def feed_forward(own, gates, ups, downs, grad, number):
    count, width = own.shape
    columns = gates[0].shape[1]
    chunks = 4 if count % 64 == 0 else 1
    row, part = (8, count, width), (8, count, columns)
    sem = pltpu.SemaphoreType.DMA
    flops = 2 * 8 * count * width * columns * 2
    args = [own, *gates, *ups, *downs, grad]
    shapes = [row, part, part, part] + [a.shape for a in downs] + [grad.shape, row]
    return pl.pallas_call(
        functools.partial(feed_kernel, False, chunks),
        in_specs=[in_hbm()] * len(args),
        out_specs=[in_hbm()] * len(shapes),
        out_shape=[jax.ShapeDtypeStruct(s, low) for s in shapes],
        scratch_shapes=[
            pltpu.VMEM(row, low),
            pltpu.VMEM((width, columns), low),
            pltpu.VMEM((width, columns), low),
            pltpu.VMEM(part, low),
            pltpu.VMEM(part, low),
            pltpu.VMEM(part, low),
            pltpu.VMEM(grad.shape, low),
            sem((7, chunks)),
            sem((7, chunks)),
            sem((7, chunks)),
            sem((7, chunks)),
            sem((16,)),
            sem((8, 4)),
            sem,
            sem((2, 5)),
            sem((4,)),
        ],
        compiler_params=pltpu.CompilerParams(
            collective_id=number, has_side_effects=True, vmem_limit_bytes=56 * 1024 * 1024
        ),
        cost_estimate=pl.CostEstimate(
            flops=flops, bytes_accessed=100 * 1024 * 1024, transcendentals=0
        ),
        name="feed_forward",
    )(*args)


def feed_back_kernel(
    even, chunks, *refs,
):
    grad_ref, a_ref, b_ref, inner_ref, all_ref = refs[:5]
    gates, ups, downs, refs = refs[5:13], refs[13:21], refs[21:29], refs[29:]
    out_ref, terms_own, terms_twin, gate_own, gate_across, up_own, up_across = refs[:7]
    down_sum, down_across, down_came, refs = refs[7], refs[8], refs[9], refs[10:]
    down_own, down_stage, came_h, refs = refs[0], refs[1], refs[2], refs[3:]
    gx, wg, wu, wd, a_s, b_s, inner_s, terms_s, own_buf, twin_buf, twin_out, down_s = refs[:12]
    far_out, side_out, near_out, far_in, side_in, near_in = refs[12:18]
    sends, recvs, weight_sems, down_sems, block_sems, all_sems, terms_sems, more_sems = refs[18:]
    over_x, over_h = {"x": other(lax.axis_index("x"))}, {"h": other(lax.axis_index("h"))}
    at_h = lax.axis_index("h")
    halves_at = [pl.ds(0, grad_ref.shape[2] // 2), pl.ds(grad_ref.shape[2] // 2, grad_ref.shape[2] // 2)]
    steps_x = [
        remote(down_across.at[:, s], down_came.at[:, s], more_sems.at[0, i], more_sems.at[1, i], over_x)
        for i, s in enumerate(halves_at)
    ]
    steps_h = []

    def down_step(i):
        s = halves_at[i]
        steps_x[i].wait_recv()
        take = pltpu.make_async_copy(down_came.at[:, s], down_stage, more_sems.at[2, i])
        take.start()
        take.wait()
        total = down_own[:, s].astype(wide) + down_stage[...].astype(wide)
        down_own[:, s] = total.astype(low)
        part_rows = came_h.shape[0]
        theirs = down_own.at[pl.ds(pl.multiple_of(other(at_h) * part_rows, 16), part_rows), s]
        copy = remote(theirs, came_h.at[:, s], more_sems.at[0, 2 + i], more_sems.at[1, 2 + i], over_h)
        copy.start()
        steps_h.append(copy)

    c, l, y, near, side, twin = row_peers(even)
    rows = out_ref.shape[0] // chunks
    columns, width = wd.shape
    used = 4 * downs[0].shape[0]
    me = l * 2 + y
    near_at, side_at = near["l"] * 2 + near["y"], side["l"] * 2 + side["y"]
    far_at = other(l) * 2 + other(y)
    own_order = (far_at, side_at, near_at, me)
    twin_order = (far_at, near_at, side_at, me) if even else own_order
    pairs = []
    for p, q in zip(twin_order, own_order):
        pairs += [(other(c) * 4 + p, p, True), (c * 4 + q, q, False)]
    downs = load_rows((downs[:4], downs[4:]), wd, down_sems)
    blocks = []
    for i, (place, _, _) in enumerate(pairs):
        loads = [
            pltpu.make_async_copy(source.at[place], buf.at[i], block_sems.at[i, j])
            for j, (source, buf) in enumerate(
                ((grad_ref, gx), (a_ref, a_s), (b_ref, b_s), (inner_ref, inner_s))
            )
        ]
        for load in loads:
            load.start()
        blocks.append(loads)
    weights = load_columns(gates, wg, weight_sems, 0) + load_columns(ups, wu, weight_sems, 8)
    for load in weights:
        load.start()
    wd[used:, :] = jnp.zeros((columns - used, width), low)
    greet([near, side, twin, over_x, over_h])
    copies = []

    def start(source, target, slot, k, peer):
        copy = remote(source, target, sends.at[slot, k], recvs.at[slot, k], peer)
        copy.start()
        copies.append(copy)

    def arrived(slot, k):
        span = far_in.at[pl.ds(k * rows, rows)]
        remote(span, span, sends.at[slot, k], recvs.at[slot, k], twin).wait_recv()

    def block_arrived(slot):
        remote(
            own_buf.at[0], twin_buf.at[0], sends.at[slot, 0], recvs.at[slot, 0], twin
        ).wait_recv()

    def term(pair, twin_target, own_target):
        span = pl.ds(2 * pair, 2)
        grads = gx[span].reshape(-1, width)

        dinner = contract(grads, wd[...], ((1,), (1,))).reshape(2, -1, columns)
        a_s[span] = (dinner * a_s[span].astype(wide)).astype(low)
        b_s[span] = (dinner * b_s[span].astype(wide)).astype(low)
        if pair == 0:
            wait_all(weights)
        dgate = a_s[span].reshape(-1, columns)
        dup = b_s[span].reshape(-1, columns)

        def second(cols):
            part = contract(dgate, wg[cols, :], ((1,), (1,)))
            part = (part + contract(dup, wu[cols, :], ((1,), (1,)))).astype(low)
            half = part.shape[0] // 2
            twin_target[:, cols] = part[:half]
            own_target[:, cols] = part[half:]

        for_tiles(width, width // 2, second)

    def both(place, span):
        return own_buf[place, span, :].astype(wide) + twin_buf[place, span, :].astype(wide)

    spans = [(k, pl.ds(k * rows, rows)) for k in range(chunks)]
    for loads in blocks:
        wait_all(loads)
    inners = inner_s[...].reshape(-1, columns)
    x_at = lax.axis_index("x")
    down_rows = down_own.shape[0]

    def down_tile(j):
        span = slice(j * (width // 4), (j + 1) * (width // 4))
        part = contract(inners, gx[:, :, span].reshape(-1, width // 4), ((0,), (0,))).astype(low)
        down_s[...] = part
        at = pl.multiple_of(x_at * down_rows, 16)
        down_own[:, span] = down_s[pl.ds(at, down_rows), :]
        at = pl.multiple_of(other(x_at) * down_rows, 16)
        down_across[:, span] = down_s[pl.ds(at, down_rows), :]

    for j in range(4):
        down_tile(j)
        if j % 2:
            steps_x[j // 2].start()
    wait_all(downs)
    for i in range(4):
        twin_place, own_place = pairs[2 * i][1], pairs[2 * i + 1][1]
        term(i, twin_out.at[i], own_buf.at[own_place])
        start(twin_out.at[i], twin_buf.at[twin_place], 3 + i, 0, twin)
        if i >= 1:
            block_arrived(2 + i)
        if i == 1:
            for k, span in spans:
                far_out[span, :] = both(far_at, span).astype(low)
                start(far_out.at[span], far_in.at[span], 0, k, side)
        if i == 2:
            down_step(0)
            for k, span in spans:
                side_out[span, :] = both(side_at, span).astype(low)
                start(side_out.at[span], side_in.at[span], 1, k, side)
    block_arrived(6)
    all_loads = [
        pltpu.make_async_copy(all_ref.at[pairs[i][0]], gx.at[i], all_sems.at[i]) for i in range(8)
    ]
    for load in all_loads:
        load.start()
    stores = []

    def output_term(pair):
        span = pl.ds(2 * pair, 2)
        if pair:
            wait_all(stores[2 * pair - 2 :])
        inner = inner_s[span].reshape(-1, columns)

        def tile(cols):
            part = jnp.dot(inner, wd[:, cols], preferred_element_type=wide)
            terms_s[:, :, cols] = part.astype(low).reshape(2, -1, width // 2)

        for_tiles(width, width // 2, tile)
        for i in range(2):
            _, place, is_twin = pairs[2 * pair + i]
            store = pltpu.make_async_copy(
                terms_s.at[i],
                (terms_twin if is_twin else terms_own).at[place],
                terms_sems.at[2 * pair + i],
            )
            store.start()
            stores.append(store)

    for i in range(2):
        output_term(i)
    for k, span in spans:
        arrived(0, k)
        near_out[span, :] = (both(near_at, span) + far_in[span, :].astype(wide)).astype(low)
        start(near_out.at[span], near_in.at[span], 2, k, near)
    down_step(1)
    for i in range(2, 4):
        output_term(i)
    wait_all(all_loads)
    dgates = a_s[...].reshape(-1, columns)
    dups = b_s[...].reshape(-1, columns)

    half = width // 2
    for gate_ref, up_ref, at in ((gate_across, up_across, other(x_at)), (gate_own, up_own, x_at)):
        for j in range(2):
            cols = pl.ds(pl.multiple_of(at * half + j * (half // 2), 128), half // 2)
            rows_out = slice(j * (half // 2), (j + 1) * (half // 2))
            x = gx[:, :, cols].reshape(-1, half // 2)
            gate_ref[rows_out, :] = contract(x, dgates, ((0,), (0,))).astype(low)
            up_ref[rows_out, :] = contract(x, dups, ((0,), (0,))).astype(low)
    for k, span in spans:
        arrived(1, k)
        arrived(2, k)
        out_ref[span, :] = (
            both(me, span) + side_in[span, :].astype(wide) + near_in[span, :].astype(wide)
        )
    wait_all(stores[6:])
    for copy in steps_h:
        copy.wait()
    part_rows = came_h.shape[0]
    mine = down_own[pl.ds(pl.multiple_of(at_h * part_rows, 16), part_rows), :]
    down_sum[...] = mine.astype(wide) + came_h[...].astype(wide)
    for copy in copies + steps_x:
        copy.wait_send()


def feed_back(grad_all, a, b, inner, all_two, gate_pieces, up_pieces, down_parts, number):
    count, width = a.shape[1], all_two.shape[2]
    columns = a.shape[2]
    chunks = 4 if count % 64 == 0 else 1
    row, part = (8, count, width), (8, count, columns)
    sem = pltpu.SemaphoreType.DMA
    block = pltpu.VMEM((count, width), low)
    vmem = pl.BlockSpec(memory_space=pltpu.VMEM)
    flops = 2 * 8 * count * width * columns * 6
    args = [grad_all.reshape(row), a, b, inner, all_two, *gate_pieces, *up_pieces]
    args += [piece for parts in down_parts for piece in parts]
    own_rows = down_parts[0][0].shape[0]
    return pl.pallas_call(
        functools.partial(feed_back_kernel, True, chunks),
        in_specs=[in_hbm()] * len(args),
        out_specs=[vmem, in_hbm(), in_hbm()] + [vmem] * 6 + [in_hbm()],
        out_shape=[jax.ShapeDtypeStruct((count, width), wide)]
        + [jax.ShapeDtypeStruct((4, count, width), low)] * 2
        + [jax.ShapeDtypeStruct((width // 2, columns), low)] * 4
        + [jax.ShapeDtypeStruct((own_rows, width), wide)]
        + [jax.ShapeDtypeStruct((2 * own_rows, width), low)] * 2,
        scratch_shapes=[
            pltpu.VMEM((2 * own_rows, width), low),
            pltpu.VMEM((2 * own_rows, width // 2), low),
            pltpu.VMEM((own_rows, width), low),
            pltpu.VMEM(row, low),
            pltpu.VMEM((width, columns), low),
            pltpu.VMEM((width, columns), low),
            pltpu.VMEM((columns, width), low),
            pltpu.VMEM(part, low),
            pltpu.VMEM(part, low),
            pltpu.VMEM(part, low),
            pltpu.VMEM((2, count, width), low),
            pltpu.VMEM((4, count, width), low),
            pltpu.VMEM((4, count, width), low),
            pltpu.VMEM((4, count, width), low),
            pltpu.VMEM((columns, width // 4), low),
        ]
        + [block] * 6
        + [
            sem((7, chunks)),
            sem((7, chunks)),
            sem((16,)),
            sem((8,)),
            sem((8, 4)),
            sem((8,)),
            sem((8,)),
            sem((3, 4)),
        ],
        compiler_params=pltpu.CompilerParams(
            collective_id=number, has_side_effects=True, vmem_limit_bytes=60 * 1024 * 1024
        ),
        cost_estimate=pl.CostEstimate(
            flops=flops, bytes_accessed=100 * 1024 * 1024, transcendentals=0
        ),
        name="feed_back",
    )(*args)


def scatter_kernel(even, chunks, n, kinds, *refs):
    m = len(kinds)
    terms, more, refs = refs[:n], refs[n : n + m], refs[n + m :]
    outs, more_out, refs = refs[:n], refs[n : n + m], refs[n + m :]
    bufs, (sends, recvs, local_sems, more_sems) = refs[: 8 * n], refs[8 * n :]
    beside = Beside(kinds, more, more_out, more_sems)
    bufs = [bufs[8 * a : 8 * a + 8] for a in range(n)]
    c, l, y, near, side, twin = row_peers(even)
    rows = outs[0].shape[0] // chunks
    me = l * 2 + y
    near_at, side_at = near["l"] * 2 + near["y"], side["l"] * 2 + side["y"]
    far_at = other(l) * 2 + other(y)
    greet([near, side, twin] + beside.peers)
    beside.start()
    copies = []

    def start(source, target, a, slot, k, peer):
        copy = remote(source, target, sends.at[a, slot, k], recvs.at[a, slot, k], peer)
        copy.start()
        copies.append(copy)

    parts = [(a, k, pl.ds(k * rows, rows)) for k in range(chunks) for a in range(n)]
    twin_side, twin_near = (near_at, side_at) if even else (side_at, near_at)
    for slot, place in ((3, far_at), (4, twin_side), (5, twin_near), (6, me)):
        for a, k, span in parts:
            start(
                terms[a].at[other(c) * 4 + place, span], bufs[a][1].at[place, span], a, slot, k, twin
            )
    loads = []
    for slot, place in ((0, far_at), (1, side_at), (2, near_at), (3, me)):
        for a in range(n):
            load = pltpu.make_async_copy(
                terms[a].at[c * 4 + place], bufs[a][0].at[place], local_sems.at[a, slot]
            )
            load.start()
            loads.append(load)

    def arrived(a, slot, k):
        span = bufs[a][5].at[pl.ds(k * rows, rows)]
        remote(span, span, sends.at[a, slot, k], recvs.at[a, slot, k], twin).wait_recv()

    def both(a, place, span):
        own, came = bufs[a][0], bufs[a][1]
        return own[place, span, :].astype(wide) + came[place, span, :].astype(wide)

    for load in loads[: 2 * n]:
        load.wait()
    for a, k, span in parts:
        far_out, far_in = bufs[a][2], bufs[a][5]
        arrived(a, 3, k)
        far_out[span, :] = both(a, far_at, span).astype(low)
        start(far_out.at[span], far_in.at[span], a, 0, k, side)
    for a, k, span in parts:
        side_out, side_in = bufs[a][3], bufs[a][6]
        arrived(a, 4, k)
        side_out[span, :] = both(a, side_at, span).astype(low)
        start(side_out.at[span], side_in.at[span], a, 1, k, side)
    for load in loads[2 * n :]:
        load.wait()
    for a, k, span in parts:
        near_out, far_in, near_in = bufs[a][4], bufs[a][5], bufs[a][7]
        arrived(a, 5, k)
        arrived(a, 0, k)
        near_out[span, :] = (both(a, near_at, span) + far_in[span, :].astype(wide)).astype(low)
        start(near_out.at[span], near_in.at[span], a, 2, k, near)
    for a, k, span in parts:
        arrived(a, 6, k)
        arrived(a, 1, k)
        outs[a][span, :] = both(a, me, span) + bufs[a][6][span, :].astype(wide)
    for a, k, span in parts:
        arrived(a, 2, k)
        outs[a][span, :] += bufs[a][7][span, :].astype(wide)
    for copy in copies:
        copy.wait_send()
    beside.wait()


def scatter_row(number, *terms, even=False, kinds=(), more=()):
    if lax.axis_size("l") != 2:
        return [
            lax.psum_scatter(t.astype(wide), group, scatter_dimension=0, tiled=True) for t in terms
        ]
    terms = [t.reshape(8, -1, t.shape[1]) for t in terms]
    n, count = len(terms), terms[0].shape[1]
    chunks = 4 if count % 64 == 0 else 1
    scratch = []
    for t in terms:
        scratch += [pltpu.VMEM((4, count, t.shape[2]), low)] * 2
        scratch += [pltpu.VMEM((count, t.shape[2]), low)] * 6
    return pl.pallas_call(
        functools.partial(scatter_kernel, even, chunks, n, kinds),
        in_specs=[in_hbm()] * (n + len(more)),
        out_specs=[pl.BlockSpec(memory_space=pltpu.VMEM)] * n + [in_hbm()] * len(more),
        out_shape=[jax.ShapeDtypeStruct((count, t.shape[2]), wide) for t in terms]
        + [jax.ShapeDtypeStruct(a.shape, low) for a in more],
        scratch_shapes=scratch
        + [
            pltpu.SemaphoreType.DMA((n, 7, chunks)),
            pltpu.SemaphoreType.DMA((n, 7, chunks)),
            pltpu.SemaphoreType.DMA((n, 4)),
            pltpu.SemaphoreType.DMA((2, max(1, len(more)))),
        ],
        compiler_params=pltpu.CompilerParams(
            collective_id=number, has_side_effects=True, vmem_limit_bytes=24 * 1024 * 1024
        ),
        cost_estimate=pl.CostEstimate(flops=0, bytes_accessed=80 * 1024 * 1024, transcendentals=0),
        name="scatter_row",
    )(*terms, *more)


class SumColumns:
    def __init__(self, mine_ref, across_ref, land_ref, out_ref, mine, stage, came_h, sems, local_sems):
        self.h = lax.axis_index("h")
        over_x, self.over_h = {"x": other(lax.axis_index("x"))}, {"h": other(self.h)}
        self.land_ref, self.out_ref = land_ref, out_ref
        self.mine, self.stage, self.came_h = mine, stage, came_h
        self.sems, self.local_sems = sems, local_sems
        rows = mine.shape[2] // 2
        self.parts = [(c, pl.ds(i * rows, rows)) for c in range(2) for i in range(2)]
        self.steps_x = [
            remote(
                across_ref.at[c, :, s], land_ref.at[c, :, s], sems.at[0, i], sems.at[1, i], over_x
            )
            for i, (c, s) in enumerate(self.parts)
        ]
        self.steps_h = []
        self.load = pltpu.make_async_copy(mine_ref, mine, local_sems.at[0])

    def start(self):
        for copy in self.steps_x:
            copy.start()
        self.load.start()

    def step(self, i):
        c, s = self.parts[i]
        if i == 0:
            self.load.wait()
        self.steps_x[i].wait_recv()
        take = pltpu.make_async_copy(self.land_ref.at[c, :, s], self.stage, self.local_sems.at[1])
        take.start()
        take.wait()
        total = self.mine[c, :, s].astype(wide) + self.stage[...].astype(wide)
        self.mine[c, :, s] = total.astype(low)
        copy = remote(
            self.mine.at[c, other(self.h), s], self.came_h.at[c, s], self.sems.at[0, 4 + i],
            self.sems.at[1, 4 + i], self.over_h,
        )
        copy.start()
        self.steps_h.append(copy)

    def end(self):
        for (c, s), copy in zip(self.parts, self.steps_h):
            copy.wait()
            total = self.mine[c, self.h, s].astype(wide) + self.came_h[c, s].astype(wide)
            self.out_ref[c, s] = total.astype(low)
        for copy in self.steps_x:
            copy.wait_send()


def middle_kernel(heads, tile, scale, chunks, *refs):
    ends_ref, branch_ref, gate_mine, gate_across, up_mine, up_across, terms_own, terms_twin = refs[:8]
    query_ref, mixed_ref, packed_ref, logs_ref, cos_in, sin_in, out_in, up_in = refs[8:16]
    resid_ref, refs = refs[16], refs[17:]
    dlow_out, dkv_out, gate_out, up_out, home_ref, by_h_ref, head_out = refs[:7]
    land_gate, land_up, land_twin, refs = *refs[7:10], refs[10:]
    xs, kv, q, o, logs, cos_ref, sin_ref, out_own, up_query, dq, dlow, dkv_sum, dkv = refs[:13]
    refs = refs[13:]
    scatter_bufs, refs = (refs[:7], refs[7:14]), refs[14:]
    stage_a, stage_b, stage_c, sp_far, sp_side, sp_near, sp_far_in, sp_side_in, sp_near_in = refs[:9]
    refs = refs[9:]
    gate_own, gate_h, up_own, up_h, column_stage, refs = *refs[:5], refs[5:]
    go, came_o, came_y, gh, came_hx, came_hh, refs = *refs[:6], refs[6:]
    sends, recvs, sc_sends, sc_recvs, sp_sems, gate_sems, up_sems = refs[:7]
    chain_sems, load_sems, block_sems, local_sems = refs[7:]
    x, h, y_at = [lax.axis_index(a) for a in ("x", "h", "y")]
    c, l, y, near, side, twin = row_peers(False)
    count = branch_ref.shape[0]
    rows = count // chunks
    width = up_query.shape[1] // heads
    half, low_width = width // 2, up_query.shape[0]
    over_x, over_h, over_y = {"x": other(x)}, {"h": other(h)}, {"y": other(y)}
    me = l * 2 + y
    near_at, side_at = near["l"] * 2 + near["y"], side["l"] * 2 + side["y"]
    far_at = other(l) * 2 + other(y)
    flow = RowGather(True, chunks, branch_ref, xs, sends, recvs)
    gate = SumColumns(
        gate_mine, gate_across, land_gate, gate_out, gate_own, column_stage, gate_h, gate_sems,
        local_sems.at[0],
    )
    up = SumColumns(
        up_mine, up_across, land_up, up_out, up_own, column_stage, up_h, up_sems, local_sems.at[1]
    )
    core, cross = lax.axis_index("c"), {"c": other(c), "h": other(h)}
    greet([near, side, twin, over_x, over_h, cross])
    flow.begin(None)
    sp_twin = remote(terms_twin, land_twin, sp_sems.at[0, 0], sp_sems.at[1, 0], twin)
    sp_twin.start()
    gate.start()
    up.start()
    own_load = pltpu.make_async_copy(branch_ref, xs.at[flow.me], load_sems.at[0])
    own_load.start()
    loads = [
        pltpu.make_async_copy(source, target, load_sems.at[1 + i])
        for i, (source, target) in enumerate(
            (
                (packed_ref.at[:, pl.ds(low_width, 2 * width)], kv), (query_ref, q), (mixed_ref, o),
                (logs_ref, logs), (cos_in, cos_ref), (sin_in, sin_ref), (out_in, out_own),
                (up_in, up_query),
            )
        )
    ]
    for load in loads:
        load.start()

    sp_copies = [sp_twin]

    def sp_pair(place):
        first = pltpu.make_async_copy(terms_own.at[place], stage_a, local_sems.at[2, 0])
        second = pltpu.make_async_copy(land_twin.at[place], stage_b, local_sems.at[2, 1])
        first.start()
        second.start()
        first.wait()
        second.wait()
        return stage_a[...].astype(wide) + stage_b[...].astype(wide)

    def sp_send(total, buf, target, slot, peer):
        buf[...] = total.astype(low)
        copy = remote(buf, target, sp_sems.at[0, slot], sp_sems.at[1, slot], peer)
        copy.start()
        sp_copies.append(copy)

    def sp_arrived(slot):
        remote(sp_far, sp_far_in, sp_sems.at[0, slot], sp_sems.at[1, slot], twin).wait_recv()

    dkv_sum[...] = jnp.zeros_like(dkv_sum)
    flow.take_near()
    gate.step(0)
    flow.take_side()
    sp_twin.wait_recv()
    sp_send(sp_pair(far_at), sp_far, sp_far_in, 1, side)
    sp_send(sp_pair(side_at), sp_side, sp_side_in, 2, side)
    gate.step(1)
    flow.take(3)
    flow.take(4)
    gate.step(2)
    flow.take_far()
    flow.take(5)
    gate.step(3)
    flow.take(6)
    own_load.wait()
    wait_all(loads)

    def grad_out(at):
        cols = pl.ds(pl.multiple_of(at * 256, 256), 256)
        for j in range(2):
            span = slice(j * 1024, (j + 1) * 1024)
            branch = xs[:, :, span].reshape(-1, 1024)
            go[at, :, span] = contract(o[:, cols], branch, ((0,), (0,))).astype(low)

    grad_out(other(x))
    out_x = remote(go.at[other(x)], came_o, chain_sems.at[0, 0], chain_sems.at[1, 0], over_x)
    out_x.start()
    grad_out(x)

    def block_rows(begin, size):
        first, offset = begin // count, begin % count
        got = min(size, count - offset)
        parts = [xs[first, offset : offset + got, :]]
        if got < size:
            parts.append(xs[first + 1, : size - got, :])
        return jnp.concatenate(parts, axis=0) if len(parts) > 1 else parts[0]

    def attention(i):
        span, length = slice(i * tile, (i + 1) * tile), (i + 1) * tile
        mask = tile_mask(ends_ref, i * tile, tile, length, heads)
        queries = stacked(q, span, heads, width)
        dmixed = contract(block_rows(i * tile, tile), out_own[...], ((1,), (1,))).astype(low)
        grads = jnp.concatenate(
            [dmixed[:, j * width : (j + 1) * width] for j in range(heads)], axis=0
        )
        outs = stacked(o, span, heads, width)
        delta = jnp.sum(grads.astype(wide) * outs.astype(wide), axis=1, keepdims=True)
        log = jnp.concatenate([logs[j, span, :1] for j in range(heads)], axis=0)
        keys, values = kv[:length, :width], kv[:length, width:]
        scores = contract(queries, keys, ((1,), (1,)))
        weights = jnp.where(mask, jnp.exp(scores - log), 0.0)
        dprob = contract(grads, values, ((1,), (1,)))
        dscore = (weights * (dprob - delta)).astype(low)
        dkv_sum[:length, width:] += contract(weights.astype(low), grads, ((0,), (0,)))
        dkv_sum[:length, :width] += contract(dscore, queries, ((0,), (0,)))
        dquery = contract(dscore, keys, ((1,), (0,))) * scale
        cosine, sine = cos_ref[span, :], sin_ref[span, :]
        for j in range(heads):
            a = dquery[j * tile : (j + 1) * tile, :half]
            b = dquery[j * tile : (j + 1) * tile, half:]
            at = j * width
            dq[span, at : at + half] = (a * cosine + b * sine).astype(low)
            dq[span, at + half : at + width] = (b * cosine - a * sine).astype(low)
        dlow[span, :] = contract(dq[span, :], up_query[...], ((1,), (1,))).astype(low)

    for i in range(q.shape[0] // tile):
        attention(i)
        if i == 3:
            up.step(0)
        if i == 4:
            sp_arrived(1)
            sp_send(
                sp_pair(near_at) + sp_far_in[...].astype(wide), sp_near, sp_near_in, 3, near
            )
    dkv[...] = dkv_sum[...].astype(low)
    flow.end()
    latents = [
        pltpu.make_async_copy(
            packed_ref.at[pl.ds(i * count, count), pl.ds(0, low_width)],
            xs.at[i, :, pl.ds(0, low_width)],
            block_sems.at[i],
        )
        for i in range(8)
    ]
    for load in latents:
        load.start()

    sc_copies = []
    terms = (dlow, dkv)
    sc_parts = [(a, k, pl.ds(k * rows, rows)) for k in range(chunks) for a in range(2)]

    def sc_start(source, target, a, slot, k, peer):
        copy = remote(source, target, sc_sends.at[a, slot, k], sc_recvs.at[a, slot, k], peer)
        copy.start()
        sc_copies.append(copy)

    def sc_arrived(a, slot, k):
        span = scatter_bufs[a][4].at[pl.ds(k * rows, rows)]
        remote(span, span, sc_sends.at[a, slot, k], sc_recvs.at[a, slot, k], twin).wait_recv()

    def term_rows(core, place, k):
        return pl.ds(pl.multiple_of((core * 4 + place) * count + k * rows, 16), rows)

    for slot, place in ((3, far_at), (4, side_at), (5, near_at), (6, me)):
        for a, k, span in sc_parts:
            sc_start(
                terms[a].at[term_rows(other(c), place, k)], scatter_bufs[a][0].at[place, span], a,
                slot, k, twin,
            )

    up.step(1)

    def both(a, place, k, span):
        own = terms[a][term_rows(c, place, k), :]
        return own.astype(wide) + scatter_bufs[a][0][place, span, :].astype(wide)

    for a, k, span in sc_parts:
        far_out, far_in = scatter_bufs[a][1], scatter_bufs[a][4]
        sc_arrived(a, 3, k)
        far_out[span, :] = both(a, far_at, k, span).astype(low)
        sc_start(far_out.at[span], far_in.at[span], a, 0, k, side)
    up.step(2)
    for a, k, span in sc_parts:
        side_out, side_in = scatter_bufs[a][2], scatter_bufs[a][5]
        sc_arrived(a, 4, k)
        side_out[span, :] = both(a, side_at, k, span).astype(low)
        sc_start(side_out.at[span], side_in.at[span], a, 1, k, side)
    wait_all(latents)
    dqs = dq[...]

    def grad_heads(at):
        cols = pl.ds(pl.multiple_of(at * (low_width // 2), 128), low_width // 2)
        latent = xs[:, :, cols].reshape(-1, low_width // 2)
        gh[at] = contract(latent, dqs, ((0,), (0,))).astype(low).reshape(gh.shape[1:])

    grad_heads(other(x))
    head_x = remote(gh.at[other(x)], came_hx, chain_sems.at[0, 1], chain_sems.at[1, 1], over_x)
    head_x.start()
    grad_heads(x)
    up.step(3)
    for a, k, span in sc_parts:
        near_out, far_in, near_in = scatter_bufs[a][3], scatter_bufs[a][4], scatter_bufs[a][6]
        sc_arrived(a, 5, k)
        sc_arrived(a, 0, k)
        near_out[span, :] = (both(a, near_at, k, span) + far_in[span, :].astype(wide)).astype(low)
        sc_start(near_out.at[span], near_in.at[span], a, 2, k, near)
    sp_arrived(2)
    sp_arrived(3)
    resid_load = pltpu.make_async_copy(resid_ref, stage_c, local_sems.at[2, 0])
    resid_load.start()
    resid_load.wait()
    total = sp_pair(me) + sp_side_in[...].astype(wide) + sp_near_in[...].astype(wide)
    sp_copies[1].wait_send()
    sp_far[...] = (stage_c[...] + total).astype(low)
    to_home = remote(sp_far, home_ref, sp_sems.at[0, 4], sp_sems.at[1, 4], cross)

    @pl.when(core != h)
    def _():
        to_home.start()

    @pl.when(core == h)
    def _():
        home_ref[...] = sp_far[...]

    out_x.wait_recv()
    total = go[x].astype(wide) + came_o[...].astype(wide)
    go[x] = total.astype(low)
    part = by_h_ref.shape[1]
    mine_rows = pl.ds(pl.multiple_of(y * part, part), part)
    their_rows = pl.ds(pl.multiple_of(other(y) * part, part), part)
    out_y = remote(
        go.at[x, their_rows], came_y, chain_sems.at[0, 2], chain_sems.at[1, 2], over_y
    )
    out_y.start()
    head_x.wait_recv()
    gh[x] = (gh[x].astype(wide) + came_hx[...].astype(wide)).astype(low)
    head_h = remote(
        gh.at[x, :, other(h)], came_hh, chain_sems.at[0, 3], chain_sems.at[1, 3], over_h
    )
    head_h.start()
    gate.end()
    outs = (dlow_out, dkv_out)
    for a, k, span in sc_parts:
        sc_arrived(a, 6, k)
        sc_arrived(a, 1, k)
        outs[a][span, :] = both(a, me, k, span) + scatter_bufs[a][5][span, :].astype(wide)
    for a, k, span in sc_parts:
        sc_arrived(a, 2, k)
        outs[a][span, :] += scatter_bufs[a][6][span, :].astype(wide)
    by_h_ref[y] = go[x, mine_rows, :]
    out_y.wait_recv()
    by_h_ref[other(y)] = came_y[...]
    head_h.wait_recv()
    head_out[...] = (gh[x, :, h].astype(wide) + came_hh[...].astype(wide)).astype(low)
    up.end()
    for copy in sp_copies[:1] + sp_copies[2:] + sc_copies + [out_x, out_y, head_x, head_h]:
        copy.wait_send()

    @pl.when(core != h)
    def _():
        to_home.wait()


def middle(
    ends, branch, gate_terms, up_terms, spread, query, mixed, packed, logs, cosine, sine, out_own,
    up_query, resid, heads, scale, number,
):
    count, width = branch.shape
    length, columns = query.shape
    low_width = up_query.shape[0]
    chunks = 4
    args = [
        ends, branch, *gate_terms, *up_terms, *spread, query, mixed, packed, logs, cosine, sine,
        out_own, up_query, resid,
    ]
    kept = (2,) + gate_terms[0].shape[2:]
    part = columns // 4
    rows_up = low_width // 8
    vmem, sem = pl.BlockSpec(memory_space=pltpu.VMEM), pltpu.SemaphoreType.DMA
    shapes = [
        ((count, low_width), wide),
        ((count, columns), wide),
        (kept, low),
        (kept, low),
        ((count, width), low),
        ((2, part, width), low),
        ((2, rows_up, columns), low),
        (gate_terms[0].shape, low),
        (up_terms[0].shape, low),
        (spread[0].shape, low),
    ]
    block = pltpu.VMEM((count, width), low)

    def scatter_scratch(w):
        return [pltpu.VMEM((4, count, w), low)] + [pltpu.VMEM((count, w), low)] * 6

    return pl.pallas_call(
        functools.partial(middle_kernel, heads, tile_of(length), scale, chunks),
        in_specs=[pl.BlockSpec(memory_space=pltpu.SMEM)] + [in_hbm()] * (len(args) - 1),
        out_specs=[vmem] * 7 + [in_hbm()] * 3,
        out_shape=[jax.ShapeDtypeStruct(*s) for s in shapes],
        scratch_shapes=[
            pltpu.VMEM((8, count, width), low),
            pltpu.VMEM((length, columns), low),
            pltpu.VMEM((length, columns), low),
            pltpu.VMEM((length, columns), low),
            pltpu.VMEM(logs.shape, wide),
            pltpu.VMEM(cosine.shape, wide),
            pltpu.VMEM(sine.shape, wide),
            pltpu.VMEM(out_own.shape, low),
            pltpu.VMEM(up_query.shape, low),
            pltpu.VMEM((length, columns), low),
            pltpu.VMEM((length, low_width), low),
            pltpu.VMEM((length, columns), wide),
            pltpu.VMEM((length, columns), low),
            *scatter_scratch(low_width),
            *scatter_scratch(columns),
            block,
            block,
            pltpu.VMEM((count, width), wide),
            *[block] * 6,
            pltpu.VMEM(gate_terms[0].shape, low),
            pltpu.VMEM(kept, low),
            pltpu.VMEM(up_terms[0].shape, low),
            pltpu.VMEM(kept, low),
            pltpu.VMEM((2, kept[1] // 2, kept[2]), low),
            pltpu.VMEM((2, columns // 2, width), low),
            pltpu.VMEM((columns // 2, width), low),
            pltpu.VMEM((part, width), low),
            pltpu.VMEM((2, 2, 2, rows_up, columns), low),
            pltpu.VMEM((2, 2, rows_up, columns), low),
            pltpu.VMEM((2, rows_up, columns), low),
            sem((7, chunks)),
            sem((7, chunks)),
            sem((2, 7, chunks)),
            sem((2, 7, chunks)),
            sem((2, 5)),
            sem((2, 8)),
            sem((2, 8)),
            sem((2, 4)),
            sem((9,)),
            sem((8,)),
            sem((3, 2)),
        ],
        compiler_params=pltpu.CompilerParams(
            collective_id=number, has_side_effects=True, vmem_limit_bytes=63 * 1024 * 1024
        ),
        cost_estimate=pl.CostEstimate(
            flops=18 * length * length * columns,
            bytes_accessed=200 * 1024 * 1024,
            transcendentals=length * length * heads // 2,
        ),
        name="middle",
    )(*args)


def norm_back_rows(incoming, source, gain):
    scale = rms_scale(source)
    weighted = incoming * gain
    mean = jnp.mean(weighted * source, axis=-1, keepdims=True)
    grad = scale * weighted - source * (scale * scale * scale) * mean
    return grad, jnp.sum(incoming * source * scale, axis=0, keepdims=True)


def shut_kernel(part, head_dim, order, n_in, n_out, *refs):
    ins, outs, refs = refs[:n_in], refs[n_in : n_in + n_out], refs[n_in + n_out :]
    (
        dlow_ref, dkv_ref, latent_ref, gain_latent_ref, cos_ref, sin_ref, hidden_ref, in_full_ref,
        home_ref, gain_one_ref, dresid_ref, gain_two_ref, gate_ref, up_ref, heads_ref, kept_ref,
        across_ref,
    ) = ins
    sum_ref, tokens_ref, gate_out, up_out, heads_out, out_ref = outs
    full, mapped, terms, gains, twin_buf, held, came, moved, swap_buf = refs[:9]
    gate_in, up_in, heads_in, across_in = refs[9:13]
    sends, recvs, set_sends, set_recvs, swap_sems, local_sems = refs[13:]
    x, c, h, l, y = [lax.axis_index(a) for a in every]
    hops = {
        1: {"h": other(h)},
        2: {"l": other(l)},
        4: {"y": other(y)},
        8: {"x": other(x)},
    }
    twin = {"c": other(c)}
    cross = {"c": other(c), "h": other(h)}
    me = (c * 2 + l) * 2 + y

    def group_peer(k):
        return {"c": other(c, k // 4), "l": other(l, k // 2 % 2), "y": other(y, k % 2)}

    def group_index(k):
        peer = group_peer(k)
        return (peer["c"] * 2 + peer["l"]) * 2 + peer["y"]

    def index(code, core):
        at_x, at_l = other(x, code // 8 % 2), other(l, code // 2 % 2)
        return (((at_x * 2 + core) * 2 + other(h, code % 2)) * 2 + at_l) * 2 + other(y, code // 4 % 2)

    load = pltpu.make_async_copy(in_full_ref, full, local_sems.at[0])
    load.start()
    greet([hops[1], hops[8], cross] + [group_peer(k) for k in range(1, 8)])
    set_copies = []
    for i, (source, target) in enumerate(
        ((heads_ref, heads_in), (gate_ref, gate_in), (up_ref, up_in))
    ):
        for k in range(1, 8):
            copy = remote(
                source.at[group_index(k)], target.at[me], set_sends.at[i, k], set_recvs.at[i, k],
                group_peer(k),
            )
            copy.start()
            set_copies.append(copy)
    set_loads = [
        pltpu.make_async_copy(source.at[me], target.at[me], local_sems.at[1 + i])
        for i, (source, target) in enumerate(
            ((heads_ref, heads_in), (gate_ref, gate_in), (up_ref, up_in))
        )
    ]
    for copy in set_loads:
        copy.start()
    exchange = remote(across_ref, across_in, swap_sems.at[0], swap_sems.at[1], hops[1])
    tokens_move = remote(swap_buf, moved, swap_sems.at[4], swap_sems.at[5], cross)
    width, low_width = hidden_ref.shape[1], latent_ref.shape[1]
    half = head_dim // 2
    dlatent, dgain_latent = norm_back_rows(dlow_ref[...], latent_ref[...], gain_latent_ref[...])
    mapped[:, :low_width] = dlatent.astype(low)
    a, b = dkv_ref[:, :half], dkv_ref[:, half:head_dim]
    cosine, sine = cos_ref[...], sin_ref[...]
    mapped[:, low_width : low_width + half] = (a * cosine + b * sine).astype(low)
    mapped[:, low_width + half : low_width + head_dim] = (b * cosine - a * sine).astype(low)
    mapped[:, low_width + head_dim : low_width + 2 * head_dim] = dkv_ref[:, head_dim:].astype(low)
    mapped[:, low_width + 2 * head_dim :] = jnp.zeros((mapped.shape[0], 128), low)
    load.wait()
    dmapped = mapped[...]
    weights = full[...].reshape(width, -1)
    dhidden = contract(dmapped, weights, ((1,), (1,)))
    dinput, dgain_one = norm_back_rows(dhidden, home_ref[...].astype(wide), gain_one_ref[...])
    dtokens = dresid_ref[...] + dinput
    tokens_ref[...] = dtokens
    swap_buf[...] = dtokens.astype(low)

    gains[...] = jnp.zeros_like(gains)
    gains[0:1, :width] = dgain_one
    gains[1:2, :width] = gain_two_ref[...]
    gains[2:3, :low_width] = dgain_latent
    rows = terms.shape[1]
    low_part = low_width // 32
    used = low_width + 2 * head_dim
    for at in range(0, 32, 4):
        left = hidden_ref[:, at * rows : (at + 4) * rows]
        block = contract(left, dmapped[:, :used], ((0,), (0,))).astype(low)
        terms[at : at + 4, :, :used] = block.reshape(4, rows, used)
        for i in range(at, at + 4):
            tile = jnp.concatenate(
                [
                    gains[0:2, i * rows : i * rows + 128],
                    gains[2:3, i * low_part : i * low_part + 128],
                    jnp.zeros((rows - 3, 128), wide),
                ],
                axis=0,
            )
            terms[i, :, used:] = tile.astype(low)
    copies = []

    def start(source, target, slot, peer):
        copy = remote(source, target, sends.at[slot], recvs.at[slot], peer)
        copy.start()
        copies.append(copy)

    def arrived(slot):
        remote(came.at[0], came.at[0], sends.at[slot], recvs.at[slot], twin).wait_recv()

    for code in range(15, -1, -1):
        start(terms.at[index(code, 1 - c)], twin_buf.at[code], 16 + code, twin)
    for code in range(15, -1, -1):
        arrived(16 + code)
        total = terms[index(code, c)].astype(wide) + twin_buf[code].astype(wide)
        for hop in (8, 4, 2, 1):
            if code < hop:
                arrived(code + hop)
                total = total + came[code + hop].astype(wide)
        if code == 0:
            sum_ref[...] = total
        else:
            held[code] = total.astype(low)
            hop = 1 << (code.bit_length() - 1)
            start(held.at[code], came.at[code], code, hops[hop])
        if code == 8:

            @pl.when(c != h)
            def _():
                tokens_move.start()

            exchange.start()

        if code == 4:
            for copy in set_loads:
                copy.wait()
            for copy in set_copies:
                copy.wait()
            for source, target in ((gate_in, gate_out), (up_in, up_out)):
                for place, blocks in enumerate(order):
                    for j, block in enumerate(blocks):
                        target[:, block * part : (block + 1) * part] = source[
                            place, :, j * part : (j + 1) * part
                        ].astype(wide)
            for place in range(8):
                core, at_l, at_y = place // 4, place // 2 % 2, place % 2
                for j in range(2):
                    head = ((j * 2 + core) * 2 + at_y) * 2 + at_l
                    heads_out[:, head * head_dim : (head + 1) * head_dim] = heads_in[
                        place, :, j * head_dim : (j + 1) * head_dim
                    ].astype(wide)
    exchange.wait()
    out_ref[...] = kept_ref[...].astype(wide) + across_in[...].astype(wide)
    for copy in copies:
        copy.wait_send()

    @pl.when(c != h)
    def _():
        tokens_move.wait()
        tokens_ref[...] = moved[...].astype(wide)


def shut(
    dlow, dkv, latent, gain_latent, cosine, sine, hidden, in_full, home, gain_one, dresid, dgain_two,
    gate_terms, up_terms, head_terms, kept, across, part, order, number,
):
    count, width = hidden.shape
    head_dim = dkv.shape[1] // 2
    rows, columns = in_full.shape[1:]
    vmem, sem = pl.BlockSpec(memory_space=pltpu.VMEM), pltpu.SemaphoreType.DMA
    args = [
        dlow, dkv, latent, gain_latent, cosine, sine, hidden, in_full, home, gain_one, dresid,
        dgain_two, gate_terms, up_terms, head_terms, kept, across,
    ]
    hbm = {7, 12, 13, 14, 16}
    ff = len(order) * len(order[0]) * part
    shapes = [
        ((rows, columns), wide),
        ((count, width), wide),
        ((gate_terms.shape[1], ff), wide),
        ((up_terms.shape[1], ff), wide),
        ((head_terms.shape[1], 8 * head_terms.shape[2]), wide),
        (kept.shape, wide),
    ]
    blocks = pltpu.VMEM((16, rows, columns), low)
    return pl.pallas_call(
        functools.partial(shut_kernel, part, head_dim, order, len(args), len(shapes)),
        in_specs=[in_hbm() if i in hbm else vmem for i in range(len(args))],
        out_specs=[vmem] * len(shapes),
        out_shape=[jax.ShapeDtypeStruct(*s) for s in shapes],
        scratch_shapes=[
            pltpu.VMEM(in_full.shape, low),
            pltpu.VMEM((count, columns), low),
            pltpu.VMEM(in_full.shape, low),
            pltpu.VMEM((16, width + 128), wide),
            blocks,
            blocks,
            blocks,
            pltpu.VMEM((count, width), low),
            pltpu.VMEM((count, width), low),
            pltpu.VMEM(gate_terms.shape, low),
            pltpu.VMEM(up_terms.shape, low),
            pltpu.VMEM(head_terms.shape, low),
            pltpu.VMEM(across.shape, low),
            sem((32,)),
            sem((32,)),
            sem((3, 8)),
            sem((3, 8)),
            sem((6,)),
            sem((6,)),
        ],
        compiler_params=pltpu.CompilerParams(
            collective_id=number, has_side_effects=True, vmem_limit_bytes=60 * 1024 * 1024
        ),
        cost_estimate=pl.CostEstimate(flops=0, bytes_accessed=150 * 1024 * 1024, transcendentals=0),
        name="shut",
    )(*args)


def split_kernel(part, order, a_ref, b_ref, a_out, b_out):
    for source, target in ((a_ref, a_out), (b_ref, b_out)):
        used, total = len(order[0]) * part, target.shape[2]
        for place, blocks in enumerate(order):
            for j, block in enumerate(blocks):
                target[place, :, j * part : (j + 1) * part] = source[
                    :, block * part : (block + 1) * part
                ]
            if used < total:
                target[place, :, used:] = jnp.zeros((target.shape[1], total - used), target.dtype)


def join_kernel(part, order, a_ref, b_ref, a_out, b_out):
    for source, target in ((a_ref, a_out), (b_ref, b_out)):
        for place, blocks in enumerate(order):
            for j, block in enumerate(blocks):
                target[:, block * part : (block + 1) * part] = source[
                    place, :, j * part : (j + 1) * part
                ].astype(wide)


def column_order(n_x, n_l):
    return [
        [
            (((x * 2 + c) * 2 + h) * n_l + l) * 2 + y
            for x in range(n_x)
            for h in range(2)
        ]
        for c in range(2)
        for l in range(n_l)
        for y in range(2)
    ]


def split_columns(a, b, part, order, total):
    shape = jax.ShapeDtypeStruct((len(order), a.shape[0], total), a.dtype)
    return pl.pallas_call(
        functools.partial(split_kernel, part, order), out_shape=[shape] * 2, name="split_columns"
    )(a, b)


def join_columns(a, b, part, order):
    shape = jax.ShapeDtypeStruct((a.shape[1], len(order) * len(order[0]) * part), wide)
    return pl.pallas_call(
        functools.partial(join_kernel, part, order), out_shape=[shape] * 2, name="join_columns"
    )(a, b)


def first_allowed(ends_ref, count, places):
    start = jnp.zeros_like(places)
    for j in range(count):
        end = ends_ref[j]
        start = jnp.where(places >= end, end, start)
    return jnp.where(places >= ends_ref[count - 1], places, start)


def contract(left, right, dims):
    return lax.dot_general(left, right, (dims, ((), ())), preferred_element_type=wide)


def stacked(ref, span, heads, width):
    return jnp.concatenate(
        [ref[span, j * width : (j + 1) * width] for j in range(heads)], axis=0
    )


def tile_mask(ends_ref, begin, tile, length, heads):
    rows = begin + lax.broadcasted_iota(jnp.int32, (tile, 1), 0)
    lows = first_allowed(ends_ref, ends_ref.shape[0], rows)
    rows = jnp.concatenate([rows] * heads, axis=0)
    lows = jnp.concatenate([lows] * heads, axis=0)
    columns = lax.broadcasted_iota(jnp.int32, (heads * tile, length), 1)
    return (columns >= lows) & (columns <= rows)


def attend_kernel(heads, tile, ends_ref, q_ref, k_ref, v_ref, o_ref, log_ref):
    width = k_ref.shape[1]
    for i in range(q_ref.shape[0] // tile):
        span, length = slice(i * tile, (i + 1) * tile), (i + 1) * tile
        mask = tile_mask(ends_ref, i * tile, tile, length, heads)
        scores = contract(stacked(q_ref, span, heads, width), k_ref[:length, :], ((1,), (1,)))
        scores = jnp.where(mask, scores, masked_value)
        top = jnp.max(scores, axis=1, keepdims=True)
        weights = jnp.exp(scores - top)
        total = jnp.sum(weights, axis=1, keepdims=True)
        mixed = contract(weights.astype(low), v_ref[:length, :], ((1,), (0,))) / total
        log = jnp.broadcast_to(top + jnp.log(total), (heads * tile, 128))
        for j in range(heads):
            part = slice(j * tile, (j + 1) * tile)
            o_ref[span, j * width : (j + 1) * width] = mixed[part].astype(low)
            log_ref[j, span, :] = log[part]


def attend_back_kernel(
    heads, tile, scale, ends_ref, q_ref, g_ref, o_ref, k_ref, v_ref, log_ref, cos_ref, sin_ref,
    dq_ref, dkv_ref, sum_ref,
):
    width = k_ref.shape[1]
    half = width // 2
    sum_ref[...] = jnp.zeros_like(sum_ref)
    for i in range(q_ref.shape[0] // tile):
        span, length = slice(i * tile, (i + 1) * tile), (i + 1) * tile
        mask = tile_mask(ends_ref, i * tile, tile, length, heads)
        queries = stacked(q_ref, span, heads, width)
        grads = stacked(g_ref, span, heads, width)
        outs = stacked(o_ref, span, heads, width)
        delta = jnp.sum(grads.astype(wide) * outs.astype(wide), axis=1, keepdims=True)
        log = jnp.concatenate([log_ref[j, span, :1] for j in range(heads)], axis=0)
        keys, values = k_ref[:length, :], v_ref[:length, :]
        scores = contract(queries, keys, ((1,), (1,)))
        weights = jnp.where(mask, jnp.exp(scores - log), 0.0)
        dprob = contract(grads, values, ((1,), (1,)))
        dscore = (weights * (dprob - delta)).astype(low)
        sum_ref[:length, width:] += contract(weights.astype(low), grads, ((0,), (0,)))
        sum_ref[:length, :width] += contract(dscore, queries, ((0,), (0,)))
        dquery = contract(dscore, keys, ((1,), (0,))) * scale
        cosine, sine = cos_ref[span, :], sin_ref[span, :]
        for j in range(heads):
            a = dquery[j * tile : (j + 1) * tile, :half]
            b = dquery[j * tile : (j + 1) * tile, half:]
            at = j * width
            dq_ref[span, at : at + half] = (a * cosine + b * sine).astype(low)
            dq_ref[span, at + half : at + width] = (b * cosine - a * sine).astype(low)
    dkv_ref[...] = sum_ref[...].astype(low)


def attend_whole_kernel(
    heads, tile, scale, ends_ref, packed_ref, up_ref, cos_ref, sin_ref, own_ref, other_ref,
    q_ref, o_ref, log_ref, terms_ref, out_ref,
):
    x = lax.axis_index("x")
    width = up_ref.shape[1] // heads
    half, low_width = width // 2, up_ref.shape[0]
    rows = own_ref.shape[0]
    out_ref[pl.ds(pl.multiple_of(x * rows, rows), rows), :] = own_ref[...]
    out_ref[pl.ds(pl.multiple_of(other(x) * rows, rows), rows), :] = other_ref[...]
    for i in range(q_ref.shape[0] // tile):
        span, length = slice(i * tile, (i + 1) * tile), (i + 1) * tile
        raw = jnp.dot(packed_ref[span, :low_width], up_ref[...], preferred_element_type=wide)
        cosine, sine = cos_ref[span, :] * scale, sin_ref[span, :] * scale
        queries = []
        for j in range(heads):
            a, b = turn(raw[:, j * width : (j + 1) * width], cosine, sine)
            q_ref[span, j * width : j * width + half] = a.astype(low)
            q_ref[span, j * width + half : (j + 1) * width] = b.astype(low)
        mask = tile_mask(ends_ref, i * tile, tile, length, heads)
        keys = packed_ref[:length, low_width : low_width + width]
        values = packed_ref[:length, low_width + width :]
        scores = contract(stacked(q_ref, span, heads, width), keys, ((1,), (1,)))
        scores = jnp.where(mask, scores, masked_value)
        top = jnp.max(scores, axis=1, keepdims=True)
        weights = jnp.exp(scores - top)
        total = jnp.sum(weights, axis=1, keepdims=True)
        mixed = contract(weights.astype(low), values, ((1,), (0,))) / total
        log = jnp.broadcast_to(top + jnp.log(total), (heads * tile, 128))
        for j in range(heads):
            part = slice(j * tile, (j + 1) * tile)
            o_ref[span, j * width : (j + 1) * width] = mixed[part].astype(low)
            log_ref[j, span, :] = log[part]
        terms_ref[span, :] = jnp.dot(
            o_ref[span, :], out_ref[...], preferred_element_type=wide
        ).astype(low)


def attend_whole(ends, packed, up_query, cosine, sine, own_heads, other_heads, heads, scale):
    length, width = packed.shape[0], own_heads.shape[1]
    columns = up_query.shape[1]
    vmem = pl.BlockSpec(memory_space=pltpu.VMEM)
    return pl.pallas_call(
        functools.partial(attend_whole_kernel, heads, tile_of(length), scale),
        in_specs=[pl.BlockSpec(memory_space=pltpu.SMEM)] + [vmem] * 6,
        out_specs=[vmem] * 5,
        out_shape=[
            jax.ShapeDtypeStruct((length, columns), low),
            jax.ShapeDtypeStruct((length, columns), low),
            jax.ShapeDtypeStruct((heads, length, 128), wide),
            jax.ShapeDtypeStruct((length, width), low),
            jax.ShapeDtypeStruct((columns, width), low),
        ],
        compiler_params=pltpu.CompilerParams(vmem_limit_bytes=56 * 1024 * 1024),
        cost_estimate=pl.CostEstimate(
            flops=12 * length * length * columns,
            bytes_accessed=16 * length * columns,
            transcendentals=length * length * heads // 2,
        ),
        name="attend",
    )(ends, packed, up_query, cosine, sine, own_heads, other_heads)


def tile_of(length):
    return next(t for t in (256, 128, 64, 32, 16, 8) if length % t == 0)


def attend(ends, query, packed, heads):
    length, width = query.shape[0], query.shape[1] // heads
    tile = tile_of(length)
    first = packed.shape[1] // width - 2
    return pl.pallas_call(
        functools.partial(attend_kernel, heads, tile),
        grid=(1,),
        in_specs=[
            pl.BlockSpec(memory_space=pltpu.SMEM),
            pl.BlockSpec((length, heads * width), lambda i: (0, 0)),
            pl.BlockSpec((length, width), lambda i: (0, first)),
            pl.BlockSpec((length, width), lambda i: (0, first + 1)),
        ],
        out_specs=[
            pl.BlockSpec((length, heads * width), lambda i: (0, 0)),
            pl.BlockSpec((heads, length, 128), lambda i: (0, 0, 0)),
        ],
        out_shape=[
            jax.ShapeDtypeStruct((length, heads * width), low),
            jax.ShapeDtypeStruct((heads, length, 128), wide),
        ],
        compiler_params=pltpu.CompilerParams(vmem_limit_bytes=56 * 1024 * 1024),
        cost_estimate=pl.CostEstimate(
            flops=6 * length * length * width * heads,
            bytes_accessed=8 * length * width * heads,
            transcendentals=length * length * heads // 2,
        ),
        name="attend",
    )(ends, query, packed, packed)


def attend_back(ends, query, grad, mixed, packed, logs, cosine, sine, heads, scale):
    length, width = query.shape[0], query.shape[1] // heads
    tile = tile_of(length)
    first = packed.shape[1] // width - 2
    rows = pl.BlockSpec((length, heads * width), lambda i: (0, 0))
    angle = pl.BlockSpec((length, width // 2), lambda i: (0, 0))
    return pl.pallas_call(
        functools.partial(attend_back_kernel, heads, tile, scale),
        grid=(1,),
        in_specs=[
            pl.BlockSpec(memory_space=pltpu.SMEM),
            rows,
            rows,
            rows,
            pl.BlockSpec((length, width), lambda i: (0, first)),
            pl.BlockSpec((length, width), lambda i: (0, first + 1)),
            pl.BlockSpec((heads, length, 128), lambda i: (0, 0, 0)),
            angle,
            angle,
        ],
        out_specs=[rows, pl.BlockSpec((length, 2 * width), lambda i: (0, 0))],
        out_shape=[
            jax.ShapeDtypeStruct((length, heads * width), low),
            jax.ShapeDtypeStruct((length, 2 * width), low),
        ],
        scratch_shapes=[pltpu.VMEM((length, 2 * width), wide)],
        compiler_params=pltpu.CompilerParams(vmem_limit_bytes=56 * 1024 * 1024),
        cost_estimate=pl.CostEstimate(
            flops=10 * length * length * width * heads,
            bytes_accessed=16 * length * width * heads,
            transcendentals=length * length * heads // 2,
        ),
        name="attend_back",
    )(ends, query, grad, mixed, packed, packed, logs, cosine, sine)


def on_device(
    tokens,
    lengths,
    cotangent,
    norm_one,
    query_down,
    query_gain,
    query_up,
    key_proj,
    value_proj,
    out_proj,
    norm_two,
    gate_proj,
    up_proj,
    down_proj,
):
    n_x, n_l = lax.axis_size("x"), lax.axis_size("l")
    x, c, h, l, y = [lax.axis_index(a) for a in every]
    n_dev = n_x * 8 * n_l
    n_group = 4 * n_l
    me = group_place()
    count, width = tokens.shape
    row_len = count * n_group
    latent_width = query_down.shape[1]
    head_dim = key_proj.shape[1]
    shard = query_down.shape[0]
    heads = query_up.shape[1] // head_dim // n_group
    ff_part = down_proj.shape[0]
    ff_own = ff_part * n_x * 2
    ff_pad = -(-ff_own // 128) * 128
    natural = n_x == 2 and n_l == 2
    scale = 1.0 / math.sqrt(head_dim)
    order = column_order(n_x, n_l)
    mapped_width = latent_width + 2 * head_dim

    gains = jnp.zeros((shard, 128), low)
    gains = gains.at[0, :shard].set(norm_one).at[1, :shard].set(norm_two)
    gains = gains.at[2, : query_gain.shape[0]].set(query_gain)
    small = jnp.concatenate([query_down, key_proj, value_proj, gains], axis=1)
    rows_up = query_up.shape[0]
    if natural:
        head_cols = query_up.reshape(rows_up, 2, 2, 2, 2, head_dim)
        head_cols = head_cols.transpose(2, 4, 3, 0, 1, 5)
    else:
        head_cols = query_up.reshape(rows_up, n_group, -1).transpose(1, 0, 2)
    head_cols = head_cols.reshape(n_group, rows_up, heads * head_dim)
    if natural:
        lens = jnp.pad(lengths, ((0, 7), (0, 128 - lengths.shape[1])))
        in_full, own_heads, (up_query, gate_rows, up_rows), (home, lens) = open_exchange(
            small, out_proj, head_cols, gate_proj, up_proj, [tokens, lens], ff_part, order, ff_pad
        )
        row_lengths = lens[0, : lengths.shape[1]]
    else:
        in_full = lax.all_gather(small, every, axis=0)
        home, grad_home, row_lengths = [swap_home(a) for a in (tokens, cotangent, lengths)]
        row_lengths = row_lengths[0]
        gate_cols, up_cols = split_columns(gate_proj, up_proj, ff_part, order, ff_pad)
        up_query, gate_rows, up_rows = [
            all_to_all_row(a) for a in (head_cols, gate_cols, up_cols)
        ]
        up_query = up_query.reshape((2, -1) + up_query.shape[1:])
        up_query = lax.all_gather(lax.all_gather(up_query, "h", axis=1), "x", axis=0)
    up_query = up_query.reshape(latent_width, -1)
    gate_rows = gate_rows.reshape(2, -1, ff_pad)
    up_rows = up_rows.reshape(2, -1, ff_pad)
    gain_one = in_full[:, 0, mapped_width : mapped_width + shard].reshape(width).astype(wide)
    gain_two = in_full[:, 1, mapped_width : mapped_width + shard].reshape(width).astype(wide)
    gain_latent = in_full[:, 2, mapped_width : mapped_width + query_gain.shape[0]]
    gain_latent = gain_latent.reshape(latent_width).astype(wide)
    in_full = in_full.reshape(width, -1)

    inputs = home.astype(wide)
    mapped_rates = jnp.exp(
        jnp.arange(head_dim // 2, dtype=wide) * (-math.log(10000.0) / (head_dim // 2))
    )
    ends = jnp.cumsum(row_lengths, dtype=jnp.int32)
    places = jnp.arange(row_len, dtype=jnp.int32)
    begins = jnp.max(jnp.where(places[:, None] >= ends[None, :], ends[None, :], 0), axis=1)
    if not natural:
        phases = (places - begins).astype(wide)[:, None] * mapped_rates
        cosine, sine = jnp.cos(phases), jnp.sin(phases)
        own_cos = lax.dynamic_slice_in_dim(cosine, me * count, count)
        own_sin = lax.dynamic_slice_in_dim(sine, me * count, count)

    if natural:
        own_heads = own_heads.reshape(-1, width)
        gate_a, gate_b, up_a, up_b = gate_rows[0], gate_rows[1], up_rows[0], up_rows[1]
        down_a, down_b = down_proj[:, : width // 2], down_proj[:, width // 2 :]
        heads_x = flip(own_heads, "x")
    else:
        out_full = lax.all_gather(out_proj, every, axis=0, tiled=True)
        out_own = lax.dynamic_slice_in_dim(out_full, me * heads * head_dim, heads * head_dim)
        gate_own, up_own = [
            lax.all_gather(lax.all_gather(a, "h", axis=1), "x", axis=0).reshape(width, -1)
            for a in (gate_rows, up_rows)
        ]
        down_own = lax.all_gather(lax.all_gather(down_proj, "h", axis=0), "x", axis=0)
        down_own = jnp.pad(down_own.reshape(-1, width), ((0, ff_pad - ff_own), (0, 0)))

    scale_one = rms_scale(inputs)
    if natural:
        packed, hidden, latent, cosine, sine, own_cos, own_sin, gate_a_h, gate_b_h = front(
            ends, home, in_full, gain_one[None], gain_latent[None], mapped_rates[None], row_len, 2,
            ("h", "h"), (gate_a, gate_b),
        )
        packed, heads_x, up_a = together(packed, heads_x, up_a)
        up_a_h, up_b_h = flip(up_a, "h"), flip(after(up_b, packed), "h")
        gate_x = [flip(a, "x") for a in (gate_a, gate_b, gate_a_h, gate_b_h)]
        all_latent = packed[:, :latent_width]
        query, mixed, logs, terms, out_own = attend_whole(
            ends, packed, up_query, cosine, sine, own_heads, heads_x, heads, scale
        )
        terms, up_a_h, up_b_h = together(terms, up_a_h, up_b_h)
        up_x = [flip(a, "x") for a in (up_a, up_b, up_a_h, up_b_h)]
        attended, down_a_h, down_b_h = scatter_row(3, terms, kinds=("h", "h"), more=(down_a, down_b))
        attended, gate_x, up_x = together(attended, gate_x, up_x)
    else:
        hidden = (inputs * scale_one * gain_one).astype(low)
        mapped = dot(hidden, in_full)
        latent = mapped[:, :latent_width]
        scale_latent = rms_scale(latent)
        latent_low = (latent * scale_latent * gain_latent).astype(low)
        keys = mapped[:, latent_width : latent_width + head_dim]
        keys = rotate(keys, own_cos, own_sin).astype(low)
        values = mapped[:, latent_width + head_dim : mapped_width].astype(low)
        packed = gather_row(jnp.concatenate([latent_low, keys, values], axis=1), 2)
        grad_all = lax.all_gather(grad_home, group, axis=0, tiled=True)
        all_latent = packed[:, :latent_width]
        query_raw = dot(all_latent, up_query)
        query = jnp.concatenate(
            [
                rotate(query_raw[:, j * head_dim : (j + 1) * head_dim], cosine, sine)
                for j in range(heads)
            ],
            axis=1,
        ).astype(low) * jnp.asarray(scale, low)
        mixed, logs = attend(ends, query, packed, heads)
        attended = scatter_row(3, dot(mixed, out_own, low))[0]
    resid = inputs + attended
    scale_two = rms_scale(resid)
    hidden_two = (resid * scale_two * gain_two).astype(low)
    if natural:
        gate_parts = [gate_a, gate_b, gate_a_h, gate_b_h] + list(gate_x)
        up_parts = [up_a, up_b, up_a_h, up_b_h] + list(up_x)
        (
            all_two, inner, gate_factor, up_factor, down_a_x, down_a_xh, down_b_x, down_b_xh,
            grad_home, grad_all,
        ) = feed_forward(
            hidden_two, gate_parts, up_parts, (down_a, down_a_h, down_b, down_b_h), cotangent, 4
        )
    else:
        all_two = gather_row(hidden_two, 4)
        gate = dot(all_two, gate_own)
        upward = dot(all_two, up_own)
        sigma = jax.nn.sigmoid(gate)
        inner = (gate * sigma * upward).astype(low)
        grad_down = outer_sum(inner, grad_all, low)

    if natural:
        (
            dhidden_two, *spread, gate_terms, gate_x, up_terms, up_x, grad_down, _, _
        ) = feed_back(
            grad_all,
            gate_factor,
            up_factor,
            inner,
            all_two,
            gate_parts,
            up_parts,
            [
                (down_a, down_a_h, down_a_x, down_a_xh),
                (down_b, down_b_h, down_b_x, down_b_xh),
            ],
            5,
        )
    else:
        dinner = times_transposed(grad_all, down_own)
        dgate = (dinner * upward * sigma * (1.0 + gate * (1.0 - sigma))).astype(low)
        dupward = (dinner * gate * sigma).astype(low)
        grad_gate, grad_upward = outer_sum(all_two, dgate, low), outer_sum(all_two, dupward, low)
        dhidden_two = times_transposed(dgate, gate_own) + times_transposed(dupward, up_own)
        dhidden_two = scatter_row(5, dhidden_two.astype(low))[0]
        spread = scatter_row(6, dot(inner, down_own, low))[0]
        grad_down = sum_columns(grad_down[:ff_own].reshape(n_x, 2, ff_part, width), 0).astype(wide)
        gate_terms, up_terms = [
            sum_columns(a.reshape(n_x, 2, 2, -1, ff_pad), 1) for a in (grad_gate, grad_upward)
        ]

    dresid_part, dgain_two = norm_back(dhidden_two, resid, scale_two, gain_two)
    dresid = grad_home.astype(wide) + dresid_part
    branch = dresid.astype(low)
    if natural:
        by_h = (2, 2, -1, ff_pad)
        dlow, dkv, gate_terms, up_terms, output, out_terms, head_terms, *_ = middle(
            ends, branch, (gate_terms.reshape(by_h), gate_x.reshape(by_h)),
            (up_terms.reshape(by_h), up_x.reshape(by_h)), spread, query, mixed, packed, logs, cosine,
            sine, out_own, up_query, resid, heads, scale, 7,
        )
        gate_terms, up_terms = [a.reshape(n_group, shard, ff_pad) for a in (gate_terms, up_terms)]
        head_terms = head_terms.reshape(n_group, rows_up, heads * head_dim)
        summed, grad_tokens, grad_gate, grad_upward, grad_uquery, grad_out = shut(
            dlow, dkv, latent, gain_latent[None], own_cos, own_sin, hidden,
            in_full.reshape(n_dev, shard, -1), home, gain_one[None], dresid, dgain_two[None],
            gate_terms, up_terms, head_terms, pick(out_terms, h), pick(out_terms, 1 - h), ff_part,
            order, 9,
        )
    else:
        branch_all = gather_row(branch, 7)
        grad_out = outer_sum(mixed, branch_all, low)
        dmixed = times_transposed(branch_all, out_own, low)
        dquery, dkv = attend_back(
            ends, query, dmixed, mixed, packed, logs, cosine, sine, heads, scale
        )
        dlow = times_transposed(dquery, up_query, low)
        head_terms = outer_sum(all_latent, dquery, low).reshape(n_x, 2, 2, -1, heads * head_dim)
        dlow, dkv = scatter_row(8, dlow, dkv)
        whole = jnp.zeros((n_group * heads * head_dim, width), wide)
        whole = lax.dynamic_update_slice_in_dim(
            whole, grad_out.astype(wide), me * heads * head_dim, 0
        )
        grad_out = lax.psum_scatter(whole, every, scatter_dimension=0, tiled=True)
        final = (resid + spread).astype(low)
        dkeys = rotate_back(dkv[:, :head_dim], own_cos, own_sin).astype(low)
        dvalues = dkv[:, head_dim:].astype(low)
        dlatent, dgain_latent = norm_back(dlow, latent, scale_latent, gain_latent)
        nothing = jnp.zeros((count, 128), low)
        dmapped = jnp.concatenate([dlatent.astype(low), dkeys, dvalues, nothing], axis=1)
        dhidden = times_transposed(dmapped, in_full)
        dinput_part, dgain_one = norm_back(dhidden, inputs, scale_one, gain_one)
        grad_tokens = (dresid + dinput_part).astype(low)
        grad_in = outer_sum(hidden, dmapped[:, :mapped_width], low).reshape(n_dev, shard, -1)
        gain_terms = jnp.zeros((n_dev, shard, 128), low)
        gain_terms = gain_terms.at[:, 0, :shard].set(dgain_one.reshape(n_dev, -1).astype(low))
        gain_terms = gain_terms.at[:, 1, :shard].set(dgain_two.reshape(n_dev, -1).astype(low))
        gain_terms = gain_terms.at[:, 2, : query_gain.shape[0]].set(
            dgain_latent.reshape(n_dev, -1).astype(low)
        )
        terms = jnp.concatenate([grad_in, gain_terms], axis=2)
        summed = lax.psum_scatter(terms.astype(wide), every, scatter_dimension=0, tiled=False)
        grad_tokens, output = swap_home(grad_tokens), swap_home(final)
        head_terms = all_to_all_row(
            sum_columns(head_terms, 1).reshape(n_group, rows_up, heads * head_dim)
        )
        gate_terms, up_terms = [
            all_to_all_row(a.reshape(n_group, shard, ff_pad)) for a in (gate_terms, up_terms)
        ]
        grad_gate, grad_upward = join_columns(gate_terms, up_terms, ff_part, order)
        grad_uquery = head_terms.transpose(1, 0, 2).reshape(rows_up, -1).astype(wide)
    return (
        output,
        grad_tokens.astype(wide),
        summed[0, mapped_width : mapped_width + shard],
        summed[:, :latent_width],
        summed[2, mapped_width : mapped_width + query_gain.shape[0]],
        grad_uquery,
        summed[:, latent_width : latent_width + head_dim],
        summed[:, latent_width + head_dim : mapped_width],
        grad_out,
        summed[1, mapped_width : mapped_width + shard],
        grad_gate,
        grad_upward,
        grad_down,
    )


def solution(mesh):
    n_dp, n_seq = mesh.shape["dp"], mesh.shape["seq"]
    fine = Mesh(mesh.devices.reshape(n_dp // 2, 2, 2, n_seq // 4, 2), every)
    rows, flat = P(every, None), P(every)
    placed = (rows, P(("x", "c"), None), rows, flat, rows, flat) + (rows,) * 4 + (flat,) + (rows,) * 3
    return jax.shard_map(
        on_device,
        mesh=fine,
        in_specs=placed,
        out_specs=(rows, rows, flat, rows, flat) + (rows,) * 4 + (flat,) + (rows,) * 3,
        check_vma=False,
    )
```
